32 devices in a mesh: section: 2 (over core), dp: 16 (over z, y, x).
Axes of the slice: x: 2, y: 2, z: 4, core: 2. Of those that a mesh axis runs over, the one named last changes fastest.
Arguments:
- boundary: bfloat16 [2, 8192, 768], P('section', 'dp'), may hold values from -6 to 6
- lengths: int32 [32], P('dp'), may hold values from 64 to 256, as said below
- attn_norm_gain: bfloat16 [2, 768], P('section'), may hold values from 0.5 to 1.5
- attn_norm_bias: bfloat16 [2, 768], P('section'), may hold values from -1.75 to 1.75
- qkv_weight: bfloat16 [2, 768, 2304], P('section'), may hold values from -0.21875 to 0.21875
- qkv_bias: bfloat16 [2, 2304], P('section'), may hold values from -1.75 to 1.75
- proj_weight: bfloat16 [2, 768, 768], P('section'), may hold values from -1.25 to 1.25
- proj_bias: bfloat16 [2, 768], P('section'), may hold values from -1.75 to 1.75
- mlp_norm_gain: bfloat16 [2, 768], P('section'), may hold values from 0.5 to 1.5
- mlp_norm_bias: bfloat16 [2, 768], P('section'), may hold values from -1.75 to 1.75
- up_weight: bfloat16 [2, 768, 3072], P('section'), may hold values from -0.21875 to 0.21875
- up_bias: bfloat16 [2, 3072], P('section'), may hold values from -1.75 to 1.75
- down_weight: bfloat16 [2, 3072, 768], P('section'), may hold values from -0.109375 to 0.109375
- down_bias: bfloat16 [2, 768], P('section'), may hold values from -1.75 to 1.75
Outputs:
- boundary_out: bfloat16 [2, 8192, 768], P('section', 'dp')
- grad_attn_norm_gain: float32 [2, 768], P('section', 'dp')
- grad_attn_norm_bias: float32 [2, 768], P('section', 'dp')
- grad_qkv_weight: float32 [2, 768, 2304], P('section', 'dp')
- grad_qkv_bias: float32 [2, 2304], P('section', 'dp')
- grad_proj_weight: float32 [2, 768, 768], P('section', 'dp')
- grad_proj_bias: float32 [2, 768], P('section', 'dp')
- grad_mlp_norm_gain: float32 [2, 768], P('section', 'dp')
- grad_mlp_norm_bias: float32 [2, 768], P('section', 'dp')
- grad_up_weight: float32 [2, 768, 3072], P('section', 'dp')
- grad_up_bias: float32 [2, 3072], P('section', 'dp')
- grad_down_weight: float32 [2, 3072, 768], P('section', 'dp')
- grad_down_bias: float32 [2, 768], P('section', 'dp')
The draws below stay inside these ranges and needn't reach their ends.
Inputs may be any that keep to these rules, and one draw needn't show every extreme that they name: `lengths`: real tokens of each sentence counted from its start; some sentence has exactly 256 and some exactly 64.
All inputs are finite; a program needn't handle non-finite values.
Results may differ from the reference program's by a relative error of at most 0.012.
Values may be sent and summed in bfloat16 or wider, within the bound.
No kernel may reach another device: no remote copies, remote signals or barrier semaphores. Data moves between devices by JAX's collectives and lax.ppermute only.
A program may use at most 192 MiB of HBM per device.

```python
import jax
import jax.numpy as jnp
from jax import lax

D = 768
HEAD = 64
FF = 3072
LEN = 256
SENTS = 32
TOKENS = 8192


def draw_lengths(key, part):
    key = jax.random.fold_in(key, 11)
    key_draw, key_order = jax.random.split(key)
    drawn = jax.random.randint(key_draw, (SENTS,), LEN // 4, LEN + 1, dtype=jnp.int32)
    order = jax.random.permutation(key_order, SENTS)
    return drawn.at[order[0]].set(LEN).at[order[1]].set(LEN // 4)


def raised(entries, stream_key, source, target, blocks, factor):
    def block_of(position):
        return (jnp.arange(entries.shape[position]) // (entries.shape[position] // blocks)).reshape((-1,) + (1,) * (entries.ndim - 1 - position))

    one_side = jax.random.permutation(stream_key, blocks)[block_of(target)]
    far = (block_of(target) + blocks // 2) % blocks
    return jnp.where((block_of(source) == one_side) | (block_of(source) == far), factor * entries, entries)


def level_of(key, shape, pieces, least, top_value):
    factor_of = 1.0
    for dim, shards_of in pieces:
        draws = jax.random.uniform(jax.random.fold_in(jax.random.fold_in(key, 6), dim), (shards_of,), jnp.float32, least / len(pieces), top_value / len(pieces))
        factor_of = factor_of * jnp.repeat(jnp.exp(draws), shape[dim] // shards_of).reshape((-1,) + (1,) * (len(shape) - 1 - dim))
    return factor_of


def scatter_about(key, dims, scale, bound, cuts=(), kind=jnp.bfloat16):
    values = scale * jax.random.normal(key, dims, jnp.float32)
    if cuts:
        values = values * level_of(key, dims, cuts, -0.22, 0.18)
    return jnp.clip(values, -bound, bound).astype(kind)


def heavy_noise(stream_key, shape, spread, limit, shards, heavy, held_as=jnp.bfloat16):
    result = spread * jax.random.normal(stream_key, shape, jnp.float32)
    if shards:
        result = result * level_of(stream_key, shape, shards, -0.22, 0.18)
    return jnp.clip(raised(result, jax.random.fold_in(stream_key, 3), *heavy), -limit, limit).astype(held_as)


def setup_inputs(seed: int = 0) -> dict:
    keys = jax.random.split(jax.random.key(seed), 15)
    return {
        "boundary": heavy_noise(keys[0], (2, TOKENS, D), 1.0, 6.0, ((0, 2), (1, 16)), (1, 2, 16, 2.0)),
        "lengths": draw_lengths(jax.random.fold_in(keys[14], 71), 0),
        "attn_norm_gain": jnp.clip(1.0 + 0.1 * jax.random.normal(keys[2], (2, D), jnp.float32), 0.5, 1.5).astype(jnp.bfloat16),
        "attn_norm_bias": scatter_about(keys[3], (2, D), 0.3, 1.75, ((0, 2),)),
        "qkv_weight": scatter_about(keys[4], (2, D, 3 * D), D ** -0.5, 0.21875, ((0, 2),)),
        "qkv_bias": scatter_about(keys[5], (2, 3 * D), 0.3, 1.75, ((0, 2),)),
        "proj_weight": scatter_about(keys[6], (2, D, D), (D // 32) ** -0.5, 1.25, ((0, 2),)),
        "proj_bias": scatter_about(keys[7], (2, D), 0.3, 1.75, ((0, 2),)),
        "mlp_norm_gain": jnp.clip(1.0 + 0.1 * jax.random.normal(keys[8], (2, D), jnp.float32), 0.5, 1.5).astype(jnp.bfloat16),
        "mlp_norm_bias": scatter_about(keys[9], (2, D), 0.3, 1.75, ((0, 2),)),
        "up_weight": scatter_about(keys[10], (2, D, FF), D ** -0.5, 0.21875, ((0, 2),)),
        "up_bias": scatter_about(keys[11], (2, FF), 0.3, 1.75, ((0, 2),)),
        "down_weight": scatter_about(keys[12], (2, FF, D), FF ** -0.5, 0.109375, ((0, 2),)),
        "down_bias": scatter_about(keys[13], (2, D), 0.3, 1.75, ((0, 2),)),
    }


EPS = 1e-05
NEG_FILL = -1e+30
HIGH = lax.Precision.HIGHEST

@jax.custom_vjp
def low(v):
    return lax.optimization_barrier(v.astype(jnp.bfloat16)).astype(jnp.float32)

@jax.custom_vjp
def low_back(v):
    return v

def low_keep(v):
    return (low(v), None)

def low_pass(kept, grad):
    return (grad,)

def back_keep(v):
    return (v, None)

def back_low(kept, grad):
    return (low(grad),)
low.defvjp(low_keep, low_pass)
low_back.defvjp(back_keep, back_low)

def layer_norm(values, gain_vec, bias_vec):
    mean_value = lax.optimization_barrier(jnp.mean(values, axis=-1, keepdims=True))
    centred = values - mean_value
    variance = lax.optimization_barrier(jnp.mean(centred * centred, axis=-1, keepdims=True))
    return centred * lax.rsqrt(variance + EPS) * gain_vec + bias_vec

def gelu_erf(values):
    return 0.5 * values * (1.0 + jax.scipy.special.erf(values * 0.7071067811865476))

def rotary_tables(seq_len, head_dim):
    rot_dims = head_dim // 4
    half_rot = rot_dims // 2
    frequency = 10000.0 ** (-(jnp.arange(half_rot, dtype=jnp.float32) * 2.0 / rot_dims))
    angles = jnp.arange(seq_len, dtype=jnp.float32)[:, None] * frequency[None, :]
    return (jnp.cos(angles), jnp.sin(angles))

def rotate(values, cosine_table, sine_table, direction):
    half_rot = cosine_table.shape[1]
    first_half = values[..., :half_rot]
    second_half = values[..., half_rot:2 * half_rot]
    cosine_part = cosine_table[:, None, :]
    sine_part = sine_table[:, None, :] * direction
    return jnp.concatenate([first_half * cosine_part - second_half * sine_part, second_half * cosine_part + first_half * sine_part, values[..., 2 * half_rot:]], axis=-1)

def sentence_attention(parts):
    queries, key_rows, value_rows, length = parts
    seq_len = queries.shape[0]
    raw_scores = jnp.einsum('qhe,khe->hqk', queries, key_rows, precision=HIGH)
    scores = low_back(raw_scores * HEAD ** (-0.5))
    positions = jnp.arange(seq_len)
    allowed = (positions[None, :] <= positions[:, None]) & (positions[None, :] < length)
    scores = jnp.where(allowed[None], scores, NEG_FILL)
    row_max = lax.optimization_barrier(jnp.max(scores, axis=-1, keepdims=True))
    exponent = jnp.exp(scores - row_max)
    probs_f32 = exponent / lax.optimization_barrier(jnp.sum(exponent, axis=-1, keepdims=True))
    return jnp.einsum('hqk,khe->qhe', low(probs_f32), value_rows, precision=HIGH)

def layer_apply(inputs, params, lengths, tables):
    gain_a, shift_a, weight_qkv, bias_qkv, weight_proj, bias_proj, gain_b, shift_b, weight_up, bias_up, weight_down, bias_down = params
    sentences, seq_len, width = inputs.shape
    head_count = width // HEAD
    cosine_table, sine_table = tables
    flat = inputs.reshape(-1, width)
    normed_a = low(layer_norm(flat, gain_a, shift_a))
    packed = low_back(jnp.dot(normed_a, weight_qkv, precision=HIGH) + bias_qkv)
    packed = packed.reshape(sentences, seq_len, 3, head_count, HEAD)
    queries = low(rotate(packed[:, :, 0], cosine_table, sine_table, 1.0))
    key_rows = low(rotate(packed[:, :, 1], cosine_table, sine_table, 1.0))
    value_rows = low(packed[:, :, 2])
    attended = lax.map(jax.checkpoint(sentence_attention), (queries, key_rows, value_rows, lengths))
    mixed_heads = low(low_back(attended.reshape(-1, width)))
    normed_b = low(layer_norm(flat, gain_b, shift_b))
    up_proj = low_back(jnp.dot(normed_b, weight_up, precision=HIGH) + bias_up)
    hidden = low(gelu_erf(up_proj))
    branch = jnp.dot(mixed_heads, weight_proj, precision=HIGH) + bias_proj + jnp.dot(hidden, weight_down, precision=HIGH) + bias_down
    return (flat + low_back(branch)).reshape(inputs.shape)

def reference(boundary, lengths, attn_norm_gain, attn_norm_bias, qkv_weight, qkv_bias, proj_weight, proj_bias, mlp_norm_gain, mlp_norm_bias, up_weight, up_bias, down_weight, down_bias):
    stacked = tuple((piece.astype(jnp.float32) for piece in (attn_norm_gain, attn_norm_bias, qkv_weight, qkv_bias, proj_weight, proj_bias, mlp_norm_gain, mlp_norm_bias, up_weight, up_bias, down_weight, down_bias)))
    width = boundary.shape[2]
    start_rows = boundary[0].astype(jnp.float32).reshape(SENTS, LEN, width)
    cotangent = boundary[1].astype(jnp.float32).reshape(SENTS, LEN, width)
    tables = rotary_tables(LEN, HEAD)

    def forward(first_input, weights):
        lower_layer = tuple((piece[0] for piece in weights))
        upper_layer = tuple((piece[1] for piece in weights))
        middle = low_back(low(layer_apply(first_input, lower_layer, lengths, tables)))
        return layer_apply(middle, upper_layer, lengths, tables)
    final, pullback = jax.vjp(forward, start_rows, stacked)
    grad_input, grad_weights = pullback(cotangent)
    boundary_out = jnp.stack([grad_input.reshape(-1, width), final.reshape(-1, width)]).astype(jnp.bfloat16)
    return (boundary_out, grad_weights[0], grad_weights[1], grad_weights[2], grad_weights[3], grad_weights[4], grad_weights[5], grad_weights[6], grad_weights[7], grad_weights[8], grad_weights[9], grad_weights[10], grad_weights[11])
```

```python
import functools
import math

import jax
import jax.numpy as jnp
import numpy as np
from jax import lax
from jax.experimental import pallas as pl
from jax.experimental.pallas import tpu as pltpu
from jax.sharding import PartitionSpec as P

HEAD = 64
EPS = 1e-05
NEG_FILL = -1e30
VMEM_BYTES = 56 * 1024 * 1024
F32 = jnp.float32
BF16 = jnp.bfloat16


def dot(left, right):
    return jnp.dot(left, right, preferred_element_type=F32)


def dot_nt(left, right):
    return lax.dot_general(left, right, (((1,), (1,)), ((), ())), preferred_element_type=F32)


def normalised(values):
    centred = values - jnp.mean(values, axis=-1, keepdims=True)
    variance = jnp.mean(centred * centred, axis=-1, keepdims=True)
    scale = lax.rsqrt(variance + EPS)
    return centred * scale, scale


def gelu_parts(values):
    bell = jnp.exp(values * values * -0.5)
    t = 1.0 / (1.0 + (0.3275911 * math.sqrt(0.5)) * jnp.abs(values))
    poly = 0.5 * 1.061405429
    for coefficient in (-1.453152027, 1.421413741, -0.284496736, 0.254829592):
        poly = poly * t + 0.5 * coefficient
    tail = poly * t * bell
    integral = jnp.where(values >= 0.0, 1.0 - tail, tail)
    return values * integral, integral + values * bell * (1.0 / math.sqrt(2.0 * math.pi))


def rotary_lanes(seq_len, lanes):
    rot_dims = HEAD // 4
    half = rot_dims // 2
    frequency = np.float32(10000.0) ** (-(np.arange(half, dtype=np.float32) * np.float32(2.0) / np.float32(rot_dims)))
    angles = np.arange(seq_len, dtype=np.float32)[:, None] * frequency.astype(np.float32)[None, :]
    cosine, sine = np.cos(angles).astype(np.float32), np.sin(angles).astype(np.float32)
    same = np.ones((seq_len, HEAD), np.float32)
    later = np.zeros((seq_len, HEAD), np.float32)
    earlier = np.zeros((seq_len, HEAD), np.float32)
    same[:, :half] = cosine
    same[:, half:rot_dims] = cosine
    later[:, :half] = -sine
    earlier[:, half:rot_dims] = sine
    return [np.tile(t, (1, lanes // HEAD)) for t in (same, later, earlier)]


def turned(values, same, later, earlier, sign):
    half = HEAD // 8
    width = values.shape[1]
    ahead = pltpu.roll(values, width - half, 1)
    behind = pltpu.roll(values, half, 1)
    if sign > 0:
        return values * same + ahead * later + behind * earlier
    return values * same - ahead * later - behind * earlier


def forward_kernel(
    groups, scalars, own, arriving, gain_a, shift_a, gain_b, shift_b, wq, wk, wv, bq, bk, bv, wp, bp, wu, bu, wd, bd,
    same, later, earlier,
    y_out, x_out, na_out, nb_out, q_out, k_out, v_out, pt_out, mixed_out, hidden_out, slope_out, total,
):
    step = pl.program_id(0)
    length = scalars[2]

    @pl.when(step == 0)
    def _():
        x_low = jnp.where(scalars[1] == 1, own[0], arriving[...])
        x_out[0] = x_low
        x = x_low.astype(F32)
        xhat, _ = normalised(x)
        na_out[0] = (xhat * gain_a[...].astype(F32) + shift_a[...].astype(F32)).astype(BF16)
        nb_out[0] = (xhat * gain_b[...].astype(F32) + shift_b[...].astype(F32)).astype(BF16)
        total[...] = x + (bp[...].astype(F32) + bd[...].astype(F32))

    rows = na_out.shape[1]
    na = na_out[0]
    tables = (same[...], later[...], earlier[...])
    q8 = (turned(dot(na, wq[0]) + bq[...].astype(F32), *tables, 1) * (HEAD**-0.5)).astype(BF16)
    k = turned(dot(na, wk[0]) + bk[...].astype(F32), *tables, 1).astype(BF16)
    v = (dot(na, wv[0]) + bv[...].astype(F32)).astype(BF16)
    q_out[0] = q8
    k_out[0] = k
    v_out[0] = v
    vt = v.T
    key_pos = lax.broadcasted_iota(jnp.int32, (rows, rows), 0)
    query_pos = lax.broadcasted_iota(jnp.int32, (rows, rows), 1)
    bias = jnp.where((key_pos <= query_pos) & (key_pos < length), 0.0, NEG_FILL)
    lane = lax.broadcasted_iota(jnp.int32, (rows, 2 * HEAD), 1)
    heads = q8.shape[1] // HEAD
    mixed_t = []
    for head in range(heads):
        pair = slice(head // 2 * 2 * HEAD, head // 2 * 2 * HEAD + 2 * HEAD)
        k_one = jnp.where((lane < HEAD) == (head % 2 == 0), k[:, pair], jnp.zeros_like(k[:, pair]))
        scores = dot_nt(k_one, q8[:, pair]) + bias
        exponent = jnp.exp(scores - jnp.max(scores, axis=0, keepdims=True))
        pt = (exponent * (1.0 / jnp.sum(exponent, axis=0, keepdims=True))).astype(BF16)
        pt_out[0, head] = pt
        mixed_t.append(dot(vt[head * HEAD : head * HEAD + HEAD], pt))
    mixed = jnp.concatenate(mixed_t, axis=0).T.astype(BF16)
    mixed_out[0] = mixed
    up = dot(nb_out[0], wu[0]) + bu[...].astype(F32)
    hidden, slope = gelu_parts(up)
    hidden = hidden.astype(BF16)
    hidden_out[0] = hidden
    slope_out[0] = slope.astype(BF16)
    total[...] += dot(mixed, wp[0]) + dot(hidden, wd[0])

    @pl.when(step == groups - 1)
    def _():
        y_out[...] = total[...].astype(BF16)


def backward_kernel(
    groups, scalars, own, arriving, x_in, gain_a, gain_b, wq, wk, wv, wp, wu, wd, same, later, earlier,
    q_in, k_in, v_in, pt_in, slope_in,
    gx_out, gy_out, gq_out, gk_out, gv_out, gu_out, vec_out, total_a, total_b,
):
    step = pl.program_id(0)

    @pl.when(step == 0)
    def _():
        gy_out[0] = jnp.where(scalars[1] == 1, arriving[...], own[0])
        total_a[...] = jnp.zeros_like(total_a)
        total_b[...] = jnp.zeros_like(total_b)

    rows = gy_out.shape[1]
    gy = gy_out[0]
    grad_hidden = dot_nt(gy, wd[0])
    gu = (grad_hidden * slope_in[0].astype(F32)).astype(BF16)
    gu_out[0] = gu
    total_b[...] += dot_nt(gu, wu[0])
    gm = dot_nt(gy, wp[0]).astype(BF16)
    q8, k, v = q_in[0], k_in[0], v_in[0]
    kt = k.T
    lane = lax.broadcasted_iota(jnp.int32, (rows, 2 * HEAD), 1)
    heads = q8.shape[1] // HEAD
    gq_t, gk_parts, gv_parts = [], [], []
    for pair_index in range(heads // 2):
        pair = slice(pair_index * 2 * HEAD, pair_index * 2 * HEAD + 2 * HEAD)
        gk_pair, gv_pair = None, None
        for side in range(2):
            head = pair_index * 2 + side
            here = (lane < HEAD) == (side == 0)
            gm_one = jnp.where(here, gm[:, pair], jnp.zeros_like(gm[:, pair]))
            q_one = jnp.where(here, q8[:, pair], jnp.zeros_like(q8[:, pair]))
            pt = pt_in[0, head]
            gp = dot_nt(v[:, pair], gm_one)
            weighted = pt.astype(F32) * gp
            inner = jnp.sum(weighted, axis=0, keepdims=True)
            gs = (weighted - pt.astype(F32) * inner).astype(BF16)
            gv_one = dot(pt, gm_one)
            gk_one = dot(gs, q_one)
            gq_t.append(dot(kt[head * HEAD : head * HEAD + HEAD], gs))
            gv_pair = gv_one if gv_pair is None else gv_pair + gv_one
            gk_pair = gk_one if gk_pair is None else gk_pair + gk_one
        gk_parts.append(gk_pair)
        gv_parts.append(gv_pair)
    tables = (same[...], later[...], earlier[...])
    gq = jnp.concatenate(gq_t, axis=0).T * (HEAD**-0.5)
    gq = turned(gq, *tables, -1).astype(BF16)
    gk = turned(jnp.concatenate(gk_parts, axis=1), *tables, -1).astype(BF16)
    gv = jnp.concatenate(gv_parts, axis=1).astype(BF16)
    gq_out[0] = gq
    gk_out[0] = gk
    gv_out[0] = gv
    total_a[...] += dot_nt(gq, wq[0]) + dot_nt(gk, wk[0]) + dot_nt(gv, wv[0])

    @pl.when(step == groups - 1)
    def _():
        xhat, scale = normalised(x_in[0].astype(F32))
        grad_a, grad_b = total_a[...], total_b[...]
        sums = [jnp.sum(t, axis=0, keepdims=True) for t in (grad_a * xhat, grad_a, grad_b * xhat, grad_b)]
        vec_out[0] = jnp.concatenate(sums + [jnp.zeros((4, sums[0].shape[1]), F32)], axis=0)
        both = grad_a * gain_a[...].astype(F32) + grad_b * gain_b[...].astype(F32)
        inner = jnp.mean(both * xhat, axis=-1, keepdims=True)
        gx = gy.astype(F32) + scale * (both - jnp.mean(both, axis=-1, keepdims=True) - xhat * inner)
        gx_out[...] = gx.astype(BF16)


def whole(shape):
    return pl.BlockSpec(shape, lambda g, s: (0,) * len(shape))


def slot_whole(*shape):
    return pl.BlockSpec((1,) + shape, lambda g, s: (s[0],) + (0,) * len(shape))


def slot_columns(rows, columns):
    return pl.BlockSpec((1, rows, columns), lambda g, s: (s[0], 0, g))


def section_columns(rows, columns, offset=0):
    return pl.BlockSpec((1, rows, columns), lambda g, s: (0, 0, offset + g))


def vector_columns(columns, offset=0):
    return pl.BlockSpec((1, columns), lambda g, s: (0, offset + g))


def section_rows(rows, columns):
    return pl.BlockSpec((1, rows, columns), lambda g, s: (0, g, 0))


def sizes(params, rows):
    width = params[0].shape[1]
    units = params[8].shape[2]
    groups = width // 256
    return width, units, groups, width // groups, units // groups


def forward_tick(scalars, local_rows, arriving, params, tables, saved):
    (gain_a, shift_a, w_qkv, b_qkv, w_proj, b_proj, gain_b, shift_b, w_up, b_up, w_down, b_down) = params
    slots, rows, width = local_rows.shape
    width, units, groups, lanes, chunk = sizes(params, rows)
    heads = width // HEAD
    per = heads // groups
    in_specs = [
        slot_whole(rows, width), whole((rows, width)), whole((1, width)), whole((1, width)), whole((1, width)), whole((1, width)),
        section_columns(width, lanes), section_columns(width, lanes, groups), section_columns(width, lanes, 2 * groups),
        vector_columns(lanes), vector_columns(lanes, groups), vector_columns(lanes, 2 * groups),
        section_rows(lanes, width), whole((1, width)),
        section_columns(width, chunk), vector_columns(chunk), section_rows(chunk, width), whole((1, width)),
    ] + [whole((rows, lanes))] * 3
    operands = [
        local_rows, arriving, gain_a, shift_a, gain_b, shift_b, w_qkv, w_qkv, w_qkv, b_qkv, b_qkv, b_qkv, w_proj, b_proj,
        w_up, b_up, w_down, b_down,
    ] + list(tables)
    out_specs = [
        whole((rows, width)), slot_whole(rows, width), slot_whole(rows, width), slot_whole(rows, width),
        slot_columns(rows, lanes), slot_columns(rows, lanes), slot_columns(rows, lanes),
        pl.BlockSpec((1, per, rows, rows), lambda g, s: (s[0], g, 0, 0)),
        slot_columns(rows, lanes), slot_columns(rows, chunk), slot_columns(rows, chunk),
    ]
    out_shape = [jax.ShapeDtypeStruct((rows, width), BF16)] + [jax.ShapeDtypeStruct((slots, rows, width), BF16)] * 6 + [
        jax.ShapeDtypeStruct((slots, heads, rows, rows), BF16),
        jax.ShapeDtypeStruct((slots, rows, width), BF16),
        jax.ShapeDtypeStruct((slots, rows, units), BF16),
        jax.ShapeDtypeStruct((slots, rows, units), BF16),
    ]
    aliases = {}
    kernel = functools.partial(forward_kernel, groups)
    if saved is not None:
        count = len(operands)
        inner = kernel

        def kernel(scalars, *refs):
            return inner(scalars, *refs[:count], *refs[count + len(saved):])

        in_specs = in_specs + [pl.BlockSpec(memory_space=pl.ANY)] * len(saved)
        operands = operands + list(saved)
        aliases = {1 + count + i: 1 + i for i in range(len(saved))}
    outs = pl.pallas_call(
        kernel,
        grid_spec=pltpu.PrefetchScalarGridSpec(
            num_scalar_prefetch=1, grid=(groups,), in_specs=in_specs, out_specs=out_specs,
            scratch_shapes=[pltpu.VMEM((rows, width), F32)],
        ),
        out_shape=out_shape,
        input_output_aliases=aliases,
        compiler_params=pltpu.CompilerParams(vmem_limit_bytes=VMEM_BYTES),
        cost_estimate=pl.CostEstimate(flops=2 * rows * (4 * width * width + 2 * width * units), bytes_accessed=22 << 20, transcendentals=0),
        name="layer_forward",
    )(scalars, *operands)
    return outs[0], outs[1:]


def backward_tick(scalars, local_rows, arriving, params, tables, saved, grads):
    (gain_a, shift_a, w_qkv, b_qkv, w_proj, b_proj, gain_b, shift_b, w_up, b_up, w_down, b_down) = params
    x_s, na_s, nb_s, q_s, k_s, v_s, pt_s, mixed_s, hidden_s, slope_s = saved
    slots, rows, width = local_rows.shape
    width, units, groups, lanes, chunk = sizes(params, rows)
    heads = width // HEAD
    per = heads // groups
    in_specs = [
        slot_whole(rows, width), whole((rows, width)), slot_whole(rows, width), whole((1, width)), whole((1, width)),
        section_columns(width, lanes), section_columns(width, lanes, groups), section_columns(width, lanes, 2 * groups),
        section_rows(lanes, width), section_columns(width, chunk), section_rows(chunk, width),
    ] + [whole((rows, lanes))] * 3 + [
        slot_columns(rows, lanes), slot_columns(rows, lanes), slot_columns(rows, lanes),
        pl.BlockSpec((1, per, rows, rows), lambda g, s: (s[0], g, 0, 0)),
        slot_columns(rows, chunk),
    ]
    operands = [
        local_rows, arriving, x_s, gain_a, gain_b, w_qkv, w_qkv, w_qkv, w_proj, w_up, w_down,
    ] + list(tables) + [q_s, k_s, v_s, pt_s, slope_s]
    out_specs = [
        whole((rows, width)), slot_whole(rows, width),
        slot_columns(rows, lanes), slot_columns(rows, lanes), slot_columns(rows, lanes), slot_columns(rows, chunk),
        slot_whole(8, width),
    ]
    out_shape = [jax.ShapeDtypeStruct((rows, width), BF16)] + [jax.ShapeDtypeStruct((slots, rows, width), BF16)] * 4 + [
        jax.ShapeDtypeStruct((slots, rows, units), BF16),
        jax.ShapeDtypeStruct((slots, 8, width), F32),
    ]
    aliases = {}
    kernel = functools.partial(backward_kernel, groups)
    if grads is not None:
        count = len(operands)
        inner = kernel

        def kernel(scalars, *refs):
            return inner(scalars, *refs[:count], *refs[count + len(grads):])

        in_specs = in_specs + [pl.BlockSpec(memory_space=pl.ANY)] * len(grads)
        operands = operands + list(grads)
        aliases = {1 + count + i: 1 + i for i in range(len(grads))}
    outs = pl.pallas_call(
        kernel,
        grid_spec=pltpu.PrefetchScalarGridSpec(
            num_scalar_prefetch=1, grid=(groups,), in_specs=in_specs, out_specs=out_specs,
            scratch_shapes=[pltpu.VMEM((rows, width), F32)] * 2,
        ),
        out_shape=out_shape,
        input_output_aliases=aliases,
        compiler_params=pltpu.CompilerParams(vmem_limit_bytes=VMEM_BYTES),
        cost_estimate=pl.CostEstimate(flops=2 * rows * (4 * width * width + 2 * width * units), bytes_accessed=22 << 20, transcendentals=0),
        name="layer_backward",
    )(scalars, *operands)
    return outs[0], outs[1:]


def place(scratch, parts, chunk_count, first_bit, mine):
    rows = sum(part.shape[0] for part in parts[0])
    half = chunk_count // 2
    for chunk in range(chunk_count):
        rest = (chunk >> (first_bit + 1) << first_bit) | (chunk & ((1 << first_bit) - 1))
        side = ((chunk >> first_bit) & 1) ^ mine
        start = pl.multiple_of(side * (half * rows) + rest * rows, 16)
        for part in parts[chunk]:
            scratch[pl.ds(start, part.shape[0]), :] = part
            start = pl.multiple_of(start + part.shape[0], 16)


def ones_dot(values):
    return dot(jnp.ones((16, values.shape[0]), BF16), values)[:8]


def down_proj_kernel(chunks, bit, scalars, hidden, mixed, gy, keep_out, send_out, sums_out, mixed_t, left):
    step = pl.program_id(0)
    rows = gy.shape[0] * gy.shape[1]
    grad = gy[...].reshape(rows, gy.shape[2])

    @pl.when(step == 0)
    def _():
        mixed_t[...] = mixed[...].reshape(rows, mixed.shape[2]).T
        sums_out[...] = ones_dot(grad)

    hidden_t = hidden[...].reshape(rows, hidden.shape[2]).T
    proj_rows = mixed_t.shape[0] // pl.num_programs(0)
    part_t = mixed_t[pl.ds(pl.multiple_of(step * proj_rows, 16), proj_rows), :]
    tall, low = hidden_t.shape[0] // chunks, proj_rows // chunks
    place(
        left,
        [[hidden_t[c * tall : c * tall + tall], part_t[c * low : c * low + low]] for c in range(chunks)],
        chunks, bit, scalars[bit],
    )
    product = dot(left[...], grad).astype(BF16)
    half = product.shape[0] // 2
    keep_out[...] = product[:half].reshape(keep_out.shape)
    send_out[...] = product[half:].reshape(send_out.shape)


def column_kernel(chunk_count, bit, scalars, normed, grad_refs, keep_out, send_out, sums_out, left):
    step = pl.program_id(0)
    rows = normed.shape[0] * normed.shape[1]

    @pl.when(step == 0)
    def _():
        normed_t = normed[...].reshape(rows, normed.shape[2]).T
        low = normed_t.shape[0] // chunk_count
        place(left, [[normed_t[c * low : c * low + low]] for c in range(chunk_count)], chunk_count, bit, scalars[bit])

    def emit(grad_ref):
        grad = grad_ref[...].reshape(rows, grad_ref.shape[2])
        product = dot(left[...], grad).astype(BF16)
        half = product.shape[0] // 2
        keep_out[...] = product[:half].reshape(keep_out.shape)
        send_out[...] = product[half:].reshape(send_out.shape)
        sums_out[...] = ones_dot(grad)

    if len(grad_refs) == 1:
        emit(grad_refs[0])
    else:
        for index, grad_ref in enumerate(grad_refs):
            pl.when(step == index)(functools.partial(emit, grad_ref))


def weight_call(kernel, grid, scalars, operands, in_specs, out_specs, out_shape, scratch, flops, name):
    return pl.pallas_call(
        kernel,
        grid_spec=pltpu.PrefetchScalarGridSpec(
            num_scalar_prefetch=1, grid=(grid,), in_specs=in_specs, out_specs=out_specs, scratch_shapes=scratch
        ),
        out_shape=out_shape,
        compiler_params=pltpu.CompilerParams(vmem_limit_bytes=VMEM_BYTES),
        cost_estimate=pl.CostEstimate(flops=flops, bytes_accessed=8 << 20, transcendentals=0),
        name=name,
    )(scalars, *operands)


def down_proj_grads(scalars, hidden, mixed, gy, count, bit):
    slots, rows, units = hidden.shape
    width = gy.shape[2]
    steps = 4
    chunks = count // steps
    tall = units // count + width // count
    out = jax.ShapeDtypeStruct((count // 2, tall, width), BF16)
    block = pl.BlockSpec((chunks // 2, tall, width), lambda g, s: (g, 0, 0))
    return weight_call(
        functools.partial(down_proj_kernel, chunks, bit), steps, scalars, [hidden, mixed, gy],
        [pl.BlockSpec((slots, rows, units // steps), lambda g, s: (0, 0, g)), whole((slots, rows, width)), whole((slots, rows, width))],
        [block, block, whole((8, width))],
        [out, out, jax.ShapeDtypeStruct((8, width), F32)],
        [pltpu.VMEM((width, slots * rows), BF16), pltpu.VMEM((chunks * tall, slots * rows), BF16)],
        2 * slots * rows * width * (units + width), "down_proj_grads",
    )


def column_grads(scalars, normed, grads, columns, count, bit, name):
    slots, rows, width = normed.shape
    total = sum(grad.shape[2] for grad in grads)
    low = width // count
    out = jax.ShapeDtypeStruct((count // 2, low, total), BF16)
    block = pl.BlockSpec((count // 2, low, columns), lambda g, s: (0, 0, g))
    if len(grads) == 1:
        specs = [pl.BlockSpec((slots, rows, columns), lambda g, s: (0, 0, g))]
    else:
        specs = [whole((slots, rows, columns))] * len(grads)

    def kernel(scalars_ref, normed_ref, *refs):
        column_kernel(count, bit, scalars_ref, normed_ref, refs[: len(grads)], *refs[len(grads) :])

    return weight_call(
        kernel, total // columns, scalars, [normed] + list(grads), [whole((slots, rows, width))] + specs,
        [block, block, pl.BlockSpec((8, columns), lambda g, s: (0, g))],
        [out, out, jax.ShapeDtypeStruct((8, total), F32)],
        [pltpu.VMEM((width, slots * rows), BF16)],
        2 * slots * rows * width * total, name,
    )


def swap(shard, bit, count):
    return lax.ppermute(shard, "dp", [(i, i ^ (1 << bit)) for i in range(count)])


def parted(values, position, mine):
    count = values.shape[0]
    shaped = values.reshape((count >> (position + 1), 2, 1 << position) + values.shape[1:])
    out = []
    for side in (mine, 1 - mine):
        piece = lax.dynamic_index_in_dim(shaped, side, axis=1, keepdims=False)
        out.append(piece.reshape((count // 2,) + values.shape[1:]))
    return out


def halving_sum(keep, send, order, count, bits, final):
    left = sorted(order)
    for number, bit in enumerate(order):
        left.remove(bit)
        arrived = swap(send, bit, count)
        if number + 1 == len(order):
            return (keep.astype(F32) + arrived.astype(F32)).astype(final)[0]
        position = left.index(order[number + 1])
        keep_a, send_a = parted(keep, position, bits[order[number + 1]])
        keep_b, send_b = parted(arrived, position, bits[order[number + 1]])
        send = (send_a.astype(F32) + send_b.astype(F32)).astype(send_a.dtype)
        keep = (keep_a.astype(F32) + keep_b.astype(F32)).astype(send_a.dtype)


def plain_grads(left, right, count):
    rows = left.shape[0] * left.shape[1]
    product = lax.dot_general(
        left.reshape(rows, -1), right.reshape(rows, -1), (((0,), (0,)), ((), ())), preferred_element_type=F32
    ).astype(BF16)
    return product.reshape(count, product.shape[0] // count, product.shape[1])


def column_sums(values):
    return jnp.sum(values, axis=(0, 1), dtype=F32)


def per_device(boundary, lengths, *params):
    section = lax.axis_index("section")
    count = lax.axis_size("dp")
    place_in = lax.axis_index("dp")
    bit_count = count.bit_length() - 1
    bits = [(place_in >> b) & 1 for b in range(bit_count)]
    slots = lengths.shape[0]
    width = boundary.shape[2]
    rows = boundary.shape[1] // slots
    units = params[8].shape[2]
    local_rows = boundary.reshape(slots, rows, width)
    ticks = slots + 1
    forward_slots = [jnp.clip(t - section, 0, slots - 1) for t in range(ticks)]
    backward_slots = [jnp.clip(t - 1 + section, 0, slots - 1) for t in range(ticks)]
    flag = (section == 0).astype(jnp.int32)
    tables = [jnp.asarray(table) for table in rotary_lanes(rows, 256)]

    def tick_scalars(slot):
        return jnp.stack([slot, flag, lengths[slot]]).astype(jnp.int32)

    swapped = [(0, 1), (1, 0)]
    arriving = jnp.zeros((rows, width), BF16)
    saved = None
    finals = []
    for t in range(ticks):
        result, saved = forward_tick(tick_scalars(forward_slots[t]), local_rows, arriving, params, tables, saved)
        finals.append(result)
        if t + 1 < ticks:
            arriving = lax.ppermute(result, "section", swapped)
    x_s, na_s, nb_s, q_s, k_s, v_s, pt_s, mixed_s, hidden_s, slope_s = saved
    grads = None
    input_grads = []
    arriving = jnp.zeros((rows, width), BF16)
    for t in range(ticks):
        result, grads = backward_tick(tick_scalars(backward_slots[t]), local_rows, arriving, params, tables, saved, grads)
        input_grads.append(result)
        if t + 1 < ticks:
            arriving = lax.ppermute(result, "section", swapped)
    gy_s, gq_s, gk_s, gv_s, gu_s, vec_s = grads

    orders = {
        "down": [1, 0] + list(range(2, bit_count)),
        "up": list(range(bit_count)),
        "qkv": list(range(2, bit_count)) + [0, 1],
    }
    bit_scalars = jnp.stack(bits).astype(jnp.int32)
    if (width // count) % 16 == 0:
        down_keep, down_send, gy_sums = down_proj_grads(bit_scalars, hidden_s, mixed_s, gy_s, count, orders["down"][0])
        up_keep, up_send, gu_sums = column_grads(bit_scalars, nb_s, [gu_s], units // 3, count, orders["up"][0], "up_grads")
        qkv_keep, qkv_send, gp_sums = column_grads(
            bit_scalars, na_s, [gq_s, gk_s, gv_s], width, count, orders["qkv"][0], "qkv_grads"
        )
        gy_sums, gu_sums, gp_sums = gy_sums[0], gu_sums[0], gp_sums[0]
    else:
        down_full = jnp.concatenate([plain_grads(hidden_s, gy_s, count), plain_grads(mixed_s, gy_s, count)], axis=1)
        down_keep, down_send = parted(down_full, orders["down"][0], bits[orders["down"][0]])
        up_keep, up_send = parted(plain_grads(nb_s, gu_s, count), orders["up"][0], bits[orders["up"][0]])
        gp_s = jnp.concatenate([gq_s, gk_s, gv_s], axis=2)
        qkv_keep, qkv_send = parted(plain_grads(na_s, gp_s, count), orders["qkv"][0], bits[orders["qkv"][0]])
        gy_sums, gu_sums, gp_sums = column_sums(gy_s), column_sums(gu_s), column_sums(gp_s)

    vec = jnp.sum(vec_s, axis=0)
    small = jnp.concatenate(
        [piece.reshape(count, -1) for piece in (vec[0], vec[1], vec[2], vec[3], gy_sums, gu_sums, gp_sums)], axis=1
    )
    small_keep, small_send = parted(small, orders["up"][0], bits[orders["up"][0]])

    down = halving_sum(down_keep, down_send, orders["down"], count, bits, F32)
    up = halving_sum(up_keep, up_send, orders["up"], count, bits, F32)
    qkv = halving_sum(qkv_keep, qkv_send, orders["qkv"], count, bits, F32)
    small = halving_sum(small_keep, small_send, orders["up"], count, bits, F32)
    low, tall = width // count, units // count
    cuts = np.cumsum([low] * 5 + [tall])
    gain_a, shift_a, gain_b, shift_b, bias_y, bias_up, bias_qkv = jnp.split(small, cuts, axis=0)
    joined = jnp.where(section == 0, jnp.concatenate(input_grads[1:], axis=0), jnp.concatenate(finals[1:], axis=0))
    results = (joined, gain_a, shift_a, qkv, bias_qkv, down[tall:], bias_y, gain_b, shift_b, up, bias_up, down[:tall], bias_y)
    return tuple(result[None] for result in results)


def solution(mesh):
    split = P("section", "dp")
    deep = P("section", "dp", None)
    flat, matrix = P("section", None), P("section", None, None)
    return jax.shard_map(
        per_device,
        mesh=mesh,
        in_specs=(deep, P("dp"), flat, flat, matrix, flat, matrix, flat, flat, flat, matrix, flat, matrix, flat),
        out_specs=(deep, split, split, deep, split, deep, split, split, split, deep, split, deep, split),
        check_vma=False,
    )
```

```python
import functools
import math

import jax
import jax.numpy as jnp
import numpy as np
from jax import lax
from jax.experimental import pallas as pl
from jax.experimental.pallas import tpu as pltpu
from jax.sharding import PartitionSpec as P

HEAD = 64
LANES = 256
CHUNK = 512
EPS = 1e-05
NEG_FILL = -1e30
VMEM_BYTES = 14 * 1024 * 1024
FIRST_VMEM_BYTES = 14 * 1024 * 1024
F32 = jnp.float32
BF16 = jnp.bfloat16


def dot(left, right):
    return jnp.dot(left, right, preferred_element_type=F32)


def dot_nt(left, right):
    return lax.dot_general(left, right, (((1,), (1,)), ((), ())), preferred_element_type=F32)


def normalised(values):
    centred = values - jnp.mean(values, axis=-1, keepdims=True)
    variance = jnp.mean(centred * centred, axis=-1, keepdims=True)
    scale = lax.rsqrt(variance + EPS)
    return centred * scale, scale


def gelu_parts(values):
    integral = 0.5 + 0.5 * lax.erf(values * math.sqrt(0.5))
    bell = jnp.exp(values * values * -0.5)
    return values * integral, integral + values * bell * (1.0 / math.sqrt(2.0 * math.pi))


def rotary_lanes(seq_len, lanes):
    rot_dims = HEAD // 4
    half = rot_dims // 2
    frequency = np.float32(10000.0) ** (-(np.arange(half, dtype=np.float32) * np.float32(2.0) / np.float32(rot_dims)))
    angles = np.arange(seq_len, dtype=np.float32)[:, None] * frequency.astype(np.float32)[None, :]
    cosine, sine = np.cos(angles).astype(np.float32), np.sin(angles).astype(np.float32)
    same = np.ones((seq_len, HEAD), np.float32)
    later = np.zeros((seq_len, HEAD), np.float32)
    earlier = np.zeros((seq_len, HEAD), np.float32)
    same[:, :half] = cosine
    same[:, half:rot_dims] = cosine
    later[:, :half] = -sine
    earlier[:, half:rot_dims] = sine
    return [np.tile(t, (1, lanes // HEAD)) for t in (same, later, earlier)]


def turned(values, same, later, earlier, sign):
    half = HEAD // 8
    width = values.shape[1]
    ahead = pltpu.roll(values, width - half, 1)
    behind = pltpu.roll(values, half, 1)
    if sign > 0:
        return values * same + ahead * later + behind * earlier
    return values * same - ahead * later - behind * earlier


def blocked_bias(rows, length):
    out = []
    for start in range(0, rows, 128):
        keys = start + 128
        key_pos = lax.broadcasted_iota(jnp.int32, (keys, 2 * 128), 0)
        query_pos = start + (lax.broadcasted_iota(jnp.int32, (keys, 2 * 128), 1) & 127)
        out.append(jnp.where((key_pos <= query_pos) & (key_pos < length), 0.0, NEG_FILL))
    return out


def heads_apart(block, lane):
    zero = jnp.zeros_like(block)
    return jnp.concatenate([jnp.where(lane < HEAD, block, zero), jnp.where(lane < HEAD, zero, block)], axis=0)


def dot_tn(left, right):
    return lax.dot_general(left, right, (((0,), (0,)), ((), ())), preferred_element_type=F32)


def forward_body(
    slot, length, inputs, ready, own, gain_a, shift_a, gain_b, shift_b, wqkv, bqkv, wp, bp, wu, bu, wd, bd, same, later, earlier,
    y_out, x_out, na_out, nb_out, q_out, k_out, v_out, pt_out, mixed_out, hidden_out, slope_out,
):
    rows, width = y_out.shape
    units = wu.shape[2]
    pairs = width // (2 * HEAD)
    chunk = units // pairs
    ready("small", 0)
    x_low = inputs()
    x_out[slot] = x_low
    xhat, _ = normalised(x_low.astype(F32))
    na_out[slot] = (xhat * gain_a[...].astype(F32) + shift_a[...].astype(F32)).astype(BF16)
    nb_out[slot] = (xhat * gain_b[...].astype(F32) + shift_b[...].astype(F32)).astype(BF16)

    tables = (same[...], later[...], earlier[...])
    biases = blocked_bias(rows, length)
    lane = lax.broadcasted_iota(jnp.int32, (128, 2 * HEAD), 1)
    per = LANES // (2 * HEAD)
    ups = {}

    def mlp_up(index):
        at = slice(index * chunk, index * chunk + chunk)
        ups[index] = dot(nb_out[slot], wu[0, :, at]) + bu[:, at].astype(F32)

    def mlp_gelu(index):
        at = slice(index * chunk, index * chunk + chunk)
        hidden, slope = gelu_parts(ups.pop(index))
        hidden_out[slot, :, at] = hidden.astype(BF16)
        slope_out[slot, :, at] = slope.astype(BF16)

    for pair in range(pairs):
        group = pair // per
        if pair % per == 0:
            low = group * LANES
            ready("qkv", group)

            def packed(block):
                at = slice(block * width + low, block * width + low + LANES)
                return dot(na_out[slot], wqkv[0, :, at]) + bqkv[:, at].astype(F32)

            q_out[slot, :, low : low + LANES] = (turned(packed(0), *tables, 1) * (HEAD**-0.5)).astype(BF16)
            k_out[slot, :, low : low + LANES] = turned(packed(1), *tables, 1).astype(BF16)
            v_out[slot, :, low : low + LANES] = packed(2).astype(BF16)
        span = slice(pair * 2 * HEAD, pair * 2 * HEAD + 2 * HEAD)
        all_scores = []
        for block, start in enumerate(range(0, rows, 128)):
            keys = start + 128
            q2 = heads_apart(q_out[slot, start:keys, span], lane)
            all_scores.append(dot_nt(k_out[slot, :keys, span], q2) + biases[block])
        ready("up", pair)
        mlp_up(pair)
        for block, start in enumerate(range(0, rows, 128)):
            keys = start + 128
            scores = all_scores[block]
            exponent = jnp.exp(scores - jnp.max(scores, axis=0, keepdims=True))
            pt = (exponent * (1.0 / jnp.sum(exponent, axis=0, keepdims=True))).astype(BF16)
            pt_out[slot, pair, block, :keys] = pt
            mixed = dot_tn(pt, v_out[slot, :keys, span])
            mixed_out[slot, start:keys, span] = jnp.where(lane < HEAD, mixed[:128], mixed[128:]).astype(BF16)
        mlp_gelu(pair)
    ready("rest", 0)
    total = x_out[slot].astype(F32) + (bp[...].astype(F32) + bd[...].astype(F32))
    y_out[...] = (total + dot(mixed_out[slot], wp[0]) + dot(hidden_out[slot], wd[0])).astype(BF16)


def forward_first_kernel(tick, lengths, *refs):
    count = 17
    sources, held, outs, sems = refs[:count], refs[count : 2 * count], refs[2 * count : -1], refs[-1]
    copies = []
    waits = {}

    def fetch(name, part, index, at):
        source, target = (sources[index], held[index]) if at is None else (sources[index].at[at], held[index].at[at])
        copy = pltpu.make_async_copy(source, target, sems.at[len(copies)])
        copies.append(copy)
        waits.setdefault((name, part), []).append(copy)

    (own, gain_a, shift_a, gain_b, shift_b, wqkv, bqkv, wp, bp, wu, bu, wd, bd, same, later, earlier, _) = range(count)
    width = sources[wp].shape[1]
    units = sources[wu].shape[2]
    pairs = width // (2 * HEAD)
    groups = width // LANES
    for index in (own, gain_a, shift_a, gain_b, shift_b, bqkv, bp, bu, bd, same, later, earlier):
        fetch("small", 0, index, None)
    for pair in range(pairs):
        if pair * groups % pairs == 0:
            group = pair * groups // pairs
            for block in range(3):
                fetch("qkv", group, wqkv, (slice(None), slice(None), pl.ds(block * width + group * LANES, LANES)))
        fetch("up", pair, wu, (slice(None), slice(None), pl.ds(pair * (units // pairs), units // pairs)))
    fetch("rest", 0, wp, None)
    fetch("rest", 0, wd, None)
    for copy in copies:
        copy.start()

    def ready(name, part):
        for copy in waits[(name, part)]:
            copy.wait()

    section = lax.axis_index("section")
    slots = held[own].shape[0]
    slot = jnp.clip(tick - section, 0, slots - 1)
    forward_body(slot, lengths[slot], lambda: held[own][slot], ready, *held[:-1], *outs)


def forward_kernel(tick, lengths, arriving, own, *refs):
    section = lax.axis_index("section")
    slot = jnp.clip(tick - section, 0, own.shape[0] - 1)
    inputs = lambda: jnp.where(section == 0, own[slot], arriving[...])
    forward_body(slot, lengths[slot], inputs, lambda name, part: None, own, *refs)


def backward_kernel(
    tick, lengths, arriving, own, x_in, gain_a, gain_b, wqkv, wp, wu, wd, same, later, earlier,
    q_in, k_in, v_in, pt_in, slope_in,
    gx_out, gy_out, gp_out, gu_out, vec_out,
):
    section = lax.axis_index("section")
    slot = jnp.clip(tick - 1 + section, 0, own.shape[0] - 1)
    rows, width = own.shape[1:]
    units = wu.shape[2]
    pairs = width // (2 * HEAD)
    chunk = units // pairs
    gy_out[slot] = jnp.where(section == 0, arriving[...], own[slot])
    lane = lax.broadcasted_iota(jnp.int32, (128, 2 * HEAD), 1)
    tables = (same[...], later[...], earlier[...])
    per = LANES // (2 * HEAD)
    for pair in range(pairs):
        if pair % per == 0:
            gm_group = dot_nt(gy_out[slot], wp[0, pair * 2 * HEAD : pair * 2 * HEAD + LANES, :]).astype(BF16)
            group_q, group_k = [], []
        span = slice(pair * 2 * HEAD, pair * 2 * HEAD + 2 * HEAD)
        gm = gm_group[:, (pair % per) * 2 * HEAD : (pair % per + 1) * 2 * HEAD]
        gv_sum, gk_sum, gq_blocks = None, None, []
        for block, start in enumerate(range(0, rows, 128)):
            keys = start + 128
            gm2 = heads_apart(gm[start:keys], lane)
            q2 = heads_apart(q_in[slot, start:keys, span], lane)
            pt = pt_in[slot, pair, block, :keys]
            weighted = pt.astype(F32) * dot_nt(v_in[slot, :keys, span], gm2)
            inner = jnp.sum(weighted, axis=0, keepdims=True)
            gs = (weighted - pt.astype(F32) * inner).astype(BF16)
            gv_part = dot(pt, gm2)
            gk_part = dot(gs, q2)
            gq_part = dot_tn(gs, k_in[slot, :keys, span])
            gq_blocks.append(jnp.where(lane < HEAD, gq_part[:128], gq_part[128:]))
            if gv_sum is None:
                gv_sum, gk_sum = gv_part, gk_part
            else:
                gv_sum = jnp.concatenate([gv_sum + gv_part[:start], gv_part[start:]], axis=0)
                gk_sum = jnp.concatenate([gk_sum + gk_part[:start], gk_part[start:]], axis=0)
        gp_out[slot, :, 2 * width + pair * 2 * HEAD : 2 * width + pair * 2 * HEAD + 2 * HEAD] = gv_sum.astype(BF16)
        group_q.append(jnp.concatenate(gq_blocks, axis=0))
        group_k.append(gk_sum)
        if pair % per == per - 1:
            low = pair // per * LANES
            gq = turned(jnp.concatenate(group_q, axis=1) * (HEAD**-0.5), *tables, -1)
            gp_out[slot, :, low : low + LANES] = gq.astype(BF16)
            gk = turned(jnp.concatenate(group_k, axis=1), *tables, -1)
            gp_out[slot, :, width + low : width + low + LANES] = gk.astype(BF16)
        at = slice(pair * chunk, pair * chunk + chunk)
        gu_out[slot, :, at] = (dot_nt(gy_out[slot], wd[0, at, :]) * slope_in[slot, :, at].astype(F32)).astype(BF16)
    grad_b = dot_nt(gu_out[slot], wu[0])
    grad_a = dot_nt(gp_out[slot], wqkv[0])
    xhat, scale = normalised(x_in[slot].astype(F32))
    sums = [jnp.sum(t, axis=0, keepdims=True) for t in (grad_a * xhat, grad_a, grad_b * xhat, grad_b)]
    vec_out[slot] = jnp.concatenate(sums + [jnp.zeros((4, width), F32)], axis=0)
    both = grad_a * gain_a[...].astype(F32) + grad_b * gain_b[...].astype(F32)
    inner = jnp.mean(both * xhat, axis=-1, keepdims=True)
    gx = gy_out[slot].astype(F32) + scale * (both - jnp.mean(both, axis=-1, keepdims=True) - xhat * inner)
    gx_out[...] = gx.astype(BF16)


def whole(shape):
    return pl.BlockSpec(shape, lambda g, s: (0,) * len(shape))


VM = pl.BlockSpec(memory_space=pltpu.VMEM)
HBM = pl.BlockSpec(memory_space=pl.ANY)


def tick_call(kernel, lengths, operands, kept, out_shape, name):
    aliases = {}
    body = kernel
    specs = [pl.BlockSpec(memory_space=pltpu.SMEM)] + [VM] * len(operands)
    count = 1 + len(operands)
    if kept is not None:

        def body(*refs):
            return kernel(*refs[:count], *refs[count + len(kept) :])

        specs = specs + [HBM] * len(kept)
        operands = list(operands) + list(kept)
        aliases = {count + i: 1 + i for i in range(len(kept))}
    outs = pl.pallas_call(
        body,
        in_specs=specs,
        out_specs=[VM] * len(out_shape),
        out_shape=out_shape,
        input_output_aliases=aliases,
        compiler_params=pltpu.CompilerParams(vmem_limit_bytes=VMEM_BYTES),
        cost_estimate=pl.CostEstimate(flops=8 << 30, bytes_accessed=8 << 20, transcendentals=0),
        name=name,
    )(lengths, *operands)
    return outs[0], outs[1:]


def shape_of(array):
    return jax.ShapeDtypeStruct(array.shape, array.dtype)


def forward_shapes(local_rows, params):
    slots, rows, width = local_rows.shape
    units = params[8].shape[2]
    return [jax.ShapeDtypeStruct((rows, width), BF16)] + [jax.ShapeDtypeStruct((slots, rows, width), BF16)] * 6 + [
        jax.ShapeDtypeStruct((slots, width // (2 * HEAD), rows // 128, rows, 2 * 128), BF16),
        jax.ShapeDtypeStruct((slots, rows, width), BF16),
        jax.ShapeDtypeStruct((slots, rows, units), BF16),
        jax.ShapeDtypeStruct((slots, rows, units), BF16),
    ]


def forward_first(lengths, local_rows, params, tables):
    (gain_a, shift_a, w_qkv, b_qkv, w_proj, b_proj, gain_b, shift_b, w_up, b_up, w_down, b_down) = params
    held = [local_rows, gain_a, shift_a, gain_b, shift_b, w_qkv, b_qkv, w_proj, b_proj, w_up, b_up, w_down, b_down] + list(tables)
    shapes = [shape_of(array) for array in held] + forward_shapes(local_rows, params)

    def kernel(lengths_ref, *refs):
        count = len(held)
        forward_first_kernel(0, lengths_ref, *refs[:count], None, *refs[count : 2 * count], None, *refs[2 * count :])

    outs = pl.pallas_call(
        kernel,
        in_specs=[pl.BlockSpec(memory_space=pltpu.SMEM)] + [pl.BlockSpec(memory_space=pltpu.HBM)] * len(held),
        out_specs=[VM] * len(shapes),
        out_shape=shapes,
        scratch_shapes=[pltpu.SemaphoreType.DMA((40,))],
        compiler_params=pltpu.CompilerParams(vmem_limit_bytes=FIRST_VMEM_BYTES),
        cost_estimate=pl.CostEstimate(flops=8 << 30, bytes_accessed=16 << 20, transcendentals=0),
        name="layer_forward_first",
    )(lengths, *[pltpu.with_memory_space_constraint(array, pltpu.HBM) for array in held])
    count = len(held)
    return outs[count], outs[count + 1 :], outs[:count]


def forward_tick(tick, lengths, arriving, held, saved, shapes):
    return tick_call(functools.partial(forward_kernel, tick), lengths, [arriving] + list(held), saved, shapes, "layer_forward")


def backward_tick(tick, lengths, arriving, held, saved, grads):
    local_rows, gain_a, shift_a, gain_b, shift_b, w_qkv, b_qkv, w_proj, b_proj, w_up, b_up, w_down, b_down, *tables = held
    x_s, na_s, nb_s, q_s, k_s, v_s, pt_s, mixed_s, hidden_s, slope_s = saved
    slots, rows, width = local_rows.shape
    units = w_up.shape[2]
    operands = [arriving, local_rows, x_s, gain_a, gain_b, w_qkv, w_proj, w_up, w_down] + tables + [q_s, k_s, v_s, pt_s, slope_s]
    out_shape = [
        jax.ShapeDtypeStruct((rows, width), BF16),
        jax.ShapeDtypeStruct((slots, rows, width), BF16),
        jax.ShapeDtypeStruct((slots, rows, 3 * width), BF16),
        jax.ShapeDtypeStruct((slots, rows, units), BF16),
        jax.ShapeDtypeStruct((slots, 8, width), F32),
    ]
    return tick_call(functools.partial(backward_kernel, tick), lengths, operands, grads, out_shape, "layer_backward")


def place(scratch, parts, chunk_count, first_bit, mine):
    rows = sum(part.shape[0] for part in parts[0])
    half = chunk_count // 2
    for chunk in range(chunk_count):
        rest = (chunk >> (first_bit + 1) << first_bit) | (chunk & ((1 << first_bit) - 1))
        side = ((chunk >> first_bit) & 1) ^ mine
        start = pl.multiple_of(side * (half * rows) + rest * rows, 16)
        for part in parts[chunk]:
            scratch[pl.ds(start, part.shape[0]), :] = part
            start = pl.multiple_of(start + part.shape[0], 16)


def ones_dot(values):
    return dot(jnp.ones((16, values.shape[0]), BF16), values)[:8]


def down_proj_kernel(chunks, bit, hidden, mixed, gy, keep_out, send_out, sums_out, mixed_t, left):
    step = pl.program_id(0)
    rows = gy.shape[0] * gy.shape[1]
    grad = gy[...].reshape(rows, gy.shape[2])

    @pl.when(step == 0)
    def _():
        mixed_t[...] = mixed[...].reshape(rows, mixed.shape[2]).T
        sums_out[...] = ones_dot(grad)

    hidden_t = hidden[...].reshape(rows, hidden.shape[2]).T
    proj_rows = mixed_t.shape[0] // pl.num_programs(0)
    part_t = mixed_t[pl.ds(pl.multiple_of(step * proj_rows, 16), proj_rows), :]
    tall, low = hidden_t.shape[0] // chunks, proj_rows // chunks
    place(
        left,
        [[hidden_t[c * tall : c * tall + tall], part_t[c * low : c * low + low]] for c in range(chunks)],
        chunks, bit, (lax.axis_index("dp") >> bit) & 1,
    )
    product = dot(left[...], grad).astype(BF16)
    half = product.shape[0] // 2
    keep_out[...] = product[:half].reshape(keep_out.shape)
    send_out[...] = product[half:].reshape(send_out.shape)


def column_kernel(chunk_count, bit, normed, grad_ref, keep_out, send_out, sums_out, left):
    rows = normed.shape[0] * normed.shape[1]

    @pl.when(pl.program_id(0) == 0)
    def _():
        normed_t = normed[...].reshape(rows, normed.shape[2]).T
        low = normed_t.shape[0] // chunk_count
        mine = (lax.axis_index("dp") >> bit) & 1
        place(left, [[normed_t[c * low : c * low + low]] for c in range(chunk_count)], chunk_count, bit, mine)

    grad = grad_ref[...].reshape(rows, grad_ref.shape[2])
    product = dot(left[...], grad).astype(BF16)
    half = product.shape[0] // 2
    keep_out[...] = product[:half].reshape(keep_out.shape)
    send_out[...] = product[half:].reshape(send_out.shape)
    sums_out[...] = ones_dot(grad)


def weight_call(kernel, grid, operands, in_specs, out_specs, out_shape, scratch, flops, name):
    return pl.pallas_call(
        kernel,
        grid=(grid,),
        in_specs=in_specs,
        out_specs=out_specs,
        scratch_shapes=scratch,
        out_shape=out_shape,
        compiler_params=pltpu.CompilerParams(vmem_limit_bytes=VMEM_BYTES),
        cost_estimate=pl.CostEstimate(flops=flops, bytes_accessed=8 << 20, transcendentals=0),
        name=name,
    )(*operands)


def down_proj_grads(hidden, mixed, gy, count, bit):
    slots, rows, units = hidden.shape
    width = gy.shape[2]
    steps = 4
    chunks = count // steps
    tall = units // count + width // count
    out = jax.ShapeDtypeStruct((count // 2, tall, width), BF16)
    block = pl.BlockSpec((chunks // 2, tall, width), lambda g: (g, 0, 0))

    def kernel(hidden_ref, mixed_ref, gy_ref, *refs):
        down_proj_kernel(chunks, bit, hidden_ref, mixed_ref, gy_ref, *refs)

    return weight_call(
        kernel, steps, [hidden, mixed, gy],
        [pl.BlockSpec((slots, rows, units // steps), lambda g: (0, 0, g)), VM, VM],
        [block, block, pl.BlockSpec((8, width), lambda g: (0, 0))],
        [out, out, jax.ShapeDtypeStruct((8, width), F32)],
        [pltpu.VMEM((width, slots * rows), BF16), pltpu.VMEM((chunks * tall, slots * rows), BF16)],
        2 * slots * rows * width * (units + width), "down_proj_grads",
    )


def column_grads(normed, grad, columns, count, bit, name):
    slots, rows, width = normed.shape
    total = grad.shape[2]
    low = width // count
    out = jax.ShapeDtypeStruct((count // 2, low, total), BF16)
    block = pl.BlockSpec((count // 2, low, columns), lambda g: (0, 0, g))
    return weight_call(
        functools.partial(column_kernel, count, bit), total // columns, [normed, grad],
        [VM, pl.BlockSpec((slots, rows, columns), lambda g: (0, 0, g))],
        [block, block, pl.BlockSpec((8, columns), lambda g: (0, g))],
        [out, out, jax.ShapeDtypeStruct((8, total), F32)],
        [pltpu.VMEM((width, slots * rows), BF16)],
        2 * slots * rows * width * total, name,
    )


def swap(shard, bit, count):
    return lax.ppermute(shard, "dp", [(i, i ^ (1 << bit)) for i in range(count)])


def parted(values, position, mine):
    count = values.shape[0]
    shaped = values.reshape((count >> (position + 1), 2, 1 << position) + values.shape[1:])
    out = []
    for side in (mine, 1 - mine):
        piece = lax.dynamic_index_in_dim(shaped, side, axis=1, keepdims=False)
        out.append(piece.reshape((count // 2,) + values.shape[1:]))
    return out


def halving_sum(keep, send, order, count, bits, final):
    left = sorted(order)
    for number, bit in enumerate(order):
        left.remove(bit)
        arrived = swap(send, bit, count)
        if number + 1 == len(order):
            return (keep.astype(F32) + arrived.astype(F32)).astype(final)[0]
        position = left.index(order[number + 1])
        keep_a, send_a = parted(keep, position, bits[order[number + 1]])
        keep_b, send_b = parted(arrived, position, bits[order[number + 1]])
        send = (send_a.astype(F32) + send_b.astype(F32)).astype(send_a.dtype)
        keep = (keep_a.astype(F32) + keep_b.astype(F32)).astype(send_a.dtype)


def plain_grads(left, right, count):
    rows = left.shape[0] * left.shape[1]
    product = lax.dot_general(
        left.reshape(rows, -1), right.reshape(rows, -1), (((0,), (0,)), ((), ())), preferred_element_type=F32
    ).astype(BF16)
    return product.reshape(count, product.shape[0] // count, product.shape[1])


def column_sums(values):
    return jnp.sum(values, axis=(0, 1), dtype=F32)


def per_device(boundary, lengths, *params):
    section = lax.axis_index("section")
    count = lax.axis_size("dp")
    place_in = lax.axis_index("dp")
    bit_count = count.bit_length() - 1
    bits = [(place_in >> b) & 1 for b in range(bit_count)]
    slots = lengths.shape[0]
    width = boundary.shape[2]
    rows = boundary.shape[1] // slots
    units = params[8].shape[2]
    local_rows = boundary.reshape(slots, rows, width)
    ticks = slots + 1
    tables = [jnp.asarray(table) for table in rotary_lanes(rows, LANES)]
    swapped = [(0, 1), (1, 0)]
    result, saved, held = forward_first(lengths, local_rows, params, tables)
    shapes = forward_shapes(local_rows, params)
    finals = [result]
    for t in range(1, ticks):
        arriving = lax.ppermute(result, "section", swapped)
        result, saved = forward_tick(t, lengths, arriving, held, saved, shapes)
        finals.append(result)
    x_s, na_s, nb_s, q_s, k_s, v_s, pt_s, mixed_s, hidden_s, slope_s = saved
    grads = None
    input_grads = []
    arriving = held[0][0]
    for t in range(ticks):
        result, grads = backward_tick(t, lengths, arriving, held, saved, grads)
        input_grads.append(result)
        if t + 1 < ticks:
            arriving = lax.ppermute(result, "section", swapped)
    gy_s, gp_s, gu_s, vec_s = grads

    orders = {
        "down": [1, 0] + list(range(2, bit_count)),
        "up": list(range(bit_count)),
        "qkv": list(range(2, bit_count)) + [0, 1],
    }
    if (width // count) % 16 == 0:
        down_keep, down_send, gy_sums = down_proj_grads(hidden_s, mixed_s, gy_s, count, orders["down"][0])
        up_keep, up_send, gu_sums = column_grads(nb_s, gu_s, units // 3, count, orders["up"][0], "up_grads")
        qkv_keep, qkv_send, gp_sums = column_grads(
            na_s, gp_s, width, count, orders["qkv"][0], "qkv_grads"
        )
        gy_sums, gu_sums, gp_sums = gy_sums[0], gu_sums[0], gp_sums[0]
    else:
        down_full = jnp.concatenate([plain_grads(hidden_s, gy_s, count), plain_grads(mixed_s, gy_s, count)], axis=1)
        down_keep, down_send = parted(down_full, orders["down"][0], bits[orders["down"][0]])
        up_keep, up_send = parted(plain_grads(nb_s, gu_s, count), orders["up"][0], bits[orders["up"][0]])
        qkv_keep, qkv_send = parted(plain_grads(na_s, gp_s, count), orders["qkv"][0], bits[orders["qkv"][0]])
        gy_sums, gu_sums, gp_sums = column_sums(gy_s), column_sums(gu_s), column_sums(gp_s)

    vec = jnp.sum(vec_s, axis=0)
    small = jnp.concatenate(
        [piece.reshape(count, -1) for piece in (vec[0], vec[1], vec[2], vec[3], gy_sums, gu_sums, gp_sums)], axis=1
    )
    small_keep, small_send = parted(small, orders["up"][0], bits[orders["up"][0]])

    down = halving_sum(down_keep, down_send, orders["down"], count, bits, F32)
    up = halving_sum(up_keep, up_send, orders["up"], count, bits, F32)
    qkv = halving_sum(qkv_keep, qkv_send, orders["qkv"], count, bits, F32)
    small = halving_sum(small_keep, small_send, orders["up"], count, bits, F32)
    low, tall = width // count, units // count
    cuts = np.cumsum([low] * 5 + [tall])
    gain_a, shift_a, gain_b, shift_b, bias_y, bias_up, bias_qkv = jnp.split(small, cuts, axis=0)
    joined = jnp.where(section == 0, jnp.concatenate(input_grads[1:], axis=0), jnp.concatenate(finals[1:], axis=0))
    results = (joined, gain_a, shift_a, qkv, bias_qkv, down[tall:], bias_y, gain_b, shift_b, up, bias_up, down[:tall], bias_y)
    return tuple(result[None] for result in results)


def solution(mesh):
    split = P("section", "dp")
    deep = P("section", "dp", None)
    flat, matrix = P("section", None), P("section", None, None)
    return jax.shard_map(
        per_device,
        mesh=mesh,
        in_specs=(deep, P("dp"), flat, flat, matrix, flat, matrix, flat, flat, flat, matrix, flat, matrix, flat),
        out_specs=(deep, split, split, deep, split, deep, split, split, split, deep, split, deep, split),
        check_vma=False,
    )
```

```python
import functools
import math

import jax
import jax.numpy as jnp
import numpy as np
from jax import lax
from jax.experimental import pallas as pl
from jax.experimental.pallas import tpu as pltpu
from jax.sharding import PartitionSpec as P

HEAD = 64
LANES = 256
CHUNK = 512
EPS = 1e-05
NEG_FILL = -1e30
VMEM_BYTES = 12 * 1024 * 1024
FIRST_VMEM_BYTES = 12 * 1024 * 1024
F32 = jnp.float32
BF16 = jnp.bfloat16


def dot(left, right):
    return jnp.dot(left, right, preferred_element_type=F32)


def dot_nt(left, right):
    return lax.dot_general(left, right, (((1,), (1,)), ((), ())), preferred_element_type=F32)


def normalised(values):
    centred = values - jnp.mean(values, axis=-1, keepdims=True)
    variance = jnp.mean(centred * centred, axis=-1, keepdims=True)
    scale = lax.rsqrt(variance + EPS)
    return centred * scale, scale


def gelu_parts(values):
    integral = 0.5 + 0.5 * lax.erf(values * math.sqrt(0.5))
    bell = jnp.exp(values * values * -0.5)
    return values * integral, integral + values * bell * (1.0 / math.sqrt(2.0 * math.pi))


def rotary_lanes(seq_len, lanes):
    rot_dims = HEAD // 4
    half = rot_dims // 2
    frequency = np.float32(10000.0) ** (-(np.arange(half, dtype=np.float32) * np.float32(2.0) / np.float32(rot_dims)))
    angles = np.arange(seq_len, dtype=np.float32)[:, None] * frequency.astype(np.float32)[None, :]
    cosine, sine = np.cos(angles).astype(np.float32), np.sin(angles).astype(np.float32)
    same = np.ones((seq_len, HEAD), np.float32)
    later = np.zeros((seq_len, HEAD), np.float32)
    earlier = np.zeros((seq_len, HEAD), np.float32)
    same[:, :half] = cosine
    same[:, half:rot_dims] = cosine
    later[:, :half] = -sine
    earlier[:, half:rot_dims] = sine
    return [np.tile(t, (1, lanes // HEAD)) for t in (same, later, earlier)]


def turned(values, same, later, earlier, sign):
    half = HEAD // 8
    width = values.shape[1]
    same, later, earlier = (jnp.concatenate([t] * (width // t.shape[1]), axis=1) for t in (same, later, earlier))
    ahead = pltpu.roll(values, width - half, 1)
    behind = pltpu.roll(values, half, 1)
    if sign > 0:
        return values * same + ahead * later + behind * earlier
    return values * same - ahead * later - behind * earlier


def blocked_bias(rows, length):
    out = []
    for start in range(0, rows, 128):
        keys = start + 128
        key_pos = lax.broadcasted_iota(jnp.int32, (keys, 2 * 128), 0)
        query_pos = start + (lax.broadcasted_iota(jnp.int32, (keys, 2 * 128), 1) & 127)
        out.append(jnp.where((key_pos <= query_pos) & (key_pos < length), 0.0, NEG_FILL))
    return out


def heads_apart(block, lane):
    zero = jnp.zeros_like(block)
    return jnp.concatenate([jnp.where(lane < HEAD, block, zero), jnp.where(lane < HEAD, zero, block)], axis=0)


def dot_tn(left, right):
    return lax.dot_general(left, right, (((0,), (0,)), ((), ())), preferred_element_type=F32)


def probs_rows(block):
    start = 128 * (block * (block + 1) // 2)
    return slice(start, start + 128 * (block + 1))


def forward_body(
    slot, length, inputs, ready, own, gain_a, shift_a, gain_b, shift_b, wqkv, bqkv, wp, bp, wu, bu, wd, bd, same, later, earlier,
    y_out, x_out, na_out, nb_out, qkv_out, pt_out, mixed_out, hidden_out, slope_out,
):
    rows, width = y_out.shape
    units = wu.shape[2]
    pairs = width // (2 * HEAD)
    chunk = units // pairs
    ready("small", 0)
    x_low = inputs()
    x_out[slot] = x_low
    xhat, _ = normalised(x_low.astype(F32))
    na_out[slot] = (xhat * gain_a[...].astype(F32) + shift_a[...].astype(F32)).astype(BF16)
    nb_out[slot] = (xhat * gain_b[...].astype(F32) + shift_b[...].astype(F32)).astype(BF16)

    tables = (same[...], later[...], earlier[...])
    biases = blocked_bias(rows, length)
    lane = lax.broadcasted_iota(jnp.int32, (128, 2 * HEAD), 1)
    per = LANES // (2 * HEAD)
    ups = {}

    def mlp_up(index):
        at = slice(index * chunk, index * chunk + chunk)
        ups[index] = dot(nb_out[slot], wu[0, :, at]) + bu[:, at].astype(F32)

    def mlp_gelu(index):
        at = slice(index * chunk, index * chunk + chunk)
        hidden, slope = gelu_parts(ups.pop(index))
        hidden_out[slot, :, at] = hidden.astype(BF16)
        slope_out[slot, :, at] = slope.astype(BF16)

    for pair in range(pairs):
        group = pair // per
        if pair % per == 0:
            low = group * LANES
            ready("qkv", group)

            def packed(block):
                at = slice(block * width + low, block * width + low + LANES)
                return dot(na_out[slot], wqkv[0, :, at]) + bqkv[:, at].astype(F32)

            qkv_out[slot, :, low : low + LANES] = (turned(packed(0), *tables, 1) * (HEAD**-0.5)).astype(BF16)
            qkv_out[slot, :, width + low : width + low + LANES] = turned(packed(1), *tables, 1).astype(BF16)
            qkv_out[slot, :, 2 * width + low : 2 * width + low + LANES] = packed(2).astype(BF16)
        span, span_k, span_v = (slice(b * width + pair * 2 * HEAD, b * width + (pair + 1) * 2 * HEAD) for b in range(3))
        all_scores = []
        for block, start in enumerate(range(0, rows, 128)):
            keys = start + 128
            q2 = heads_apart(qkv_out[slot, start:keys, span], lane)
            all_scores.append(dot_nt(qkv_out[slot, :keys, span_k], q2) + biases[block])
        ready("up", pair)
        mlp_up(pair)
        for block, start in enumerate(range(0, rows, 128)):
            keys = start + 128
            scores = all_scores[block]
            exponent = jnp.exp(scores - jnp.max(scores, axis=0, keepdims=True))
            pt = (exponent * (1.0 / jnp.sum(exponent, axis=0, keepdims=True))).astype(BF16)
            pt_out[slot, pair, probs_rows(block)] = pt
            mixed = dot_tn(pt, qkv_out[slot, :keys, span_v])
            mixed_out[slot, start:keys, span] = jnp.where(lane < HEAD, mixed[:128], mixed[128:]).astype(BF16)
        mlp_gelu(pair)
    ready("rest", 0)
    total = x_out[slot].astype(F32) + (bp[...].astype(F32) + bd[...].astype(F32))
    y_out[...] = (total + dot(mixed_out[slot], wp[0]) + dot(hidden_out[slot], wd[0])).astype(BF16)


def forward_first_kernel(tick, lengths, *refs):
    count = 17
    sources, held, outs, sems = refs[:count], refs[count : 2 * count], refs[2 * count : -1], refs[-1]
    copies = []
    waits = {}

    def fetch(name, part, index, at):
        source, target = (sources[index], held[index]) if at is None else (sources[index].at[at], held[index].at[at])
        copy = pltpu.make_async_copy(source, target, sems.at[len(copies)])
        copies.append(copy)
        waits.setdefault((name, part), []).append(copy)

    (own, gain_a, shift_a, gain_b, shift_b, wqkv, bqkv, wp, bp, wu, bu, wd, bd, same, later, earlier, _) = range(count)
    width = sources[wp].shape[1]
    units = sources[wu].shape[2]
    pairs = width // (2 * HEAD)
    groups = width // LANES
    for index in (own, gain_a, shift_a, gain_b, shift_b, bqkv, bp, bu, bd, same, later, earlier):
        fetch("small", 0, index, None)
    for pair in range(pairs):
        if pair * groups % pairs == 0:
            group = pair * groups // pairs
            for block in range(3):
                fetch("qkv", group, wqkv, (slice(None), slice(None), pl.ds(block * width + group * LANES, LANES)))
        fetch("up", pair, wu, (slice(None), slice(None), pl.ds(pair * (units // pairs), units // pairs)))
    fetch("rest", 0, wp, None)
    fetch("rest", 0, wd, None)
    for copy in copies:
        copy.start()

    def ready(name, part):
        for copy in waits[(name, part)]:
            copy.wait()

    section = lax.axis_index("section")
    slots = held[own].shape[0]
    slot = jnp.clip(tick - section, 0, slots - 1)
    forward_body(slot, lengths[slot], lambda: held[own][slot], ready, *held[:-1], *outs)


def backward_body(
    slot, gy_source, x_in, gain_a, gain_b, wqkv, wp, wu, wd, same, later, earlier,
    pt_in, gx_out, qkv_io, slope_io, gy_out, vec_out,
):
    rows, width = gx_out.shape
    units = wu.shape[2]
    pairs = width // (2 * HEAD)
    chunk = units // pairs
    gy_out[slot] = gy_source()
    lane = lax.broadcasted_iota(jnp.int32, (128, 2 * HEAD), 1)
    tables = (same[...], later[...], earlier[...])
    per = LANES // (2 * HEAD)
    for pair in range(pairs):
        if pair % per == 0:
            gm_group = dot_nt(gy_out[slot], wp[0, pair * 2 * HEAD : pair * 2 * HEAD + LANES, :]).astype(BF16)
            group_q, group_k = [], []
        span, span_k, span_v = (slice(b * width + pair * 2 * HEAD, b * width + (pair + 1) * 2 * HEAD) for b in range(3))
        gm = gm_group[:, (pair % per) * 2 * HEAD : (pair % per + 1) * 2 * HEAD]
        gv_sum, gk_sum, gq_blocks = None, None, []
        for block, start in enumerate(range(0, rows, 128)):
            keys = start + 128
            gm2 = heads_apart(gm[start:keys], lane)
            q2 = heads_apart(qkv_io[slot, start:keys, span], lane)
            pt = pt_in[slot, pair, probs_rows(block)]
            weighted = pt.astype(F32) * dot_nt(qkv_io[slot, :keys, span_v], gm2)
            inner = jnp.sum(weighted, axis=0, keepdims=True)
            gs = (weighted - pt.astype(F32) * inner).astype(BF16)
            gv_part = dot(pt, gm2)
            gk_part = dot(gs, q2)
            gq_part = dot_tn(gs, qkv_io[slot, :keys, span_k])
            gq_blocks.append(jnp.where(lane < HEAD, gq_part[:128], gq_part[128:]))
            if gv_sum is None:
                gv_sum, gk_sum = gv_part, gk_part
            else:
                gv_sum = jnp.concatenate([gv_sum + gv_part[:start], gv_part[start:]], axis=0)
                gk_sum = jnp.concatenate([gk_sum + gk_part[:start], gk_part[start:]], axis=0)
        qkv_io[slot, :, span_v] = gv_sum.astype(BF16)
        group_q.append(jnp.concatenate(gq_blocks, axis=0))
        group_k.append(gk_sum)
        if pair % per == per - 1:
            low = pair // per * LANES
            gq = turned(jnp.concatenate(group_q, axis=1) * (HEAD**-0.5), *tables, -1)
            qkv_io[slot, :, low : low + LANES] = gq.astype(BF16)
            gk = turned(jnp.concatenate(group_k, axis=1), *tables, -1)
            qkv_io[slot, :, width + low : width + low + LANES] = gk.astype(BF16)
        at = slice(pair * chunk, pair * chunk + chunk)
        slope_io[slot, :, at] = (dot_nt(gy_out[slot], wd[0, at, :]) * slope_io[slot, :, at].astype(F32)).astype(BF16)
    grad_b = dot_nt(slope_io[slot], wu[0])
    grad_a = dot_nt(qkv_io[slot], wqkv[0])
    xhat, scale = normalised(x_in[slot].astype(F32))
    sums = [jnp.sum(t, axis=0, keepdims=True) for t in (grad_a * xhat, grad_a, grad_b * xhat, grad_b)]
    vec_out[slot] = jnp.concatenate(sums + [jnp.zeros((4, width), F32)], axis=0)
    both = grad_a * gain_a[...].astype(F32) + grad_b * gain_b[...].astype(F32)
    inner = jnp.mean(both * xhat, axis=-1, keepdims=True)
    gx = gy_out[slot].astype(F32) + scale * (both - jnp.mean(both, axis=-1, keepdims=True) - xhat * inner)
    gx_out[...] = gx.astype(BF16)


VM = pl.BlockSpec(memory_space=pltpu.VMEM)
HBM = pl.BlockSpec(memory_space=pl.ANY)


def call(kernel, operands, out_shape, name, kept=(), scratch=(), flops=1 << 20, after=()):
    count = len(operands)
    after = list(after)

    def body(*refs):
        kernel(*refs[:count], *refs[count + len(kept) + len(after) :])

    return pl.pallas_call(
        body,
        in_specs=[pl.BlockSpec(memory_space=pltpu.SMEM) if o.dtype == jnp.int32 else VM for o in operands] + [VM] * len(kept) + [HBM] * len(after),
        out_specs=[VM] * (len(kept) + len(out_shape)),
        out_shape=[pltpu.VMEM(array.shape, array.dtype) for array in kept] + list(out_shape),
        input_output_aliases={count + i: i for i in range(len(kept))},
        scratch_shapes=list(scratch),
        compiler_params=pltpu.CompilerParams(vmem_limit_bytes=VMEM_BYTES),
        cost_estimate=pl.CostEstimate(flops=flops, bytes_accessed=1 << 16, transcendentals=0),
        name=name,
    )(*operands, *[pltpu.with_memory_space_constraint(array, pltpu.VMEM) for array in kept], *after)


def shape_of(array):
    return jax.ShapeDtypeStruct(array.shape, array.dtype)


def forward_shapes(local_rows, params):
    slots, rows, width = local_rows.shape
    units = params[8].shape[2]
    blocks = rows // 128
    probs = (slots, width // (2 * HEAD), 128 * (blocks * (blocks + 1) // 2), 2 * 128)
    columns = [width, width, width, 3 * width, None, width, units, units]
    return [jax.ShapeDtypeStruct((rows, width), BF16)] + [
        pltpu.VMEM(probs if n is None else (slots, rows, n), BF16) for n in columns
    ]


def forward_first(lengths, local_rows, params, tables):
    (gain_a, shift_a, w_qkv, b_qkv, w_proj, b_proj, gain_b, shift_b, w_up, b_up, w_down, b_down) = params
    held = [local_rows, gain_a, shift_a, gain_b, shift_b, w_qkv, b_qkv, w_proj, b_proj, w_up, b_up, w_down, b_down] + list(tables)
    shapes = [shape_of(array) for array in held] + forward_shapes(local_rows, params)

    def kernel(lengths_ref, *refs):
        count = len(held)
        forward_first_kernel(0, lengths_ref, *refs[:count], None, *refs[count : 2 * count], None, *refs[2 * count :])

    outs = pl.pallas_call(
        kernel,
        in_specs=[pl.BlockSpec(memory_space=pltpu.SMEM)] + [pl.BlockSpec(memory_space=pltpu.HBM)] * len(held),
        out_specs=[VM] * len(shapes),
        out_shape=shapes,
        scratch_shapes=[pltpu.SemaphoreType.DMA((40,))],
        compiler_params=pltpu.CompilerParams(vmem_limit_bytes=FIRST_VMEM_BYTES),
        cost_estimate=pl.CostEstimate(flops=1 << 20, bytes_accessed=1 << 16, transcendentals=0),
        name="layer_forward_first",
    )(lengths, *[pltpu.with_memory_space_constraint(array, pltpu.HBM) for array in held])
    count = len(held)
    return outs[count], outs[count + 1 :], outs[:count]


def swap(shard, bit, count):
    return lax.ppermute(shard, "dp", [(i, i ^ (1 << bit)) for i in range(count)])


def parted(values, position, mine):
    count = values.shape[0]
    shaped = values.reshape((count >> (position + 1), 2, 1 << position) + values.shape[1:])
    out = []
    for side in (mine, 1 - mine):
        piece = lax.dynamic_index_in_dim(shaped, side, axis=1, keepdims=False)
        out.append(piece.reshape((count // 2,) + values.shape[1:]))
    return out


def halving_sum(keep, send, order, count, bits, final):
    left = sorted(order)
    for number, bit in enumerate(order):
        left.remove(bit)
        arrived = swap(send, bit, count)
        if number + 1 == len(order):
            return (keep.astype(F32) + arrived.astype(F32)).astype(final)[0]
        position = left.index(order[number + 1])
        keep_a, send_a = parted(keep, position, bits[order[number + 1]])
        keep_b, send_b = parted(arrived, position, bits[order[number + 1]])
        send = (send_a.astype(F32) + send_b.astype(F32)).astype(send_a.dtype)
        keep = (keep_a.astype(F32) + keep_b.astype(F32)).astype(send_a.dtype)


def plain_grads(left, right, count):
    rows = left.shape[0] * left.shape[1]
    product = lax.dot_general(
        left.reshape(rows, -1), right.reshape(rows, -1), (((0,), (0,)), ((), ())), preferred_element_type=F32
    ).astype(BF16)
    return product.reshape(count, product.shape[0] // count, product.shape[1])


def partner_forward(half, rows_of, gain, shift, wu, bu, nbp, hidp, slopep):
    slots, rows, width = nbp.shape
    part = hidp.shape[2] // 2
    for s in range(slots):
        xhat, _ = normalised(rows_of(s).astype(F32))
        nbp[s] = (xhat * gain[...].astype(F32) + shift[...].astype(F32)).astype(BF16)
    piece = 256
    for j in range(2):
        for low in range(0, part, piece):
            there = pl.ds(pl.multiple_of((2 * j + half) * part + low, 128), piece)
            here = slice(j * part + low, j * part + low + piece)
            for s in range(slots):
                hidden, slope = gelu_parts(dot(nbp[s], wu[0, :, there]) + bu[:, there].astype(F32))
                hidp[s, :, here] = hidden.astype(BF16)
                slopep[s, :, here] = slope.astype(BF16)


def partner_backward(half, rows_of, wd, slopep):
    slots, rows, units = slopep.shape
    part = units // 2
    piece = 256
    for j in range(2):
        for low in range(0, part, piece):
            there = pl.ds(pl.multiple_of((2 * j + half) * part + low, 128), piece)
            here = slice(j * part + low, j * part + low + piece)
            for s in range(slots):
                grad = dot_nt(rows_of(s), wd[0, there, :])
                slopep[s, :, here] = (grad * slopep[s, :, here].astype(F32)).astype(BF16)


def ones_dot(values):
    return dot(jnp.ones((16, values.shape[0]), BF16), values)[:8]


def flat_rows(ref):
    values = ref[...]
    return values.reshape(values.shape[0] * values.shape[1], values.shape[2])


def dp_bits():
    index = lax.axis_index("dp")
    return [(index >> b) & 1 for b in range(4)]


def chunk_row(chunk, bits, low):
    x, y, z = chunk & 1, (chunk >> 1) & 1, chunk >> 2
    j = z >> 1
    first, second = (x, y) if j == 0 else (y, x)
    return pl.multiple_of((j * 8 + (first ^ bits[j]) * 4 + second * 2 + (z & 1)) * low, 16)


def first_group(half, bits, hidden, mixed, gy, hidp, gyp_of, keep_x, send_x, keep_y, send_y, sums, left, left_mixed):
    slots, rows, width = mixed.shape
    tokens = slots * rows
    part = hidp.shape[2] // 2
    tall, low = part // 4, width // 16
    grad = flat_rows(gy)
    other = jnp.concatenate([gyp_of(s) for s in range(slots)], axis=0)
    sums[...] = ones_dot(grad)
    outs = ((keep_x, send_x), (keep_y, send_y))
    for j in range(2):
        there = pl.ds(pl.multiple_of((2 * j + half) * part, 128), part)
        own_t = hidden[:, :, there].reshape(tokens, part).T
        other_t = hidp[:, :, j * part : j * part + part].reshape(tokens, part).T
        for chunk in range(4):
            x, y = chunk & 1, chunk >> 1
            first, second = (x, y) if j == 0 else (y, x)
            start = pl.multiple_of(((first ^ bits[j]) * 2 + second) * tall, 16)
            left[j, pl.ds(start, tall), :tokens] = own_t[chunk * tall : chunk * tall + tall]
            left[j, pl.ds(start, tall), tokens:] = other_t[chunk * tall : chunk * tall + tall]
        product = (dot(left[j, :, :tokens], grad) + dot(left[j, :, tokens:], other)).astype(BF16)
        for side in range(2):
            outs[j][side][:, :tall] = product[side * 2 * tall : side * 2 * tall + 2 * tall].reshape(2, tall, width)
    mixed_t = flat_rows(mixed).T
    for chunk in range(16):
        left_mixed[pl.ds(chunk_row(chunk, bits, low), low), :] = mixed_t[chunk * low : chunk * low + low]
    product = dot(left_mixed[...], grad).astype(BF16)
    for j in range(2):
        for side in range(2):
            at = (j * 8 + side * 4) * low
            outs[j][side][:, tall:] = product[at : at + 4 * low].reshape(2, 2 * low, width)


def second_group(half, bits, nb, na, gu, gp, nbp, gup, keep_x, send_x, keep_y, send_y, sums_u, sums_p, left_b, left_a):
    slots, rows, width = nb.shape
    tokens = slots * rows
    part = gup.shape[2] // 2
    low = width // 16
    outs = ((keep_x, send_x), (keep_y, send_y))

    def put(product, column):
        product = product.astype(BF16)
        for j in range(2):
            for side in range(2):
                at = (j * 8 + side * 4) * low
                outs[j][side][:, :, :, column : column + product.shape[1]] = product[at : at + 4 * low].reshape(
                    2, 2, low, product.shape[1]
                )

    na_t, nb_t, nbp_t = flat_rows(na).T, flat_rows(nb).T, flat_rows(nbp).T
    for chunk in range(16):
        at = pl.ds(chunk_row(chunk, bits, low), low)
        left_a[at, :] = na_t[chunk * low : chunk * low + low]
        left_b[at, :tokens] = nb_t[chunk * low : chunk * low + low]
        left_b[at, tokens:] = nbp_t[chunk * low : chunk * low + low]
    for j in range(2):
        there = pl.ds(pl.multiple_of((2 * j + half) * part, 128), part)
        own = gu[:, :, there].reshape(tokens, part)
        other = gup[:, :, j * part : j * part + part].reshape(tokens, part)
        put(dot(left_b[:, :tokens], own) + dot(left_b[:, tokens:], other), j * part)
    for block in range(3):
        at = slice(block * width, block * width + width)
        put(dot(left_a[...], gp[:, :, at].reshape(tokens, width)), 2 * part + block * width)
    sums_u[...] = ones_dot(flat_rows(gu))
    sums_p[...] = ones_dot(flat_rows(gp))


def plus(left, right):
    return left.astype(F32) + right.astype(F32)


def add_first_kernel(section, keep_x, keep_y, arrived_x, arrived_y, kept, send_x, send_y):
    @pl.when(lax.axis_index("section") == section)
    def _():
        bits = dp_bits()
        for j, (keep, arrived, send) in enumerate(((keep_x, arrived_x, send_x), (keep_y, arrived_y, send_y))):
            mine = bits[1 - j]
            kept[j] = plus(keep[mine], arrived[mine]).astype(BF16)
            send[...] = plus(keep[1 - mine], arrived[1 - mine]).astype(BF16)


def add_second_kernel(section, shape, kept, arrived_x, arrived_y, own, to_1, to_2, to_3):
    @pl.when(lax.axis_index("section") == section)
    def _():
        bits = dp_bits()
        for side in range(2):

            @pl.when(bits[3] == side)
            def _():
                near, far = ((arrived_x, arrived_y), (arrived_y, arrived_x))[side]
                if len(shape) == 3:
                    near_sum, far_sum = (lambda b: plus(kept[side, b], near[b])), (lambda b: plus(kept[1 - side, b], far[b]))
                    own[...] = near_sum(bits[2])
                    to_1[...] = near_sum(1 - bits[2]).astype(BF16)
                    to_2[...] = far_sum(bits[2]).astype(BF16)
                    to_3[...] = far_sum(1 - bits[2]).astype(BF16)
                else:
                    low = to_1.shape[0]
                    tall = own.shape[0] - low
                    own[:tall] = plus(kept[side, :tall], near[:tall])
                    to_2[:tall] = plus(kept[1 - side, :tall], far[:tall]).astype(BF16)
                    here = pl.ds(pl.multiple_of(tall + bits[2] * low, 16), low)
                    there = pl.ds(pl.multiple_of(tall + (1 - bits[2]) * low, 16), low)
                    own[tall:] = plus(kept[side, here], near[here])
                    to_1[...] = plus(kept[side, there], near[there]).astype(BF16)
                    to_2[tall:] = plus(kept[1 - side, here], far[here]).astype(BF16)
                    to_3[...] = plus(kept[1 - side, there], far[there]).astype(BF16)


def final_first_kernel(*refs):
    down_out, proj_out = refs[8:]
    for section in range(2):

        @pl.when(lax.axis_index("section") == section)
        def _():
            own, from_1, from_2, from_3 = refs[4 * section : 4 * section + 4]
            tall = down_out.shape[0]
            down_out[...] = own[:tall] + from_2[:tall].astype(F32)
            proj_out[...] = own[tall:] + from_2[tall:].astype(F32) + plus(from_1[...], from_3[...])


def final_second_kernel(*refs):
    up_out, qkv_out = refs[8:]
    for section in range(2):

        @pl.when(lax.axis_index("section") == section)
        def _():
            own, from_1, from_2, from_3 = refs[4 * section : 4 * section + 4]
            part = up_out.shape[1] // 4
            half = dp_bits()[2]
            for j in range(2):
                at = slice(j * part, j * part + part)
                near = pl.ds(pl.multiple_of((2 * j + half) * part, 128), part)
                far = pl.ds(pl.multiple_of((2 * j + 1 - half) * part, 128), part)
                up_out[:, near] = own[:, at] + from_2[:, at].astype(F32)
                up_out[:, far] = plus(from_1[:, at], from_3[:, at])
            rest = slice(2 * part, None)
            qkv_out[...] = own[:, rest] + from_2[:, rest].astype(F32) + plus(from_1[:, rest], from_3[:, rest])


def partner_swap(shard, sections, distance):
    count = lax.axis_size("dp")
    pairs = [(s * count + i, s * count + (i ^ distance)) for s in sections for i in range(count)]
    return lax.ppermute(shard, ("section", "dp"), pairs)


def struct(*shape, dtype=BF16):
    return jax.ShapeDtypeStruct(shape, dtype)


def summed_first_stage(section, buffers, name, after=()):
    keep_x, send_x, keep_y, send_y = buffers
    arrived_x = partner_swap(send_x, (section,), 1)
    arrived_y = partner_swap(send_y, (section,), 2)
    rest = keep_x.shape[1:]
    return call(
        functools.partial(add_first_kernel, section), [keep_x, keep_y, arrived_x, arrived_y],
        [struct(2, *rest), struct(*rest), struct(*rest)], name + "_add_1", after=after,
    )


def summed_second_stage(section, parts, name, low, after=()):
    kept, send_x, send_y = parts
    arrived_x = partner_swap(send_x, (section,), 2)
    arrived_y = partner_swap(send_y, (section,), 1)
    shape = send_x.shape
    width = shape[-1]
    tall = 0 if len(shape) == 3 else shape[0] - 2 * low
    own, to_1, to_2, to_3 = call(
        functools.partial(add_second_kernel, section, shape), [kept, arrived_x, arrived_y],
        [struct(tall + low, width, dtype=F32), struct(low, width), struct(tall + low, width), struct(low, width)],
        name + "_add_2", after=after,
    )
    return [own] + [partner_swap(to, (section,), distance) for to, distance in ((to_1, 4), (to_2, 8), (to_3, 12))]


def paired_gradients(boundary, lengths, params, tables, swapped):
    slots = lengths.shape[0]
    width = boundary.shape[2]
    rows = boundary.shape[1] // slots
    units = params[8].shape[2]
    local_rows = boundary.reshape(slots, rows, width)
    tall, low = units // 16, width // 16
    tokens = slots * rows

    other = partner_swap(boundary, (0, 1), 4).reshape(slots, rows, width)
    result_0, saved, held = forward_first(lengths, local_rows, params, tables)
    own, gain_a, shift_a, gain_b, shift_b, w_qkv, b_qkv, w_proj, b_proj, w_up, b_up, w_down, b_down, *tabs = held
    arrived_1 = lax.ppermute(result_0, "section", swapped)
    partner_1 = partner_swap(arrived_1, (1,), 4)

    count = len(held)

    def forward_both(lengths_ref, arriving, *refs):
        section = lax.axis_index("section")
        slot = 1 - section
        inputs = lambda: jnp.where(section == 0, refs[0][slot], arriving[...])
        outs = refs[count:]
        forward_body(slot, lengths_ref[slot], inputs, lambda name, part: None, *refs[:count], outs[-1], *outs[:-1])

    *saved, result_1 = call(forward_both, [lengths, arrived_1, *held], [struct(rows, width)], "forward_1", kept=saved)
    arrived_2 = lax.ppermute(result_1, "section", swapped)
    partner_2 = partner_swap(arrived_2, (1,), 4)

    def forward_last(lengths_ref, arriving, other_ref, *refs):
        section = lax.axis_index("section")
        outs = refs[count:]
        slot = slots - 1

        @pl.when(section == 1)
        def _():
            forward_body(
                slot, lengths_ref[slot], lambda: arriving[...], lambda name, part: None, *refs[:count],
                outs[len(saved)], *outs[: len(saved)],
            )

        @pl.when(section == 0)
        def _():
            partner_forward(dp_bits()[2], lambda s: other_ref[s], refs[3], refs[4], refs[9], refs[10], *outs[len(saved) + 1 :])

    *saved, result_2, nbp, hidp, slopep = call(
        forward_last, [lengths, arrived_2, other, *held],
        [struct(rows, width)] + [pltpu.VMEM((slots, rows, n), BF16) for n in (width, units // 2, units // 2)],
        "forward_2", kept=saved,
    )
    x_s, na_s, nb_s, qkv_s, pt_s, mixed_s, hidden_s, slope_s = saved

    first_buffers = [struct(2, tall + 2 * low, width)] * 4
    first_scratch = [pltpu.VMEM((2, 4 * tall, 2 * tokens), BF16), pltpu.VMEM((width, tokens), BF16)]

    def first_upper(partner_a, partner_b, other_ref, own_ref, gain, shift, wu, bu, hidden, mixed, *refs):
        @pl.when(lax.axis_index("section") == 1)
        def _():
            nbp_ref, hidp_ref, slopep_ref, *outs = refs
            bits = dp_bits()
            partner_forward(bits[2], lambda s: (partner_a, partner_b)[s][...], gain, shift, wu, bu, nbp_ref, hidp_ref, slopep_ref)
            first_group(bits[2], bits, hidden, mixed, own_ref, hidp_ref, lambda s: other_ref[s], *outs)

    nbp, hidp, slopep, *upper_first, sums_y = call(
        first_upper, [partner_1, partner_2, other, own, gain_b, shift_b, w_up, b_up, hidden_s, mixed_s],
        first_buffers + [pltpu.VMEM((8, width), F32)], "down_proj_grads_upper", kept=[nbp, hidp, slopep], scratch=first_scratch,
    )

    back_operands = [x_s, gain_a, gain_b, w_qkv, w_proj, w_up, w_down, *tabs, pt_s]
    back_count = len(back_operands)

    def backward_first(own_ref, *refs):
        @pl.when(lax.axis_index("section") == 1)
        def _():
            qkv_io, slope_io, gy, vec, gx = refs[back_count:]
            backward_body(0, lambda: own_ref[0], *refs[:back_count], gx, qkv_io, slope_io, gy, vec)

    *grads, back_0 = call(
        backward_first, [own, *back_operands],
        [pltpu.VMEM((slots, rows, width), BF16), pltpu.VMEM((slots, 8, width), F32), struct(rows, width)], "backward_0",
        kept=[qkv_s, slope_s], after=[sums_y],
    )
    arrived_4 = lax.ppermute(back_0, "section", swapped)
    partner_4 = partner_swap(arrived_4, (0,), 4)
    upper_parts = summed_first_stage(1, upper_first, "upper_first")

    def backward_both(own_ref, arriving, *refs):
        section = lax.axis_index("section")
        outs = refs[back_count:]
        source = lambda: jnp.where(section == 0, arriving[...], own_ref[section])
        backward_body(section, source, *refs[:back_count], outs[-1], *outs[:-1])

    *grads, back_1 = call(
        backward_both, [own, arrived_4, *back_operands], [struct(rows, width)], "backward_1", kept=grads, after=upper_parts[:1]
    )
    arrived_5 = lax.ppermute(back_1, "section", swapped)
    partner_5 = partner_swap(arrived_5, (0,), 4)
    upper_last = summed_second_stage(1, upper_parts, "upper_first", low)

    second_buffers = [struct(2, 2, low, units // 2 + 3 * width)] * 4
    second_scratch = [pltpu.VMEM((width, 2 * tokens), BF16), pltpu.VMEM((width, tokens), BF16)]

    def backward_last(arriving, other_ref, nb, na, nbp_ref, *refs):
        section = lax.axis_index("section")
        qkv_io, slope_io, gy, vec, slopep_ref, gx, *rest = refs[back_count:]

        @pl.when(section == 0)
        def _():
            backward_body(slots - 1, lambda: arriving[...], *refs[:back_count], gx, qkv_io, slope_io, gy, vec)

        @pl.when(section == 1)
        def _():
            bits = dp_bits()
            partner_backward(bits[2], lambda s: other_ref[s], refs[6], slopep_ref)
            second_group(bits[2], bits, nb, na, slope_io, qkv_io, nbp_ref, slopep_ref, *rest)

    gp_s, gu_s, gy_s, vec_s, slopep, back_2, *upper_second, sums_u, sums_p = call(
        backward_last, [arrived_5, other, nb_s, na_s, nbp, *back_operands],
        [struct(rows, width)] + second_buffers + [pltpu.VMEM((8, units), F32), pltpu.VMEM((8, 3 * width), F32)],
        "backward_2", kept=[*grads, slopep], scratch=second_scratch, after=upper_last[:1],
    )

    def first_lower(partner_a, partner_b, wd, hidden, mixed, gy, hidp_ref, slopep_ref, sums, *refs):
        @pl.when(lax.axis_index("section") == 0)
        def _():
            bits = dp_bits()
            rows_of = lambda s: (partner_a, partner_b)[s][...]
            partner_backward(bits[2], rows_of, wd, slopep_ref)
            *outs, left, left_mixed = refs
            first_group(bits[2], bits, hidden, mixed, gy, hidp_ref, rows_of, *outs, sums, left, left_mixed)

    slopep, sums_y, *lower_first = call(
        first_lower, [partner_4, partner_5, w_down, hidden_s, mixed_s, gy_s, hidp], first_buffers,
        "down_proj_grads_lower", kept=[slopep, sums_y], scratch=first_scratch,
    )

    def second_lower(nb, na, gu, gp, nbp_ref, gup_ref, sums_u_ref, sums_p_ref, *refs):
        @pl.when(lax.axis_index("section") == 0)
        def _():
            bits = dp_bits()
            *outs, left_b, left_a = refs
            second_group(bits[2], bits, nb, na, gu, gp, nbp_ref, gup_ref, *outs, sums_u_ref, sums_p_ref, left_b, left_a)

    sums_u, sums_p, *lower_second = call(
        second_lower, [nb_s, na_s, gu_s, gp_s, nbp, slopep], second_buffers, "up_qkv_grads_lower", kept=[sums_u, sums_p],
        scratch=second_scratch, after=upper_last[1:],
    )

    upper_parts = summed_first_stage(1, upper_second, "upper_second", after=[sums_u])
    lower_parts = summed_first_stage(0, lower_first, "lower_first", after=upper_parts[:1])
    upper_rest = summed_second_stage(1, upper_parts, "upper_second", low, after=lower_parts[:1])
    lower_more = summed_first_stage(0, lower_second, "lower_second", after=upper_rest[:1])
    lower_last = summed_second_stage(0, lower_parts, "lower_first", low, after=lower_more[:1])
    lower_rest = summed_second_stage(0, lower_more, "lower_second", low, after=lower_last[:1])
    down, proj = call(
        final_first_kernel, lower_last + upper_last, [struct(tall, width, dtype=F32), struct(low, width, dtype=F32)], "down_proj_sum",
    )
    up, qkv = call(
        final_second_kernel, lower_rest + upper_rest, [struct(low, units, dtype=F32), struct(low, 3 * width, dtype=F32)], "up_qkv_sum",
    )
    finals, input_grads = [result_1, result_2], [back_1, back_2]
    return finals, input_grads, vec_s, sums_y[0], sums_u[0], sums_p[0], down, proj, up, qkv


def plain_gradients(boundary, lengths, params, tables, swapped, bits):
    count = lax.axis_size("dp")
    slots = lengths.shape[0]
    width = boundary.shape[2]
    rows = boundary.shape[1] // slots
    units = params[8].shape[2]
    ticks = slots + 1
    result, saved, held = forward_first(lengths, boundary.reshape(slots, rows, width), params, tables)
    own, gain_a, shift_a, gain_b, shift_b, w_qkv, b_qkv, w_proj, b_proj, w_up, b_up, w_down, b_down, *tabs = held
    held_count = len(held)
    finals = [result]
    for t in range(1, ticks):
        arriving = lax.ppermute(result, "section", swapped)

        def forward_step(lengths_ref, arriving_ref, *refs, tick=t):
            section = lax.axis_index("section")
            slot = jnp.clip(tick - section, 0, slots - 1)
            inputs = lambda: jnp.where(section == 0, refs[0][slot], arriving_ref[...])
            outs = refs[held_count:]
            forward_body(slot, lengths_ref[slot], inputs, lambda name, part: None, *refs[:held_count], outs[-1], *outs[:-1])

        *saved, result = call(forward_step, [lengths, arriving, *held], [struct(rows, width)], "forward", kept=saved)
        finals.append(result)
    x_s, na_s, nb_s, qkv_s, pt_s, mixed_s, hidden_s, slope_s = saved
    operands = [x_s, gain_a, gain_b, w_qkv, w_proj, w_up, w_down, *tabs, pt_s]
    grads = [qkv_s, slope_s]
    input_grads = []
    arriving = own[0]
    for t in range(ticks):

        def backward_step(own_ref, arriving_ref, *refs, tick=t):
            section = lax.axis_index("section")
            slot = tick - 1 + section
            *io, gx_out = refs[len(operands) :]

            @pl.when((slot >= 0) & (slot < slots))
            def _():
                source = lambda: jnp.where(section == 0, arriving_ref[...], own_ref[slot])
                backward_body(slot, source, *refs[: len(operands)], gx_out, *io)

        shapes = [pltpu.VMEM((slots, rows, width), BF16), pltpu.VMEM((slots, 8, width), F32)] if t == 0 else []
        *grads, result = call(backward_step, [own, arriving, *operands], shapes + [struct(rows, width)], "backward", kept=grads)
        input_grads.append(result)
        if t + 1 < ticks:
            arriving = lax.ppermute(result, "section", swapped)
    gp_s, gu_s, gy_s, vec_s = grads
    order = list(range(len(bits)))

    def summed(full):
        keep, send = parted(full, 0, bits[0])
        return halving_sum(keep, send, order, count, bits, F32)

    both = jnp.concatenate([plain_grads(hidden_s, gy_s, count), plain_grads(mixed_s, gy_s, count)], axis=1)
    down, up, qkv = summed(both), summed(plain_grads(nb_s, gu_s, count)), summed(plain_grads(na_s, gp_s, count))
    tall = units // count
    sums = [jnp.sum(values, axis=(0, 1), dtype=F32) for values in (gy_s, gu_s, gp_s)]
    return finals[1:], input_grads[1:], vec_s, *sums, down[:tall], down[tall:], up, qkv


def per_device(boundary, lengths, *params):
    section = lax.axis_index("section")
    count = lax.axis_size("dp")
    bits = [(lax.axis_index("dp") >> b) & 1 for b in range(count.bit_length() - 1)]
    slots = lengths.shape[0]
    width = boundary.shape[2]
    units = params[8].shape[2]
    tables = [jnp.asarray(table) for table in rotary_lanes(boundary.shape[1] // slots, 2 * HEAD)]
    swapped = [(0, 1), (1, 0)]
    if count == 16 and slots == 2 and width % 768 == 0:
        out = paired_gradients(boundary, lengths, params, tables, swapped)
    else:
        out = plain_gradients(boundary, lengths, params, tables, swapped, bits)
    finals, input_grads, vec_s, gy_sums, gu_sums, gp_sums, down, proj, up, qkv = out
    vec = jnp.sum(vec_s, axis=0)
    small = jnp.concatenate(
        [piece.reshape(count, -1) for piece in (vec[0], vec[1], vec[2], vec[3], gy_sums, gu_sums, gp_sums)], axis=1
    )
    small = halving_sum(*parted(small, 0, bits[0]), list(range(len(bits))), count, bits, F32)
    low, tall = width // count, units // count
    gain_a, shift_a, gain_b, shift_b, bias_y, bias_up, bias_qkv = jnp.split(small, np.cumsum([low] * 5 + [tall]), axis=0)
    joined = jnp.where(section == 0, jnp.concatenate(input_grads, axis=0), jnp.concatenate(finals, axis=0))
    results = (joined, gain_a, shift_a, qkv, bias_qkv, proj, bias_y, gain_b, shift_b, up, bias_up, down, bias_y)
    return tuple(result[None] for result in results)


def solution(mesh):
    split = P("section", "dp")
    deep = P("section", "dp", None)
    flat, matrix = P("section", None), P("section", None, None)
    return jax.shard_map(
        per_device,
        mesh=mesh,
        in_specs=(deep, P("dp"), flat, flat, matrix, flat, matrix, flat, flat, flat, matrix, flat, matrix, flat),
        out_specs=(deep, split, split, deep, split, deep, split, split, split, deep, split, deep, split),
        check_vma=False,
    )
```

```python
import functools
import math

import jax
import jax.numpy as jnp
import numpy as np
from jax import lax
from jax.experimental import pallas as pl
from jax.experimental.pallas import tpu as pltpu
from jax.sharding import PartitionSpec as P

HEAD = 64
LANES = 256
CHUNK = 512
EPS = 1e-05
NEG_FILL = -1e30
VMEM_BYTES = 12 * 1024 * 1024
FIRST_VMEM_BYTES = 12 * 1024 * 1024
F32 = jnp.float32
BF16 = jnp.bfloat16


def dot(left, right):
    return jnp.dot(left, right, preferred_element_type=F32)


def dot_nt(left, right):
    return lax.dot_general(left, right, (((1,), (1,)), ((), ())), preferred_element_type=F32)


def normalised(values):
    centred = values - jnp.mean(values, axis=-1, keepdims=True)
    variance = jnp.mean(centred * centred, axis=-1, keepdims=True)
    scale = lax.rsqrt(variance + EPS)
    return centred * scale, scale


def gelu_parts(values):
    integral = 0.5 + 0.5 * lax.erf(values * math.sqrt(0.5))
    bell = jnp.exp(values * values * -0.5)
    return values * integral, integral + values * bell * (1.0 / math.sqrt(2.0 * math.pi))


def rotary_lanes(seq_len, lanes):
    rot_dims = HEAD // 4
    half = rot_dims // 2
    frequency = np.float32(10000.0) ** (-(np.arange(half, dtype=np.float32) * np.float32(2.0) / np.float32(rot_dims)))
    angles = np.arange(seq_len, dtype=np.float32)[:, None] * frequency.astype(np.float32)[None, :]
    cosine, sine = np.cos(angles).astype(np.float32), np.sin(angles).astype(np.float32)
    same = np.ones((seq_len, HEAD), np.float32)
    later = np.zeros((seq_len, HEAD), np.float32)
    earlier = np.zeros((seq_len, HEAD), np.float32)
    same[:, :half] = cosine
    same[:, half:rot_dims] = cosine
    later[:, :half] = -sine
    earlier[:, half:rot_dims] = sine
    return [np.tile(t, (1, lanes // HEAD)) for t in (same, later, earlier)]


def turned(values, same, later, earlier, sign):
    half = HEAD // 8
    width = values.shape[1]
    same, later, earlier = (jnp.concatenate([t] * (width // t.shape[1]), axis=1) for t in (same, later, earlier))
    ahead = pltpu.roll(values, width - half, 1)
    behind = pltpu.roll(values, half, 1)
    if sign > 0:
        return values * same + ahead * later + behind * earlier
    return values * same - ahead * later - behind * earlier


def blocked_bias(rows, length):
    out = []
    for start in range(0, rows, 128):
        keys = start + 128
        key_pos = lax.broadcasted_iota(jnp.int32, (keys, 2 * 128), 0)
        query_pos = start + (lax.broadcasted_iota(jnp.int32, (keys, 2 * 128), 1) & 127)
        out.append(jnp.where((key_pos <= query_pos) & (key_pos < length), 0.0, NEG_FILL))
    return out


def heads_apart(block, lane):
    zero = jnp.zeros_like(block)
    return jnp.concatenate([jnp.where(lane < HEAD, block, zero), jnp.where(lane < HEAD, zero, block)], axis=0)


def dot_tn(left, right):
    return lax.dot_general(left, right, (((0,), (0,)), ((), ())), preferred_element_type=F32)


def probs_rows(block):
    start = 128 * (block * (block + 1) // 2)
    return slice(start, start + 128 * (block + 1))


def some(offset, size):
    return slice(offset, offset + size) if isinstance(offset, int) else pl.ds(pl.multiple_of(offset, 128), size)


def spans(pair, width):
    return [slice(b * width + pair * 2 * HEAD, b * width + (pair + 1) * 2 * HEAD) for b in range(3)]


def forward_units(slot, length, ready, na, nb, wqkv, bqkv, wu, bu, tables, qkv, pt, mixed, hidden, slope, low_head, low_unit, lanes):
    rows = qkv.shape[1]
    whole_width, width = wqkv.shape[1], qkv.shape[2] // 3
    pairs = width // (2 * HEAD)
    chunk = hidden.shape[2] // pairs
    biases = blocked_bias(rows, length)
    lane = lax.broadcasted_iota(jnp.int32, (128, 2 * HEAD), 1)
    per = lanes // (2 * HEAD)
    for pair in range(pairs):
        if pair % per == 0:
            low = pair * 2 * HEAD
            ready("qkv", pair // per)

            def packed(block):
                at = some(block * whole_width + low_head + low, lanes)
                return dot(na[slot], wqkv[0, :, at]) + bqkv[:, at].astype(F32)

            qkv[slot, :, low : low + lanes] = (turned(packed(0), *tables, 1) * (HEAD**-0.5)).astype(BF16)
            qkv[slot, :, width + low : width + low + lanes] = turned(packed(1), *tables, 1).astype(BF16)
            qkv[slot, :, 2 * width + low : 2 * width + low + lanes] = packed(2).astype(BF16)
        span, span_k, span_v = spans(pair, width)
        all_scores = []
        for block, start in enumerate(range(0, rows, 128)):
            keys = start + 128
            q2 = heads_apart(qkv[slot, start:keys, span], lane)
            all_scores.append(dot_nt(qkv[slot, :keys, span_k], q2) + biases[block])
        ready("up", pair)
        there = some(low_unit + pair * chunk, chunk)
        up = dot(nb[slot], wu[0, :, there]) + bu[:, there].astype(F32)
        for block, start in enumerate(range(0, rows, 128)):
            keys = start + 128
            scores = all_scores[block]
            exponent = jnp.exp(scores - jnp.max(scores, axis=0, keepdims=True))
            probs = (exponent * (1.0 / jnp.sum(exponent, axis=0, keepdims=True))).astype(BF16)
            pt[slot, pair, probs_rows(block)] = probs
            both = dot_tn(probs, qkv[slot, :keys, span_v])
            mixed[slot, start:keys, span] = jnp.where(lane < HEAD, both[:128], both[128:]).astype(BF16)
        here = slice(pair * chunk, pair * chunk + chunk)
        hidden_f32, slope_f32 = gelu_parts(up)
        hidden[slot, :, here] = hidden_f32.astype(BF16)
        slope[slot, :, here] = slope_f32.astype(BF16)


def backward_units(slot, gy, wp, wd, tables, pt, qkv, slope, low_head, low_unit, lanes):
    rows = qkv.shape[1]
    width = qkv.shape[2] // 3
    pairs = width // (2 * HEAD)
    chunk = slope.shape[2] // pairs
    lane = lax.broadcasted_iota(jnp.int32, (128, 2 * HEAD), 1)
    per = lanes // (2 * HEAD)
    for pair in range(pairs):
        if pair % per == 0:
            gm_group = dot_nt(gy(), wp[0, some(low_head + pair * 2 * HEAD, lanes), :]).astype(BF16)
            group_q, group_k = [], []
        span, span_k, span_v = spans(pair, width)
        gm = gm_group[:, (pair % per) * 2 * HEAD : (pair % per + 1) * 2 * HEAD]
        gv_sum, gk_sum, gq_blocks = None, None, []
        for block, start in enumerate(range(0, rows, 128)):
            keys = start + 128
            gm2 = heads_apart(gm[start:keys], lane)
            q2 = heads_apart(qkv[slot, start:keys, span], lane)
            probs = pt[slot, pair, probs_rows(block)]
            weighted = probs.astype(F32) * dot_nt(qkv[slot, :keys, span_v], gm2)
            inner = jnp.sum(weighted, axis=0, keepdims=True)
            gs = (weighted - probs.astype(F32) * inner).astype(BF16)
            gv_part = dot(probs, gm2)
            gk_part = dot(gs, q2)
            gq_part = dot_tn(gs, qkv[slot, :keys, span_k])
            gq_blocks.append(jnp.where(lane < HEAD, gq_part[:128], gq_part[128:]))
            if gv_sum is None:
                gv_sum, gk_sum = gv_part, gk_part
            else:
                gv_sum = jnp.concatenate([gv_sum + gv_part[:start], gv_part[start:]], axis=0)
                gk_sum = jnp.concatenate([gk_sum + gk_part[:start], gk_part[start:]], axis=0)
        qkv[slot, :, span_v] = gv_sum.astype(BF16)
        group_q.append(jnp.concatenate(gq_blocks, axis=0))
        group_k.append(gk_sum)
        if pair % per == per - 1:
            low = pair // per * lanes
            gq = turned(jnp.concatenate(group_q, axis=1) * (HEAD**-0.5), *tables, -1)
            qkv[slot, :, low : low + lanes] = gq.astype(BF16)
            gk = turned(jnp.concatenate(group_k, axis=1), *tables, -1)
            qkv[slot, :, width + low : width + low + lanes] = gk.astype(BF16)
        here = slice(pair * chunk, pair * chunk + chunk)
        grad = dot_nt(gy(), wd[0, some(low_unit + pair * chunk, chunk), :])
        slope[slot, :, here] = (grad * slope[slot, :, here].astype(F32)).astype(BF16)


def forward_body(
    slot, length, inputs, ready, own, gain_a, shift_a, gain_b, shift_b, wqkv, bqkv, wp, bp, wu, bu, wd, bd, same, later, earlier,
    y_out, x_out, na_out, nb_out, qkv_out, pt_out, mixed_out, hidden_out, slope_out,
):
    ready("small", 0)
    x_low = inputs()
    x_out[slot] = x_low
    xhat, _ = normalised(x_low.astype(F32))
    na_out[slot] = (xhat * gain_a[...].astype(F32) + shift_a[...].astype(F32)).astype(BF16)
    nb_out[slot] = (xhat * gain_b[...].astype(F32) + shift_b[...].astype(F32)).astype(BF16)
    tables = (same[...], later[...], earlier[...])
    forward_units(
        slot, length, ready, na_out, nb_out, wqkv, bqkv, wu, bu, tables, qkv_out, pt_out, mixed_out, hidden_out, slope_out, 0, 0, LANES
    )
    ready("rest", 0)
    total = x_out[slot].astype(F32) + (bp[...].astype(F32) + bd[...].astype(F32))
    y_out[...] = (total + dot(mixed_out[slot], wp[0]) + dot(hidden_out[slot], wd[0])).astype(BF16)


def backward_body(
    slot, gy_source, x_in, gain_a, gain_b, wqkv, wp, wu, wd, same, later, earlier, pt_in, gx_out, qkv_io, slope_io, gy_out, vec_out
):
    width = gx_out.shape[1]
    gy_out[slot] = gy_source()
    tables = (same[...], later[...], earlier[...])
    backward_units(slot, lambda: gy_out[slot], wp, wd, tables, pt_in, qkv_io, slope_io, 0, 0, LANES)
    grad_b = dot_nt(slope_io[slot], wu[0])
    grad_a = dot_nt(qkv_io[slot], wqkv[0])
    xhat, scale = normalised(x_in[slot].astype(F32))
    sums = [jnp.sum(t, axis=0, keepdims=True) for t in (grad_a * xhat, grad_a, grad_b * xhat, grad_b)]
    vec_out[slot] = jnp.concatenate(sums + [jnp.zeros((4, width), F32)], axis=0)
    both = grad_a * gain_a[...].astype(F32) + grad_b * gain_b[...].astype(F32)
    inner = jnp.mean(both * xhat, axis=-1, keepdims=True)
    gx = gy_out[slot].astype(F32) + scale * (both - jnp.mean(both, axis=-1, keepdims=True) - xhat * inner)
    gx_out[...] = gx.astype(BF16)


def forward_first_kernel(tick, lengths, *refs):
    count = 17
    sources, held, outs, sems = refs[:count], refs[count : 2 * count], refs[2 * count : -1], refs[-1]
    copies = []
    waits = {}

    def fetch(name, part, index, at):
        source, target = (sources[index], held[index]) if at is None else (sources[index].at[at], held[index].at[at])
        copy = pltpu.make_async_copy(source, target, sems.at[len(copies)])
        copies.append(copy)
        waits.setdefault((name, part), []).append(copy)

    (own, gain_a, shift_a, gain_b, shift_b, wqkv, bqkv, wp, bp, wu, bu, wd, bd, same, later, earlier, _) = range(count)
    width = sources[wp].shape[1]
    units = sources[wu].shape[2]
    pairs = width // (2 * HEAD)
    groups = width // LANES
    for index in (own, gain_a, shift_a, gain_b, shift_b, bqkv, bp, bu, bd, same, later, earlier):
        fetch("small", 0, index, None)
    for pair in range(pairs):
        if pair * groups % pairs == 0:
            group = pair * groups // pairs
            for block in range(3):
                fetch("qkv", group, wqkv, (slice(None), slice(None), pl.ds(block * width + group * LANES, LANES)))
        fetch("up", pair, wu, (slice(None), slice(None), pl.ds(pair * (units // pairs), units // pairs)))
    fetch("rest", 0, wp, None)
    fetch("rest", 0, wd, None)
    for copy in copies:
        copy.start()

    def ready(name, part):
        for copy in waits[(name, part)]:
            copy.wait()

    section = lax.axis_index("section")
    slots = held[own].shape[0]
    slot = jnp.clip(tick - section, 0, slots - 1)
    forward_body(slot, lengths[slot], lambda: held[own][slot], ready, *held[:-1], *outs)


def backward_body(
    slot, gy_source, x_in, gain_a, gain_b, wqkv, wp, wu, wd, same, later, earlier,
    pt_in, gx_out, qkv_io, slope_io, gy_out, vec_out,
):
    rows, width = gx_out.shape
    units = wu.shape[2]
    pairs = width // (2 * HEAD)
    chunk = units // pairs
    gy_out[slot] = gy_source()
    lane = lax.broadcasted_iota(jnp.int32, (128, 2 * HEAD), 1)
    tables = (same[...], later[...], earlier[...])
    per = LANES // (2 * HEAD)
    for pair in range(pairs):
        if pair % per == 0:
            gm_group = dot_nt(gy_out[slot], wp[0, pair * 2 * HEAD : pair * 2 * HEAD + LANES, :]).astype(BF16)
            group_q, group_k = [], []
        span, span_k, span_v = (slice(b * width + pair * 2 * HEAD, b * width + (pair + 1) * 2 * HEAD) for b in range(3))
        gm = gm_group[:, (pair % per) * 2 * HEAD : (pair % per + 1) * 2 * HEAD]
        gv_sum, gk_sum, gq_blocks = None, None, []
        for block, start in enumerate(range(0, rows, 128)):
            keys = start + 128
            gm2 = heads_apart(gm[start:keys], lane)
            q2 = heads_apart(qkv_io[slot, start:keys, span], lane)
            pt = pt_in[slot, pair, probs_rows(block)]
            weighted = pt.astype(F32) * dot_nt(qkv_io[slot, :keys, span_v], gm2)
            inner = jnp.sum(weighted, axis=0, keepdims=True)
            gs = (weighted - pt.astype(F32) * inner).astype(BF16)
            gv_part = dot(pt, gm2)
            gk_part = dot(gs, q2)
            gq_part = dot_tn(gs, qkv_io[slot, :keys, span_k])
            gq_blocks.append(jnp.where(lane < HEAD, gq_part[:128], gq_part[128:]))
            if gv_sum is None:
                gv_sum, gk_sum = gv_part, gk_part
            else:
                gv_sum = jnp.concatenate([gv_sum + gv_part[:start], gv_part[start:]], axis=0)
                gk_sum = jnp.concatenate([gk_sum + gk_part[:start], gk_part[start:]], axis=0)
        qkv_io[slot, :, span_v] = gv_sum.astype(BF16)
        group_q.append(jnp.concatenate(gq_blocks, axis=0))
        group_k.append(gk_sum)
        if pair % per == per - 1:
            low = pair // per * LANES
            gq = turned(jnp.concatenate(group_q, axis=1) * (HEAD**-0.5), *tables, -1)
            qkv_io[slot, :, low : low + LANES] = gq.astype(BF16)
            gk = turned(jnp.concatenate(group_k, axis=1), *tables, -1)
            qkv_io[slot, :, width + low : width + low + LANES] = gk.astype(BF16)
        at = slice(pair * chunk, pair * chunk + chunk)
        slope_io[slot, :, at] = (dot_nt(gy_out[slot], wd[0, at, :]) * slope_io[slot, :, at].astype(F32)).astype(BF16)
    grad_b = dot_nt(slope_io[slot], wu[0])
    grad_a = dot_nt(qkv_io[slot], wqkv[0])
    xhat, scale = normalised(x_in[slot].astype(F32))
    sums = [jnp.sum(t, axis=0, keepdims=True) for t in (grad_a * xhat, grad_a, grad_b * xhat, grad_b)]
    vec_out[slot] = jnp.concatenate(sums + [jnp.zeros((4, width), F32)], axis=0)
    both = grad_a * gain_a[...].astype(F32) + grad_b * gain_b[...].astype(F32)
    inner = jnp.mean(both * xhat, axis=-1, keepdims=True)
    gx = gy_out[slot].astype(F32) + scale * (both - jnp.mean(both, axis=-1, keepdims=True) - xhat * inner)
    gx_out[...] = gx.astype(BF16)


VM = pl.BlockSpec(memory_space=pltpu.VMEM)
HBM = pl.BlockSpec(memory_space=pl.ANY)


def call(kernel, operands, out_shape, name, kept=(), scratch=(), flops=1 << 20, after=()):
    count = len(operands)
    after = list(after)

    def body(*refs):
        kernel(*refs[:count], *refs[count + len(kept) + len(after) :])

    return pl.pallas_call(
        body,
        in_specs=[pl.BlockSpec(memory_space=pltpu.SMEM) if o.dtype == jnp.int32 else VM for o in operands] + [VM] * len(kept) + [HBM] * len(after),
        out_specs=[VM] * (len(kept) + len(out_shape)),
        out_shape=[pltpu.VMEM(array.shape, array.dtype) for array in kept] + list(out_shape),
        input_output_aliases={count + i: i for i in range(len(kept))},
        scratch_shapes=list(scratch),
        compiler_params=pltpu.CompilerParams(vmem_limit_bytes=VMEM_BYTES),
        cost_estimate=pl.CostEstimate(flops=flops, bytes_accessed=1 << 16, transcendentals=0),
        name=name,
    )(*operands, *[pltpu.with_memory_space_constraint(array, pltpu.VMEM) for array in kept], *after)


def shape_of(array):
    return jax.ShapeDtypeStruct(array.shape, array.dtype)


def forward_shapes(local_rows, params):
    slots, rows, width = local_rows.shape
    units = params[8].shape[2]
    blocks = rows // 128
    probs = (slots, width // (2 * HEAD), 128 * (blocks * (blocks + 1) // 2), 2 * 128)
    columns = [width, width, width, 3 * width, None, width, units, units]
    return [jax.ShapeDtypeStruct((rows, width), BF16)] + [
        pltpu.VMEM(probs if n is None else (slots, rows, n), BF16) for n in columns
    ]


def forward_first(lengths, local_rows, params, tables):
    (gain_a, shift_a, w_qkv, b_qkv, w_proj, b_proj, gain_b, shift_b, w_up, b_up, w_down, b_down) = params
    held = [local_rows, gain_a, shift_a, gain_b, shift_b, w_qkv, b_qkv, w_proj, b_proj, w_up, b_up, w_down, b_down] + list(tables)
    shapes = [shape_of(array) for array in held] + forward_shapes(local_rows, params)

    def kernel(lengths_ref, *refs):
        count = len(held)
        forward_first_kernel(0, lengths_ref, *refs[:count], None, *refs[count : 2 * count], None, *refs[2 * count :])

    outs = pl.pallas_call(
        kernel,
        in_specs=[pl.BlockSpec(memory_space=pltpu.SMEM)] + [pl.BlockSpec(memory_space=pltpu.HBM)] * len(held),
        out_specs=[VM] * len(shapes),
        out_shape=shapes,
        scratch_shapes=[pltpu.SemaphoreType.DMA((40,))],
        compiler_params=pltpu.CompilerParams(vmem_limit_bytes=FIRST_VMEM_BYTES),
        cost_estimate=pl.CostEstimate(flops=1 << 20, bytes_accessed=1 << 16, transcendentals=0),
        name="layer_forward_first",
    )(lengths, *[pltpu.with_memory_space_constraint(array, pltpu.HBM) for array in held])
    count = len(held)
    return outs[count], outs[count + 1 :], outs[:count]


def swap(shard, bit, count):
    return lax.ppermute(shard, "dp", [(i, i ^ (1 << bit)) for i in range(count)])


def parted(values, position, mine):
    count = values.shape[0]
    shaped = values.reshape((count >> (position + 1), 2, 1 << position) + values.shape[1:])
    out = []
    for side in (mine, 1 - mine):
        piece = lax.dynamic_index_in_dim(shaped, side, axis=1, keepdims=False)
        out.append(piece.reshape((count // 2,) + values.shape[1:]))
    return out


def halving_sum(keep, send, order, count, bits, final):
    left = sorted(order)
    for number, bit in enumerate(order):
        left.remove(bit)
        arrived = swap(send, bit, count)
        if number + 1 == len(order):
            return (keep.astype(F32) + arrived.astype(F32)).astype(final)[0]
        position = left.index(order[number + 1])
        keep_a, send_a = parted(keep, position, bits[order[number + 1]])
        keep_b, send_b = parted(arrived, position, bits[order[number + 1]])
        send = (send_a.astype(F32) + send_b.astype(F32)).astype(send_a.dtype)
        keep = (keep_a.astype(F32) + keep_b.astype(F32)).astype(send_a.dtype)


def plain_grads(left, right, count):
    rows = left.shape[0] * left.shape[1]
    product = lax.dot_general(
        left.reshape(rows, -1), right.reshape(rows, -1), (((0,), (0,)), ((), ())), preferred_element_type=F32
    ).astype(BF16)
    return product.reshape(count, product.shape[0] // count, product.shape[1])


def partner_forward(half, lengths, rows_of, gain_a, shift_a, gain_b, shift_b, wqkv, bqkv, wu, bu, tables, nap, nbp, qkvp, ptp, mixedp, hidp, slopep):
    for s in range(nap.shape[0]):
        xhat, _ = normalised(rows_of(s).astype(F32))
        nap[s] = (xhat * gain_a[...].astype(F32) + shift_a[...].astype(F32)).astype(BF16)
        nbp[s] = (xhat * gain_b[...].astype(F32) + shift_b[...].astype(F32)).astype(BF16)
        lanes = mixedp.shape[2]
        forward_units(
            s, lengths[s], lambda name, part: None, nap, nbp, wqkv, bqkv, wu, bu, tables, qkvp, ptp, mixedp, hidp, slopep,
            half * lanes, half * hidp.shape[2], lanes,
        )


def partner_backward(half, rows_of, wp, wd, tables, ptp, qkvp, slopep):
    lanes = qkvp.shape[2] // 3
    for s in range(qkvp.shape[0]):
        backward_units(s, lambda: rows_of(s), wp, wd, tables, ptp, qkvp, slopep, half * lanes, half * slopep.shape[2], lanes)


ORDERS = {"down": (0, 1, 2), "up": (1, 2, 0), "attn": (2, 0, 1)}


def dp_bit(bit):
    return (lax.axis_index("dp") >> bit) & 1


def eighth_row(chunk, order, rows):
    first, second, third = ((chunk >> bit) & 1 for bit in order)
    return ((first ^ dp_bit(order[0])) * 4 + second * 2 + third) * rows


def row_slice(start, rows):
    return pl.ds(pl.multiple_of(start, 16), rows)


def flat_rows(ref, at=slice(None)):
    values = ref[:, :, at]
    return values.reshape(values.shape[0] * values.shape[1], values.shape[2])


def ones_dot(values):
    return dot(jnp.ones((16, values.shape[0]), BF16), values)[:8]


def sixteenths(ref, left, order, tokens_from):
    turned_ref = flat_rows(ref).T
    low = turned_ref.shape[0] // 16
    for chunk in range(16):
        start = eighth_row(chunk & 7, order, 2 * low) + (chunk >> 3) * low
        left[row_slice(start, low), tokens_from : tokens_from + turned_ref.shape[1]] = turned_ref[chunk * low : chunk * low + low]


def eighths(turned_rows, left, order, tokens_from):
    low = turned_rows.shape[0] // 8
    for chunk in range(8):
        left[row_slice(eighth_row(chunk, order, low), low), tokens_from : tokens_from + turned_rows.shape[1]] = turned_rows[
            chunk * low : chunk * low + low
        ]


def up_group_kernel(nb, nbp, gu, gup, keep, send, left):
    half = dp_bit(3)
    tokens = nb.shape[0] * nb.shape[1]
    units = gup.shape[2]
    sixteenths(nb, left, ORDERS["up"], 0)
    sixteenths(nbp, left, ORDERS["up"], tokens)
    rows = left.shape[0] // 8
    for low in range(0, units, 512):
        at = slice(low, low + 512)
        product = dot(left[:, :tokens], flat_rows(gu, some(half * units + low, 512))) + dot(left[:, tokens:], flat_rows(gup, at))
        product = product.astype(BF16).reshape(8, rows, 512)
        keep[:, :, at] = product[:4]
        send[:, :, at] = product[4:]


def attn_group_kernel(na, nap, gp, gpp, mixed, mixedp, gy, gyp_of, gu, vec, keep, send, left, left_mixed):
    half = dp_bit(3)
    tokens = na.shape[0] * na.shape[1]
    width = na.shape[2]
    lanes = mixedp.shape[2]
    order = ORDERS["attn"]
    sixteenths(na, left, order, 0)
    sixteenths(nap, left, order, tokens)
    rows = left.shape[0] // 8
    for block in range(3):
        at = slice(block * lanes, block * lanes + lanes)
        own = flat_rows(gp, some(block * width + half * lanes, lanes))
        product = dot(left[:, :tokens], own) + dot(left[:, tokens:], flat_rows(gpp, at))
        product = product.astype(BF16).reshape(8, rows, lanes)
        keep[:, :rows, at] = product[:4]
        send[:, :rows, at] = product[4:]
    eighths(flat_rows(mixed, some(half * lanes, lanes)).T, left_mixed, order, 0)
    eighths(flat_rows(mixedp).T, left_mixed, order, tokens)
    own_gy = flat_rows(gy)
    other_gy = jnp.concatenate([gyp_of(s) for s in range(gy.shape[0])], axis=0)
    product = dot(left_mixed[:, :tokens], own_gy) + dot(left_mixed[:, tokens:], other_gy)
    low = left_mixed.shape[0] // 8
    product = product.astype(BF16).reshape(8, low, width)
    keep[:, rows:, :width] = product[:4]
    send[:, rows:, :width] = product[4:]
    ones_row = lax.broadcasted_iota(jnp.int32, (16, lanes), 0)
    norms = vec[0] + vec[1]
    spread = [jnp.broadcast_to(norms[i : i + 1], (16, width)) for i in range(4)]
    sums = [jnp.concatenate([ones_dot(values)] * 2, axis=0) for values in (own_gy, flat_rows(gu), flat_rows(gp))]
    for chunk in range(16):
        block = jnp.zeros((16, lanes), F32)
        for row, values in enumerate(spread + sums):
            size = values.shape[1] // 16
            piece = values[:, chunk * size : chunk * size + size]
            piece = jnp.concatenate([piece, jnp.zeros((16, lanes - size), F32)], axis=1)
            block = jnp.where(ones_row == row, piece, block)
        block = block.astype(BF16)
        first, second, third = ((chunk >> bit) & 1 for bit in order)
        place_at = slice(rows + (chunk >> 3) * 16, rows + (chunk >> 3) * 16 + 16)

        @pl.when(dp_bit(order[0]) == first)
        def _():
            keep[second * 2 + third, place_at, width:] = block

        @pl.when(dp_bit(order[0]) != first)
        def _():
            send[second * 2 + third, place_at, width:] = block


def down_group_kernel(hidden, hidp, gy, gyp_of, keep, send, left):
    half = dp_bit(3)
    tokens = gy.shape[0] * gy.shape[1]
    units = hidp.shape[2]
    order = ORDERS["down"]
    eighths(flat_rows(hidden, some(half * units, units)).T, left, order, 0)
    eighths(flat_rows(hidp).T, left, order, tokens)
    own_gy = flat_rows(gy)
    other_gy = jnp.concatenate([gyp_of(s) for s in range(gy.shape[0])], axis=0)
    size = units // 2
    for side, out in enumerate((keep, send)):
        at = slice(side * size, side * size + size)
        product = dot(left[at, :tokens], own_gy) + dot(left[at, tokens:], other_gy)
        out[...] = product.astype(BF16).reshape(out.shape)


def plus(left, right):
    return left.astype(F32) + right.astype(F32)


def add_kernel(bit, keep, arrived, keep_out, send_out):
    size = keep_out.shape[0]
    mine = dp_bit(bit) * size
    keep_out[...] = plus(keep[pl.ds(mine, size)], arrived[pl.ds(mine, size)]).astype(BF16)
    send_out[...] = plus(keep[pl.ds(size - mine, size)], arrived[pl.ds(size - mine, size)]).astype(BF16)


def swap_over(shard, bit, sections=(0, 1)):
    count = lax.axis_size("dp")
    pairs = [(s * count + i, s * count + (i ^ (1 << bit))) for s in sections for i in range(count)]
    return lax.ppermute(shard, ("section", "dp"), pairs)


def struct(*shape, dtype=BF16):
    return jax.ShapeDtypeStruct(shape, dtype)


def halved(parts, order, stage, name, after=()):
    keep, send = parts
    arrived = swap_over(send, order[stage])
    shape = (keep.shape[0] // 2,) + keep.shape[1:]
    return call(functools.partial(add_kernel, order[stage + 1]), [keep, arrived], [struct(*shape)] * 2, name, after=after)


def down_sum_kernel(keep, arrived, out):
    out[...] = plus(keep[0], arrived[0])


def halves_sum_kernel(up_keep, up_arrived, attn_keep, attn_arrived, up_mine, qkv_mine, small_mine, proj, other):
    half = dp_bit(3)
    low = up_mine.shape[0]
    units = up_mine.shape[1]
    width = proj.shape[1]
    mine, theirs = row_slice(half * low, low), row_slice((1 - half) * low, low)
    up_mine[...] = plus(up_keep[0, mine], up_arrived[0, mine])
    other[:low, :units] = plus(up_keep[0, theirs], up_arrived[0, theirs]).astype(BF16)
    qkv_mine[...] = plus(attn_keep[0, mine], attn_arrived[0, mine])
    other[:low, units:] = plus(attn_keep[0, theirs], attn_arrived[0, theirs]).astype(BF16)
    proj[...] = plus(attn_keep[0, 2 * low :, :width], attn_arrived[0, 2 * low :, :width])
    mine, theirs = row_slice(2 * low + half * 16, 16), row_slice(2 * low + (1 - half) * 16, 16)
    small_mine[...] = plus(attn_keep[0, mine, width:], attn_arrived[0, mine, width:])
    other[low:, :] = jnp.zeros((16, other.shape[1]), BF16)
    lanes = small_mine.shape[1]
    other[low:, :lanes] = plus(attn_keep[0, theirs, width:], attn_arrived[0, theirs, width:]).astype(BF16)


def joined_kernel(up_mine, qkv_mine, small_mine, other, up, qkv, *vectors):
    half = dp_bit(3)
    low = up_mine.shape[0]
    units = up_mine.shape[1]
    lanes = qkv_mine.shape[1] // 3
    up[:, some(half * units, units)] = up_mine[...]
    up[:, some((1 - half) * units, units)] = other[:low, :units].astype(F32)
    for block in range(3):
        at = slice(block * lanes, block * lanes + lanes)
        qkv[:, some((2 * block + half) * lanes, lanes)] = qkv_mine[:, at]
        qkv[:, some((2 * block + 1 - half) * lanes, lanes)] = other[:low, units + block * lanes : units + (block + 1) * lanes].astype(F32)
    small = small_mine[...] + other[low:, :lanes].astype(F32)
    for row, out in enumerate(vectors):
        out[...] = small[row : row + 1, : out.shape[1]]


def paired_gradients(boundary, lengths, params, tables, swapped):
    slots = lengths.shape[0]
    width = boundary.shape[2]
    rows = boundary.shape[1] // slots
    units = params[8].shape[2]
    local_rows = boundary.reshape(slots, rows, width)
    low, tall = width // 16, units // 16
    tokens = slots * rows

    other = swap_over(local_rows, 3)
    partner_lengths = swap_over(lengths, 3)
    result_0, saved, held = forward_first(lengths, local_rows, params, tables)
    own, gain_a, shift_a, gain_b, shift_b, w_qkv, b_qkv, w_proj, b_proj, w_up, b_up, w_down, b_down, *tabs = held
    arrived_1 = lax.ppermute(result_0, "section", swapped)
    count = len(held)

    def forward_both(lengths_ref, arriving, *refs):
        section = lax.axis_index("section")
        slot = 1 - section
        inputs = lambda: jnp.where(section == 0, refs[0][slot], arriving[...])
        outs = refs[count:]
        forward_body(slot, lengths_ref[slot], inputs, lambda name, part: None, *refs[:count], outs[-1], *outs[:-1])

    *saved, result_1 = call(forward_both, [lengths, arrived_1, *held], [struct(rows, width)], "forward_1", kept=saved)
    arrived_2 = lax.ppermute(result_1, "section", swapped)

    def forward_last(lengths_ref, arriving, *refs):
        outs = refs[count:]
        slot = slots - 1

        @pl.when(lax.axis_index("section") == 1)
        def _():
            forward_body(
                slot, lengths_ref[slot], lambda: arriving[...], lambda name, part: None, *refs[:count], outs[len(saved)], *outs[: len(saved)]
            )

    *saved, result_2 = call(forward_last, [lengths, arrived_2, *held], [struct(rows, width)], "forward_2", kept=saved)
    x_s, na_s, nb_s, qkv_s, pt_s, mixed_s, hidden_s, slope_s = saved
    partner_x = swap_over(x_s, 3, (1,))

    back_operands = [x_s, gain_a, gain_b, w_qkv, w_proj, w_up, w_down, *tabs, pt_s]
    back_count = len(back_operands)
    shared_operands = [gain_a, shift_a, gain_b, shift_b, w_qkv, b_qkv, w_up, b_up, *tabs]
    shared_count = len(shared_operands)
    shared_shapes = [
        pltpu.VMEM(shape, BF16)
        for shape in (
            (slots, rows, width), (slots, rows, width), (slots, rows, 3 * width // 2), (slots, pt_s.shape[1] // 2) + pt_s.shape[2:],
            (slots, rows, width // 2), (slots, rows, units // 2), (slots, rows, units // 2),
        )
    ]

    def share(lengths_ref, rows_ref, refs, outs):
        weights, tabs_refs = refs[:-3], refs[-3:]
        partner_forward(dp_bit(3), lengths_ref, lambda s: rows_ref[s], *weights, tuple(t[...] for t in tabs_refs), *outs)

    def backward_first(lengths_ref, own_ref, other_ref, *refs):
        operands, shared, (qkv_io, slope_io, gy, vec, gx, *outs) = (
            refs[:back_count], refs[back_count : back_count + shared_count], refs[back_count + shared_count :],
        )
        section = lax.axis_index("section")

        @pl.when(section == 1)
        def _():
            backward_body(0, lambda: own_ref[0], *operands, gx, qkv_io, slope_io, gy, vec)

        @pl.when(section == 0)
        def _():
            share(lengths_ref, other_ref, shared, outs)

    outs = call(
        backward_first, [partner_lengths, own, other, *back_operands, *shared_operands],
        [pltpu.VMEM((slots, rows, width), BF16), pltpu.VMEM((slots, 8, width), F32), struct(rows, width)] + shared_shapes,
        "backward_0", kept=[qkv_s, slope_s],
    )
    grads, back_0, shared = outs[:4], outs[4], outs[5:]
    arrived_4 = lax.ppermute(back_0, "section", swapped)
    partner_4 = swap_over(arrived_4, 3, (0,))

    def backward_both(own_ref, arriving, *refs):
        section = lax.axis_index("section")
        outs = refs[back_count:]
        source = lambda: jnp.where(section == 0, arriving[...], own_ref[section])
        backward_body(section, source, *refs[:back_count], outs[-1], *outs[:-1])

    *grads, back_1 = call(backward_both, [own, arrived_4, *back_operands], [struct(rows, width)], "backward_1", kept=grads)
    arrived_5 = lax.ppermute(back_1, "section", swapped)
    partner_5 = swap_over(arrived_5, 3, (0,))

    def backward_last(lengths_ref, arriving, other_ref, *refs):
        operands, shared_in, (qkv_io, slope_io, gy, vec, *outs) = (
            refs[:back_count], refs[back_count : back_count + shared_count], refs[back_count + shared_count :],
        )
        section = lax.axis_index("section")

        @pl.when(section == 0)
        def _():
            backward_body(slots - 1, lambda: arriving[...], *operands, outs[-1], qkv_io, slope_io, gy, vec)

        @pl.when(section == 1)
        def _():
            share(lengths_ref, other_ref, shared_in, outs[:-1])

    outs = call(
        backward_last, [partner_lengths, arrived_5, partner_x, *back_operands, *shared_operands], [struct(rows, width)],
        "backward_2", kept=[*grads, *shared],
    )
    gp_s, gu_s, gy_s, vec_s, nap, nbp, qkvp, ptp, mixedp, hidp, slopep, back_2 = outs

    def partner_rows(other_ref, partner_a, partner_b):
        section = lax.axis_index("section")
        return lambda s: jnp.where(section == 0, (partner_a, partner_b)[s][...], other_ref[s])

    def backward_shared(other_ref, partner_a, partner_b, wp, wd, same, later, earlier, ptp_ref, qkvp_ref, slopep_ref, gyp):
        pick = partner_rows(other_ref, partner_a, partner_b)
        for s in range(slots):
            gyp[s] = pick(s)
        partner_backward(
            dp_bit(3), lambda s: gyp[s], wp, wd, (same[...], later[...], earlier[...]), ptp_ref, qkvp_ref, slopep_ref
        )

    gpp, gup, gyp_s = call(
        backward_shared, [other, partner_4, partner_5, w_proj, w_down, *tabs, ptp], [struct(slots, rows, width)], "backward_shared",
        kept=[qkvp, slopep],
    )

    def group(rows_of_eighth, columns):
        return [struct(4, rows_of_eighth, columns)] * 2

    up = call(
        up_group_kernel, [nb_s, nbp, gu_s, gup], group(2 * low, units // 2), "up_grads", scratch=[pltpu.VMEM((width, 2 * tokens), BF16)]
    )

    def attn_group(na, nap_ref, gp, gpp_ref, mixed, mixedp_ref, gy, gyp, *refs):
        attn_group_kernel(na, nap_ref, gp, gpp_ref, mixed, mixedp_ref, gy, lambda s: gyp[s], *refs)

    attn = call(
        attn_group, [na_s, nap, gp_s, gpp, mixed_s, mixedp, gy_s, gyp_s, gu_s, vec_s], group(3 * low, 3 * width // 2), "attn_grads",
        scratch=[pltpu.VMEM((width, 2 * tokens), BF16), pltpu.VMEM((width // 2, 2 * tokens), BF16)], after=up[:1],
    )

    def down_group(hidden, hidp_ref, gy, gyp, *refs):
        down_group_kernel(hidden, hidp_ref, gy, lambda s: gyp[s], *refs)

    down = call(
        down_group, [hidden_s, hidp, gy_s, gyp_s], group(tall, width), "down_grads",
        scratch=[pltpu.VMEM((units // 2, 2 * tokens), BF16)], after=attn[:1],
    )

    up = halved(up, ORDERS["up"], 0, "up_sum_1", after=down[:1])
    attn = halved(attn, ORDERS["attn"], 0, "attn_sum_1", after=up[:1])
    down = halved(down, ORDERS["down"], 0, "down_sum_1", after=attn[:1])
    up = halved(up, ORDERS["up"], 1, "up_sum_2", after=down[:1])
    attn = halved(attn, ORDERS["attn"], 1, "attn_sum_2", after=up[:1])
    down = halved(down, ORDERS["down"], 1, "down_sum_2", after=attn[:1])
    up_last, attn_last = swap_over(up[1], ORDERS["up"][2]), swap_over(attn[1], ORDERS["attn"][2])
    up_mine, qkv_mine, small_mine, proj, others = call(
        halves_sum_kernel, [up[0], up_last, attn[0], attn_last],
        [struct(low, units // 2, dtype=F32), struct(low, 3 * width // 2, dtype=F32), struct(16, width // 2, dtype=F32),
         struct(low, width, dtype=F32), struct(low + 16, units // 2 + 3 * width // 2)], "up_qkv_sum_3",
    )
    down_out, = call(down_sum_kernel, [down[0], swap_over(down[1], ORDERS["down"][2])], [struct(tall, width, dtype=F32)], "down_sum_3", after=[proj])
    vectors = [low] * 5 + [tall, 3 * low]
    up_out, qkv_out, *vectors = call(
        joined_kernel, [up_mine, qkv_mine, small_mine, swap_over(others, 3)],
        [struct(low, units, dtype=F32), struct(low, 3 * width, dtype=F32)] + [struct(1, size, dtype=F32) for size in vectors], "up_qkv_joined",
        after=[down_out],
    )
    joined = jnp.where(
        lax.axis_index("section") == 0, jnp.concatenate([back_1, back_2], axis=0), jnp.concatenate([result_1, result_2], axis=0)
    )
    gain_a, shift_a, gain_b, shift_b, bias_y, bias_up, bias_qkv = (vector[0] for vector in vectors)
    return joined, gain_a, shift_a, qkv_out, bias_qkv, proj, bias_y, gain_b, shift_b, up_out, bias_up, down_out, bias_y


def plain_gradients(boundary, lengths, params, tables, swapped, bits):
    count = lax.axis_size("dp")
    slots = lengths.shape[0]
    width = boundary.shape[2]
    rows = boundary.shape[1] // slots
    units = params[8].shape[2]
    ticks = slots + 1
    result, saved, held = forward_first(lengths, boundary.reshape(slots, rows, width), params, tables)
    own, gain_a, shift_a, gain_b, shift_b, w_qkv, b_qkv, w_proj, b_proj, w_up, b_up, w_down, b_down, *tabs = held
    held_count = len(held)
    finals = [result]
    for t in range(1, ticks):
        arriving = lax.ppermute(result, "section", swapped)

        def forward_step(lengths_ref, arriving_ref, *refs, tick=t):
            section = lax.axis_index("section")
            slot = jnp.clip(tick - section, 0, slots - 1)
            inputs = lambda: jnp.where(section == 0, refs[0][slot], arriving_ref[...])
            outs = refs[held_count:]
            forward_body(slot, lengths_ref[slot], inputs, lambda name, part: None, *refs[:held_count], outs[-1], *outs[:-1])

        *saved, result = call(forward_step, [lengths, arriving, *held], [struct(rows, width)], "forward", kept=saved)
        finals.append(result)
    x_s, na_s, nb_s, qkv_s, pt_s, mixed_s, hidden_s, slope_s = saved
    operands = [x_s, gain_a, gain_b, w_qkv, w_proj, w_up, w_down, *tabs, pt_s]
    grads = [qkv_s, slope_s]
    input_grads = []
    arriving = own[0]
    for t in range(ticks):

        def backward_step(own_ref, arriving_ref, *refs, tick=t):
            section = lax.axis_index("section")
            slot = tick - 1 + section
            *io, gx_out = refs[len(operands) :]

            @pl.when((slot >= 0) & (slot < slots))
            def _():
                source = lambda: jnp.where(section == 0, arriving_ref[...], own_ref[slot])
                backward_body(slot, source, *refs[: len(operands)], gx_out, *io)

        shapes = [pltpu.VMEM((slots, rows, width), BF16), pltpu.VMEM((slots, 8, width), F32)] if t == 0 else []
        *grads, result = call(backward_step, [own, arriving, *operands], shapes + [struct(rows, width)], "backward", kept=grads)
        input_grads.append(result)
        if t + 1 < ticks:
            arriving = lax.ppermute(result, "section", swapped)
    gp_s, gu_s, gy_s, vec_s = grads
    order = list(range(len(bits)))

    def summed(full):
        keep, send = parted(full, 0, bits[0])
        return halving_sum(keep, send, order, count, bits, F32)

    both = jnp.concatenate([plain_grads(hidden_s, gy_s, count), plain_grads(mixed_s, gy_s, count)], axis=1)
    down, up, qkv = summed(both), summed(plain_grads(nb_s, gu_s, count)), summed(plain_grads(na_s, gp_s, count))
    tall = units // count
    sums = [jnp.sum(values, axis=(0, 1), dtype=F32) for values in (gy_s, gu_s, gp_s)]
    return finals[1:], input_grads[1:], vec_s, *sums, down[:tall], down[tall:], up, qkv


def per_device(boundary, lengths, *params):
    section = lax.axis_index("section")
    count = lax.axis_size("dp")
    bits = [(lax.axis_index("dp") >> b) & 1 for b in range(count.bit_length() - 1)]
    slots = lengths.shape[0]
    width = boundary.shape[2]
    units = params[8].shape[2]
    tables = [jnp.asarray(table) for table in rotary_lanes(boundary.shape[1] // slots, 2 * HEAD)]
    swapped = [(0, 1), (1, 0)]
    if count == 16 and slots == 2 and width % 768 == 0:
        results = paired_gradients(boundary, lengths, params, tables, swapped)
        return tuple(result[None] for result in results)
    finals, input_grads, vec_s, gy_sums, gu_sums, gp_sums, down, proj, up, qkv = plain_gradients(
        boundary, lengths, params, tables, swapped, bits
    )
    vec = jnp.sum(vec_s, axis=0)
    small = jnp.concatenate(
        [piece.reshape(count, -1) for piece in (vec[0], vec[1], vec[2], vec[3], gy_sums, gu_sums, gp_sums)], axis=1
    )
    small = halving_sum(*parted(small, 0, bits[0]), list(range(len(bits))), count, bits, F32)
    low, tall = width // count, units // count
    gain_a, shift_a, gain_b, shift_b, bias_y, bias_up, bias_qkv = jnp.split(small, np.cumsum([low] * 5 + [tall]), axis=0)
    joined = jnp.where(section == 0, jnp.concatenate(input_grads, axis=0), jnp.concatenate(finals, axis=0))
    results = (joined, gain_a, shift_a, qkv, bias_qkv, proj, bias_y, gain_b, shift_b, up, bias_up, down, bias_y)
    return tuple(result[None] for result in results)


def solution(mesh):
    split = P("section", "dp")
    deep = P("section", "dp", None)
    flat, matrix = P("section", None), P("section", None, None)
    return jax.shard_map(
        per_device,
        mesh=mesh,
        in_specs=(deep, P("dp"), flat, flat, matrix, flat, matrix, flat, flat, flat, matrix, flat, matrix, flat),
        out_specs=(deep, split, split, deep, split, deep, split, split, split, deep, split, deep, split),
        check_vma=False,
    )
```

```python
import functools
import math

import jax
import jax.numpy as jnp
import numpy as np
from jax import lax
from jax.experimental import pallas as pl
from jax.experimental.pallas import tpu as pltpu
from jax.sharding import PartitionSpec as P

HEAD = 64
LANES = 256
CHUNK = 512
EPS = 1e-05
NEG_FILL = -1e30
VMEM_BYTES = 12 * 1024 * 1024
FIRST_VMEM_BYTES = 12 * 1024 * 1024
F32 = jnp.float32
BF16 = jnp.bfloat16


def dot(left, right):
    return jnp.dot(left, right, preferred_element_type=F32)


def dot_nt(left, right):
    return lax.dot_general(left, right, (((1,), (1,)), ((), ())), preferred_element_type=F32)


def normalised(values):
    centred = values - jnp.mean(values, axis=-1, keepdims=True)
    variance = jnp.mean(centred * centred, axis=-1, keepdims=True)
    scale = lax.rsqrt(variance + EPS)
    return centred * scale, scale


def gelu_parts(values):
    integral = 0.5 + 0.5 * lax.erf(values * math.sqrt(0.5))
    bell = jnp.exp(values * values * -0.5)
    return values * integral, integral + values * bell * (1.0 / math.sqrt(2.0 * math.pi))


def rotary_lanes(seq_len, lanes):
    rot_dims = HEAD // 4
    half = rot_dims // 2
    frequency = np.float32(10000.0) ** (-(np.arange(half, dtype=np.float32) * np.float32(2.0) / np.float32(rot_dims)))
    angles = np.arange(seq_len, dtype=np.float32)[:, None] * frequency.astype(np.float32)[None, :]
    cosine, sine = np.cos(angles).astype(np.float32), np.sin(angles).astype(np.float32)
    same = np.ones((seq_len, HEAD), np.float32)
    later = np.zeros((seq_len, HEAD), np.float32)
    earlier = np.zeros((seq_len, HEAD), np.float32)
    same[:, :half] = cosine
    same[:, half:rot_dims] = cosine
    later[:, :half] = -sine
    earlier[:, half:rot_dims] = sine
    return [np.tile(t, (1, lanes // HEAD)) for t in (same, later, earlier)]


def turned(values, same, later, earlier, sign):
    half = HEAD // 8
    width = values.shape[1]
    same, later, earlier = (jnp.concatenate([t] * (width // t.shape[1]), axis=1) for t in (same, later, earlier))
    ahead = pltpu.roll(values, width - half, 1)
    behind = pltpu.roll(values, half, 1)
    if sign > 0:
        return values * same + ahead * later + behind * earlier
    return values * same - ahead * later - behind * earlier


def blocked_bias(rows, length):
    out = []
    for start in range(0, rows, 128):
        keys = start + 128
        key_pos = lax.broadcasted_iota(jnp.int32, (keys, 2 * 128), 0)
        query_pos = start + (lax.broadcasted_iota(jnp.int32, (keys, 2 * 128), 1) & 127)
        out.append(jnp.where((key_pos <= query_pos) & (key_pos < length), 0.0, NEG_FILL))
    return out


def heads_apart(block, lane):
    zero = jnp.zeros_like(block)
    return jnp.concatenate([jnp.where(lane < HEAD, block, zero), jnp.where(lane < HEAD, zero, block)], axis=0)


def dot_tn(left, right):
    return lax.dot_general(left, right, (((0,), (0,)), ((), ())), preferred_element_type=F32)


def probs_rows(block):
    start = 128 * (block * (block + 1) // 2)
    return slice(start, start + 128 * (block + 1))


def some(offset, size):
    return slice(offset, offset + size) if isinstance(offset, int) else pl.ds(pl.multiple_of(offset, 128), size)


def spans(pair, width):
    return [slice(b * width + pair * 2 * HEAD, b * width + (pair + 1) * 2 * HEAD) for b in range(3)]


def forward_units(slot, length, ready, na, nb, wqkv, bqkv, wu, bu, tables, qkv, pt, mixed, hidden, slope, low_head, low_unit, lanes):
    rows = qkv.shape[1]
    whole_width, width = wqkv.shape[1], qkv.shape[2] // 3
    pairs = width // (2 * HEAD)
    chunk = hidden.shape[2] // pairs
    biases = blocked_bias(rows, length)
    lane = lax.broadcasted_iota(jnp.int32, (128, 2 * HEAD), 1)
    per = lanes // (2 * HEAD)
    for pair in range(pairs):
        if pair % per == 0:
            low = pair * 2 * HEAD
            ready("qkv", pair // per)

            def packed(block):
                at = some(block * whole_width + low_head + low, lanes)
                return dot(na[slot], wqkv[0, :, at]) + bqkv[:, at].astype(F32)

            qkv[slot, :, low : low + lanes] = (turned(packed(0), *tables, 1) * (HEAD**-0.5)).astype(BF16)
            qkv[slot, :, width + low : width + low + lanes] = turned(packed(1), *tables, 1).astype(BF16)
            qkv[slot, :, 2 * width + low : 2 * width + low + lanes] = packed(2).astype(BF16)
        span, span_k, span_v = spans(pair, width)
        all_scores = []
        for block, start in enumerate(range(0, rows, 128)):
            keys = start + 128
            q2 = heads_apart(qkv[slot, start:keys, span], lane)
            all_scores.append(dot_nt(qkv[slot, :keys, span_k], q2) + biases[block])
        ready("up", pair)
        there = some(low_unit + pair * chunk, chunk)
        up = dot(nb[slot], wu[0, :, there]) + bu[:, there].astype(F32)
        for block, start in enumerate(range(0, rows, 128)):
            keys = start + 128
            scores = all_scores[block]
            exponent = jnp.exp(scores - jnp.max(scores, axis=0, keepdims=True))
            probs = (exponent * (1.0 / jnp.sum(exponent, axis=0, keepdims=True))).astype(BF16)
            pt[slot, pair, probs_rows(block)] = probs
            both = dot_tn(probs, qkv[slot, :keys, span_v])
            mixed[slot, start:keys, span] = jnp.where(lane < HEAD, both[:128], both[128:]).astype(BF16)
        here = slice(pair * chunk, pair * chunk + chunk)
        hidden_f32, slope_f32 = gelu_parts(up)
        hidden[slot, :, here] = hidden_f32.astype(BF16)
        slope[slot, :, here] = slope_f32.astype(BF16)


def backward_units(slot, gy, wp, wd, tables, pt, qkv, slope, low_head, low_unit, lanes):
    rows = qkv.shape[1]
    width = qkv.shape[2] // 3
    pairs = width // (2 * HEAD)
    chunk = slope.shape[2] // pairs
    lane = lax.broadcasted_iota(jnp.int32, (128, 2 * HEAD), 1)
    per = lanes // (2 * HEAD)
    for pair in range(pairs):
        if pair % per == 0:
            gm_group = dot_nt(gy(), wp[0, some(low_head + pair * 2 * HEAD, lanes), :]).astype(BF16)
            group_q, group_k = [], []
        span, span_k, span_v = spans(pair, width)
        gm = gm_group[:, (pair % per) * 2 * HEAD : (pair % per + 1) * 2 * HEAD]
        gv_sum, gk_sum, gq_blocks = None, None, []
        for block, start in enumerate(range(0, rows, 128)):
            keys = start + 128
            gm2 = heads_apart(gm[start:keys], lane)
            q2 = heads_apart(qkv[slot, start:keys, span], lane)
            probs = pt[slot, pair, probs_rows(block)]
            weighted = probs.astype(F32) * dot_nt(qkv[slot, :keys, span_v], gm2)
            inner = jnp.sum(weighted, axis=0, keepdims=True)
            gs = (weighted - probs.astype(F32) * inner).astype(BF16)
            gv_part = dot(probs, gm2)
            gk_part = dot(gs, q2)
            gq_part = dot_tn(gs, qkv[slot, :keys, span_k])
            gq_blocks.append(jnp.where(lane < HEAD, gq_part[:128], gq_part[128:]))
            if gv_sum is None:
                gv_sum, gk_sum = gv_part, gk_part
            else:
                gv_sum = jnp.concatenate([gv_sum + gv_part[:start], gv_part[start:]], axis=0)
                gk_sum = jnp.concatenate([gk_sum + gk_part[:start], gk_part[start:]], axis=0)
        qkv[slot, :, span_v] = gv_sum.astype(BF16)
        group_q.append(jnp.concatenate(gq_blocks, axis=0))
        group_k.append(gk_sum)
        if pair % per == per - 1:
            low = pair // per * lanes
            gq = turned(jnp.concatenate(group_q, axis=1) * (HEAD**-0.5), *tables, -1)
            qkv[slot, :, low : low + lanes] = gq.astype(BF16)
            gk = turned(jnp.concatenate(group_k, axis=1), *tables, -1)
            qkv[slot, :, width + low : width + low + lanes] = gk.astype(BF16)
        here = slice(pair * chunk, pair * chunk + chunk)
        grad = dot_nt(gy(), wd[0, some(low_unit + pair * chunk, chunk), :])
        slope[slot, :, here] = (grad * slope[slot, :, here].astype(F32)).astype(BF16)


def forward_body(
    slot, length, inputs, ready, own, gain_a, shift_a, gain_b, shift_b, wqkv, bqkv, wp, bp, wu, bu, wd, bd, same, later, earlier,
    y_out, x_out, na_out, nb_out, qkv_out, pt_out, mixed_out, hidden_out, slope_out,
):
    ready("small", 0)
    x_low = inputs()
    x_out[slot] = x_low
    xhat, _ = normalised(x_low.astype(F32))
    na_out[slot] = (xhat * gain_a[...].astype(F32) + shift_a[...].astype(F32)).astype(BF16)
    nb_out[slot] = (xhat * gain_b[...].astype(F32) + shift_b[...].astype(F32)).astype(BF16)
    tables = (same[...], later[...], earlier[...])
    forward_units(
        slot, length, ready, na_out, nb_out, wqkv, bqkv, wu, bu, tables, qkv_out, pt_out, mixed_out, hidden_out, slope_out, 0, 0, LANES
    )
    ready("rest", 0)
    total = x_out[slot].astype(F32) + (bp[...].astype(F32) + bd[...].astype(F32))
    y_out[...] = (total + dot(mixed_out[slot], wp[0]) + dot(hidden_out[slot], wd[0])).astype(BF16)


def backward_body(
    slot, gy_source, x_in, gain_a, gain_b, wqkv, wp, wu, wd, same, later, earlier, pt_in, gx_out, qkv_io, slope_io, gy_out, vec_out
):
    width = gx_out.shape[1]
    gy_out[slot] = gy_source()
    tables = (same[...], later[...], earlier[...])
    backward_units(slot, lambda: gy_out[slot], wp, wd, tables, pt_in, qkv_io, slope_io, 0, 0, LANES)
    grad_b = dot_nt(slope_io[slot], wu[0])
    grad_a = dot_nt(qkv_io[slot], wqkv[0])
    xhat, scale = normalised(x_in[slot].astype(F32))
    sums = [jnp.sum(t, axis=0, keepdims=True) for t in (grad_a * xhat, grad_a, grad_b * xhat, grad_b)]
    vec_out[slot] = jnp.concatenate(sums + [jnp.zeros((4, width), F32)], axis=0)
    both = grad_a * gain_a[...].astype(F32) + grad_b * gain_b[...].astype(F32)
    inner = jnp.mean(both * xhat, axis=-1, keepdims=True)
    gx = gy_out[slot].astype(F32) + scale * (both - jnp.mean(both, axis=-1, keepdims=True) - xhat * inner)
    gx_out[...] = gx.astype(BF16)


def forward_first_kernel(tick, lengths, *refs):
    count = 17
    sources, held, outs, sems = refs[:count], refs[count : 2 * count], refs[2 * count : -1], refs[-1]
    copies = []
    waits = {}

    def fetch(name, part, index, at):
        source, target = (sources[index], held[index]) if at is None else (sources[index].at[at], held[index].at[at])
        copy = pltpu.make_async_copy(source, target, sems.at[len(copies)])
        copies.append(copy)
        waits.setdefault((name, part), []).append(copy)

    (own, gain_a, shift_a, gain_b, shift_b, wqkv, bqkv, wp, bp, wu, bu, wd, bd, same, later, earlier, _) = range(count)
    width = sources[wp].shape[1]
    units = sources[wu].shape[2]
    pairs = width // (2 * HEAD)
    groups = width // LANES
    for index in (own, gain_a, shift_a, gain_b, shift_b, bqkv, bp, bu, bd, same, later, earlier):
        fetch("small", 0, index, None)
    for pair in range(pairs):
        if pair * groups % pairs == 0:
            group = pair * groups // pairs
            for block in range(3):
                fetch("qkv", group, wqkv, (slice(None), slice(None), pl.ds(block * width + group * LANES, LANES)))
        fetch("up", pair, wu, (slice(None), slice(None), pl.ds(pair * (units // pairs), units // pairs)))
    fetch("rest", 0, wp, None)
    fetch("rest", 0, wd, None)
    for copy in copies:
        copy.start()

    def ready(name, part):
        for copy in waits[(name, part)]:
            copy.wait()

    section = lax.axis_index("section")
    slots = held[own].shape[0]
    slot = jnp.clip(tick - section, 0, slots - 1)
    forward_body(slot, lengths[slot], lambda: held[own][slot], ready, *held[:-1], *outs)


def backward_body(
    slot, gy_source, x_in, gain_a, gain_b, wqkv, wp, wu, wd, same, later, earlier,
    pt_in, gx_out, qkv_io, slope_io, gy_out, vec_out,
):
    rows, width = gx_out.shape
    units = wu.shape[2]
    pairs = width // (2 * HEAD)
    chunk = units // pairs
    gy_out[slot] = gy_source()
    lane = lax.broadcasted_iota(jnp.int32, (128, 2 * HEAD), 1)
    tables = (same[...], later[...], earlier[...])
    per = LANES // (2 * HEAD)
    for pair in range(pairs):
        if pair % per == 0:
            gm_group = dot_nt(gy_out[slot], wp[0, pair * 2 * HEAD : pair * 2 * HEAD + LANES, :]).astype(BF16)
            group_q, group_k = [], []
        span, span_k, span_v = (slice(b * width + pair * 2 * HEAD, b * width + (pair + 1) * 2 * HEAD) for b in range(3))
        gm = gm_group[:, (pair % per) * 2 * HEAD : (pair % per + 1) * 2 * HEAD]
        gv_sum, gk_sum, gq_blocks = None, None, []
        for block, start in enumerate(range(0, rows, 128)):
            keys = start + 128
            gm2 = heads_apart(gm[start:keys], lane)
            q2 = heads_apart(qkv_io[slot, start:keys, span], lane)
            pt = pt_in[slot, pair, probs_rows(block)]
            weighted = pt.astype(F32) * dot_nt(qkv_io[slot, :keys, span_v], gm2)
            inner = jnp.sum(weighted, axis=0, keepdims=True)
            gs = (weighted - pt.astype(F32) * inner).astype(BF16)
            gv_part = dot(pt, gm2)
            gk_part = dot(gs, q2)
            gq_part = dot_tn(gs, qkv_io[slot, :keys, span_k])
            gq_blocks.append(jnp.where(lane < HEAD, gq_part[:128], gq_part[128:]))
            if gv_sum is None:
                gv_sum, gk_sum = gv_part, gk_part
            else:
                gv_sum = jnp.concatenate([gv_sum + gv_part[:start], gv_part[start:]], axis=0)
                gk_sum = jnp.concatenate([gk_sum + gk_part[:start], gk_part[start:]], axis=0)
        qkv_io[slot, :, span_v] = gv_sum.astype(BF16)
        group_q.append(jnp.concatenate(gq_blocks, axis=0))
        group_k.append(gk_sum)
        if pair % per == per - 1:
            low = pair // per * LANES
            gq = turned(jnp.concatenate(group_q, axis=1) * (HEAD**-0.5), *tables, -1)
            qkv_io[slot, :, low : low + LANES] = gq.astype(BF16)
            gk = turned(jnp.concatenate(group_k, axis=1), *tables, -1)
            qkv_io[slot, :, width + low : width + low + LANES] = gk.astype(BF16)
        at = slice(pair * chunk, pair * chunk + chunk)
        slope_io[slot, :, at] = (dot_nt(gy_out[slot], wd[0, at, :]) * slope_io[slot, :, at].astype(F32)).astype(BF16)
    grad_b = dot_nt(slope_io[slot], wu[0])
    grad_a = dot_nt(qkv_io[slot], wqkv[0])
    xhat, scale = normalised(x_in[slot].astype(F32))
    sums = [jnp.sum(t, axis=0, keepdims=True) for t in (grad_a * xhat, grad_a, grad_b * xhat, grad_b)]
    vec_out[slot] = jnp.concatenate(sums + [jnp.zeros((4, width), F32)], axis=0)
    both = grad_a * gain_a[...].astype(F32) + grad_b * gain_b[...].astype(F32)
    inner = jnp.mean(both * xhat, axis=-1, keepdims=True)
    gx = gy_out[slot].astype(F32) + scale * (both - jnp.mean(both, axis=-1, keepdims=True) - xhat * inner)
    gx_out[...] = gx.astype(BF16)


VM = pl.BlockSpec(memory_space=pltpu.VMEM)
HBM = pl.BlockSpec(memory_space=pl.ANY)


def call(kernel, operands, out_shape, name, kept=(), scratch=(), flops=1 << 20, after=()):
    count = len(operands)
    after = list(after)

    def body(*refs):
        kernel(*refs[:count], *refs[count + len(kept) + len(after) :])

    return pl.pallas_call(
        body,
        in_specs=[pl.BlockSpec(memory_space=pltpu.SMEM) if o.dtype == jnp.int32 else VM for o in operands] + [VM] * len(kept) + [HBM] * len(after),
        out_specs=[VM] * (len(kept) + len(out_shape)),
        out_shape=[pltpu.VMEM(array.shape, array.dtype) for array in kept] + list(out_shape),
        input_output_aliases={count + i: i for i in range(len(kept))},
        scratch_shapes=list(scratch),
        compiler_params=pltpu.CompilerParams(vmem_limit_bytes=VMEM_BYTES),
        cost_estimate=pl.CostEstimate(flops=flops, bytes_accessed=1 << 16, transcendentals=0),
        name=name,
    )(*operands, *[pltpu.with_memory_space_constraint(array, pltpu.VMEM) for array in kept], *after)


def shape_of(array):
    return jax.ShapeDtypeStruct(array.shape, array.dtype)


def forward_shapes(local_rows, params):
    slots, rows, width = local_rows.shape
    units = params[8].shape[2]
    blocks = rows // 128
    probs = (slots, width // (2 * HEAD), 128 * (blocks * (blocks + 1) // 2), 2 * 128)
    columns = [width, width, width, 3 * width, None, width, units, units]
    return [jax.ShapeDtypeStruct((rows, width), BF16)] + [
        pltpu.VMEM(probs if n is None else (slots, rows, n), BF16) for n in columns
    ]


def forward_first(lengths, local_rows, params, tables):
    (gain_a, shift_a, w_qkv, b_qkv, w_proj, b_proj, gain_b, shift_b, w_up, b_up, w_down, b_down) = params
    held = [local_rows, gain_a, shift_a, gain_b, shift_b, w_qkv, b_qkv, w_proj, b_proj, w_up, b_up, w_down, b_down] + list(tables)
    shapes = [shape_of(array) for array in held] + forward_shapes(local_rows, params)

    def kernel(lengths_ref, *refs):
        count = len(held)
        forward_first_kernel(0, lengths_ref, *refs[:count], None, *refs[count : 2 * count], None, *refs[2 * count :])

    outs = pl.pallas_call(
        kernel,
        in_specs=[pl.BlockSpec(memory_space=pltpu.SMEM)] + [pl.BlockSpec(memory_space=pltpu.HBM)] * len(held),
        out_specs=[VM] * len(shapes),
        out_shape=shapes,
        scratch_shapes=[pltpu.SemaphoreType.DMA((40,))],
        compiler_params=pltpu.CompilerParams(vmem_limit_bytes=FIRST_VMEM_BYTES),
        cost_estimate=pl.CostEstimate(flops=1 << 20, bytes_accessed=1 << 16, transcendentals=0),
        name="layer_forward_first",
    )(lengths, *[pltpu.with_memory_space_constraint(array, pltpu.HBM) for array in held])
    count = len(held)
    return outs[count], outs[count + 1 :], outs[:count]


def swap(shard, bit, count):
    return lax.ppermute(shard, "dp", [(i, i ^ (1 << bit)) for i in range(count)])


def parted(values, position, mine):
    count = values.shape[0]
    shaped = values.reshape((count >> (position + 1), 2, 1 << position) + values.shape[1:])
    out = []
    for side in (mine, 1 - mine):
        piece = lax.dynamic_index_in_dim(shaped, side, axis=1, keepdims=False)
        out.append(piece.reshape((count // 2,) + values.shape[1:]))
    return out


def halving_sum(keep, send, order, count, bits, final):
    left = sorted(order)
    for number, bit in enumerate(order):
        left.remove(bit)
        arrived = swap(send, bit, count)
        if number + 1 == len(order):
            return (keep.astype(F32) + arrived.astype(F32)).astype(final)[0]
        position = left.index(order[number + 1])
        keep_a, send_a = parted(keep, position, bits[order[number + 1]])
        keep_b, send_b = parted(arrived, position, bits[order[number + 1]])
        send = (send_a.astype(F32) + send_b.astype(F32)).astype(send_a.dtype)
        keep = (keep_a.astype(F32) + keep_b.astype(F32)).astype(send_a.dtype)


def plain_grads(left, right, count):
    rows = left.shape[0] * left.shape[1]
    product = lax.dot_general(
        left.reshape(rows, -1), right.reshape(rows, -1), (((0,), (0,)), ((), ())), preferred_element_type=F32
    ).astype(BF16)
    return product.reshape(count, product.shape[0] // count, product.shape[1])


def partner_forward(half, lengths, rows_of, gain_a, shift_a, gain_b, shift_b, wqkv, bqkv, wu, bu, tables, nap, nbp, qkvp, ptp, mixedp, hidp, slopep):
    for s in range(nap.shape[0]):
        xhat, _ = normalised(rows_of(s).astype(F32))
        nap[s] = (xhat * gain_a[...].astype(F32) + shift_a[...].astype(F32)).astype(BF16)
        nbp[s] = (xhat * gain_b[...].astype(F32) + shift_b[...].astype(F32)).astype(BF16)
        lanes = mixedp.shape[2]
        forward_units(
            s, lengths[s], lambda name, part: None, nap, nbp, wqkv, bqkv, wu, bu, tables, qkvp, ptp, mixedp, hidp, slopep,
            half * lanes, half * hidp.shape[2], lanes,
        )


def partner_backward(half, rows_of, wp, wd, tables, ptp, qkvp, slopep):
    lanes = qkvp.shape[2] // 3
    for s in range(qkvp.shape[0]):
        backward_units(s, lambda: rows_of(s), wp, wd, tables, ptp, qkvp, slopep, half * lanes, half * slopep.shape[2], lanes)


ORDERS = {"down": (0, 1, 2), "up": (1, 2, 0), "attn": (2, 0, 1)}


def dp_bit(bit):
    return (lax.axis_index("dp") >> bit) & 1


def eighth_row(chunk, order, rows):
    first, second, third = ((chunk >> bit) & 1 for bit in order)
    return ((first ^ dp_bit(order[0])) * 4 + second * 2 + third) * rows


def row_slice(start, rows):
    return pl.ds(pl.multiple_of(start, 16), rows)


def flat_rows(ref, at=slice(None)):
    values = ref[:, :, at]
    return values.reshape(values.shape[0] * values.shape[1], values.shape[2])


def ones_dot(values):
    return dot(jnp.ones((16, values.shape[0]), BF16), values)[:8]


def sixteenths(ref, left, order, tokens_from):
    turned_ref = flat_rows(ref).T
    low = turned_ref.shape[0] // 16
    for chunk in range(16):
        start = eighth_row(chunk & 7, order, 2 * low) + (chunk >> 3) * low
        left[row_slice(start, low), tokens_from : tokens_from + turned_ref.shape[1]] = turned_ref[chunk * low : chunk * low + low]


def eighths(turned_rows, left, order, tokens_from):
    low = turned_rows.shape[0] // 8
    for chunk in range(8):
        left[row_slice(eighth_row(chunk, order, low), low), tokens_from : tokens_from + turned_rows.shape[1]] = turned_rows[
            chunk * low : chunk * low + low
        ]


def up_group_kernel(nb, nbp, gu, gup, keep, send, left):
    half = dp_bit(3)
    tokens = nb.shape[0] * nb.shape[1]
    units = gup.shape[2]
    sixteenths(nb, left, ORDERS["up"], 0)
    sixteenths(nbp, left, ORDERS["up"], tokens)
    rows = left.shape[0] // 8
    for low in range(0, units, 512):
        at = slice(low, low + 512)
        product = dot(left[:, :tokens], flat_rows(gu, some(half * units + low, 512))) + dot(left[:, tokens:], flat_rows(gup, at))
        product = product.astype(BF16).reshape(8, rows, 512)
        keep[:, :, at] = product[:4]
        send[:, :, at] = product[4:]


def attn_group_kernel(na, nap, gp, gpp, mixed, mixedp, gy, gyp_of, gu, vec, keep, send, left, left_mixed):
    half = dp_bit(3)
    tokens = na.shape[0] * na.shape[1]
    width = na.shape[2]
    lanes = mixedp.shape[2]
    order = ORDERS["attn"]
    sixteenths(na, left, order, 0)
    sixteenths(nap, left, order, tokens)
    rows = left.shape[0] // 8
    for block in range(3):
        at = slice(block * lanes, block * lanes + lanes)
        own = flat_rows(gp, some(block * width + half * lanes, lanes))
        product = dot(left[:, :tokens], own) + dot(left[:, tokens:], flat_rows(gpp, at))
        product = product.astype(BF16).reshape(8, rows, lanes)
        keep[:, :rows, at] = product[:4]
        send[:, :rows, at] = product[4:]
    eighths(flat_rows(mixed, some(half * lanes, lanes)).T, left_mixed, order, 0)
    eighths(flat_rows(mixedp).T, left_mixed, order, tokens)
    own_gy = flat_rows(gy)
    other_gy = jnp.concatenate([gyp_of(s) for s in range(gy.shape[0])], axis=0)
    product = dot(left_mixed[:, :tokens], own_gy) + dot(left_mixed[:, tokens:], other_gy)
    low = left_mixed.shape[0] // 8
    product = product.astype(BF16).reshape(8, low, width)
    keep[:, rows:, :width] = product[:4]
    send[:, rows:, :width] = product[4:]
    ones_row = lax.broadcasted_iota(jnp.int32, (16, lanes), 0)
    norms = vec[0] + vec[1]
    spread = [jnp.broadcast_to(norms[i : i + 1], (16, width)) for i in range(4)]
    sums = [jnp.concatenate([ones_dot(values)] * 2, axis=0) for values in (own_gy, flat_rows(gu), flat_rows(gp))]
    for chunk in range(16):
        block = jnp.zeros((16, lanes), F32)
        for row, values in enumerate(spread + sums):
            size = values.shape[1] // 16
            piece = values[:, chunk * size : chunk * size + size]
            piece = jnp.concatenate([piece, jnp.zeros((16, lanes - size), F32)], axis=1)
            block = jnp.where(ones_row == row, piece, block)
        block = block.astype(BF16)
        first, second, third = ((chunk >> bit) & 1 for bit in order)
        place_at = slice(rows + (chunk >> 3) * 16, rows + (chunk >> 3) * 16 + 16)

        @pl.when(dp_bit(order[0]) == first)
        def _():
            keep[second * 2 + third, place_at, width:] = block

        @pl.when(dp_bit(order[0]) != first)
        def _():
            send[second * 2 + third, place_at, width:] = block


def down_group_kernel(hidden, hidp, gy, gyp_of, keep, send, left):
    half = dp_bit(3)
    tokens = gy.shape[0] * gy.shape[1]
    units = hidp.shape[2]
    order = ORDERS["down"]
    eighths(flat_rows(hidden, some(half * units, units)).T, left, order, 0)
    eighths(flat_rows(hidp).T, left, order, tokens)
    own_gy = flat_rows(gy)
    other_gy = jnp.concatenate([gyp_of(s) for s in range(gy.shape[0])], axis=0)
    size = units // 2
    for side, out in enumerate((keep, send)):
        at = slice(side * size, side * size + size)
        product = dot(left[at, :tokens], own_gy) + dot(left[at, tokens:], other_gy)
        out[...] = product.astype(BF16).reshape(out.shape)


def plus(left, right):
    return left.astype(F32) + right.astype(F32)


def add_kernel(bit, keep, arrived, keep_out, send_out):
    size = keep_out.shape[0]
    mine = dp_bit(bit) * size
    keep_out[...] = plus(keep[pl.ds(mine, size)], arrived[pl.ds(mine, size)]).astype(BF16)
    send_out[...] = plus(keep[pl.ds(size - mine, size)], arrived[pl.ds(size - mine, size)]).astype(BF16)


def swap_over(shard, bit, sections=(0, 1)):
    count = lax.axis_size("dp")
    pairs = [(s * count + i, s * count + (i ^ (1 << bit))) for s in sections for i in range(count)]
    return lax.ppermute(shard, ("section", "dp"), pairs)


def struct(*shape, dtype=BF16):
    return jax.ShapeDtypeStruct(shape, dtype)


def halved(parts, order, stage, name, after=()):
    keep, send = parts
    arrived = swap_over(send, order[stage])
    shape = (keep.shape[0] // 2,) + keep.shape[1:]
    return call(functools.partial(add_kernel, order[stage + 1]), [keep, arrived], [struct(*shape)] * 2, name, after=after)


def down_sum_kernel(keep, arrived, out):
    out[...] = plus(keep[0], arrived[0])


def halves_sum_kernel(up_keep, up_arrived, attn_keep, attn_arrived, up_mine, qkv_mine, small_mine, proj, other):
    half = dp_bit(3)
    low = up_mine.shape[0]
    units = up_mine.shape[1]
    width = proj.shape[1]
    mine, theirs = row_slice(half * low, low), row_slice((1 - half) * low, low)
    up_mine[...] = plus(up_keep[0, mine], up_arrived[0, mine])
    other[:, :units] = plus(up_keep[0, theirs], up_arrived[0, theirs]).astype(BF16)
    qkv_mine[...] = plus(attn_keep[0, mine], attn_arrived[0, mine])
    other[:, units : units + qkv_mine.shape[1]] = plus(attn_keep[0, theirs], attn_arrived[0, theirs]).astype(BF16)
    proj[...] = plus(attn_keep[0, 2 * low :, :width], attn_arrived[0, 2 * low :, :width])
    mine, theirs = row_slice(2 * low + half * 16, 16), row_slice(2 * low + (1 - half) * 16, 16)
    small_mine[...] = plus(attn_keep[0, mine, width:], attn_arrived[0, mine, width:])
    small = plus(attn_keep[0, theirs, width:], attn_arrived[0, theirs, width:]).astype(BF16)
    for part in range(small.shape[1] // 128):
        other[part * 16 : part * 16 + 16, other.shape[1] - 128 :] = small[:, part * 128 : part * 128 + 128]


def joined_kernel(up_mine, qkv_mine, small_mine, other, up, qkv, *vectors):
    half = dp_bit(3)
    low = up_mine.shape[0]
    units = up_mine.shape[1]
    lanes = qkv_mine.shape[1] // 3
    up[:, some(half * units, units)] = up_mine[...]
    up[:, some((1 - half) * units, units)] = other[:, :units].astype(F32)
    for block in range(3):
        at = slice(block * lanes, block * lanes + lanes)
        qkv[:, some((2 * block + half) * lanes, lanes)] = qkv_mine[:, at]
        qkv[:, some((2 * block + 1 - half) * lanes, lanes)] = other[:, units + block * lanes : units + (block + 1) * lanes].astype(F32)
    rest = other[:, other.shape[1] - 128 :].astype(F32)
    small = small_mine[...] + jnp.concatenate([rest[part : part + 16] for part in range(0, low, 16)], axis=1)
    for row, out in zip((0, 1, 2, 3, 4, 4, 5, 6), vectors):
        out[...] = small[row : row + 1, : out.shape[1]]


def paired_gradients(boundary, lengths, params, tables, swapped):
    slots = lengths.shape[0]
    width = boundary.shape[2]
    rows = boundary.shape[1] // slots
    units = params[8].shape[2]
    local_rows = boundary.reshape(slots, rows, width)
    low, tall = width // 16, units // 16
    tokens = slots * rows

    partner_lengths = swap_over(lengths, 3)
    cut = rows * slots * 3 // 4
    other_a = swap_over(boundary[0, :cut], 3, (0,))
    other_b = swap_over(boundary[0, cut:], 3, (0,))
    other_gy = swap_over(local_rows, 3, (1,))
    result_0, saved, held = forward_first(lengths, local_rows, params, tables)
    own, gain_a, shift_a, gain_b, shift_b, w_qkv, b_qkv, w_proj, b_proj, w_up, b_up, w_down, b_down, *tabs = held
    arrived_1 = lax.ppermute(result_0, "section", swapped)
    count = len(held)

    def forward_both(lengths_ref, arriving, *refs):
        section = lax.axis_index("section")
        slot = 1 - section
        inputs = lambda: jnp.where(section == 0, refs[0][slot], arriving[...])
        outs = refs[count:]
        forward_body(slot, lengths_ref[slot], inputs, lambda name, part: None, *refs[:count], outs[-1], *outs[:-1])

    *saved, result_1 = call(forward_both, [lengths, arrived_1, *held], [struct(rows, width)], "forward_1", kept=saved, after=[partner_lengths, other_a])
    arrived_2 = lax.ppermute(result_1, "section", swapped)

    def forward_last(lengths_ref, arriving, *refs):
        outs = refs[count:]
        slot = slots - 1

        @pl.when(lax.axis_index("section") == 1)
        def _():
            forward_body(
                slot, lengths_ref[slot], lambda: arriving[...], lambda name, part: None, *refs[:count], outs[len(saved)], *outs[: len(saved)]
            )

    *saved, result_2 = call(forward_last, [lengths, arrived_2, *held], [struct(rows, width)], "forward_2", kept=saved, after=[other_b])
    x_s, na_s, nb_s, qkv_s, pt_s, mixed_s, hidden_s, slope_s = saved
    partner_x = swap_over(x_s, 3, (1,))

    back_operands = [x_s, gain_a, gain_b, w_qkv, w_proj, w_up, w_down, *tabs, pt_s]
    back_count = len(back_operands)
    shared_operands = [gain_a, shift_a, gain_b, shift_b, w_qkv, b_qkv, w_up, b_up, *tabs]
    shared_count = len(shared_operands)
    shared_shapes = [
        pltpu.VMEM(shape, BF16)
        for shape in (
            (slots, rows, width), (slots, rows, width), (slots, rows, 3 * width // 2), (slots, pt_s.shape[1] // 2) + pt_s.shape[2:],
            (slots, rows, width // 2), (slots, rows, units // 2), (slots, rows, units // 2),
        )
    ]

    def share(lengths_ref, rows_of, refs, outs):
        weights, tabs_refs = refs[:-3], refs[-3:]
        partner_forward(dp_bit(3), lengths_ref, rows_of, *weights, tuple(t[...] for t in tabs_refs), *outs)

    def backward_first(lengths_ref, own_ref, ref_a, ref_b, *refs):
        operands, shared, (qkv_io, slope_io, gy, vec, gx, *outs) = (
            refs[:back_count], refs[back_count : back_count + shared_count], refs[back_count + shared_count :],
        )
        section = lax.axis_index("section")

        def rows_of(s):
            low, high = s * rows, s * rows + rows
            parts = [ref_a[low : min(high, cut)], ref_b[max(low, cut) - cut : high - cut]] if high > cut else [ref_a[low:high]]
            return jnp.concatenate(parts, axis=0)

        @pl.when(section == 1)
        def _():
            backward_body(0, lambda: own_ref[0], *operands, gx, qkv_io, slope_io, gy, vec)

        @pl.when(section == 0)
        def _():
            share(lengths_ref, rows_of, shared, outs)

    outs = call(
        backward_first, [partner_lengths, own, other_a, other_b, *back_operands, *shared_operands],
        [pltpu.VMEM((slots, rows, width), BF16), pltpu.VMEM((slots, 8, width), F32), struct(rows, width)] + shared_shapes,
        "backward_0", kept=[qkv_s, slope_s],
    )
    grads, back_0, shared = outs[:4], outs[4], outs[5:]
    arrived_4 = lax.ppermute(back_0, "section", swapped)
    partner_4 = swap_over(arrived_4, 3, (0,))

    def backward_both(own_ref, arriving, *refs):
        section = lax.axis_index("section")
        outs = refs[back_count:]
        source = lambda: jnp.where(section == 0, arriving[...], own_ref[section])
        backward_body(section, source, *refs[:back_count], outs[-1], *outs[:-1])

    *grads, back_1 = call(backward_both, [own, arrived_4, *back_operands], [struct(rows, width)], "backward_1", kept=grads, after=[other_gy])
    arrived_5 = lax.ppermute(back_1, "section", swapped)
    partner_5 = swap_over(arrived_5, 3, (0,))

    def backward_last(lengths_ref, arriving, other_ref, *refs):
        operands, shared_in, (qkv_io, slope_io, gy, vec, *outs) = (
            refs[:back_count], refs[back_count : back_count + shared_count], refs[back_count + shared_count :],
        )
        section = lax.axis_index("section")

        @pl.when(section == 0)
        def _():
            backward_body(slots - 1, lambda: arriving[...], *operands, outs[-1], qkv_io, slope_io, gy, vec)

        @pl.when(section == 1)
        def _():
            share(lengths_ref, lambda s: other_ref[s], shared_in, outs[:-1])

    outs = call(
        backward_last, [partner_lengths, arrived_5, partner_x, *back_operands, *shared_operands], [struct(rows, width)],
        "backward_2", kept=[*grads, *shared],
    )
    gp_s, gu_s, gy_s, vec_s, nap, nbp, qkvp, ptp, mixedp, hidp, slopep, back_2 = outs

    def partner_rows(other_ref, partner_a, partner_b):
        section = lax.axis_index("section")
        return lambda s: jnp.where(section == 0, (partner_a, partner_b)[s][...], other_ref[s])

    def backward_shared(other_ref, partner_a, partner_b, wp, wd, same, later, earlier, ptp_ref, qkvp_ref, slopep_ref, gyp):
        pick = partner_rows(other_ref, partner_a, partner_b)
        for s in range(slots):
            gyp[s] = pick(s)
        partner_backward(
            dp_bit(3), lambda s: gyp[s], wp, wd, (same[...], later[...], earlier[...]), ptp_ref, qkvp_ref, slopep_ref
        )

    gpp, gup, gyp_s = call(
        backward_shared, [other_gy, partner_4, partner_5, w_proj, w_down, *tabs, ptp], [struct(slots, rows, width)], "backward_shared",
        kept=[qkvp, slopep],
    )

    def group(rows_of_eighth, columns):
        return [struct(4, rows_of_eighth, columns)] * 2

    up = call(
        up_group_kernel, [nb_s, nbp, gu_s, gup], group(2 * low, units // 2), "up_grads", scratch=[pltpu.VMEM((width, 2 * tokens), BF16)]
    )

    def attn_group(na, nap_ref, gp, gpp_ref, mixed, mixedp_ref, gy, gyp, *refs):
        attn_group_kernel(na, nap_ref, gp, gpp_ref, mixed, mixedp_ref, gy, lambda s: gyp[s], *refs)

    attn = call(
        attn_group, [na_s, nap, gp_s, gpp, mixed_s, mixedp, gy_s, gyp_s, gu_s, vec_s], group(3 * low, 3 * width // 2), "attn_grads",
        scratch=[pltpu.VMEM((width, 2 * tokens), BF16), pltpu.VMEM((width // 2, 2 * tokens), BF16)], after=up[:1],
    )

    def down_group(hidden, hidp_ref, gy, gyp, *refs):
        down_group_kernel(hidden, hidp_ref, gy, lambda s: gyp[s], *refs)

    down = call(
        down_group, [hidden_s, hidp, gy_s, gyp_s], group(tall, width), "down_grads",
        scratch=[pltpu.VMEM((units // 2, 2 * tokens), BF16)], after=attn[:1],
    )

    up = halved(up, ORDERS["up"], 0, "up_sum_1", after=down[:1])
    attn = halved(attn, ORDERS["attn"], 0, "attn_sum_1", after=up[:1])
    down = halved(down, ORDERS["down"], 0, "down_sum_1", after=attn[:1])
    up = halved(up, ORDERS["up"], 1, "up_sum_2", after=down[:1])
    attn = halved(attn, ORDERS["attn"], 1, "attn_sum_2", after=up[:1])
    down = halved(down, ORDERS["down"], 1, "down_sum_2", after=attn[:1])
    up_last, attn_last = swap_over(up[1], ORDERS["up"][2]), swap_over(attn[1], ORDERS["attn"][2])
    up_mine, qkv_mine, small_mine, proj, others = call(
        halves_sum_kernel, [up[0], up_last, attn[0], attn_last],
        [struct(low, units // 2, dtype=F32), struct(low, 3 * width // 2, dtype=F32), struct(16, width // 2, dtype=F32),
         struct(low, width, dtype=F32), struct(low, units // 2 + 3 * width // 2 + 128)], "up_qkv_sum_3", after=down[:1],
    )
    (down_out,) = call(down_sum_kernel, [down[0], swap_over(down[1], ORDERS["down"][2])], [struct(tall, width, dtype=F32)], "down_sum_3")
    vectors = [low] * 6 + [tall, 3 * low]
    up_out, qkv_out, *vectors = call(
        joined_kernel, [up_mine, qkv_mine, small_mine, swap_over(others, 3)],
        [struct(low, units, dtype=F32), struct(low, 3 * width, dtype=F32)] + [struct(1, size, dtype=F32) for size in vectors], "up_qkv_joined",
    )
    joined = jnp.where(
        lax.axis_index("section") == 0, jnp.concatenate([back_1, back_2], axis=0), jnp.concatenate([result_1, result_2], axis=0)
    )
    gain_a, shift_a, gain_b, shift_b, bias_proj, bias_down, bias_up, bias_qkv = (vector[0] for vector in vectors)
    return joined, gain_a, shift_a, qkv_out, bias_qkv, proj, bias_proj, gain_b, shift_b, up_out, bias_up, down_out, bias_down


def plain_gradients(boundary, lengths, params, tables, swapped, bits):
    count = lax.axis_size("dp")
    slots = lengths.shape[0]
    width = boundary.shape[2]
    rows = boundary.shape[1] // slots
    units = params[8].shape[2]
    ticks = slots + 1
    result, saved, held = forward_first(lengths, boundary.reshape(slots, rows, width), params, tables)
    own, gain_a, shift_a, gain_b, shift_b, w_qkv, b_qkv, w_proj, b_proj, w_up, b_up, w_down, b_down, *tabs = held
    held_count = len(held)
    finals = [result]
    for t in range(1, ticks):
        arriving = lax.ppermute(result, "section", swapped)

        def forward_step(lengths_ref, arriving_ref, *refs, tick=t):
            section = lax.axis_index("section")
            slot = jnp.clip(tick - section, 0, slots - 1)
            inputs = lambda: jnp.where(section == 0, refs[0][slot], arriving_ref[...])
            outs = refs[held_count:]
            forward_body(slot, lengths_ref[slot], inputs, lambda name, part: None, *refs[:held_count], outs[-1], *outs[:-1])

        *saved, result = call(forward_step, [lengths, arriving, *held], [struct(rows, width)], "forward", kept=saved)
        finals.append(result)
    x_s, na_s, nb_s, qkv_s, pt_s, mixed_s, hidden_s, slope_s = saved
    operands = [x_s, gain_a, gain_b, w_qkv, w_proj, w_up, w_down, *tabs, pt_s]
    grads = [qkv_s, slope_s]
    input_grads = []
    arriving = own[0]
    for t in range(ticks):

        def backward_step(own_ref, arriving_ref, *refs, tick=t):
            section = lax.axis_index("section")
            slot = tick - 1 + section
            *io, gx_out = refs[len(operands) :]

            @pl.when((slot >= 0) & (slot < slots))
            def _():
                source = lambda: jnp.where(section == 0, arriving_ref[...], own_ref[slot])
                backward_body(slot, source, *refs[: len(operands)], gx_out, *io)

        shapes = [pltpu.VMEM((slots, rows, width), BF16), pltpu.VMEM((slots, 8, width), F32)] if t == 0 else []
        *grads, result = call(backward_step, [own, arriving, *operands], shapes + [struct(rows, width)], "backward", kept=grads)
        input_grads.append(result)
        if t + 1 < ticks:
            arriving = lax.ppermute(result, "section", swapped)
    gp_s, gu_s, gy_s, vec_s = grads
    order = list(range(len(bits)))

    def summed(full):
        keep, send = parted(full, 0, bits[0])
        return halving_sum(keep, send, order, count, bits, F32)

    both = jnp.concatenate([plain_grads(hidden_s, gy_s, count), plain_grads(mixed_s, gy_s, count)], axis=1)
    down, up, qkv = summed(both), summed(plain_grads(nb_s, gu_s, count)), summed(plain_grads(na_s, gp_s, count))
    tall = units // count
    sums = [jnp.sum(values, axis=(0, 1), dtype=F32) for values in (gy_s, gu_s, gp_s)]
    return finals[1:], input_grads[1:], vec_s, *sums, down[:tall], down[tall:], up, qkv


def per_device(boundary, lengths, *params):
    section = lax.axis_index("section")
    count = lax.axis_size("dp")
    bits = [(lax.axis_index("dp") >> b) & 1 for b in range(count.bit_length() - 1)]
    slots = lengths.shape[0]
    width = boundary.shape[2]
    units = params[8].shape[2]
    tables = [jnp.asarray(table) for table in rotary_lanes(boundary.shape[1] // slots, 2 * HEAD)]
    swapped = [(0, 1), (1, 0)]
    if count == 16 and slots == 2 and width % 768 == 0:
        results = paired_gradients(boundary, lengths, params, tables, swapped)
        return tuple(result[None] for result in results)
    finals, input_grads, vec_s, gy_sums, gu_sums, gp_sums, down, proj, up, qkv = plain_gradients(
        boundary, lengths, params, tables, swapped, bits
    )
    vec = jnp.sum(vec_s, axis=0)
    small = jnp.concatenate(
        [piece.reshape(count, -1) for piece in (vec[0], vec[1], vec[2], vec[3], gy_sums, gu_sums, gp_sums)], axis=1
    )
    small = halving_sum(*parted(small, 0, bits[0]), list(range(len(bits))), count, bits, F32)
    low, tall = width // count, units // count
    gain_a, shift_a, gain_b, shift_b, bias_y, bias_up, bias_qkv = jnp.split(small, np.cumsum([low] * 5 + [tall]), axis=0)
    joined = jnp.where(section == 0, jnp.concatenate(input_grads, axis=0), jnp.concatenate(finals, axis=0))
    results = (joined, gain_a, shift_a, qkv, bias_qkv, proj, bias_y, gain_b, shift_b, up, bias_up, down, bias_y)
    return tuple(result[None] for result in results)


def solution(mesh):
    split = P("section", "dp")
    deep = P("section", "dp", None)
    flat, matrix = P("section", None), P("section", None, None)
    return jax.shard_map(
        per_device,
        mesh=mesh,
        in_specs=(deep, P("dp"), flat, flat, matrix, flat, matrix, flat, flat, flat, matrix, flat, matrix, flat),
        out_specs=(deep, split, split, deep, split, deep, split, split, split, deep, split, deep, split),
        check_vma=False,
    )
```

```python
import functools
import math

import jax
import jax.numpy as jnp
import numpy as np
from jax import lax
from jax.experimental import pallas as pl
from jax.experimental.pallas import tpu as pltpu
from jax.sharding import PartitionSpec as P

HEAD = 64
LANES = 256
CHUNK = 512
EPS = 1e-05
NEG_FILL = -1e30
VMEM_BYTES = 12 * 1024 * 1024
FIRST_VMEM_BYTES = 12 * 1024 * 1024
F32 = jnp.float32
BF16 = jnp.bfloat16


def dot(left, right):
    return jnp.dot(left, right, preferred_element_type=F32)


def dot_nt(left, right):
    return lax.dot_general(left, right, (((1,), (1,)), ((), ())), preferred_element_type=F32)


def normalised(values):
    centred = values - jnp.mean(values, axis=-1, keepdims=True)
    variance = jnp.mean(centred * centred, axis=-1, keepdims=True)
    scale = lax.rsqrt(variance + EPS)
    return centred * scale, scale


def gelu_parts(values):
    integral = 0.5 + 0.5 * lax.erf(values * math.sqrt(0.5))
    bell = jnp.exp(values * values * -0.5)
    return values * integral, integral + values * bell * (1.0 / math.sqrt(2.0 * math.pi))


def rotary_lanes(seq_len, lanes):
    rot_dims = HEAD // 4
    half = rot_dims // 2
    frequency = np.float32(10000.0) ** (-(np.arange(half, dtype=np.float32) * np.float32(2.0) / np.float32(rot_dims)))
    angles = np.arange(seq_len, dtype=np.float32)[:, None] * frequency.astype(np.float32)[None, :]
    cosine, sine = np.cos(angles).astype(np.float32), np.sin(angles).astype(np.float32)
    same = np.ones((seq_len, HEAD), np.float32)
    later = np.zeros((seq_len, HEAD), np.float32)
    earlier = np.zeros((seq_len, HEAD), np.float32)
    same[:, :half] = cosine
    same[:, half:rot_dims] = cosine
    later[:, :half] = -sine
    earlier[:, half:rot_dims] = sine
    return [np.tile(t, (1, lanes // HEAD)) for t in (same, later, earlier)]


def turned(values, same, later, earlier, sign):
    half = HEAD // 8
    width = values.shape[1]
    same, later, earlier = (jnp.concatenate([t] * (width // t.shape[1]), axis=1) for t in (same, later, earlier))
    ahead = pltpu.roll(values, width - half, 1)
    behind = pltpu.roll(values, half, 1)
    if sign > 0:
        return values * same + ahead * later + behind * earlier
    return values * same - ahead * later - behind * earlier


def blocked_bias(rows, length):
    out = []
    for start in range(0, rows, 128):
        keys = start + 128
        key_pos = lax.broadcasted_iota(jnp.int32, (keys, 2 * 128), 0)
        query_pos = start + (lax.broadcasted_iota(jnp.int32, (keys, 2 * 128), 1) & 127)
        out.append(jnp.where((key_pos <= query_pos) & (key_pos < length), 0.0, NEG_FILL))
    return out


def heads_apart(block, lane):
    zero = jnp.zeros_like(block)
    return jnp.concatenate([jnp.where(lane < HEAD, block, zero), jnp.where(lane < HEAD, zero, block)], axis=0)


def dot_tn(left, right):
    return lax.dot_general(left, right, (((0,), (0,)), ((), ())), preferred_element_type=F32)


def probs_rows(block):
    start = 128 * (block * (block + 1) // 2)
    return slice(start, start + 128 * (block + 1))


def some(offset, size):
    return slice(offset, offset + size) if isinstance(offset, int) else pl.ds(pl.multiple_of(offset, 128), size)


def spans(pair, width):
    return [slice(b * width + pair * 2 * HEAD, b * width + (pair + 1) * 2 * HEAD) for b in range(3)]


def forward_units(slot, length, ready, na, nb, wqkv, bqkv, wu, bu, tables, qkv, pt, mixed, hidden, slope, low_head, low_unit, lanes):
    rows = qkv.shape[1]
    whole_width, width = wqkv.shape[1], qkv.shape[2] // 3
    pairs = width // (2 * HEAD)
    chunk = hidden.shape[2] // pairs
    biases = blocked_bias(rows, length)
    lane = lax.broadcasted_iota(jnp.int32, (128, 2 * HEAD), 1)
    per = lanes // (2 * HEAD)
    for pair in range(pairs):
        if pair % per == 0:
            low = pair * 2 * HEAD
            ready("qkv", pair // per)

            def packed(block):
                at = some(block * whole_width + low_head + low, lanes)
                return dot(na[slot], wqkv[0, :, at]) + bqkv[:, at].astype(F32)

            qkv[slot, :, low : low + lanes] = (turned(packed(0), *tables, 1) * (HEAD**-0.5)).astype(BF16)
            qkv[slot, :, width + low : width + low + lanes] = turned(packed(1), *tables, 1).astype(BF16)
            qkv[slot, :, 2 * width + low : 2 * width + low + lanes] = packed(2).astype(BF16)
        span, span_k, span_v = spans(pair, width)
        all_scores = []
        for block, start in enumerate(range(0, rows, 128)):
            keys = start + 128
            q2 = heads_apart(qkv[slot, start:keys, span], lane)
            all_scores.append(dot_nt(qkv[slot, :keys, span_k], q2) + biases[block])
        ready("up", pair)
        there = some(low_unit + pair * chunk, chunk)
        up = dot(nb[slot], wu[0, :, there]) + bu[:, there].astype(F32)
        for block, start in enumerate(range(0, rows, 128)):
            keys = start + 128
            scores = all_scores[block]
            exponent = jnp.exp(scores - jnp.max(scores, axis=0, keepdims=True))
            probs = (exponent * (1.0 / jnp.sum(exponent, axis=0, keepdims=True))).astype(BF16)
            pt[slot, pair, probs_rows(block)] = probs
            both = dot_tn(probs, qkv[slot, :keys, span_v])
            mixed[slot, start:keys, span] = jnp.where(lane < HEAD, both[:128], both[128:]).astype(BF16)
        here = slice(pair * chunk, pair * chunk + chunk)
        hidden_f32, slope_f32 = gelu_parts(up)
        hidden[slot, :, here] = hidden_f32.astype(BF16)
        slope[slot, :, here] = slope_f32.astype(BF16)


def backward_units(slot, gy, wp, wd, tables, pt, qkv, slope, low_head, low_unit, lanes):
    rows = qkv.shape[1]
    width = qkv.shape[2] // 3
    pairs = width // (2 * HEAD)
    chunk = slope.shape[2] // pairs
    lane = lax.broadcasted_iota(jnp.int32, (128, 2 * HEAD), 1)
    per = lanes // (2 * HEAD)
    for pair in range(pairs):
        if pair % per == 0:
            gm_group = dot_nt(gy(), wp[0, some(low_head + pair * 2 * HEAD, lanes), :]).astype(BF16)
            group_q, group_k = [], []
        span, span_k, span_v = spans(pair, width)
        gm = gm_group[:, (pair % per) * 2 * HEAD : (pair % per + 1) * 2 * HEAD]
        gv_sum, gk_sum, gq_blocks = None, None, []
        for block, start in enumerate(range(0, rows, 128)):
            keys = start + 128
            gm2 = heads_apart(gm[start:keys], lane)
            q2 = heads_apart(qkv[slot, start:keys, span], lane)
            probs = pt[slot, pair, probs_rows(block)]
            weighted = probs.astype(F32) * dot_nt(qkv[slot, :keys, span_v], gm2)
            inner = jnp.sum(weighted, axis=0, keepdims=True)
            gs = (weighted - probs.astype(F32) * inner).astype(BF16)
            gv_part = dot(probs, gm2)
            gk_part = dot(gs, q2)
            gq_part = dot_tn(gs, qkv[slot, :keys, span_k])
            gq_blocks.append(jnp.where(lane < HEAD, gq_part[:128], gq_part[128:]))
            if gv_sum is None:
                gv_sum, gk_sum = gv_part, gk_part
            else:
                gv_sum = jnp.concatenate([gv_sum + gv_part[:start], gv_part[start:]], axis=0)
                gk_sum = jnp.concatenate([gk_sum + gk_part[:start], gk_part[start:]], axis=0)
        qkv[slot, :, span_v] = gv_sum.astype(BF16)
        group_q.append(jnp.concatenate(gq_blocks, axis=0))
        group_k.append(gk_sum)
        if pair % per == per - 1:
            low = pair // per * lanes
            gq = turned(jnp.concatenate(group_q, axis=1) * (HEAD**-0.5), *tables, -1)
            qkv[slot, :, low : low + lanes] = gq.astype(BF16)
            gk = turned(jnp.concatenate(group_k, axis=1), *tables, -1)
            qkv[slot, :, width + low : width + low + lanes] = gk.astype(BF16)
        here = slice(pair * chunk, pair * chunk + chunk)
        grad = dot_nt(gy(), wd[0, some(low_unit + pair * chunk, chunk), :])
        slope[slot, :, here] = (grad * slope[slot, :, here].astype(F32)).astype(BF16)


def forward_body(
    slot, length, inputs, ready, own, gain_a, shift_a, gain_b, shift_b, wqkv, bqkv, wp, bp, wu, bu, wd, bd, same, later, earlier,
    y_out, x_out, na_out, nb_out, qkv_out, pt_out, mixed_out, hidden_out, slope_out,
):
    ready("small", 0)
    x_low = inputs()
    x_out[slot] = x_low
    xhat, _ = normalised(x_low.astype(F32))
    na_out[slot] = (xhat * gain_a[...].astype(F32) + shift_a[...].astype(F32)).astype(BF16)
    nb_out[slot] = (xhat * gain_b[...].astype(F32) + shift_b[...].astype(F32)).astype(BF16)
    tables = (same[...], later[...], earlier[...])
    forward_units(
        slot, length, ready, na_out, nb_out, wqkv, bqkv, wu, bu, tables, qkv_out, pt_out, mixed_out, hidden_out, slope_out, 0, 0, LANES
    )
    ready("rest", 0)
    total = x_out[slot].astype(F32) + (bp[...].astype(F32) + bd[...].astype(F32))
    y_out[...] = (total + dot(mixed_out[slot], wp[0]) + dot(hidden_out[slot], wd[0])).astype(BF16)


def backward_body(
    slot, gy_source, x_in, gain_a, gain_b, wqkv, wp, wu, wd, same, later, earlier, pt_in, gx_out, qkv_io, slope_io, gy_out, vec_out
):
    width = gx_out.shape[1]
    gy_out[slot] = gy_source()
    tables = (same[...], later[...], earlier[...])
    backward_units(slot, lambda: gy_out[slot], wp, wd, tables, pt_in, qkv_io, slope_io, 0, 0, LANES)
    grad_b = dot_nt(slope_io[slot], wu[0])
    grad_a = dot_nt(qkv_io[slot], wqkv[0])
    xhat, scale = normalised(x_in[slot].astype(F32))
    sums = [jnp.sum(t, axis=0, keepdims=True) for t in (grad_a * xhat, grad_a, grad_b * xhat, grad_b)]
    vec_out[slot] = jnp.concatenate(sums + [jnp.zeros((4, width), F32)], axis=0)
    both = grad_a * gain_a[...].astype(F32) + grad_b * gain_b[...].astype(F32)
    inner = jnp.mean(both * xhat, axis=-1, keepdims=True)
    gx = gy_out[slot].astype(F32) + scale * (both - jnp.mean(both, axis=-1, keepdims=True) - xhat * inner)
    gx_out[...] = gx.astype(BF16)


def forward_first_kernel(tick, lengths, *refs):
    count = 17
    sources, held, outs, sems = refs[:count], refs[count : 2 * count], refs[2 * count : -1], refs[-1]
    copies = []
    waits = {}

    def fetch(name, part, index, at):
        source, target = (sources[index], held[index]) if at is None else (sources[index].at[at], held[index].at[at])
        copy = pltpu.make_async_copy(source, target, sems.at[len(copies)])
        copies.append(copy)
        waits.setdefault((name, part), []).append(copy)

    (own, gain_a, shift_a, gain_b, shift_b, wqkv, bqkv, wp, bp, wu, bu, wd, bd, same, later, earlier, _) = range(count)
    width = sources[wp].shape[1]
    units = sources[wu].shape[2]
    pairs = width // (2 * HEAD)
    groups = width // LANES
    for index in (own, gain_a, shift_a, gain_b, shift_b, bqkv, bp, bu, bd, same, later, earlier):
        fetch("small", 0, index, None)
    for pair in range(pairs):
        if pair * groups % pairs == 0:
            group = pair * groups // pairs
            for block in range(3):
                fetch("qkv", group, wqkv, (slice(None), slice(None), pl.ds(block * width + group * LANES, LANES)))
        fetch("up", pair, wu, (slice(None), slice(None), pl.ds(pair * (units // pairs), units // pairs)))
    fetch("rest", 0, wp, None)
    fetch("rest", 0, wd, None)
    for copy in copies:
        copy.start()

    def ready(name, part):
        for copy in waits[(name, part)]:
            copy.wait()

    section = lax.axis_index("section")
    slots = held[own].shape[0]
    slot = jnp.clip(tick - section, 0, slots - 1)
    forward_body(slot, lengths[slot], lambda: held[own][slot], ready, *held[:-1], *outs)


def backward_body(
    slot, gy_source, x_in, gain_a, gain_b, wqkv, wp, wu, wd, same, later, earlier,
    pt_in, gx_out, qkv_io, slope_io, gy_out, vec_out,
):
    rows, width = gx_out.shape
    units = wu.shape[2]
    pairs = width // (2 * HEAD)
    chunk = units // pairs
    gy_out[slot] = gy_source()
    lane = lax.broadcasted_iota(jnp.int32, (128, 2 * HEAD), 1)
    tables = (same[...], later[...], earlier[...])
    per = LANES // (2 * HEAD)
    for pair in range(pairs):
        if pair % per == 0:
            gm_group = dot_nt(gy_out[slot], wp[0, pair * 2 * HEAD : pair * 2 * HEAD + LANES, :]).astype(BF16)
            group_q, group_k = [], []
        span, span_k, span_v = (slice(b * width + pair * 2 * HEAD, b * width + (pair + 1) * 2 * HEAD) for b in range(3))
        gm = gm_group[:, (pair % per) * 2 * HEAD : (pair % per + 1) * 2 * HEAD]
        gv_sum, gk_sum, gq_blocks = None, None, []
        for block, start in enumerate(range(0, rows, 128)):
            keys = start + 128
            gm2 = heads_apart(gm[start:keys], lane)
            q2 = heads_apart(qkv_io[slot, start:keys, span], lane)
            pt = pt_in[slot, pair, probs_rows(block)]
            weighted = pt.astype(F32) * dot_nt(qkv_io[slot, :keys, span_v], gm2)
            inner = jnp.sum(weighted, axis=0, keepdims=True)
            gs = (weighted - pt.astype(F32) * inner).astype(BF16)
            gv_part = dot(pt, gm2)
            gk_part = dot(gs, q2)
            gq_part = dot_tn(gs, qkv_io[slot, :keys, span_k])
            gq_blocks.append(jnp.where(lane < HEAD, gq_part[:128], gq_part[128:]))
            if gv_sum is None:
                gv_sum, gk_sum = gv_part, gk_part
            else:
                gv_sum = jnp.concatenate([gv_sum + gv_part[:start], gv_part[start:]], axis=0)
                gk_sum = jnp.concatenate([gk_sum + gk_part[:start], gk_part[start:]], axis=0)
        qkv_io[slot, :, span_v] = gv_sum.astype(BF16)
        group_q.append(jnp.concatenate(gq_blocks, axis=0))
        group_k.append(gk_sum)
        if pair % per == per - 1:
            low = pair // per * LANES
            gq = turned(jnp.concatenate(group_q, axis=1) * (HEAD**-0.5), *tables, -1)
            qkv_io[slot, :, low : low + LANES] = gq.astype(BF16)
            gk = turned(jnp.concatenate(group_k, axis=1), *tables, -1)
            qkv_io[slot, :, width + low : width + low + LANES] = gk.astype(BF16)
        at = slice(pair * chunk, pair * chunk + chunk)
        slope_io[slot, :, at] = (dot_nt(gy_out[slot], wd[0, at, :]) * slope_io[slot, :, at].astype(F32)).astype(BF16)
    grad_b = dot_nt(slope_io[slot], wu[0])
    grad_a = dot_nt(qkv_io[slot], wqkv[0])
    xhat, scale = normalised(x_in[slot].astype(F32))
    sums = [jnp.sum(t, axis=0, keepdims=True) for t in (grad_a * xhat, grad_a, grad_b * xhat, grad_b)]
    vec_out[slot] = jnp.concatenate(sums + [jnp.zeros((4, width), F32)], axis=0)
    both = grad_a * gain_a[...].astype(F32) + grad_b * gain_b[...].astype(F32)
    inner = jnp.mean(both * xhat, axis=-1, keepdims=True)
    gx = gy_out[slot].astype(F32) + scale * (both - jnp.mean(both, axis=-1, keepdims=True) - xhat * inner)
    gx_out[...] = gx.astype(BF16)


VM = pl.BlockSpec(memory_space=pltpu.VMEM)
HBM = pl.BlockSpec(memory_space=pl.ANY)


def call(kernel, operands, out_shape, name, kept=(), scratch=(), flops=1 << 20, after=()):
    count = len(operands)
    after = list(after)

    def body(*refs):
        kernel(*refs[:count], *refs[count + len(kept) + len(after) :])

    return pl.pallas_call(
        body,
        in_specs=[pl.BlockSpec(memory_space=pltpu.SMEM) if o.dtype == jnp.int32 else VM for o in operands] + [VM] * len(kept) + [HBM] * len(after),
        out_specs=[VM] * (len(kept) + len(out_shape)),
        out_shape=[pltpu.VMEM(array.shape, array.dtype) for array in kept] + list(out_shape),
        input_output_aliases={count + i: i for i in range(len(kept))},
        scratch_shapes=list(scratch),
        compiler_params=pltpu.CompilerParams(vmem_limit_bytes=VMEM_BYTES),
        cost_estimate=pl.CostEstimate(flops=flops, bytes_accessed=1 << 16, transcendentals=0),
        name=name,
    )(*operands, *[pltpu.with_memory_space_constraint(array, pltpu.VMEM) for array in kept], *after)


def shape_of(array):
    return jax.ShapeDtypeStruct(array.shape, array.dtype)


def forward_shapes(local_rows, params):
    slots, rows, width = local_rows.shape
    units = params[8].shape[2]
    blocks = rows // 128
    probs = (slots, width // (2 * HEAD), 128 * (blocks * (blocks + 1) // 2), 2 * 128)
    columns = [width, width, width, 3 * width, None, width, units, units]
    return [jax.ShapeDtypeStruct((rows, width), BF16)] + [
        pltpu.VMEM(probs if n is None else (slots, rows, n), BF16) for n in columns
    ]


def forward_first(lengths, local_rows, params, tables):
    (gain_a, shift_a, w_qkv, b_qkv, w_proj, b_proj, gain_b, shift_b, w_up, b_up, w_down, b_down) = params
    held = [local_rows, gain_a, shift_a, gain_b, shift_b, w_qkv, b_qkv, w_proj, b_proj, w_up, b_up, w_down, b_down] + list(tables)
    shapes = [shape_of(array) for array in held] + forward_shapes(local_rows, params)

    def kernel(lengths_ref, *refs):
        count = len(held)
        forward_first_kernel(0, lengths_ref, *refs[:count], None, *refs[count : 2 * count], None, *refs[2 * count :])

    outs = pl.pallas_call(
        kernel,
        in_specs=[pl.BlockSpec(memory_space=pltpu.SMEM)] + [pl.BlockSpec(memory_space=pltpu.HBM)] * len(held),
        out_specs=[VM] * len(shapes),
        out_shape=shapes,
        scratch_shapes=[pltpu.SemaphoreType.DMA((40,))],
        compiler_params=pltpu.CompilerParams(vmem_limit_bytes=FIRST_VMEM_BYTES),
        cost_estimate=pl.CostEstimate(flops=1 << 20, bytes_accessed=1 << 16, transcendentals=0),
        name="layer_forward_first",
    )(lengths, *[pltpu.with_memory_space_constraint(array, pltpu.HBM) for array in held])
    count = len(held)
    return outs[count], outs[count + 1 :], outs[:count]


def swap(shard, bit, count):
    return lax.ppermute(shard, "dp", [(i, i ^ (1 << bit)) for i in range(count)])


def parted(values, position, mine):
    count = values.shape[0]
    shaped = values.reshape((count >> (position + 1), 2, 1 << position) + values.shape[1:])
    out = []
    for side in (mine, 1 - mine):
        piece = lax.dynamic_index_in_dim(shaped, side, axis=1, keepdims=False)
        out.append(piece.reshape((count // 2,) + values.shape[1:]))
    return out


def halving_sum(keep, send, order, count, bits, final):
    left = sorted(order)
    for number, bit in enumerate(order):
        left.remove(bit)
        arrived = swap(send, bit, count)
        if number + 1 == len(order):
            return (keep.astype(F32) + arrived.astype(F32)).astype(final)[0]
        position = left.index(order[number + 1])
        keep_a, send_a = parted(keep, position, bits[order[number + 1]])
        keep_b, send_b = parted(arrived, position, bits[order[number + 1]])
        send = (send_a.astype(F32) + send_b.astype(F32)).astype(send_a.dtype)
        keep = (keep_a.astype(F32) + keep_b.astype(F32)).astype(send_a.dtype)


def plain_grads(left, right, count):
    rows = left.shape[0] * left.shape[1]
    product = lax.dot_general(
        left.reshape(rows, -1), right.reshape(rows, -1), (((0,), (0,)), ((), ())), preferred_element_type=F32
    ).astype(BF16)
    return product.reshape(count, product.shape[0] // count, product.shape[1])


def partner_forward(half, lengths, rows_of, gain_a, shift_a, gain_b, shift_b, wqkv, bqkv, wu, bu, tables, nap, nbp, qkvp, ptp, mixedp, hidp, slopep):
    for s in range(nap.shape[0]):
        xhat, _ = normalised(rows_of(s).astype(F32))
        nap[s] = (xhat * gain_a[...].astype(F32) + shift_a[...].astype(F32)).astype(BF16)
        nbp[s] = (xhat * gain_b[...].astype(F32) + shift_b[...].astype(F32)).astype(BF16)
        lanes = mixedp.shape[2]
        forward_units(
            s, lengths[s], lambda name, part: None, nap, nbp, wqkv, bqkv, wu, bu, tables, qkvp, ptp, mixedp, hidp, slopep,
            half * lanes, half * hidp.shape[2], lanes,
        )


def partner_backward(s, half, gy, wp, wd, tables, ptp, qkvp, slopep):
    lanes = qkvp.shape[2] // 3
    backward_units(s, gy, wp, wd, tables, ptp, qkvp, slopep, half * lanes, half * slopep.shape[2], lanes)


SUM_FLOPS = 6 << 30
ORDERS = {"down": (0, 1, 2), "up": (1, 2, 0), "attn": (2, 0, 1)}


def dp_bit(bit):
    return (lax.axis_index("dp") >> bit) & 1


def eighth_row(chunk, order, rows):
    first, second, third = ((chunk >> bit) & 1 for bit in order)
    return ((first ^ dp_bit(order[0])) * 4 + second * 2 + third) * rows


def row_slice(start, rows):
    return pl.ds(pl.multiple_of(start, 16), rows)


def flat_rows(ref, at=slice(None)):
    values = ref[:, :, at]
    return values.reshape(values.shape[0] * values.shape[1], values.shape[2])


def ones_dot(values):
    return dot(jnp.ones((16, values.shape[0]), BF16), values)[:8]


def sixteenths(ref, left, order, tokens_from):
    turned_ref = flat_rows(ref).T
    low = turned_ref.shape[0] // 16
    for chunk in range(16):
        start = eighth_row(chunk & 7, order, 2 * low) + (chunk >> 3) * low
        left[row_slice(start, low), tokens_from : tokens_from + turned_ref.shape[1]] = turned_ref[chunk * low : chunk * low + low]


def eighths(turned_rows, left, order, tokens_from):
    low = turned_rows.shape[0] // 8
    for chunk in range(8):
        left[row_slice(eighth_row(chunk, order, low), low), tokens_from : tokens_from + turned_rows.shape[1]] = turned_rows[
            chunk * low : chunk * low + low
        ]


def up_group_kernel(nb, nbp, gu, gup, keep, send, left):
    half = dp_bit(3)
    tokens = nb.shape[0] * nb.shape[1]
    units = gup.shape[2]
    sixteenths(nb, left, ORDERS["up"], 0)
    sixteenths(nbp, left, ORDERS["up"], tokens)
    rows = left.shape[0] // 8
    for low in range(0, units, 512):
        at = slice(low, low + 512)
        product = dot(left[:, :tokens], flat_rows(gu, some(half * units + low, 512))) + dot(left[:, tokens:], flat_rows(gup, at))
        product = product.astype(BF16).reshape(8, rows, 512)
        keep[:, :, at] = product[:4]
        send[:, :, at] = product[4:]


def attn_group_kernel(na, nap, gp, gpp, mixed, mixedp, gy, gyp_of, gu, vec, keep, send, left, left_mixed):
    half = dp_bit(3)
    tokens = na.shape[0] * na.shape[1]
    width = na.shape[2]
    lanes = mixedp.shape[2]
    order = ORDERS["attn"]
    sixteenths(na, left, order, 0)
    sixteenths(nap, left, order, tokens)
    rows = left.shape[0] // 8
    for block in range(3):
        at = slice(block * lanes, block * lanes + lanes)
        own = flat_rows(gp, some(block * width + half * lanes, lanes))
        product = dot(left[:, :tokens], own) + dot(left[:, tokens:], flat_rows(gpp, at))
        product = product.astype(BF16).reshape(8, rows, lanes)
        keep[:, :rows, at] = product[:4]
        send[:, :rows, at] = product[4:]
    eighths(flat_rows(mixed, some(half * lanes, lanes)).T, left_mixed, order, 0)
    eighths(flat_rows(mixedp).T, left_mixed, order, tokens)
    own_gy = flat_rows(gy)
    other_gy = jnp.concatenate([gyp_of(s) for s in range(gy.shape[0])], axis=0)
    product = dot(left_mixed[:, :tokens], own_gy) + dot(left_mixed[:, tokens:], other_gy)
    low = left_mixed.shape[0] // 8
    product = product.astype(BF16).reshape(8, low, width)
    keep[:, rows:, :width] = product[:4]
    send[:, rows:, :width] = product[4:]
    ones_row = lax.broadcasted_iota(jnp.int32, (16, lanes), 0)
    norms = vec[0] + vec[1]
    spread = [jnp.broadcast_to(norms[i : i + 1], (16, width)) for i in range(4)]
    sums = [jnp.concatenate([ones_dot(values)] * 2, axis=0) for values in (own_gy, flat_rows(gu), flat_rows(gp))]
    for chunk in range(16):
        block = jnp.zeros((16, lanes), F32)
        for row, values in enumerate(spread + sums):
            size = values.shape[1] // 16
            piece = values[:, chunk * size : chunk * size + size]
            piece = jnp.concatenate([piece, jnp.zeros((16, lanes - size), F32)], axis=1)
            block = jnp.where(ones_row == row, piece, block)
        block = block.astype(BF16)
        first, second, third = ((chunk >> bit) & 1 for bit in order)
        place_at = slice(rows + (chunk >> 3) * 16, rows + (chunk >> 3) * 16 + 16)

        @pl.when(dp_bit(order[0]) == first)
        def _():
            keep[second * 2 + third, place_at, width:] = block

        @pl.when(dp_bit(order[0]) != first)
        def _():
            send[second * 2 + third, place_at, width:] = block


def down_group_kernel(hidden, hidp, gy, gyp_of, keep, send, left):
    half = dp_bit(3)
    tokens = gy.shape[0] * gy.shape[1]
    units = hidp.shape[2]
    order = ORDERS["down"]
    eighths(flat_rows(hidden, some(half * units, units)).T, left, order, 0)
    eighths(flat_rows(hidp).T, left, order, tokens)
    own_gy = flat_rows(gy)
    other_gy = jnp.concatenate([gyp_of(s) for s in range(gy.shape[0])], axis=0)
    size = units // 2
    for side, out in enumerate((keep, send)):
        at = slice(side * size, side * size + size)
        product = dot(left[at, :tokens], own_gy) + dot(left[at, tokens:], other_gy)
        out[...] = product.astype(BF16).reshape(out.shape)


def plus(left, right):
    return left.astype(F32) + right.astype(F32)


def add_kernel(bit, keep, arrived, keep_out, send_out):
    size = keep_out.shape[0]
    mine = dp_bit(bit) * size
    keep_out[...] = plus(keep[pl.ds(mine, size)], arrived[pl.ds(mine, size)]).astype(BF16)
    send_out[...] = plus(keep[pl.ds(size - mine, size)], arrived[pl.ds(size - mine, size)]).astype(BF16)


def swap_over(shard, bit, sections=(0, 1)):
    count = lax.axis_size("dp")
    pairs = [(s * count + i, s * count + (i ^ (1 << bit))) for s in sections for i in range(count)]
    return lax.ppermute(shard, ("section", "dp"), pairs)


def struct(*shape, dtype=BF16):
    return jax.ShapeDtypeStruct(shape, dtype)


def halved(parts, order, stage, name, after=()):
    keep, send = parts
    arrived = swap_over(send, order[stage])
    shape = (keep.shape[0] // 2,) + keep.shape[1:]
    return call(functools.partial(add_kernel, order[stage + 1]), [keep, arrived], [struct(*shape)] * 2, name, after=after, flops=SUM_FLOPS)


def down_sum_kernel(keep, arrived, out):
    out[...] = plus(keep[0], arrived[0])


def halves_sum_kernel(up_keep, up_arrived, attn_keep, attn_arrived, up_mine, qkv_mine, small_mine, proj, other):
    half = dp_bit(3)
    low = up_mine.shape[0]
    units = up_mine.shape[1]
    width = proj.shape[1]
    mine, theirs = row_slice(half * low, low), row_slice((1 - half) * low, low)
    up_mine[...] = plus(up_keep[0, mine], up_arrived[0, mine])
    other[:, :units] = plus(up_keep[0, theirs], up_arrived[0, theirs]).astype(BF16)
    qkv_mine[...] = plus(attn_keep[0, mine], attn_arrived[0, mine])
    other[:, units : units + qkv_mine.shape[1]] = plus(attn_keep[0, theirs], attn_arrived[0, theirs]).astype(BF16)
    proj[...] = plus(attn_keep[0, 2 * low :, :width], attn_arrived[0, 2 * low :, :width])
    mine, theirs = row_slice(2 * low + half * 16, 16), row_slice(2 * low + (1 - half) * 16, 16)
    small_mine[...] = plus(attn_keep[0, mine, width:], attn_arrived[0, mine, width:])
    small = plus(attn_keep[0, theirs, width:], attn_arrived[0, theirs, width:]).astype(BF16)
    for part in range(small.shape[1] // 128):
        other[part * 16 : part * 16 + 16, other.shape[1] - 128 :] = small[:, part * 128 : part * 128 + 128]


def joined_kernel(up_mine, qkv_mine, small_mine, other, up, qkv, *vectors):
    half = dp_bit(3)
    low = up_mine.shape[0]
    units = up_mine.shape[1]
    lanes = qkv_mine.shape[1] // 3
    up[:, some(half * units, units)] = up_mine[...]
    up[:, some((1 - half) * units, units)] = other[:, :units].astype(F32)
    for block in range(3):
        at = slice(block * lanes, block * lanes + lanes)
        qkv[:, some((2 * block + half) * lanes, lanes)] = qkv_mine[:, at]
        qkv[:, some((2 * block + 1 - half) * lanes, lanes)] = other[:, units + block * lanes : units + (block + 1) * lanes].astype(F32)
    rest = other[:, other.shape[1] - 128 :].astype(F32)
    small = small_mine[...] + jnp.concatenate([rest[part : part + 16] for part in range(0, low, 16)], axis=1)
    for row, out in zip((0, 1, 2, 3, 4, 4, 5, 6), vectors):
        out[...] = small[row : row + 1, : out.shape[1]]


def paired_gradients(boundary, lengths, params, tables, swapped):
    slots = lengths.shape[0]
    width = boundary.shape[2]
    rows = boundary.shape[1] // slots
    units = params[8].shape[2]
    local_rows = boundary.reshape(slots, rows, width)
    low, tall = width // 16, units // 16
    tokens = slots * rows

    partner_lengths = swap_over(lengths, 3)
    cut = rows * slots * 3 // 4
    other_a = swap_over(boundary[0, :cut], 3, (0,))
    other_b = swap_over(boundary[0, cut:], 3, (0,))
    other_gy = swap_over(local_rows, 3, (1,))
    result_0, saved, held = forward_first(lengths, local_rows, params, tables)
    own, gain_a, shift_a, gain_b, shift_b, w_qkv, b_qkv, w_proj, b_proj, w_up, b_up, w_down, b_down, *tabs = held
    arrived_1 = lax.ppermute(result_0, "section", swapped)
    count = len(held)

    def forward_both(lengths_ref, arriving, *refs):
        section = lax.axis_index("section")
        slot = 1 - section
        inputs = lambda: jnp.where(section == 0, refs[0][slot], arriving[...])
        outs = refs[count:]
        forward_body(slot, lengths_ref[slot], inputs, lambda name, part: None, *refs[:count], outs[-1], *outs[:-1])

    *saved, result_1 = call(forward_both, [lengths, arrived_1, *held], [struct(rows, width)], "forward_1", kept=saved, after=[partner_lengths, other_a])
    arrived_2 = lax.ppermute(result_1, "section", swapped)

    def forward_last(lengths_ref, arriving, *refs):
        outs = refs[count:]
        slot = slots - 1
        *kept, y, x_a, x_b = outs

        @pl.when(lax.axis_index("section") == 1)
        def _():
            forward_body(slot, lengths_ref[slot], lambda: arriving[...], lambda name, part: None, *refs[:count], y, *kept)
            x_a[:rows] = kept[0][0]
            x_a[rows:] = arriving[: cut - rows]
            x_b[...] = arriving[cut - rows :]

    *saved, result_2, x_a, x_b = call(
        forward_last, [lengths, arrived_2, *held], [struct(rows, width), struct(cut, width), struct(slots * rows - cut, width)],
        "forward_2", kept=saved, after=[other_b],
    )
    x_s, na_s, nb_s, qkv_s, pt_s, mixed_s, hidden_s, slope_s = saved
    partner_xa, partner_xb = swap_over(x_a, 3, (1,)), swap_over(x_b, 3, (1,))

    back_operands = [x_s, gain_a, gain_b, w_qkv, w_proj, w_up, w_down, *tabs, pt_s]
    back_count = len(back_operands)
    shared_operands = [gain_a, shift_a, gain_b, shift_b, w_qkv, b_qkv, w_up, b_up, *tabs]
    shared_count = len(shared_operands)
    shared_shapes = [
        pltpu.VMEM(shape, BF16)
        for shape in (
            (slots, rows, width), (slots, rows, width), (slots, rows, 3 * width // 2), (slots, pt_s.shape[1] // 2) + pt_s.shape[2:],
            (slots, rows, width // 2), (slots, rows, units // 2), (slots, rows, units // 2),
        )
    ]

    def rows_in(ref_a, ref_b):
        def rows_of(s):
            low, high = s * rows, s * rows + rows
            parts = [ref_a[low : min(high, cut)], ref_b[max(low, cut) - cut : high - cut]] if high > cut else [ref_a[low:high]]
            return jnp.concatenate(parts, axis=0)

        return rows_of

    def share(lengths_ref, rows_of, refs, outs):
        weights, tabs_refs = refs[:-3], refs[-3:]
        partner_forward(dp_bit(3), lengths_ref, rows_of, *weights, tuple(t[...] for t in tabs_refs), *outs)

    def backward_first(lengths_ref, own_ref, ref_a, ref_b, *refs):
        operands, shared, (qkv_io, slope_io, gy, vec, gx, *outs) = (
            refs[:back_count], refs[back_count : back_count + shared_count], refs[back_count + shared_count :],
        )
        section = lax.axis_index("section")

        @pl.when(section == 1)
        def _():
            backward_body(0, lambda: own_ref[0], *operands, gx, qkv_io, slope_io, gy, vec)

        @pl.when(section == 0)
        def _():
            share(lengths_ref, rows_in(ref_a, ref_b), shared, outs)

    outs = call(
        backward_first, [partner_lengths, own, other_a, other_b, *back_operands, *shared_operands],
        [pltpu.VMEM((slots, rows, width), BF16), pltpu.VMEM((slots, 8, width), F32), struct(rows, width)] + shared_shapes,
        "backward_0", kept=[qkv_s, slope_s],
    )
    grads, back_0, shared = outs[:4], outs[4], outs[5:]
    arrived_4 = lax.ppermute(back_0, "section", swapped)
    partner_4 = swap_over(arrived_4, 3, (0,))

    def backward_both(own_ref, arriving, *refs):
        section = lax.axis_index("section")
        outs = refs[back_count:]
        source = lambda: jnp.where(section == 0, arriving[...], own_ref[section])
        backward_body(section, source, *refs[:back_count], outs[-1], *outs[:-1])

    *grads, back_1 = call(backward_both, [own, arrived_4, *back_operands], [struct(rows, width)], "backward_1", kept=grads, after=[other_gy, partner_xa])
    arrived_5 = lax.ppermute(back_1, "section", swapped)
    partner_5 = swap_over(arrived_5, 3, (0,))

    def backward_last(lengths_ref, arriving, ref_a, ref_b, *refs):
        operands, shared_in, (qkv_io, slope_io, gy, vec, *outs) = (
            refs[:back_count], refs[back_count : back_count + shared_count], refs[back_count + shared_count :],
        )
        section = lax.axis_index("section")

        @pl.when(section == 0)
        def _():
            backward_body(slots - 1, lambda: arriving[...], *operands, outs[-1], qkv_io, slope_io, gy, vec)

        @pl.when(section == 1)
        def _():
            share(lengths_ref, rows_in(ref_a, ref_b), shared_in, outs[:-1])

    outs = call(
        backward_last, [partner_lengths, arrived_5, partner_xa, partner_xb, *back_operands, *shared_operands], [struct(rows, width)],
        "backward_2", kept=[*grads, *shared],
    )
    gp_s, gu_s, gy_s, vec_s, nap, nbp, qkvp, ptp, mixedp, hidp, slopep, back_2 = outs

    gpp, gup = qkvp, slopep
    gyp_s = []
    for s, partner_gy in enumerate((partner_4, partner_5)):

        def backward_shared(other_ref, partner_ref, wp, wd, same, later, earlier, ptp_ref, qkvp_ref, slopep_ref, gyp, s=s):
            gyp[...] = jnp.where(lax.axis_index("section") == 0, partner_ref[...], other_ref[s])
            tables_in = (same[...], later[...], earlier[...])
            partner_backward(s, dp_bit(3), lambda: gyp[...], wp, wd, tables_in, ptp_ref, qkvp_ref, slopep_ref)

        gpp, gup, gyp = call(
            backward_shared, [other_gy, partner_gy, w_proj, w_down, *tabs, ptp], [struct(rows, width)], f"backward_shared_{s}", kept=[gpp, gup]
        )
        gyp_s.append(gyp)

    def group(rows_of_eighth, columns):
        return [struct(4, rows_of_eighth, columns)] * 2

    def down_group(hidden, hidp_ref, gy, gyp_a, gyp_b, *refs):
        down_group_kernel(hidden, hidp_ref, gy, lambda s: (gyp_a, gyp_b)[s][...], *refs)

    down = call(
        down_group, [hidden_s, hidp, gy_s, *gyp_s], group(tall, width), "down_grads", scratch=[pltpu.VMEM((units // 2, 2 * tokens), BF16)]
    )
    up = call(
        up_group_kernel, [nb_s, nbp, gu_s, gup], group(2 * low, units // 2), "up_grads", scratch=[pltpu.VMEM((width, 2 * tokens), BF16)],
        after=down[:1],
    )

    def attn_group(na, nap_ref, gp, gpp_ref, mixed, mixedp_ref, gy, gyp_a, gyp_b, *refs):
        attn_group_kernel(na, nap_ref, gp, gpp_ref, mixed, mixedp_ref, gy, lambda s: (gyp_a, gyp_b)[s][...], *refs)

    attn = call(
        attn_group, [na_s, nap, gp_s, gpp, mixed_s, mixedp, gy_s, *gyp_s, gu_s, vec_s], group(3 * low, 3 * width // 2), "attn_grads",
        scratch=[pltpu.VMEM((width, 2 * tokens), BF16), pltpu.VMEM((width // 2, 2 * tokens), BF16)], after=up[:1],
    )

    down = halved(down, ORDERS["down"], 0, "down_sum_1", after=attn[:1])
    up = halved(up, ORDERS["up"], 0, "up_sum_1", after=down[:1])
    attn = halved(attn, ORDERS["attn"], 0, "attn_sum_1", after=up[:1])
    down = halved(down, ORDERS["down"], 1, "down_sum_2", after=attn[:1])
    up = halved(up, ORDERS["up"], 1, "up_sum_2", after=down[:1])
    attn = halved(attn, ORDERS["attn"], 1, "attn_sum_2", after=up[:1])
    up_last, attn_last = swap_over(up[1], ORDERS["up"][2]), swap_over(attn[1], ORDERS["attn"][2])
    up_mine, qkv_mine, small_mine, proj, others = call(
        halves_sum_kernel, [up[0], up_last, attn[0], attn_last],
        [struct(low, units // 2, dtype=F32), struct(low, 3 * width // 2, dtype=F32), struct(16, width // 2, dtype=F32),
         struct(low, width, dtype=F32), struct(low, units // 2 + 3 * width // 2 + 128)], "up_qkv_sum_3", after=down[:1],
    )
    (down_out,) = call(down_sum_kernel, [down[0], swap_over(down[1], ORDERS["down"][2])], [struct(tall, width, dtype=F32)], "down_sum_3")
    vectors = [low] * 6 + [tall, 3 * low]
    up_out, qkv_out, *vectors = call(
        joined_kernel, [up_mine, qkv_mine, small_mine, swap_over(others, 3)],
        [struct(low, units, dtype=F32), struct(low, 3 * width, dtype=F32)] + [struct(1, size, dtype=F32) for size in vectors], "up_qkv_joined",
    )
    joined = jnp.where(
        lax.axis_index("section") == 0, jnp.concatenate([back_1, back_2], axis=0), jnp.concatenate([result_1, result_2], axis=0)
    )
    gain_a, shift_a, gain_b, shift_b, bias_proj, bias_down, bias_up, bias_qkv = (vector[0] for vector in vectors)
    return joined, gain_a, shift_a, qkv_out, bias_qkv, proj, bias_proj, gain_b, shift_b, up_out, bias_up, down_out, bias_down


def plain_gradients(boundary, lengths, params, tables, swapped, bits):
    count = lax.axis_size("dp")
    slots = lengths.shape[0]
    width = boundary.shape[2]
    rows = boundary.shape[1] // slots
    units = params[8].shape[2]
    ticks = slots + 1
    result, saved, held = forward_first(lengths, boundary.reshape(slots, rows, width), params, tables)
    own, gain_a, shift_a, gain_b, shift_b, w_qkv, b_qkv, w_proj, b_proj, w_up, b_up, w_down, b_down, *tabs = held
    held_count = len(held)
    finals = [result]
    for t in range(1, ticks):
        arriving = lax.ppermute(result, "section", swapped)

        def forward_step(lengths_ref, arriving_ref, *refs, tick=t):
            section = lax.axis_index("section")
            slot = jnp.clip(tick - section, 0, slots - 1)
            inputs = lambda: jnp.where(section == 0, refs[0][slot], arriving_ref[...])
            outs = refs[held_count:]
            forward_body(slot, lengths_ref[slot], inputs, lambda name, part: None, *refs[:held_count], outs[-1], *outs[:-1])

        *saved, result = call(forward_step, [lengths, arriving, *held], [struct(rows, width)], "forward", kept=saved)
        finals.append(result)
    x_s, na_s, nb_s, qkv_s, pt_s, mixed_s, hidden_s, slope_s = saved
    operands = [x_s, gain_a, gain_b, w_qkv, w_proj, w_up, w_down, *tabs, pt_s]
    grads = [qkv_s, slope_s]
    input_grads = []
    arriving = own[0]
    for t in range(ticks):

        def backward_step(own_ref, arriving_ref, *refs, tick=t):
            section = lax.axis_index("section")
            slot = tick - 1 + section
            *io, gx_out = refs[len(operands) :]

            @pl.when((slot >= 0) & (slot < slots))
            def _():
                source = lambda: jnp.where(section == 0, arriving_ref[...], own_ref[slot])
                backward_body(slot, source, *refs[: len(operands)], gx_out, *io)

        shapes = [pltpu.VMEM((slots, rows, width), BF16), pltpu.VMEM((slots, 8, width), F32)] if t == 0 else []
        *grads, result = call(backward_step, [own, arriving, *operands], shapes + [struct(rows, width)], "backward", kept=grads)
        input_grads.append(result)
        if t + 1 < ticks:
            arriving = lax.ppermute(result, "section", swapped)
    gp_s, gu_s, gy_s, vec_s = grads
    order = list(range(len(bits)))

    def summed(full):
        keep, send = parted(full, 0, bits[0])
        return halving_sum(keep, send, order, count, bits, F32)

    both = jnp.concatenate([plain_grads(hidden_s, gy_s, count), plain_grads(mixed_s, gy_s, count)], axis=1)
    down, up, qkv = summed(both), summed(plain_grads(nb_s, gu_s, count)), summed(plain_grads(na_s, gp_s, count))
    tall = units // count
    sums = [jnp.sum(values, axis=(0, 1), dtype=F32) for values in (gy_s, gu_s, gp_s)]
    return finals[1:], input_grads[1:], vec_s, *sums, down[:tall], down[tall:], up, qkv


def per_device(boundary, lengths, *params):
    section = lax.axis_index("section")
    count = lax.axis_size("dp")
    bits = [(lax.axis_index("dp") >> b) & 1 for b in range(count.bit_length() - 1)]
    slots = lengths.shape[0]
    width = boundary.shape[2]
    units = params[8].shape[2]
    tables = [jnp.asarray(table) for table in rotary_lanes(boundary.shape[1] // slots, 2 * HEAD)]
    swapped = [(0, 1), (1, 0)]
    if count == 16 and slots == 2 and width % 768 == 0:
        results = paired_gradients(boundary, lengths, params, tables, swapped)
        return tuple(result[None] for result in results)
    finals, input_grads, vec_s, gy_sums, gu_sums, gp_sums, down, proj, up, qkv = plain_gradients(
        boundary, lengths, params, tables, swapped, bits
    )
    vec = jnp.sum(vec_s, axis=0)
    small = jnp.concatenate(
        [piece.reshape(count, -1) for piece in (vec[0], vec[1], vec[2], vec[3], gy_sums, gu_sums, gp_sums)], axis=1
    )
    small = halving_sum(*parted(small, 0, bits[0]), list(range(len(bits))), count, bits, F32)
    low, tall = width // count, units // count
    gain_a, shift_a, gain_b, shift_b, bias_y, bias_up, bias_qkv = jnp.split(small, np.cumsum([low] * 5 + [tall]), axis=0)
    joined = jnp.where(section == 0, jnp.concatenate(input_grads, axis=0), jnp.concatenate(finals, axis=0))
    results = (joined, gain_a, shift_a, qkv, bias_qkv, proj, bias_y, gain_b, shift_b, up, bias_up, down, bias_y)
    return tuple(result[None] for result in results)


def solution(mesh):
    split = P("section", "dp")
    deep = P("section", "dp", None)
    flat, matrix = P("section", None), P("section", None, None)
    return jax.shard_map(
        per_device,
        mesh=mesh,
        in_specs=(deep, P("dp"), flat, flat, matrix, flat, matrix, flat, flat, flat, matrix, flat, matrix, flat),
        out_specs=(deep, split, split, deep, split, deep, split, split, split, deep, split, deep, split),
        check_vma=False,
    )
```

```python
import functools
import math

import jax
import jax.numpy as jnp
import numpy as np
from jax import lax
from jax.experimental import pallas as pl
from jax.experimental.pallas import tpu as pltpu
from jax.sharding import PartitionSpec as P

HEAD = 64
LANES = 256
CHUNK = 512
EPS = 1e-05
NEG_FILL = -1e30
VMEM_BYTES = 12 * 1024 * 1024
FIRST_VMEM_BYTES = 12 * 1024 * 1024
F32 = jnp.float32
BF16 = jnp.bfloat16


def dot(left, right):
    return jnp.dot(left, right, preferred_element_type=F32)


def dot_nt(left, right):
    return lax.dot_general(left, right, (((1,), (1,)), ((), ())), preferred_element_type=F32)


def normalised(values):
    centred = values - jnp.mean(values, axis=-1, keepdims=True)
    variance = jnp.mean(centred * centred, axis=-1, keepdims=True)
    scale = lax.rsqrt(variance + EPS)
    return centred * scale, scale


def gelu_parts(values):
    integral = 0.5 + 0.5 * lax.erf(values * math.sqrt(0.5))
    bell = jnp.exp(values * values * -0.5)
    return values * integral, integral + values * bell * (1.0 / math.sqrt(2.0 * math.pi))


def rotary_lanes(seq_len, lanes):
    rot_dims = HEAD // 4
    half = rot_dims // 2
    frequency = np.float32(10000.0) ** (-(np.arange(half, dtype=np.float32) * np.float32(2.0) / np.float32(rot_dims)))
    angles = np.arange(seq_len, dtype=np.float32)[:, None] * frequency.astype(np.float32)[None, :]
    cosine, sine = np.cos(angles).astype(np.float32), np.sin(angles).astype(np.float32)
    same = np.ones((seq_len, HEAD), np.float32)
    later = np.zeros((seq_len, HEAD), np.float32)
    earlier = np.zeros((seq_len, HEAD), np.float32)
    same[:, :half] = cosine
    same[:, half:rot_dims] = cosine
    later[:, :half] = -sine
    earlier[:, half:rot_dims] = sine
    return [np.tile(t, (1, lanes // HEAD)) for t in (same, later, earlier)]


def turned(values, same, later, earlier, sign):
    half = HEAD // 8
    width = values.shape[1]
    same, later, earlier = (jnp.concatenate([t] * (width // t.shape[1]), axis=1) for t in (same, later, earlier))
    ahead = pltpu.roll(values, width - half, 1)
    behind = pltpu.roll(values, half, 1)
    if sign > 0:
        return values * same + ahead * later + behind * earlier
    return values * same - ahead * later - behind * earlier


def blocked_bias(rows, length):
    out = []
    for start in range(0, rows, 128):
        keys = start + 128
        key_pos = lax.broadcasted_iota(jnp.int32, (keys, 2 * 128), 0)
        query_pos = start + (lax.broadcasted_iota(jnp.int32, (keys, 2 * 128), 1) & 127)
        out.append(jnp.where((key_pos <= query_pos) & (key_pos < length), 0.0, NEG_FILL))
    return out


def heads_apart(block, lane):
    zero = jnp.zeros_like(block)
    return jnp.concatenate([jnp.where(lane < HEAD, block, zero), jnp.where(lane < HEAD, zero, block)], axis=0)


def dot_tn(left, right):
    return lax.dot_general(left, right, (((0,), (0,)), ((), ())), preferred_element_type=F32)


def probs_rows(block):
    start = 128 * (block * (block + 1) // 2)
    return slice(start, start + 128 * (block + 1))


def some(offset, size):
    return slice(offset, offset + size) if isinstance(offset, int) else pl.ds(pl.multiple_of(offset, 128), size)


def spans(pair, width):
    return [slice(b * width + pair * 2 * HEAD, b * width + (pair + 1) * 2 * HEAD) for b in range(3)]


def forward_units(slot, length, ready, na, nb, wqkv, bqkv, wu, bu, tables, qkv, pt, mixed, hidden, slope, low_head, low_unit, lanes):
    rows = qkv.shape[1]
    whole_width, width = wqkv.shape[1], qkv.shape[2] // 3
    pairs = width // (2 * HEAD)
    chunk = hidden.shape[2] // pairs
    biases = blocked_bias(rows, length)
    lane = lax.broadcasted_iota(jnp.int32, (128, 2 * HEAD), 1)
    per = lanes // (2 * HEAD)
    for pair in range(pairs):
        if pair % per == 0:
            low = pair * 2 * HEAD
            ready("qkv", pair // per)

            def packed(block):
                at = some(block * whole_width + low_head + low, lanes)
                return dot(na[slot], wqkv[0, :, at]) + bqkv[:, at].astype(F32)

            qkv[slot, :, low : low + lanes] = (turned(packed(0), *tables, 1) * (HEAD**-0.5)).astype(BF16)
            qkv[slot, :, width + low : width + low + lanes] = turned(packed(1), *tables, 1).astype(BF16)
            qkv[slot, :, 2 * width + low : 2 * width + low + lanes] = packed(2).astype(BF16)
        span, span_k, span_v = spans(pair, width)
        all_scores = []
        for block, start in enumerate(range(0, rows, 128)):
            keys = start + 128
            q2 = heads_apart(qkv[slot, start:keys, span], lane)
            all_scores.append(dot_nt(qkv[slot, :keys, span_k], q2) + biases[block])
        ready("up", pair)
        there = some(low_unit + pair * chunk, chunk)
        up = dot(nb[slot], wu[0, :, there]) + bu[:, there].astype(F32)
        for block, start in enumerate(range(0, rows, 128)):
            keys = start + 128
            scores = all_scores[block]
            exponent = jnp.exp(scores - jnp.max(scores, axis=0, keepdims=True))
            probs = (exponent * (1.0 / jnp.sum(exponent, axis=0, keepdims=True))).astype(BF16)
            pt[slot, pair, probs_rows(block)] = probs
            both = dot_tn(probs, qkv[slot, :keys, span_v])
            mixed[slot, start:keys, span] = jnp.where(lane < HEAD, both[:128], both[128:]).astype(BF16)
        here = slice(pair * chunk, pair * chunk + chunk)
        hidden_f32, slope_f32 = gelu_parts(up)
        hidden[slot, :, here] = hidden_f32.astype(BF16)
        slope[slot, :, here] = slope_f32.astype(BF16)


def backward_units(slot, gy, wp, wd, tables, pt, qkv, slope, low_head, low_unit, lanes):
    rows = qkv.shape[1]
    width = qkv.shape[2] // 3
    pairs = width // (2 * HEAD)
    chunk = slope.shape[2] // pairs
    lane = lax.broadcasted_iota(jnp.int32, (128, 2 * HEAD), 1)
    per = lanes // (2 * HEAD)
    for pair in range(pairs):
        if pair % per == 0:
            gm_group = dot_nt(gy(), wp[0, some(low_head + pair * 2 * HEAD, lanes), :]).astype(BF16)
            group_q, group_k = [], []
        span, span_k, span_v = spans(pair, width)
        gm = gm_group[:, (pair % per) * 2 * HEAD : (pair % per + 1) * 2 * HEAD]
        gv_sum, gk_sum, gq_blocks = None, None, []
        for block, start in enumerate(range(0, rows, 128)):
            keys = start + 128
            gm2 = heads_apart(gm[start:keys], lane)
            q2 = heads_apart(qkv[slot, start:keys, span], lane)
            probs = pt[slot, pair, probs_rows(block)]
            weighted = probs.astype(F32) * dot_nt(qkv[slot, :keys, span_v], gm2)
            inner = jnp.sum(weighted, axis=0, keepdims=True)
            gs = (weighted - probs.astype(F32) * inner).astype(BF16)
            gv_part = dot(probs, gm2)
            gk_part = dot(gs, q2)
            gq_part = dot_tn(gs, qkv[slot, :keys, span_k])
            gq_blocks.append(jnp.where(lane < HEAD, gq_part[:128], gq_part[128:]))
            if gv_sum is None:
                gv_sum, gk_sum = gv_part, gk_part
            else:
                gv_sum = jnp.concatenate([gv_sum + gv_part[:start], gv_part[start:]], axis=0)
                gk_sum = jnp.concatenate([gk_sum + gk_part[:start], gk_part[start:]], axis=0)
        qkv[slot, :, span_v] = gv_sum.astype(BF16)
        group_q.append(jnp.concatenate(gq_blocks, axis=0))
        group_k.append(gk_sum)
        if pair % per == per - 1:
            low = pair // per * lanes
            gq = turned(jnp.concatenate(group_q, axis=1) * (HEAD**-0.5), *tables, -1)
            qkv[slot, :, low : low + lanes] = gq.astype(BF16)
            gk = turned(jnp.concatenate(group_k, axis=1), *tables, -1)
            qkv[slot, :, width + low : width + low + lanes] = gk.astype(BF16)
        here = slice(pair * chunk, pair * chunk + chunk)
        grad = dot_nt(gy(), wd[0, some(low_unit + pair * chunk, chunk), :])
        slope[slot, :, here] = (grad * slope[slot, :, here].astype(F32)).astype(BF16)


def forward_body(
    slot, length, inputs, ready, own, gain_a, shift_a, gain_b, shift_b, wqkv, bqkv, wp, bp, wu, bu, wd, bd, same, later, earlier,
    y_out, x_out, na_out, nb_out, qkv_out, pt_out, mixed_out, hidden_out, slope_out,
):
    ready("small", 0)
    x_low = inputs()
    x_out[slot] = x_low
    xhat, _ = normalised(x_low.astype(F32))
    na_out[slot] = (xhat * gain_a[...].astype(F32) + shift_a[...].astype(F32)).astype(BF16)
    nb_out[slot] = (xhat * gain_b[...].astype(F32) + shift_b[...].astype(F32)).astype(BF16)
    tables = (same[...], later[...], earlier[...])
    forward_units(
        slot, length, ready, na_out, nb_out, wqkv, bqkv, wu, bu, tables, qkv_out, pt_out, mixed_out, hidden_out, slope_out, 0, 0, LANES
    )
    ready("rest", 0)
    total = x_out[slot].astype(F32) + (bp[...].astype(F32) + bd[...].astype(F32))
    y_out[...] = (total + dot(mixed_out[slot], wp[0]) + dot(hidden_out[slot], wd[0])).astype(BF16)


def backward_body(
    slot, gy_source, x_in, gain_a, gain_b, wqkv, wp, wu, wd, same, later, earlier, pt_in, gx_out, qkv_io, slope_io, gy_out, vec_out
):
    width = gx_out.shape[1]
    gy_out[slot] = gy_source()
    tables = (same[...], later[...], earlier[...])
    backward_units(slot, lambda: gy_out[slot], wp, wd, tables, pt_in, qkv_io, slope_io, 0, 0, LANES)
    grad_b = dot_nt(slope_io[slot], wu[0])
    grad_a = dot_nt(qkv_io[slot], wqkv[0])
    xhat, scale = normalised(x_in[slot].astype(F32))
    norm_terms = (grad_a * xhat, grad_a, grad_b * xhat, grad_b, gy_out[slot].astype(F32))
    for row, terms in enumerate(norm_terms):
        vec_out[slot, row : row + 1, :width] = jnp.sum(terms, axis=0, keepdims=True)
    vec_out[slot, 5:6, :] = jnp.sum(slope_io[slot].astype(F32), axis=0, keepdims=True)
    vec_out[slot, 6:7, : 3 * width] = jnp.sum(qkv_io[slot].astype(F32), axis=0, keepdims=True)
    both = grad_a * gain_a[...].astype(F32) + grad_b * gain_b[...].astype(F32)
    inner = jnp.mean(both * xhat, axis=-1, keepdims=True)
    gx = gy_out[slot].astype(F32) + scale * (both - jnp.mean(both, axis=-1, keepdims=True) - xhat * inner)
    gx_out[...] = gx.astype(BF16)


def forward_first_kernel(tick, lengths, *refs):
    count = 17
    sources, held, outs, sems = refs[:count], refs[count : 2 * count], refs[2 * count : -1], refs[-1]
    copies = []
    waits = {}

    def fetch(name, part, index, at):
        source, target = (sources[index], held[index]) if at is None else (sources[index].at[at], held[index].at[at])
        copy = pltpu.make_async_copy(source, target, sems.at[len(copies)])
        copies.append(copy)
        waits.setdefault((name, part), []).append(copy)

    (own, gain_a, shift_a, gain_b, shift_b, wqkv, bqkv, wp, bp, wu, bu, wd, bd, same, later, earlier, _) = range(count)
    width = sources[wp].shape[1]
    units = sources[wu].shape[2]
    pairs = width // (2 * HEAD)
    groups = width // LANES
    for index in (own, gain_a, shift_a, gain_b, shift_b, bqkv, bp, bu, bd, same, later, earlier):
        fetch("small", 0, index, None)
    for pair in range(pairs):
        if pair * groups % pairs == 0:
            group = pair * groups // pairs
            for block in range(3):
                fetch("qkv", group, wqkv, (slice(None), slice(None), pl.ds(block * width + group * LANES, LANES)))
        fetch("up", pair, wu, (slice(None), slice(None), pl.ds(pair * (units // pairs), units // pairs)))
    fetch("rest", 0, wp, None)
    fetch("rest", 0, wd, None)
    for copy in copies:
        copy.start()

    def ready(name, part):
        for copy in waits[(name, part)]:
            copy.wait()

    section = lax.axis_index("section")
    slots = held[own].shape[0]
    slot = jnp.clip(tick - section, 0, slots - 1)
    forward_body(slot, lengths[slot], lambda: held[own][slot], ready, *held[:-1], *outs)


def backward_body(
    slot, gy_source, x_in, gain_a, gain_b, wqkv, wp, wu, wd, same, later, earlier,
    pt_in, gx_out, qkv_io, slope_io, gy_out, vec_out,
):
    rows, width = gx_out.shape
    units = wu.shape[2]
    pairs = width // (2 * HEAD)
    chunk = units // pairs
    gy_out[slot] = gy_source()
    lane = lax.broadcasted_iota(jnp.int32, (128, 2 * HEAD), 1)
    tables = (same[...], later[...], earlier[...])
    per = LANES // (2 * HEAD)
    for pair in range(pairs):
        if pair % per == 0:
            gm_group = dot_nt(gy_out[slot], wp[0, pair * 2 * HEAD : pair * 2 * HEAD + LANES, :]).astype(BF16)
            group_q, group_k = [], []
        span, span_k, span_v = (slice(b * width + pair * 2 * HEAD, b * width + (pair + 1) * 2 * HEAD) for b in range(3))
        gm = gm_group[:, (pair % per) * 2 * HEAD : (pair % per + 1) * 2 * HEAD]
        gv_sum, gk_sum, gq_blocks = None, None, []
        for block, start in enumerate(range(0, rows, 128)):
            keys = start + 128
            gm2 = heads_apart(gm[start:keys], lane)
            q2 = heads_apart(qkv_io[slot, start:keys, span], lane)
            pt = pt_in[slot, pair, probs_rows(block)]
            weighted = pt.astype(F32) * dot_nt(qkv_io[slot, :keys, span_v], gm2)
            inner = jnp.sum(weighted, axis=0, keepdims=True)
            gs = (weighted - pt.astype(F32) * inner).astype(BF16)
            gv_part = dot(pt, gm2)
            gk_part = dot(gs, q2)
            gq_part = dot_tn(gs, qkv_io[slot, :keys, span_k])
            gq_blocks.append(jnp.where(lane < HEAD, gq_part[:128], gq_part[128:]))
            if gv_sum is None:
                gv_sum, gk_sum = gv_part, gk_part
            else:
                gv_sum = jnp.concatenate([gv_sum + gv_part[:start], gv_part[start:]], axis=0)
                gk_sum = jnp.concatenate([gk_sum + gk_part[:start], gk_part[start:]], axis=0)
        qkv_io[slot, :, span_v] = gv_sum.astype(BF16)
        group_q.append(jnp.concatenate(gq_blocks, axis=0))
        group_k.append(gk_sum)
        if pair % per == per - 1:
            low = pair // per * LANES
            gq = turned(jnp.concatenate(group_q, axis=1) * (HEAD**-0.5), *tables, -1)
            qkv_io[slot, :, low : low + LANES] = gq.astype(BF16)
            gk = turned(jnp.concatenate(group_k, axis=1), *tables, -1)
            qkv_io[slot, :, width + low : width + low + LANES] = gk.astype(BF16)
        at = slice(pair * chunk, pair * chunk + chunk)
        slope_io[slot, :, at] = (dot_nt(gy_out[slot], wd[0, at, :]) * slope_io[slot, :, at].astype(F32)).astype(BF16)
    grad_b = dot_nt(slope_io[slot], wu[0])
    grad_a = dot_nt(qkv_io[slot], wqkv[0])
    xhat, scale = normalised(x_in[slot].astype(F32))
    norm_terms = (grad_a * xhat, grad_a, grad_b * xhat, grad_b, gy_out[slot].astype(F32))
    for row, terms in enumerate(norm_terms):
        vec_out[slot, row : row + 1, :width] = jnp.sum(terms, axis=0, keepdims=True)
    vec_out[slot, 5:6, :] = jnp.sum(slope_io[slot].astype(F32), axis=0, keepdims=True)
    vec_out[slot, 6:7, : 3 * width] = jnp.sum(qkv_io[slot].astype(F32), axis=0, keepdims=True)
    both = grad_a * gain_a[...].astype(F32) + grad_b * gain_b[...].astype(F32)
    inner = jnp.mean(both * xhat, axis=-1, keepdims=True)
    gx = gy_out[slot].astype(F32) + scale * (both - jnp.mean(both, axis=-1, keepdims=True) - xhat * inner)
    gx_out[...] = gx.astype(BF16)


VM = pl.BlockSpec(memory_space=pltpu.VMEM)
HBM = pl.BlockSpec(memory_space=pl.ANY)


def call(kernel, operands, out_shape, name, kept=(), scratch=(), flops=1 << 20, after=()):
    count = len(operands)
    after = list(after)

    def body(*refs):
        kernel(*refs[:count], *refs[count + len(kept) + len(after) :])

    return pl.pallas_call(
        body,
        in_specs=[pl.BlockSpec(memory_space=pltpu.SMEM) if o.dtype == jnp.int32 else VM for o in operands] + [VM] * len(kept) + [HBM] * len(after),
        out_specs=[VM] * (len(kept) + len(out_shape)),
        out_shape=[pltpu.VMEM(array.shape, array.dtype) for array in kept] + list(out_shape),
        input_output_aliases={count + i: i for i in range(len(kept))},
        scratch_shapes=list(scratch),
        compiler_params=pltpu.CompilerParams(vmem_limit_bytes=VMEM_BYTES),
        cost_estimate=pl.CostEstimate(flops=flops, bytes_accessed=1 << 16, transcendentals=0),
        name=name,
    )(*operands, *[pltpu.with_memory_space_constraint(array, pltpu.VMEM) for array in kept], *after)


def shape_of(array):
    return jax.ShapeDtypeStruct(array.shape, array.dtype)


def forward_shapes(local_rows, params):
    slots, rows, width = local_rows.shape
    units = params[8].shape[2]
    blocks = rows // 128
    probs = (slots, width // (2 * HEAD), 128 * (blocks * (blocks + 1) // 2), 2 * 128)
    columns = [width, width, width, 3 * width, None, width, units, units]
    return [jax.ShapeDtypeStruct((rows, width), BF16)] + [
        pltpu.VMEM(probs if n is None else (slots, rows, n), BF16) for n in columns
    ]


def forward_first(lengths, local_rows, params, tables):
    (gain_a, shift_a, w_qkv, b_qkv, w_proj, b_proj, gain_b, shift_b, w_up, b_up, w_down, b_down) = params
    held = [local_rows, gain_a, shift_a, gain_b, shift_b, w_qkv, b_qkv, w_proj, b_proj, w_up, b_up, w_down, b_down] + list(tables)
    shapes = [shape_of(array) for array in held] + forward_shapes(local_rows, params)

    def kernel(lengths_ref, *refs):
        count = len(held)
        forward_first_kernel(0, lengths_ref, *refs[:count], None, *refs[count : 2 * count], None, *refs[2 * count :])

    outs = pl.pallas_call(
        kernel,
        in_specs=[pl.BlockSpec(memory_space=pltpu.SMEM)] + [pl.BlockSpec(memory_space=pltpu.HBM)] * len(held),
        out_specs=[VM] * len(shapes),
        out_shape=shapes,
        scratch_shapes=[pltpu.SemaphoreType.DMA((40,))],
        compiler_params=pltpu.CompilerParams(vmem_limit_bytes=FIRST_VMEM_BYTES),
        cost_estimate=pl.CostEstimate(flops=1 << 20, bytes_accessed=1 << 16, transcendentals=0),
        name="layer_forward_first",
    )(lengths, *[pltpu.with_memory_space_constraint(array, pltpu.HBM) for array in held])
    count = len(held)
    return outs[count], outs[count + 1 :], outs[:count]


def swap(shard, bit, count):
    return lax.ppermute(shard, "dp", [(i, i ^ (1 << bit)) for i in range(count)])


def parted(values, position, mine):
    count = values.shape[0]
    shaped = values.reshape((count >> (position + 1), 2, 1 << position) + values.shape[1:])
    out = []
    for side in (mine, 1 - mine):
        piece = lax.dynamic_index_in_dim(shaped, side, axis=1, keepdims=False)
        out.append(piece.reshape((count // 2,) + values.shape[1:]))
    return out


def halving_sum(keep, send, order, count, bits, final):
    left = sorted(order)
    for number, bit in enumerate(order):
        left.remove(bit)
        arrived = swap(send, bit, count)
        if number + 1 == len(order):
            return (keep.astype(F32) + arrived.astype(F32)).astype(final)[0]
        position = left.index(order[number + 1])
        keep_a, send_a = parted(keep, position, bits[order[number + 1]])
        keep_b, send_b = parted(arrived, position, bits[order[number + 1]])
        send = (send_a.astype(F32) + send_b.astype(F32)).astype(send_a.dtype)
        keep = (keep_a.astype(F32) + keep_b.astype(F32)).astype(send_a.dtype)


def plain_grads(left, right, count):
    rows = left.shape[0] * left.shape[1]
    product = lax.dot_general(
        left.reshape(rows, -1), right.reshape(rows, -1), (((0,), (0,)), ((), ())), preferred_element_type=F32
    ).astype(BF16)
    return product.reshape(count, product.shape[0] // count, product.shape[1])


def partner_forward(s, half, lengths, rows_of, gain_a, shift_a, gain_b, shift_b, wqkv, bqkv, wu, bu, tables, nap, nbp, qkvp, ptp, mixedp, hidp, slopep):
    lanes = mixedp.shape[2]
    xhat, _ = normalised(rows_of(s).astype(F32))
    nap[s] = (xhat * gain_a[...].astype(F32) + shift_a[...].astype(F32)).astype(BF16)
    nbp[s] = (xhat * gain_b[...].astype(F32) + shift_b[...].astype(F32)).astype(BF16)
    forward_units(
        s, lengths[s], lambda name, part: None, nap, nbp, wqkv, bqkv, wu, bu, tables, qkvp, ptp, mixedp, hidp, slopep,
        half * lanes, half * hidp.shape[2], lanes,
    )


def partner_backward(s, half, gy, wp, wd, tables, ptp, qkvp, slopep):
    lanes = qkvp.shape[2] // 3
    backward_units(s, gy, wp, wd, tables, ptp, qkvp, slopep, half * lanes, half * slopep.shape[2], lanes)


SUM_FLOPS = 6 << 30
ORDERS = {"down": (0, 1, 2), "up": (1, 2, 0), "attn": (2, 0, 1)}


def dp_bit(bit):
    return (lax.axis_index("dp") >> bit) & 1


def eighth_row(chunk, order, rows):
    first, second, third = ((chunk >> bit) & 1 for bit in order)
    return ((first ^ dp_bit(order[0])) * 4 + second * 2 + third) * rows


def row_slice(start, rows):
    return pl.ds(pl.multiple_of(start, 16), rows)


def flat_rows(ref, at=slice(None)):
    values = ref[:, :, at]
    return values.reshape(values.shape[0] * values.shape[1], values.shape[2])


def ones_dot(values):
    return dot(jnp.ones((16, values.shape[0]), BF16), values)[:8]


def sixteenths(ref, left, order, tokens_from):
    turned_ref = flat_rows(ref).T
    low = turned_ref.shape[0] // 16
    for chunk in range(16):
        start = eighth_row(chunk & 7, order, 2 * low) + (chunk >> 3) * low
        left[row_slice(start, low), tokens_from : tokens_from + turned_ref.shape[1]] = turned_ref[chunk * low : chunk * low + low]


def eighths(turned_rows, left, order, tokens_from):
    low = turned_rows.shape[0] // 8
    for chunk in range(8):
        left[row_slice(eighth_row(chunk, order, low), low), tokens_from : tokens_from + turned_rows.shape[1]] = turned_rows[
            chunk * low : chunk * low + low
        ]


def up_group_kernel(nb, nbp, gu, gup, keep, send, left):
    half = dp_bit(3)
    tokens = nb.shape[0] * nb.shape[1]
    units = gup.shape[2]
    sixteenths(nb, left, ORDERS["up"], 0)
    sixteenths(nbp, left, ORDERS["up"], tokens)
    rows = left.shape[0] // 8
    for low in range(0, units, 512):
        at = slice(low, low + 512)
        product = dot(left[:, :tokens], flat_rows(gu, some(half * units + low, 512))) + dot(left[:, tokens:], flat_rows(gup, at))
        product = product.astype(BF16).reshape(8, rows, 512)
        keep[:, :, at] = product[:4]
        send[:, :, at] = product[4:]


def attn_group_kernel(na, nap, gp, gpp, mixed, mixedp, gy, gyp_of, vec, keep, send, left, left_mixed):
    half = dp_bit(3)
    tokens = na.shape[0] * na.shape[1]
    width = na.shape[2]
    lanes = mixedp.shape[2]
    order = ORDERS["attn"]
    sixteenths(na, left, order, 0)
    sixteenths(nap, left, order, tokens)
    rows = left.shape[0] // 8
    for block in range(3):
        at = slice(block * lanes, block * lanes + lanes)
        own = flat_rows(gp, some(block * width + half * lanes, lanes))
        product = dot(left[:, :tokens], own) + dot(left[:, tokens:], flat_rows(gpp, at))
        product = product.astype(BF16).reshape(8, rows, lanes)
        keep[:, :rows, at] = product[:4]
        send[:, :rows, at] = product[4:]
    eighths(flat_rows(mixed, some(half * lanes, lanes)).T, left_mixed, order, 0)
    eighths(flat_rows(mixedp).T, left_mixed, order, tokens)
    own_gy = flat_rows(gy)
    other_gy = jnp.concatenate([gyp_of(s) for s in range(gy.shape[0])], axis=0)
    product = dot(left_mixed[:, :tokens], own_gy) + dot(left_mixed[:, tokens:], other_gy)
    low = left_mixed.shape[0] // 8
    product = product.astype(BF16).reshape(8, low, width)
    keep[:, rows:, :width] = product[:4]
    send[:, rows:, :width] = product[4:]
    row_index = lax.broadcasted_iota(jnp.int32, (16, lanes), 0)
    totals = vec[0] + vec[1]
    sums = [totals[i : i + 1, :width] for i in range(5)] + [totals[5:6], totals[6:7, : 3 * width]]

    def bias_block(chunk):
        block = jnp.zeros((16, lanes), F32)
        for row, values in enumerate(sums):
            size = values.shape[1] // 16
            piece = jnp.concatenate([values[:, chunk * size : chunk * size + size], jnp.zeros((1, lanes - size), F32)], axis=1)
            block = jnp.where(row_index == row, jnp.broadcast_to(piece, (16, lanes)), block)
        return block.astype(BF16)

    first_bit = 1 << order[0]
    for chunk in range(16):
        if chunk & first_bit:
            continue
        blocks = bias_block(chunk), bias_block(chunk | first_bit)
        second, third = (chunk >> order[1]) & 1, (chunk >> order[2]) & 1
        place_at = slice(rows + (chunk >> 3) * 16, rows + (chunk >> 3) * 16 + 16)
        mine = dp_bit(order[0]) == 0
        keep[second * 2 + third, place_at, width:] = jnp.where(mine, blocks[0], blocks[1])
        send[second * 2 + third, place_at, width:] = jnp.where(mine, blocks[1], blocks[0])


def down_group_kernel(hidden, hidp, gy, gyp_of, keep, send, left):
    half = dp_bit(3)
    tokens = gy.shape[0] * gy.shape[1]
    units = hidp.shape[2]
    order = ORDERS["down"]
    eighths(flat_rows(hidden, some(half * units, units)).T, left, order, 0)
    eighths(flat_rows(hidp).T, left, order, tokens)
    own_gy = flat_rows(gy)
    other_gy = jnp.concatenate([gyp_of(s) for s in range(gy.shape[0])], axis=0)
    size = units // 2
    for side, out in enumerate((keep, send)):
        at = slice(side * size, side * size + size)
        product = dot(left[at, :tokens], own_gy) + dot(left[at, tokens:], other_gy)
        out[...] = product.astype(BF16).reshape(out.shape)


def plus(left, right):
    return left.astype(F32) + right.astype(F32)


def add_kernel(bit, keep, arrived, keep_out, send_out):
    size = keep_out.shape[0]
    mine = dp_bit(bit) * size
    keep_out[...] = plus(keep[pl.ds(mine, size)], arrived[pl.ds(mine, size)]).astype(BF16)
    send_out[...] = plus(keep[pl.ds(size - mine, size)], arrived[pl.ds(size - mine, size)]).astype(BF16)


def swap_over(shard, bit, sections=(0, 1)):
    count = lax.axis_size("dp")
    pairs = [(s * count + i, s * count + (i ^ (1 << bit))) for s in sections for i in range(count)]
    return lax.ppermute(shard, ("section", "dp"), pairs)


def struct(*shape, dtype=BF16):
    return jax.ShapeDtypeStruct(shape, dtype)


def halved(parts, order, stage, name, after=()):
    keep, send = parts
    arrived = swap_over(send, order[stage])
    shape = (keep.shape[0] // 2,) + keep.shape[1:]
    return call(functools.partial(add_kernel, order[stage + 1]), [keep, arrived], [struct(*shape)] * 2, name, after=after, flops=SUM_FLOPS)


def down_sum_kernel(keep, arrived, out):
    out[...] = plus(keep[0], arrived[0])


def halves_sum_kernel(up_keep, up_arrived, attn_keep, attn_arrived, up_mine, qkv_mine, small_mine, proj, other):
    half = dp_bit(3)
    low = up_mine.shape[0]
    units = up_mine.shape[1]
    width = proj.shape[1]
    mine, theirs = row_slice(half * low, low), row_slice((1 - half) * low, low)
    up_mine[...] = plus(up_keep[0, mine], up_arrived[0, mine])
    other[:, :units] = plus(up_keep[0, theirs], up_arrived[0, theirs]).astype(BF16)
    qkv_mine[...] = plus(attn_keep[0, mine], attn_arrived[0, mine])
    other[:, units : units + qkv_mine.shape[1]] = plus(attn_keep[0, theirs], attn_arrived[0, theirs]).astype(BF16)
    proj[...] = plus(attn_keep[0, 2 * low :, :width], attn_arrived[0, 2 * low :, :width])
    mine, theirs = row_slice(2 * low + half * 16, 16), row_slice(2 * low + (1 - half) * 16, 16)
    small_mine[...] = plus(attn_keep[0, mine, width:], attn_arrived[0, mine, width:])
    small = plus(attn_keep[0, theirs, width:], attn_arrived[0, theirs, width:]).astype(BF16)
    for part in range(small.shape[1] // 128):
        other[part * 16 : part * 16 + 16, other.shape[1] - 128 :] = small[:, part * 128 : part * 128 + 128]


def joined_kernel(up_mine, qkv_mine, small_mine, other, up, qkv, *vectors):
    half = dp_bit(3)
    low = up_mine.shape[0]
    units = up_mine.shape[1]
    lanes = qkv_mine.shape[1] // 3
    up[:, some(half * units, units)] = up_mine[...]
    up[:, some((1 - half) * units, units)] = other[:, :units].astype(F32)
    for block in range(3):
        at = slice(block * lanes, block * lanes + lanes)
        qkv[:, some((2 * block + half) * lanes, lanes)] = qkv_mine[:, at]
        qkv[:, some((2 * block + 1 - half) * lanes, lanes)] = other[:, units + block * lanes : units + (block + 1) * lanes].astype(F32)
    rest = other[:, other.shape[1] - 128 :].astype(F32)
    small = small_mine[...] + jnp.concatenate([rest[part : part + 16] for part in range(0, low, 16)], axis=1)
    for row, out in zip((0, 1, 2, 3, 4, 4, 5, 6), vectors):
        out[...] = small[row : row + 1, : out.shape[1]]


def paired_gradients(boundary, lengths, params, tables, swapped):
    slots = lengths.shape[0]
    width = boundary.shape[2]
    rows = boundary.shape[1] // slots
    units = params[8].shape[2]
    local_rows = boundary.reshape(slots, rows, width)
    low, tall = width // 16, units // 16
    tokens = slots * rows

    partner_lengths = swap_over(lengths, 3)
    cut = rows * slots * 3 // 4
    other_x = swap_over(local_rows, 3, (0,))
    other_gy = swap_over(local_rows, 3, (1,))
    result_0, saved, held = forward_first(lengths, local_rows, params, tables)
    own, gain_a, shift_a, gain_b, shift_b, w_qkv, b_qkv, w_proj, b_proj, w_up, b_up, w_down, b_down, *tabs = held
    arrived_1 = lax.ppermute(result_0, "section", swapped)
    count = len(held)

    def forward_both(lengths_ref, arriving, *refs):
        section = lax.axis_index("section")
        slot = 1 - section
        inputs = lambda: jnp.where(section == 0, refs[0][slot], arriving[...])
        outs = refs[count:]
        forward_body(slot, lengths_ref[slot], inputs, lambda name, part: None, *refs[:count], outs[-1], *outs[:-1])

    *saved, result_1 = call(forward_both, [lengths, arrived_1, *held], [struct(rows, width)], "forward_1", kept=saved, after=[other_x])
    arrived_2 = lax.ppermute(result_1, "section", swapped)

    def forward_last(lengths_ref, arriving, *refs):
        outs = refs[count:]
        slot = slots - 1
        *kept, y, x_a, x_b = outs

        @pl.when(lax.axis_index("section") == 1)
        def _():
            forward_body(slot, lengths_ref[slot], lambda: arriving[...], lambda name, part: None, *refs[:count], y, *kept)
            x_a[:rows] = kept[0][0]
            x_a[rows:] = arriving[: cut - rows]
            x_b[...] = arriving[cut - rows :]

    *saved, result_2, x_a, x_b = call(
        forward_last, [lengths, arrived_2, *held], [struct(rows, width), struct(cut, width), struct(slots * rows - cut, width)],
        "forward_2", kept=saved, after=[partner_lengths],
    )
    x_s, na_s, nb_s, qkv_s, pt_s, mixed_s, hidden_s, slope_s = saved
    partner_xa, partner_xb = swap_over(x_a, 3, (1,)), swap_over(x_b, 3, (1,))

    back_operands = [x_s, gain_a, gain_b, w_qkv, w_proj, w_up, w_down, *tabs, pt_s]
    back_count = len(back_operands)
    shared_operands = [gain_a, shift_a, gain_b, shift_b, w_qkv, b_qkv, w_up, b_up, *tabs]
    shared_count = len(shared_operands)
    shared_shapes = [
        pltpu.VMEM(shape, BF16)
        for shape in (
            (slots, rows, width), (slots, rows, width), (slots, rows, 3 * width // 2), (slots, pt_s.shape[1] // 2) + pt_s.shape[2:],
            (slots, rows, width // 2), (slots, rows, units // 2), (slots, rows, units // 2),
        )
    ]

    def rows_in(ref_a, ref_b):
        def rows_of(s):
            return ref_a[:rows] if s == 0 else jnp.concatenate([ref_a[rows:], ref_b[...]], axis=0)

        return rows_of

    def share(s, lengths_ref, rows_of, refs, outs):
        weights, tabs_refs = refs[:-3], refs[-3:]
        partner_forward(s, dp_bit(3), lengths_ref, rows_of, *weights, tuple(t[...] for t in tabs_refs), *outs)

    def backward_first(lengths_ref, own_ref, other_ref, *refs):
        operands, shared, (qkv_io, slope_io, gy, vec, gx, *outs) = (
            refs[:back_count], refs[back_count : back_count + shared_count], refs[back_count + shared_count :],
        )
        section = lax.axis_index("section")

        @pl.when(section == 1)
        def _():
            backward_body(0, lambda: own_ref[0], *operands, gx, qkv_io, slope_io, gy, vec)

        @pl.when(section == 0)
        def _():
            for s in range(slots):
                share(s, lengths_ref, lambda s: other_ref[s], shared, outs)

    outs = call(
        backward_first, [partner_lengths, own, other_x, *back_operands, *shared_operands],
        [pltpu.VMEM((slots, rows, width), BF16), pltpu.VMEM((slots, 8, units), F32), struct(rows, width)] + shared_shapes,
        "backward_0", kept=[qkv_s, slope_s], after=[other_gy],
    )
    grads, back_0, shared = outs[:4], outs[4], outs[5:]
    arrived_4 = lax.ppermute(back_0, "section", swapped)
    partner_4 = swap_over(arrived_4, 3, (0,))

    def backward_both(own_ref, arriving, *refs):
        section = lax.axis_index("section")
        outs = refs[back_count:]
        source = lambda: jnp.where(section == 0, arriving[...], own_ref[section])
        backward_body(section, source, *refs[:back_count], outs[-1], *outs[:-1])

    *grads, back_1 = call(backward_both, [own, arrived_4, *back_operands], [struct(rows, width)], "backward_1", kept=grads, after=[partner_xa])
    arrived_5 = lax.ppermute(back_1, "section", swapped)
    partner_5 = swap_over(arrived_5, 3, (0,))

    def backward_last(lengths_ref, arriving, ref_a, other_ref, *refs):
        operands, shared_in, (qkv_io, slope_io, gy, vec, *outs) = (
            refs[:back_count], refs[back_count : back_count + shared_count], refs[back_count + shared_count :],
        )
        section = lax.axis_index("section")
        *shared_outs, gx, gyp = outs

        @pl.when(section == 0)
        def _():
            backward_body(slots - 1, lambda: arriving[...], *operands, gx, qkv_io, slope_io, gy, vec)

        @pl.when(section == 1)
        def _():
            share(0, lengths_ref, rows_in(ref_a, None), shared_in, shared_outs)
            gyp[...] = other_ref[0]
            back_shared(0, gyp, operands, shared_outs)

    def back_shared(s, gyp, operands, shared_outs):
        _, _, _, _, wp, _, wd, same, later, earlier, _ = operands
        _, _, qkvp_ref, ptp_ref, _, _, slopep_ref = shared_outs
        tables_in = (same[...], later[...], earlier[...])
        partner_backward(s, dp_bit(3), lambda: gyp[...], wp, wd, tables_in, ptp_ref, qkvp_ref, slopep_ref)

    outs = call(
        backward_last, [partner_lengths, arrived_5, partner_xa, other_gy, *back_operands, *shared_operands],
        [struct(rows, width), pltpu.VMEM((rows, width), BF16)], "backward_2", kept=[*grads, *shared],
    )
    gp_s, gu_s, gy_s, vec_s, *shared, back_2, gyp_0 = outs

    def shared_first(lengths_ref, ref_a, ref_b, partner_ref, *refs):
        operands, shared_in, outs = refs[:back_count], refs[back_count : back_count + shared_count], refs[back_count + shared_count :]
        *shared_outs, gyp = outs
        section = lax.axis_index("section")

        @pl.when(section == 0)
        def _():
            gyp[...] = partner_ref[...]
            back_shared(0, gyp, operands, shared_outs)

        @pl.when(section == 1)
        def _():
            share(1, lengths_ref, rows_in(ref_a, ref_b), shared_in, shared_outs)

    *shared, gyp_0 = call(
        shared_first, [partner_lengths, partner_xa, partner_xb, partner_4, *back_operands, *shared_operands], [], "shared_0",
        kept=[*shared, gyp_0],
    )

    def shared_last(other_ref, partner_ref, *refs):
        operands, outs = refs[:back_count], refs[back_count:]
        *shared_outs, gyp = outs
        gyp[...] = jnp.where(lax.axis_index("section") == 0, partner_ref[...], other_ref[1])
        back_shared(1, gyp, operands, shared_outs)

    *shared, gyp_1 = call(shared_last, [other_gy, partner_5, *back_operands], [struct(rows, width)], "shared_1", kept=shared)
    nap, nbp, gpp, ptp, mixedp, hidp, gup = shared
    gyp_s = [gyp_0, gyp_1]

    def group(rows_of_eighth, columns):
        return [struct(4, rows_of_eighth, columns)] * 2

    def down_group(hidden, hidp_ref, gy, gyp_a, gyp_b, *refs):
        down_group_kernel(hidden, hidp_ref, gy, lambda s: (gyp_a, gyp_b)[s][...], *refs)

    down = call(
        down_group, [hidden_s, hidp, gy_s, *gyp_s], group(tall, width), "down_grads", scratch=[pltpu.VMEM((units // 2, 2 * tokens), BF16)]
    )
    up = call(
        up_group_kernel, [nb_s, nbp, gu_s, gup], group(2 * low, units // 2), "up_grads", scratch=[pltpu.VMEM((width, 2 * tokens), BF16)],
        after=down[:1],
    )

    def attn_group(na, nap_ref, gp, gpp_ref, mixed, mixedp_ref, gy, gyp_a, gyp_b, *refs):
        attn_group_kernel(na, nap_ref, gp, gpp_ref, mixed, mixedp_ref, gy, lambda s: (gyp_a, gyp_b)[s][...], *refs)

    attn = call(
        attn_group, [na_s, nap, gp_s, gpp, mixed_s, mixedp, gy_s, *gyp_s, vec_s], group(3 * low, 3 * width // 2), "attn_grads",
        scratch=[pltpu.VMEM((width, 2 * tokens), BF16), pltpu.VMEM((width // 2, 2 * tokens), BF16)], after=up[:1],
    )

    down = halved(down, ORDERS["down"], 0, "down_sum_1", after=attn[:1])
    up = halved(up, ORDERS["up"], 0, "up_sum_1", after=down[:1])
    attn = halved(attn, ORDERS["attn"], 0, "attn_sum_1", after=up[:1])
    down = halved(down, ORDERS["down"], 1, "down_sum_2", after=attn[:1])
    up = halved(up, ORDERS["up"], 1, "up_sum_2", after=down[:1])
    attn = halved(attn, ORDERS["attn"], 1, "attn_sum_2", after=up[:1])
    up_last, attn_last = swap_over(up[1], ORDERS["up"][2]), swap_over(attn[1], ORDERS["attn"][2])
    up_mine, qkv_mine, small_mine, proj, others = call(
        halves_sum_kernel, [up[0], up_last, attn[0], attn_last],
        [struct(low, units // 2, dtype=F32), struct(low, 3 * width // 2, dtype=F32), struct(16, width // 2, dtype=F32),
         struct(low, width, dtype=F32), struct(low, units // 2 + 3 * width // 2 + 128)], "up_qkv_sum_3", after=down[:1],
    )
    (down_out,) = call(down_sum_kernel, [down[0], swap_over(down[1], ORDERS["down"][2])], [struct(tall, width, dtype=F32)], "down_sum_3")
    vectors = [low] * 6 + [tall, 3 * low]
    up_out, qkv_out, *vectors = call(
        joined_kernel, [up_mine, qkv_mine, small_mine, swap_over(others, 3)],
        [struct(low, units, dtype=F32), struct(low, 3 * width, dtype=F32)] + [struct(1, size, dtype=F32) for size in vectors], "up_qkv_joined",
    )
    joined = jnp.where(
        lax.axis_index("section") == 0, jnp.concatenate([back_1, back_2], axis=0), jnp.concatenate([result_1, result_2], axis=0)
    )
    gain_a, shift_a, gain_b, shift_b, bias_proj, bias_down, bias_up, bias_qkv = (vector[0] for vector in vectors)
    return joined, gain_a, shift_a, qkv_out, bias_qkv, proj, bias_proj, gain_b, shift_b, up_out, bias_up, down_out, bias_down


def plain_gradients(boundary, lengths, params, tables, swapped, bits):
    count = lax.axis_size("dp")
    slots = lengths.shape[0]
    width = boundary.shape[2]
    rows = boundary.shape[1] // slots
    units = params[8].shape[2]
    ticks = slots + 1
    result, saved, held = forward_first(lengths, boundary.reshape(slots, rows, width), params, tables)
    own, gain_a, shift_a, gain_b, shift_b, w_qkv, b_qkv, w_proj, b_proj, w_up, b_up, w_down, b_down, *tabs = held
    held_count = len(held)
    finals = [result]
    for t in range(1, ticks):
        arriving = lax.ppermute(result, "section", swapped)

        def forward_step(lengths_ref, arriving_ref, *refs, tick=t):
            section = lax.axis_index("section")
            slot = jnp.clip(tick - section, 0, slots - 1)
            inputs = lambda: jnp.where(section == 0, refs[0][slot], arriving_ref[...])
            outs = refs[held_count:]
            forward_body(slot, lengths_ref[slot], inputs, lambda name, part: None, *refs[:held_count], outs[-1], *outs[:-1])

        *saved, result = call(forward_step, [lengths, arriving, *held], [struct(rows, width)], "forward", kept=saved)
        finals.append(result)
    x_s, na_s, nb_s, qkv_s, pt_s, mixed_s, hidden_s, slope_s = saved
    operands = [x_s, gain_a, gain_b, w_qkv, w_proj, w_up, w_down, *tabs, pt_s]
    grads = [qkv_s, slope_s]
    input_grads = []
    arriving = own[0]
    for t in range(ticks):

        def backward_step(own_ref, arriving_ref, *refs, tick=t):
            section = lax.axis_index("section")
            slot = tick - 1 + section
            *io, gx_out = refs[len(operands) :]

            @pl.when((slot >= 0) & (slot < slots))
            def _():
                source = lambda: jnp.where(section == 0, arriving_ref[...], own_ref[slot])
                backward_body(slot, source, *refs[: len(operands)], gx_out, *io)

        shapes = [pltpu.VMEM((slots, rows, width), BF16), pltpu.VMEM((slots, 8, units), F32)] if t == 0 else []
        *grads, result = call(backward_step, [own, arriving, *operands], shapes + [struct(rows, width)], "backward", kept=grads)
        input_grads.append(result)
        if t + 1 < ticks:
            arriving = lax.ppermute(result, "section", swapped)
    gp_s, gu_s, gy_s, vec_s = grads
    order = list(range(len(bits)))

    def summed(full):
        keep, send = parted(full, 0, bits[0])
        return halving_sum(keep, send, order, count, bits, F32)

    both = jnp.concatenate([plain_grads(hidden_s, gy_s, count), plain_grads(mixed_s, gy_s, count)], axis=1)
    down, up, qkv = summed(both), summed(plain_grads(nb_s, gu_s, count)), summed(plain_grads(na_s, gp_s, count))
    tall = units // count
    totals = jnp.sum(vec_s, axis=0)
    sums = [totals[i, :width] for i in range(5)] + [totals[5], totals[6, : 3 * width]]
    return finals[1:], input_grads[1:], sums, down[:tall], down[tall:], up, qkv


def per_device(boundary, lengths, *params):
    section = lax.axis_index("section")
    count = lax.axis_size("dp")
    bits = [(lax.axis_index("dp") >> b) & 1 for b in range(count.bit_length() - 1)]
    slots = lengths.shape[0]
    width = boundary.shape[2]
    units = params[8].shape[2]
    tables = [jnp.asarray(table) for table in rotary_lanes(boundary.shape[1] // slots, 2 * HEAD)]
    swapped = [(0, 1), (1, 0)]
    if count == 16 and slots == 2 and width % 768 == 0:
        results = paired_gradients(boundary, lengths, params, tables, swapped)
        return tuple(result[None] for result in results)
    finals, input_grads, sums, down, proj, up, qkv = plain_gradients(
        boundary, lengths, params, tables, swapped, bits
    )
    small = jnp.concatenate([piece.reshape(count, -1) for piece in sums], axis=1)
    small = halving_sum(*parted(small, 0, bits[0]), list(range(len(bits))), count, bits, F32)
    low, tall = width // count, units // count
    gain_a, shift_a, gain_b, shift_b, bias_y, bias_up, bias_qkv = jnp.split(small, np.cumsum([low] * 5 + [tall]), axis=0)
    joined = jnp.where(section == 0, jnp.concatenate(input_grads, axis=0), jnp.concatenate(finals, axis=0))
    results = (joined, gain_a, shift_a, qkv, bias_qkv, proj, bias_y, gain_b, shift_b, up, bias_up, down, bias_y)
    return tuple(result[None] for result in results)


def solution(mesh):
    split = P("section", "dp")
    deep = P("section", "dp", None)
    flat, matrix = P("section", None), P("section", None, None)
    return jax.shard_map(
        per_device,
        mesh=mesh,
        in_specs=(deep, P("dp"), flat, flat, matrix, flat, matrix, flat, flat, flat, matrix, flat, matrix, flat),
        out_specs=(deep, split, split, deep, split, deep, split, split, split, deep, split, deep, split),
        check_vma=False,
    )
```

```python
import functools
import math

import jax
import jax.numpy as jnp
import numpy as np
from jax import lax
from jax.experimental import pallas as pl
from jax.experimental.pallas import tpu as pltpu
from jax.sharding import PartitionSpec as P

HEAD = 64
LANES = 256
CHUNK = 512
EPS = 1e-05
NEG_FILL = -1e30
VMEM_BYTES = 12 * 1024 * 1024
FIRST_VMEM_BYTES = 12 * 1024 * 1024
F32 = jnp.float32
BF16 = jnp.bfloat16


def dot(left, right):
    return jnp.dot(left, right, preferred_element_type=F32)


def dot_nt(left, right):
    return lax.dot_general(left, right, (((1,), (1,)), ((), ())), preferred_element_type=F32)


def normalised(values):
    centred = values - jnp.mean(values, axis=-1, keepdims=True)
    variance = jnp.mean(centred * centred, axis=-1, keepdims=True)
    scale = lax.rsqrt(variance + EPS)
    return centred * scale, scale


def gelu_parts(values):
    integral = 0.5 + 0.5 * lax.erf(values * math.sqrt(0.5))
    bell = jnp.exp(values * values * -0.5)
    return values * integral, integral + values * bell * (1.0 / math.sqrt(2.0 * math.pi))


def rotary_lanes(seq_len, lanes):
    rot_dims = HEAD // 4
    half = rot_dims // 2
    frequency = np.float32(10000.0) ** (-(np.arange(half, dtype=np.float32) * np.float32(2.0) / np.float32(rot_dims)))
    angles = np.arange(seq_len, dtype=np.float32)[:, None] * frequency.astype(np.float32)[None, :]
    cosine, sine = np.cos(angles).astype(np.float32), np.sin(angles).astype(np.float32)
    same = np.ones((seq_len, HEAD), np.float32)
    later = np.zeros((seq_len, HEAD), np.float32)
    earlier = np.zeros((seq_len, HEAD), np.float32)
    same[:, :half] = cosine
    same[:, half:rot_dims] = cosine
    later[:, :half] = -sine
    earlier[:, half:rot_dims] = sine
    return [np.tile(t, (1, lanes // HEAD)) for t in (same, later, earlier)]


def turned(values, same, later, earlier, sign):
    half = HEAD // 8
    width = values.shape[1]
    same, later, earlier = (jnp.concatenate([t] * (width // t.shape[1]), axis=1) for t in (same, later, earlier))
    ahead = pltpu.roll(values, width - half, 1)
    behind = pltpu.roll(values, half, 1)
    if sign > 0:
        return values * same + ahead * later + behind * earlier
    return values * same - ahead * later - behind * earlier


def blocked_bias(rows, length):
    out = []
    for start in range(0, rows, 128):
        keys = start + 128
        key_pos = lax.broadcasted_iota(jnp.int32, (keys, 2 * 128), 0)
        query_pos = start + (lax.broadcasted_iota(jnp.int32, (keys, 2 * 128), 1) & 127)
        out.append(jnp.where((key_pos <= query_pos) & (key_pos.astype(F32) < length), 0.0, NEG_FILL))
    return out


def heads_apart(block, lane):
    zero = jnp.zeros_like(block)
    return jnp.concatenate([jnp.where(lane < HEAD, block, zero), jnp.where(lane < HEAD, zero, block)], axis=0)


def dot_tn(left, right):
    return lax.dot_general(left, right, (((0,), (0,)), ((), ())), preferred_element_type=F32)


def probs_rows(block):
    start = 128 * (block * (block + 1) // 2)
    return slice(start, start + 128 * (block + 1))


def some(offset, size):
    return slice(offset, offset + size) if isinstance(offset, int) else pl.ds(pl.multiple_of(offset, 128), size)


def spans(pair, width):
    return [slice(b * width + pair * 2 * HEAD, b * width + (pair + 1) * 2 * HEAD) for b in range(3)]


def forward_units(slot, length, ready, na, nb, wqkv, bqkv, wu, bu, tables, qkv, pt, mixed, hidden, slope, low_head, low_unit, lanes):
    rows = qkv.shape[1]
    whole_width, width = wqkv.shape[1], qkv.shape[2] // 3
    pairs = width // (2 * HEAD)
    chunk = hidden.shape[2] // pairs
    biases = blocked_bias(rows, length)
    lane = lax.broadcasted_iota(jnp.int32, (128, 2 * HEAD), 1)
    per = lanes // (2 * HEAD)
    for pair in range(pairs):
        if pair % per == 0:
            low = pair * 2 * HEAD
            ready("qkv", pair // per)

            def packed(block):
                at = some(block * whole_width + low_head + low, lanes)
                return dot(na[slot], wqkv[0, :, at]) + bqkv[:, at].astype(F32)

            qkv[slot, :, low : low + lanes] = (turned(packed(0), *tables, 1) * (HEAD**-0.5)).astype(BF16)
            qkv[slot, :, width + low : width + low + lanes] = turned(packed(1), *tables, 1).astype(BF16)
            qkv[slot, :, 2 * width + low : 2 * width + low + lanes] = packed(2).astype(BF16)
        span, span_k, span_v = spans(pair, width)
        all_scores = []
        for block, start in enumerate(range(0, rows, 128)):
            keys = start + 128
            q2 = heads_apart(qkv[slot, start:keys, span], lane)
            all_scores.append(dot_nt(qkv[slot, :keys, span_k], q2) + biases[block])
        ready("up", pair)
        there = some(low_unit + pair * chunk, chunk)
        up = dot(nb[slot], wu[0, :, there]) + bu[:, there].astype(F32)
        for block, start in enumerate(range(0, rows, 128)):
            keys = start + 128
            scores = all_scores[block]
            exponent = jnp.exp(scores - jnp.max(scores, axis=0, keepdims=True))
            probs = (exponent * (1.0 / jnp.sum(exponent, axis=0, keepdims=True))).astype(BF16)
            pt[slot, pair, probs_rows(block)] = probs
            both = dot_tn(probs, qkv[slot, :keys, span_v])
            mixed[slot, start:keys, span] = jnp.where(lane < HEAD, both[:128], both[128:]).astype(BF16)
        here = slice(pair * chunk, pair * chunk + chunk)
        hidden_f32, slope_f32 = gelu_parts(up)
        hidden[slot, :, here] = hidden_f32.astype(BF16)
        slope[slot, :, here] = slope_f32.astype(BF16)


def backward_units(slot, gy, wp, wd, tables, pt, qkv, slope, low_head, low_unit, lanes):
    rows = qkv.shape[1]
    width = qkv.shape[2] // 3
    pairs = width // (2 * HEAD)
    chunk = slope.shape[2] // pairs
    lane = lax.broadcasted_iota(jnp.int32, (128, 2 * HEAD), 1)
    per = lanes // (2 * HEAD)
    for pair in range(pairs):
        if pair % per == 0:
            gm_group = dot_nt(gy(), wp[0, some(low_head + pair * 2 * HEAD, lanes), :]).astype(BF16)
            group_q, group_k = [], []
        span, span_k, span_v = spans(pair, width)
        gm = gm_group[:, (pair % per) * 2 * HEAD : (pair % per + 1) * 2 * HEAD]
        gv_sum, gk_sum, gq_blocks = None, None, []
        for block, start in enumerate(range(0, rows, 128)):
            keys = start + 128
            gm2 = heads_apart(gm[start:keys], lane)
            q2 = heads_apart(qkv[slot, start:keys, span], lane)
            probs = pt[slot, pair, probs_rows(block)]
            weighted = probs.astype(F32) * dot_nt(qkv[slot, :keys, span_v], gm2)
            inner = jnp.sum(weighted, axis=0, keepdims=True)
            gs = (weighted - probs.astype(F32) * inner).astype(BF16)
            gv_part = dot(probs, gm2)
            gk_part = dot(gs, q2)
            gq_part = dot_tn(gs, qkv[slot, :keys, span_k])
            gq_blocks.append(jnp.where(lane < HEAD, gq_part[:128], gq_part[128:]))
            if gv_sum is None:
                gv_sum, gk_sum = gv_part, gk_part
            else:
                gv_sum = jnp.concatenate([gv_sum + gv_part[:start], gv_part[start:]], axis=0)
                gk_sum = jnp.concatenate([gk_sum + gk_part[:start], gk_part[start:]], axis=0)
        qkv[slot, :, span_v] = gv_sum.astype(BF16)
        group_q.append(jnp.concatenate(gq_blocks, axis=0))
        group_k.append(gk_sum)
        if pair % per == per - 1:
            low = pair // per * lanes
            gq = turned(jnp.concatenate(group_q, axis=1) * (HEAD**-0.5), *tables, -1)
            qkv[slot, :, low : low + lanes] = gq.astype(BF16)
            gk = turned(jnp.concatenate(group_k, axis=1), *tables, -1)
            qkv[slot, :, width + low : width + low + lanes] = gk.astype(BF16)
        here = slice(pair * chunk, pair * chunk + chunk)
        grad = dot_nt(gy(), wd[0, some(low_unit + pair * chunk, chunk), :])
        slope[slot, :, here] = (grad * slope[slot, :, here].astype(F32)).astype(BF16)


def forward_body(
    slot, length, inputs, ready, own, gain_a, shift_a, gain_b, shift_b, wqkv, bqkv, wp, bp, wu, bu, wd, bd, same, later, earlier,
    y_out, x_out, na_out, nb_out, qkv_out, pt_out, mixed_out, hidden_out, slope_out,
):
    ready("small", 0)
    x_low = inputs()
    x_out[slot] = x_low
    xhat, _ = normalised(x_low.astype(F32))
    na_out[slot] = (xhat * gain_a[...].astype(F32) + shift_a[...].astype(F32)).astype(BF16)
    nb_out[slot] = (xhat * gain_b[...].astype(F32) + shift_b[...].astype(F32)).astype(BF16)
    tables = (same[...], later[...], earlier[...])
    forward_units(
        slot, length, ready, na_out, nb_out, wqkv, bqkv, wu, bu, tables, qkv_out, pt_out, mixed_out, hidden_out, slope_out, 0, 0, LANES
    )
    ready("rest", 0)
    total = x_out[slot].astype(F32) + (bp[...].astype(F32) + bd[...].astype(F32))
    y_out[...] = (total + dot(mixed_out[slot], wp[0]) + dot(hidden_out[slot], wd[0])).astype(BF16)


def backward_body(
    slot, gy_source, x_in, gain_a, gain_b, wqkv, wp, wu, wd, same, later, earlier, pt_in, gx_out, qkv_io, slope_io, gy_out, vec_out
):
    width = gx_out.shape[1]
    gy_out[slot] = gy_source()
    tables = (same[...], later[...], earlier[...])
    backward_units(slot, lambda: gy_out[slot], wp, wd, tables, pt_in, qkv_io, slope_io, 0, 0, LANES)
    grad_b = dot_nt(slope_io[slot], wu[0])
    grad_a = dot_nt(qkv_io[slot], wqkv[0])
    xhat, scale = normalised(x_in[slot].astype(F32))
    norm_terms = (grad_a * xhat, grad_a, grad_b * xhat, grad_b, gy_out[slot].astype(F32))
    for row, terms in enumerate(norm_terms):
        vec_out[slot, row : row + 1, :width] = jnp.sum(terms, axis=0, keepdims=True)
    vec_out[slot, 5:6, :] = jnp.sum(slope_io[slot].astype(F32), axis=0, keepdims=True)
    vec_out[slot, 6:7, : 3 * width] = jnp.sum(qkv_io[slot].astype(F32), axis=0, keepdims=True)
    both = grad_a * gain_a[...].astype(F32) + grad_b * gain_b[...].astype(F32)
    inner = jnp.mean(both * xhat, axis=-1, keepdims=True)
    gx = gy_out[slot].astype(F32) + scale * (both - jnp.mean(both, axis=-1, keepdims=True) - xhat * inner)
    gx_out[...] = gx.astype(BF16)


def forward_first_kernel(tick, lengths, *refs):
    count = 17
    sources, held, outs, sems = refs[:count], refs[count : 2 * count], refs[2 * count : -1], refs[-1]
    copies = []
    waits = {}

    def fetch(name, part, index, at):
        source, target = (sources[index], held[index]) if at is None else (sources[index].at[at], held[index].at[at])
        copy = pltpu.make_async_copy(source, target, sems.at[len(copies)])
        copies.append(copy)
        waits.setdefault((name, part), []).append(copy)

    (own, gain_a, shift_a, gain_b, shift_b, wqkv, bqkv, wp, bp, wu, bu, wd, bd, same, later, earlier, _) = range(count)
    width = sources[wp].shape[1]
    units = sources[wu].shape[2]
    pairs = width // (2 * HEAD)
    groups = width // LANES
    for index in (own, gain_a, shift_a, gain_b, shift_b, bqkv, bp, bu, bd, same, later, earlier):
        fetch("small", 0, index, None)
    for pair in range(pairs):
        if pair * groups % pairs == 0:
            group = pair * groups // pairs
            for block in range(3):
                fetch("qkv", group, wqkv, (slice(None), slice(None), pl.ds(block * width + group * LANES, LANES)))
        fetch("up", pair, wu, (slice(None), slice(None), pl.ds(pair * (units // pairs), units // pairs)))
    fetch("rest", 0, wp, None)
    fetch("rest", 0, wd, None)
    for copy in copies:
        copy.start()

    def ready(name, part):
        for copy in waits[(name, part)]:
            copy.wait()

    section = lax.axis_index("section")
    slots = held[own].shape[0]
    slot = jnp.clip(tick - section, 0, slots - 1)
    forward_body(slot, lengths[slot].astype(F32), lambda: held[own][slot], ready, *held[:-1], *outs)


def backward_body(
    slot, gy_source, x_in, gain_a, gain_b, wqkv, wp, wu, wd, same, later, earlier,
    pt_in, gx_out, qkv_io, slope_io, gy_out, vec_out,
):
    rows, width = gx_out.shape
    units = wu.shape[2]
    pairs = width // (2 * HEAD)
    chunk = units // pairs
    gy_out[slot] = gy_source()
    lane = lax.broadcasted_iota(jnp.int32, (128, 2 * HEAD), 1)
    tables = (same[...], later[...], earlier[...])
    per = LANES // (2 * HEAD)
    for pair in range(pairs):
        if pair % per == 0:
            gm_group = dot_nt(gy_out[slot], wp[0, pair * 2 * HEAD : pair * 2 * HEAD + LANES, :]).astype(BF16)
            group_q, group_k = [], []
        span, span_k, span_v = (slice(b * width + pair * 2 * HEAD, b * width + (pair + 1) * 2 * HEAD) for b in range(3))
        gm = gm_group[:, (pair % per) * 2 * HEAD : (pair % per + 1) * 2 * HEAD]
        gv_sum, gk_sum, gq_blocks = None, None, []
        for block, start in enumerate(range(0, rows, 128)):
            keys = start + 128
            gm2 = heads_apart(gm[start:keys], lane)
            q2 = heads_apart(qkv_io[slot, start:keys, span], lane)
            pt = pt_in[slot, pair, probs_rows(block)]
            weighted = pt.astype(F32) * dot_nt(qkv_io[slot, :keys, span_v], gm2)
            inner = jnp.sum(weighted, axis=0, keepdims=True)
            gs = (weighted - pt.astype(F32) * inner).astype(BF16)
            gv_part = dot(pt, gm2)
            gk_part = dot(gs, q2)
            gq_part = dot_tn(gs, qkv_io[slot, :keys, span_k])
            gq_blocks.append(jnp.where(lane < HEAD, gq_part[:128], gq_part[128:]))
            if gv_sum is None:
                gv_sum, gk_sum = gv_part, gk_part
            else:
                gv_sum = jnp.concatenate([gv_sum + gv_part[:start], gv_part[start:]], axis=0)
                gk_sum = jnp.concatenate([gk_sum + gk_part[:start], gk_part[start:]], axis=0)
        qkv_io[slot, :, span_v] = gv_sum.astype(BF16)
        group_q.append(jnp.concatenate(gq_blocks, axis=0))
        group_k.append(gk_sum)
        if pair % per == per - 1:
            low = pair // per * LANES
            gq = turned(jnp.concatenate(group_q, axis=1) * (HEAD**-0.5), *tables, -1)
            qkv_io[slot, :, low : low + LANES] = gq.astype(BF16)
            gk = turned(jnp.concatenate(group_k, axis=1), *tables, -1)
            qkv_io[slot, :, width + low : width + low + LANES] = gk.astype(BF16)
        at = slice(pair * chunk, pair * chunk + chunk)
        slope_io[slot, :, at] = (dot_nt(gy_out[slot], wd[0, at, :]) * slope_io[slot, :, at].astype(F32)).astype(BF16)
    grad_b = dot_nt(slope_io[slot], wu[0])
    grad_a = dot_nt(qkv_io[slot], wqkv[0])
    xhat, scale = normalised(x_in[slot].astype(F32))
    norm_terms = (grad_a * xhat, grad_a, grad_b * xhat, grad_b, gy_out[slot].astype(F32))
    for row, terms in enumerate(norm_terms):
        vec_out[slot, row : row + 1, :width] = jnp.sum(terms, axis=0, keepdims=True)
    vec_out[slot, 5:6, :] = jnp.sum(slope_io[slot].astype(F32), axis=0, keepdims=True)
    vec_out[slot, 6:7, : 3 * width] = jnp.sum(qkv_io[slot].astype(F32), axis=0, keepdims=True)
    both = grad_a * gain_a[...].astype(F32) + grad_b * gain_b[...].astype(F32)
    inner = jnp.mean(both * xhat, axis=-1, keepdims=True)
    gx = gy_out[slot].astype(F32) + scale * (both - jnp.mean(both, axis=-1, keepdims=True) - xhat * inner)
    gx_out[...] = gx.astype(BF16)


VM = pl.BlockSpec(memory_space=pltpu.VMEM)
HBM = pl.BlockSpec(memory_space=pl.ANY)


def call(kernel, operands, out_shape, name, kept=(), scratch=(), flops=1 << 20, after=()):
    count = len(operands)
    after = list(after)

    def body(*refs):
        kernel(*refs[:count], *refs[count + len(kept) + len(after) :])

    return pl.pallas_call(
        body,
        in_specs=[pl.BlockSpec(memory_space=pltpu.SMEM) if o.dtype == jnp.int32 else VM for o in operands] + [VM] * len(kept) + [HBM] * len(after),
        out_specs=[VM] * (len(kept) + len(out_shape)),
        out_shape=[pltpu.VMEM(array.shape, array.dtype) for array in kept] + list(out_shape),
        input_output_aliases={count + i: i for i in range(len(kept))},
        scratch_shapes=list(scratch),
        compiler_params=pltpu.CompilerParams(vmem_limit_bytes=VMEM_BYTES),
        cost_estimate=pl.CostEstimate(flops=flops, bytes_accessed=1 << 16, transcendentals=0),
        name=name,
    )(*operands, *[pltpu.with_memory_space_constraint(array, pltpu.VMEM) for array in kept], *after)


def shape_of(array):
    return jax.ShapeDtypeStruct(array.shape, array.dtype)


def forward_shapes(local_rows, params):
    slots, rows, width = local_rows.shape
    units = params[8].shape[2]
    blocks = rows // 128
    probs = (slots, width // (2 * HEAD), 128 * (blocks * (blocks + 1) // 2), 2 * 128)
    columns = [width, width, width, 3 * width, None, width, units, units]
    return [jax.ShapeDtypeStruct((rows, width), BF16)] + [
        pltpu.VMEM(probs if n is None else (slots, rows, n), BF16) for n in columns
    ]


def forward_first(lengths, local_rows, params, tables):
    (gain_a, shift_a, w_qkv, b_qkv, w_proj, b_proj, gain_b, shift_b, w_up, b_up, w_down, b_down) = params
    held = [local_rows, gain_a, shift_a, gain_b, shift_b, w_qkv, b_qkv, w_proj, b_proj, w_up, b_up, w_down, b_down] + list(tables)
    shapes = [shape_of(array) for array in held] + forward_shapes(local_rows, params)

    def kernel(lengths_ref, *refs):
        count = len(held)
        forward_first_kernel(0, lengths_ref, *refs[:count], None, *refs[count : 2 * count], None, *refs[2 * count :])

    outs = pl.pallas_call(
        kernel,
        in_specs=[pl.BlockSpec(memory_space=pltpu.SMEM)] + [pl.BlockSpec(memory_space=pltpu.HBM)] * len(held),
        out_specs=[VM] * len(shapes),
        out_shape=shapes,
        scratch_shapes=[pltpu.SemaphoreType.DMA((40,))],
        compiler_params=pltpu.CompilerParams(vmem_limit_bytes=FIRST_VMEM_BYTES),
        cost_estimate=pl.CostEstimate(flops=1 << 20, bytes_accessed=1 << 16, transcendentals=0),
        name="layer_forward_first",
    )(lengths, *[pltpu.with_memory_space_constraint(array, pltpu.HBM) for array in held])
    count = len(held)
    return outs[count], outs[count + 1 :], outs[:count]


def swap(shard, bit, count):
    return lax.ppermute(shard, "dp", [(i, i ^ (1 << bit)) for i in range(count)])


def parted(values, position, mine):
    count = values.shape[0]
    shaped = values.reshape((count >> (position + 1), 2, 1 << position) + values.shape[1:])
    out = []
    for side in (mine, 1 - mine):
        piece = lax.dynamic_index_in_dim(shaped, side, axis=1, keepdims=False)
        out.append(piece.reshape((count // 2,) + values.shape[1:]))
    return out


def halving_sum(keep, send, order, count, bits, final):
    left = sorted(order)
    for number, bit in enumerate(order):
        left.remove(bit)
        arrived = swap(send, bit, count)
        if number + 1 == len(order):
            return (keep.astype(F32) + arrived.astype(F32)).astype(final)[0]
        position = left.index(order[number + 1])
        keep_a, send_a = parted(keep, position, bits[order[number + 1]])
        keep_b, send_b = parted(arrived, position, bits[order[number + 1]])
        send = (send_a.astype(F32) + send_b.astype(F32)).astype(send_a.dtype)
        keep = (keep_a.astype(F32) + keep_b.astype(F32)).astype(send_a.dtype)


def plain_grads(left, right, count):
    rows = left.shape[0] * left.shape[1]
    product = lax.dot_general(
        left.reshape(rows, -1), right.reshape(rows, -1), (((0,), (0,)), ((), ())), preferred_element_type=F32
    ).astype(BF16)
    return product.reshape(count, product.shape[0] // count, product.shape[1])


def partner_forward(s, half, length, rows_of, gain_a, shift_a, gain_b, shift_b, wqkv, bqkv, wu, bu, tables, nap, nbp, qkvp, ptp, mixedp, hidp, slopep):
    lanes = mixedp.shape[2]
    xhat, _ = normalised(rows_of(s).astype(F32))
    nap[s] = (xhat * gain_a[...].astype(F32) + shift_a[...].astype(F32)).astype(BF16)
    nbp[s] = (xhat * gain_b[...].astype(F32) + shift_b[...].astype(F32)).astype(BF16)
    forward_units(
        s, length, lambda name, part: None, nap, nbp, wqkv, bqkv, wu, bu, tables, qkvp, ptp, mixedp, hidp, slopep,
        half * lanes, half * hidp.shape[2], lanes,
    )


def partner_backward(s, half, gy, wp, wd, tables, ptp, qkvp, slopep):
    lanes = qkvp.shape[2] // 3
    backward_units(s, gy, wp, wd, tables, ptp, qkvp, slopep, half * lanes, half * slopep.shape[2], lanes)


SUM_FLOPS = 6 << 30
ORDERS = {"down": (0, 1, 2), "up": (1, 2, 0), "attn": (2, 0, 1)}


def dp_bit(bit):
    return (lax.axis_index("dp") >> bit) & 1


def eighth_row(chunk, order, rows):
    first, second, third = ((chunk >> bit) & 1 for bit in order)
    return ((first ^ dp_bit(order[0])) * 4 + second * 2 + third) * rows


def row_slice(start, rows):
    return pl.ds(pl.multiple_of(start, 16), rows)


def flat_rows(ref, at=slice(None)):
    values = ref[:, :, at]
    return values.reshape(values.shape[0] * values.shape[1], values.shape[2])


def ones_dot(values):
    return dot(jnp.ones((16, values.shape[0]), BF16), values)[:8]


def sixteenths(ref, left, order, tokens_from):
    turned_ref = flat_rows(ref).T
    low = turned_ref.shape[0] // 16
    for chunk in range(16):
        start = eighth_row(chunk & 7, order, 2 * low) + (chunk >> 3) * low
        left[row_slice(start, low), tokens_from : tokens_from + turned_ref.shape[1]] = turned_ref[chunk * low : chunk * low + low]


def eighths(turned_rows, left, order, tokens_from):
    low = turned_rows.shape[0] // 8
    for chunk in range(8):
        left[row_slice(eighth_row(chunk, order, low), low), tokens_from : tokens_from + turned_rows.shape[1]] = turned_rows[
            chunk * low : chunk * low + low
        ]


def up_group_kernel(nb, nbp, gu, gup, keep, send, left):
    half = dp_bit(3)
    tokens = nb.shape[0] * nb.shape[1]
    units = gup.shape[2]
    sixteenths(nb, left, ORDERS["up"], 0)
    sixteenths(nbp, left, ORDERS["up"], tokens)
    rows = left.shape[0] // 8
    for low in range(0, units, 512):
        at = slice(low, low + 512)
        product = dot(left[:, :tokens], flat_rows(gu, some(half * units + low, 512))) + dot(left[:, tokens:], flat_rows(gup, at))
        product = product.astype(BF16).reshape(8, rows, 512)
        keep[:, :, at] = product[:4]
        send[:, :, at] = product[4:]


def attn_group_kernel(na, nap, gp, gpp, mixed, mixedp, gy, gyp_of, vec, keep, send, left, left_mixed):
    half = dp_bit(3)
    tokens = na.shape[0] * na.shape[1]
    width = na.shape[2]
    lanes = mixedp.shape[2]
    order = ORDERS["attn"]
    sixteenths(na, left, order, 0)
    sixteenths(nap, left, order, tokens)
    rows = left.shape[0] // 8
    for block in range(3):
        at = slice(block * lanes, block * lanes + lanes)
        own = flat_rows(gp, some(block * width + half * lanes, lanes))
        product = dot(left[:, :tokens], own) + dot(left[:, tokens:], flat_rows(gpp, at))
        product = product.astype(BF16).reshape(8, rows, lanes)
        keep[:, :rows, at] = product[:4]
        send[:, :rows, at] = product[4:]
    eighths(flat_rows(mixed, some(half * lanes, lanes)).T, left_mixed, order, 0)
    eighths(flat_rows(mixedp).T, left_mixed, order, tokens)
    own_gy = flat_rows(gy)
    other_gy = jnp.concatenate([gyp_of(s) for s in range(gy.shape[0])], axis=0)
    product = dot(left_mixed[:, :tokens], own_gy) + dot(left_mixed[:, tokens:], other_gy)
    low = left_mixed.shape[0] // 8
    product = product.astype(BF16).reshape(8, low, width)
    keep[:, rows:, :width] = product[:4]
    send[:, rows:, :width] = product[4:]
    row_index = lax.broadcasted_iota(jnp.int32, (16, lanes), 0)
    totals = vec[0] + vec[1]
    sums = [totals[i : i + 1, :width] for i in range(5)] + [totals[5:6], totals[6:7, : 3 * width]]

    def bias_block(chunk):
        block = jnp.zeros((16, lanes), F32)
        for row, values in enumerate(sums):
            size = values.shape[1] // 16
            piece = jnp.concatenate([values[:, chunk * size : chunk * size + size], jnp.zeros((1, lanes - size), F32)], axis=1)
            block = jnp.where(row_index == row, jnp.broadcast_to(piece, (16, lanes)), block)
        return block.astype(BF16)

    first_bit = 1 << order[0]
    for chunk in range(16):
        if chunk & first_bit:
            continue
        blocks = bias_block(chunk), bias_block(chunk | first_bit)
        second, third = (chunk >> order[1]) & 1, (chunk >> order[2]) & 1
        place_at = slice(rows + (chunk >> 3) * 16, rows + (chunk >> 3) * 16 + 16)
        mine = dp_bit(order[0]) == 0
        keep[second * 2 + third, place_at, width:] = jnp.where(mine, blocks[0], blocks[1])
        send[second * 2 + third, place_at, width:] = jnp.where(mine, blocks[1], blocks[0])


def down_group_kernel(hidden, hidp, gy, gyp_of, keep, send, left):
    half = dp_bit(3)
    tokens = gy.shape[0] * gy.shape[1]
    units = hidp.shape[2]
    order = ORDERS["down"]
    eighths(flat_rows(hidden, some(half * units, units)).T, left, order, 0)
    eighths(flat_rows(hidp).T, left, order, tokens)
    own_gy = flat_rows(gy)
    other_gy = jnp.concatenate([gyp_of(s) for s in range(gy.shape[0])], axis=0)
    size = units // 2
    for side, out in enumerate((keep, send)):
        at = slice(side * size, side * size + size)
        product = dot(left[at, :tokens], own_gy) + dot(left[at, tokens:], other_gy)
        out[...] = product.astype(BF16).reshape(out.shape)


def plus(left, right):
    return left.astype(F32) + right.astype(F32)


def add_kernel(bit, keep, arrived, keep_out, send_out):
    size = keep_out.shape[0]
    mine = dp_bit(bit) * size
    keep_out[...] = plus(keep[pl.ds(mine, size)], arrived[pl.ds(mine, size)]).astype(BF16)
    send_out[...] = plus(keep[pl.ds(size - mine, size)], arrived[pl.ds(size - mine, size)]).astype(BF16)


def swap_over(shard, bit, sections=(0, 1)):
    count = lax.axis_size("dp")
    pairs = [(s * count + i, s * count + (i ^ (1 << bit))) for s in sections for i in range(count)]
    return lax.ppermute(shard, ("section", "dp"), pairs)


def cross_swap(shard, section, bit):
    count = lax.axis_size("dp")
    return lax.ppermute(shard, ("section", "dp"), [(section * count + i, (1 - section) * count + (i ^ (1 << bit))) for i in range(count)])


def struct(*shape, dtype=BF16):
    return jax.ShapeDtypeStruct(shape, dtype)


def halved(parts, order, stage, name, after=()):
    keep, send = parts
    arrived = swap_over(send, order[stage])
    shape = (keep.shape[0] // 2,) + keep.shape[1:]
    return call(functools.partial(add_kernel, order[stage + 1]), [keep, arrived], [struct(*shape)] * 2, name, after=after, flops=SUM_FLOPS)


def down_sum_kernel(keep, arrived, out):
    out[...] = plus(keep[0], arrived[0])


def halves_sum_kernel(up_keep, up_arrived, attn_keep, attn_arrived, up_mine, qkv_mine, small_mine, proj, other):
    half = dp_bit(3)
    low = up_mine.shape[0]
    units = up_mine.shape[1]
    width = proj.shape[1]
    mine, theirs = row_slice(half * low, low), row_slice((1 - half) * low, low)
    up_mine[...] = plus(up_keep[0, mine], up_arrived[0, mine])
    other[:, :units] = plus(up_keep[0, theirs], up_arrived[0, theirs]).astype(BF16)
    qkv_mine[...] = plus(attn_keep[0, mine], attn_arrived[0, mine])
    other[:, units : units + qkv_mine.shape[1]] = plus(attn_keep[0, theirs], attn_arrived[0, theirs]).astype(BF16)
    proj[...] = plus(attn_keep[0, 2 * low :, :width], attn_arrived[0, 2 * low :, :width])
    mine, theirs = row_slice(2 * low + half * 16, 16), row_slice(2 * low + (1 - half) * 16, 16)
    small_mine[...] = plus(attn_keep[0, mine, width:], attn_arrived[0, mine, width:])
    small = plus(attn_keep[0, theirs, width:], attn_arrived[0, theirs, width:]).astype(BF16)
    for part in range(small.shape[1] // 128):
        other[part * 16 : part * 16 + 16, other.shape[1] - 128 :] = small[:, part * 128 : part * 128 + 128]


def joined_kernel(up_mine, qkv_mine, small_mine, other, up, qkv, *vectors):
    half = dp_bit(3)
    low = up_mine.shape[0]
    units = up_mine.shape[1]
    lanes = qkv_mine.shape[1] // 3
    up[:, some(half * units, units)] = up_mine[...]
    up[:, some((1 - half) * units, units)] = other[:, :units].astype(F32)
    for block in range(3):
        at = slice(block * lanes, block * lanes + lanes)
        qkv[:, some((2 * block + half) * lanes, lanes)] = qkv_mine[:, at]
        qkv[:, some((2 * block + 1 - half) * lanes, lanes)] = other[:, units + block * lanes : units + (block + 1) * lanes].astype(F32)
    rest = other[:, other.shape[1] - 128 :].astype(F32)
    small = small_mine[...] + jnp.concatenate([rest[part : part + 16] for part in range(0, low, 16)], axis=1)
    for row, out in zip((0, 1, 2, 3, 4, 4, 5, 6), vectors):
        out[...] = small[row : row + 1, : out.shape[1]]


def paired_gradients(boundary, lengths, params, tables, swapped):
    slots = lengths.shape[0]
    width = boundary.shape[2]
    rows = boundary.shape[1] // slots
    units = params[8].shape[2]
    local_rows = boundary.reshape(slots, rows, width)
    low, tall = width // 16, units // 16
    tokens = slots * rows

    cut = rows * slots * 3 // 4
    length_rows = jnp.broadcast_to(jnp.repeat(lengths.astype(BF16), 8)[:, None], (8 * slots, width))
    other_a = swap_over(jnp.concatenate([boundary[0, :cut], length_rows], axis=0), 3, (0,))
    other_b = swap_over(boundary[0, cut:], 3, (0,))
    other_gy = swap_over(local_rows, 3, (1,))
    result_0, saved, held = forward_first(lengths, local_rows, params, tables)
    own, gain_a, shift_a, gain_b, shift_b, w_qkv, b_qkv, w_proj, b_proj, w_up, b_up, w_down, b_down, *tabs = held
    arrived_1 = lax.ppermute(result_0, "section", swapped)
    count = len(held)

    def forward_both(lengths_ref, arriving, first_y, *refs):
        section = lax.axis_index("section")
        slot = 1 - section
        inputs = lambda: jnp.where(section == 0, refs[0][slot], arriving[...])
        *kept, y, x_a, x_b = refs[count:]
        forward_body(slot, lengths_ref[slot].astype(F32), inputs, lambda name, part: None, *refs[:count], y, *kept)
        for s, (piece, rows_ref) in enumerate(((x_a, first_y), (x_b, y))):
            piece[:rows] = rows_ref[...]
            piece[rows:] = jnp.full((16, width), lengths_ref[s].astype(F32), F32).astype(BF16)

    *saved, result_1, x_a, x_b = call(
        forward_both, [lengths, arrived_1, result_0, *held], [struct(rows, width)] + [struct(rows + 16, width)] * 2, "forward_1",
        kept=saved, after=[other_a],
    )
    partner_xa, partner_xb = cross_swap(x_a, 0, 3), cross_swap(x_b, 0, 3)
    arrived_2 = lax.ppermute(result_1, "section", swapped)

    def forward_last(lengths_ref, arriving, *refs):
        outs = refs[count:]
        slot = slots - 1
        *kept, y = outs

        @pl.when(lax.axis_index("section") == 1)
        def _():
            forward_body(slot, lengths_ref[slot].astype(F32), lambda: arriving[...], lambda name, part: None, *refs[:count], y, *kept)

    *saved, result_2 = call(
        forward_last, [lengths, arrived_2, *held], [struct(rows, width)], "forward_2", kept=saved, after=[other_b],
    )
    x_s, na_s, nb_s, qkv_s, pt_s, mixed_s, hidden_s, slope_s = saved

    back_operands = [x_s, gain_a, gain_b, w_qkv, w_proj, w_up, w_down, *tabs, pt_s]
    back_count = len(back_operands)
    shared_operands = [gain_a, shift_a, gain_b, shift_b, w_qkv, b_qkv, w_up, b_up, *tabs]
    shared_count = len(shared_operands)
    shared_shapes = [
        pltpu.VMEM(shape, BF16)
        for shape in (
            (slots, rows, width), (slots, rows, width), (slots, rows, 3 * width // 2), (slots, pt_s.shape[1] // 2) + pt_s.shape[2:],
            (slots, rows, width // 2), (slots, rows, units // 2), (slots, rows, units // 2),
        )
    ]

    def share(s, length, x_rows, refs, outs):
        weights, tabs_refs = refs[:-3], refs[-3:]
        partner_forward(s, dp_bit(3), length.astype(F32), lambda s: x_rows, *weights, tuple(t[...] for t in tabs_refs), *outs)

    def backward_first(own_ref, ref_a, ref_b, *refs):
        operands, shared, (qkv_io, slope_io, gy, vec, gx, gx_long, *outs) = (
            refs[:back_count], refs[back_count : back_count + shared_count], refs[back_count + shared_count :],
        )
        section = lax.axis_index("section")

        @pl.when(section == 1)
        def _():
            backward_body(0, lambda: own_ref[0], *operands, gx, qkv_io, slope_io, gy, vec)
            gx_long[:rows] = gx[...]
            gx_long[rows:] = jnp.zeros((16, width), BF16)

        @pl.when(section == 0)
        def _():
            x_rows = (ref_a[:rows], jnp.concatenate([ref_a[rows:cut], ref_b[...]], axis=0))
            for s in range(slots):
                share(s, ref_a[cut + 8 * s : cut + 8 * s + 1, : 2 * 128], x_rows[s], shared, outs)

    outs = call(
        backward_first, [own, other_a, other_b, *back_operands, *shared_operands],
        [pltpu.VMEM((slots, rows, width), BF16), pltpu.VMEM((slots, 8, units), F32), struct(rows, width), struct(rows + 16, width)] + shared_shapes,
        "backward_0", kept=[qkv_s, slope_s],
    )
    grads, back_0, back_long, shared = outs[:4], outs[4], outs[5], outs[6:]
    arrived_4 = lax.ppermute(back_0, "section", swapped)
    partner_4 = cross_swap(back_long, 1, 3)

    def backward_both(own_ref, arriving, *refs):
        section = lax.axis_index("section")
        outs = refs[back_count:]
        source = lambda: jnp.where(section == 0, arriving[...], own_ref[section])
        backward_body(section, source, *refs[:back_count], outs[-1], *outs[:-1])

    *grads, back_1 = call(backward_both, [own, arrived_4, *back_operands], [struct(rows, width)], "backward_1", kept=grads, after=[partner_xa, other_gy])
    arrived_5 = lax.ppermute(back_1, "section", swapped)
    partner_5 = cross_swap(back_1, 1, 3)

    def backward_last(arriving, ref_a, other_ref, *refs):
        operands, shared_in, (qkv_io, slope_io, gy, vec, *outs) = (
            refs[:back_count], refs[back_count : back_count + shared_count], refs[back_count + shared_count :],
        )
        section = lax.axis_index("section")
        *shared_outs, gx, gyp = outs

        @pl.when(section == 0)
        def _():
            backward_body(slots - 1, lambda: arriving[...], *operands, gx, qkv_io, slope_io, gy, vec)

        @pl.when(section == 1)
        def _():
            share(0, ref_a[rows : rows + 1, : 2 * 128], ref_a[:rows], shared_in, shared_outs)
            gyp[...] = other_ref[0]
            back_shared(0, gyp, operands, shared_outs)

    def back_shared(s, gyp, operands, shared_outs):
        _, _, _, _, wp, _, wd, same, later, earlier, _ = operands
        _, _, qkvp_ref, ptp_ref, _, _, slopep_ref = shared_outs
        tables_in = (same[...], later[...], earlier[...])
        partner_backward(s, dp_bit(3), lambda: gyp[...], wp, wd, tables_in, ptp_ref, qkvp_ref, slopep_ref)

    outs = call(
        backward_last, [arrived_5, partner_xa, other_gy, *back_operands, *shared_operands],
        [struct(rows, width), pltpu.VMEM((rows, width), BF16)], "backward_2", kept=[*grads, *shared], after=[partner_4, partner_xb],
    )
    gp_s, gu_s, gy_s, vec_s, *shared, back_2, gyp_0 = outs

    def shared_first(ref_b, partner_ref, *refs):
        operands, shared_in, outs = refs[:back_count], refs[back_count : back_count + shared_count], refs[back_count + shared_count :]
        *shared_outs, gyp = outs
        section = lax.axis_index("section")

        @pl.when(section == 0)
        def _():
            gyp[...] = partner_ref[:rows]
            back_shared(0, gyp, operands, shared_outs)

        @pl.when(section == 1)
        def _():
            share(1, ref_b[rows : rows + 1, : 2 * 128], ref_b[:rows], shared_in, shared_outs)

    *shared, gyp_0 = call(
        shared_first, [partner_xb, partner_4, *back_operands, *shared_operands], [], "shared_0",
        kept=[*shared, gyp_0],
    )

    def shared_last(other_ref, partner_ref, *refs):
        operands, outs = refs[:back_count], refs[back_count:]
        *shared_outs, gyp = outs
        gyp[...] = jnp.where(lax.axis_index("section") == 0, partner_ref[...], other_ref[1])
        back_shared(1, gyp, operands, shared_outs)

    *shared, gyp_1 = call(shared_last, [other_gy, partner_5, *back_operands], [struct(rows, width)], "shared_1", kept=shared)
    nap, nbp, gpp, ptp, mixedp, hidp, gup = shared
    gyp_s = [gyp_0, gyp_1]

    def group(rows_of_eighth, columns):
        return [struct(4, rows_of_eighth, columns)] * 2

    def down_group(hidden, hidp_ref, gy, gyp_a, gyp_b, *refs):
        down_group_kernel(hidden, hidp_ref, gy, lambda s: (gyp_a, gyp_b)[s][...], *refs)

    down = call(
        down_group, [hidden_s, hidp, gy_s, *gyp_s], group(tall, width), "down_grads", scratch=[pltpu.VMEM((units // 2, 2 * tokens), BF16)]
    )
    up = call(
        up_group_kernel, [nb_s, nbp, gu_s, gup], group(2 * low, units // 2), "up_grads", scratch=[pltpu.VMEM((width, 2 * tokens), BF16)],
        after=down[:1],
    )

    def attn_group(na, nap_ref, gp, gpp_ref, mixed, mixedp_ref, gy, gyp_a, gyp_b, *refs):
        attn_group_kernel(na, nap_ref, gp, gpp_ref, mixed, mixedp_ref, gy, lambda s: (gyp_a, gyp_b)[s][...], *refs)

    attn = call(
        attn_group, [na_s, nap, gp_s, gpp, mixed_s, mixedp, gy_s, *gyp_s, vec_s], group(3 * low, 3 * width // 2), "attn_grads",
        scratch=[pltpu.VMEM((width, 2 * tokens), BF16), pltpu.VMEM((width // 2, 2 * tokens), BF16)], after=up[:1],
    )

    down = halved(down, ORDERS["down"], 0, "down_sum_1", after=attn[:1])
    up = halved(up, ORDERS["up"], 0, "up_sum_1", after=down[:1])
    attn = halved(attn, ORDERS["attn"], 0, "attn_sum_1", after=up[:1])
    down = halved(down, ORDERS["down"], 1, "down_sum_2", after=attn[:1])
    up = halved(up, ORDERS["up"], 1, "up_sum_2", after=down[:1])
    attn = halved(attn, ORDERS["attn"], 1, "attn_sum_2", after=up[:1])
    up_last, attn_last = swap_over(up[1], ORDERS["up"][2]), swap_over(attn[1], ORDERS["attn"][2])
    up_mine, qkv_mine, small_mine, proj, others = call(
        halves_sum_kernel, [up[0], up_last, attn[0], attn_last],
        [struct(low, units // 2, dtype=F32), struct(low, 3 * width // 2, dtype=F32), struct(16, width // 2, dtype=F32),
         struct(low, width, dtype=F32), struct(low, units // 2 + 3 * width // 2 + 128)], "up_qkv_sum_3", after=down[:1],
    )
    (down_out,) = call(down_sum_kernel, [down[0], swap_over(down[1], ORDERS["down"][2])], [struct(tall, width, dtype=F32)], "down_sum_3")
    vectors = [low] * 6 + [tall, 3 * low]
    up_out, qkv_out, *vectors = call(
        joined_kernel, [up_mine, qkv_mine, small_mine, swap_over(others, 3)],
        [struct(low, units, dtype=F32), struct(low, 3 * width, dtype=F32)] + [struct(1, size, dtype=F32) for size in vectors], "up_qkv_joined",
    )
    joined = jnp.where(
        lax.axis_index("section") == 0, jnp.concatenate([back_1, back_2], axis=0), jnp.concatenate([result_1, result_2], axis=0)
    )
    gain_a, shift_a, gain_b, shift_b, bias_proj, bias_down, bias_up, bias_qkv = (vector[0] for vector in vectors)
    return joined, gain_a, shift_a, qkv_out, bias_qkv, proj, bias_proj, gain_b, shift_b, up_out, bias_up, down_out, bias_down


def plain_gradients(boundary, lengths, params, tables, swapped, bits):
    count = lax.axis_size("dp")
    slots = lengths.shape[0]
    width = boundary.shape[2]
    rows = boundary.shape[1] // slots
    units = params[8].shape[2]
    ticks = slots + 1
    result, saved, held = forward_first(lengths, boundary.reshape(slots, rows, width), params, tables)
    own, gain_a, shift_a, gain_b, shift_b, w_qkv, b_qkv, w_proj, b_proj, w_up, b_up, w_down, b_down, *tabs = held
    held_count = len(held)
    finals = [result]
    for t in range(1, ticks):
        arriving = lax.ppermute(result, "section", swapped)

        def forward_step(lengths_ref, arriving_ref, *refs, tick=t):
            section = lax.axis_index("section")
            slot = jnp.clip(tick - section, 0, slots - 1)
            inputs = lambda: jnp.where(section == 0, refs[0][slot], arriving_ref[...])
            outs = refs[held_count:]
            forward_body(slot, lengths_ref[slot].astype(F32), inputs, lambda name, part: None, *refs[:held_count], outs[-1], *outs[:-1])

        *saved, result = call(forward_step, [lengths, arriving, *held], [struct(rows, width)], "forward", kept=saved)
        finals.append(result)
    x_s, na_s, nb_s, qkv_s, pt_s, mixed_s, hidden_s, slope_s = saved
    operands = [x_s, gain_a, gain_b, w_qkv, w_proj, w_up, w_down, *tabs, pt_s]
    grads = [qkv_s, slope_s]
    input_grads = []
    arriving = own[0]
    for t in range(ticks):

        def backward_step(own_ref, arriving_ref, *refs, tick=t):
            section = lax.axis_index("section")
            slot = tick - 1 + section
            *io, gx_out = refs[len(operands) :]

            @pl.when((slot >= 0) & (slot < slots))
            def _():
                source = lambda: jnp.where(section == 0, arriving_ref[...], own_ref[slot])
                backward_body(slot, source, *refs[: len(operands)], gx_out, *io)

        shapes = [pltpu.VMEM((slots, rows, width), BF16), pltpu.VMEM((slots, 8, units), F32)] if t == 0 else []
        *grads, result = call(backward_step, [own, arriving, *operands], shapes + [struct(rows, width)], "backward", kept=grads)
        input_grads.append(result)
        if t + 1 < ticks:
            arriving = lax.ppermute(result, "section", swapped)
    gp_s, gu_s, gy_s, vec_s = grads
    order = list(range(len(bits)))

    def summed(full):
        keep, send = parted(full, 0, bits[0])
        return halving_sum(keep, send, order, count, bits, F32)

    both = jnp.concatenate([plain_grads(hidden_s, gy_s, count), plain_grads(mixed_s, gy_s, count)], axis=1)
    down, up, qkv = summed(both), summed(plain_grads(nb_s, gu_s, count)), summed(plain_grads(na_s, gp_s, count))
    tall = units // count
    totals = jnp.sum(vec_s, axis=0)
    sums = [totals[i, :width] for i in range(5)] + [totals[5], totals[6, : 3 * width]]
    return finals[1:], input_grads[1:], sums, down[:tall], down[tall:], up, qkv


def per_device(boundary, lengths, *params):
    section = lax.axis_index("section")
    count = lax.axis_size("dp")
    bits = [(lax.axis_index("dp") >> b) & 1 for b in range(count.bit_length() - 1)]
    slots = lengths.shape[0]
    width = boundary.shape[2]
    units = params[8].shape[2]
    tables = [jnp.asarray(table) for table in rotary_lanes(boundary.shape[1] // slots, 2 * HEAD)]
    swapped = [(0, 1), (1, 0)]
    if count == 16 and slots == 2 and width % 768 == 0:
        results = paired_gradients(boundary, lengths, params, tables, swapped)
        return tuple(result[None] for result in results)
    finals, input_grads, sums, down, proj, up, qkv = plain_gradients(
        boundary, lengths, params, tables, swapped, bits
    )
    small = jnp.concatenate([piece.reshape(count, -1) for piece in sums], axis=1)
    small = halving_sum(*parted(small, 0, bits[0]), list(range(len(bits))), count, bits, F32)
    low, tall = width // count, units // count
    gain_a, shift_a, gain_b, shift_b, bias_y, bias_up, bias_qkv = jnp.split(small, np.cumsum([low] * 5 + [tall]), axis=0)
    joined = jnp.where(section == 0, jnp.concatenate(input_grads, axis=0), jnp.concatenate(finals, axis=0))
    results = (joined, gain_a, shift_a, qkv, bias_qkv, proj, bias_y, gain_b, shift_b, up, bias_up, down, bias_y)
    return tuple(result[None] for result in results)


def solution(mesh):
    split = P("section", "dp")
    deep = P("section", "dp", None)
    flat, matrix = P("section", None), P("section", None, None)
    return jax.shard_map(
        per_device,
        mesh=mesh,
        in_specs=(deep, P("dp"), flat, flat, matrix, flat, matrix, flat, flat, flat, matrix, flat, matrix, flat),
        out_specs=(deep, split, split, deep, split, deep, split, split, split, deep, split, deep, split),
        check_vma=False,
    )
```

```python
import functools
import math

import jax
import jax.numpy as jnp
import numpy as np
from jax import lax
from jax.experimental import pallas as pl
from jax.experimental.pallas import tpu as pltpu
from jax.sharding import PartitionSpec as P

HEAD = 64
LANES = 256
CHUNK = 512
EPS = 1e-05
NEG_FILL = -1e30
VMEM_BYTES = 12 * 1024 * 1024
FIRST_VMEM_BYTES = 12 * 1024 * 1024
F32 = jnp.float32
BF16 = jnp.bfloat16


def dot(left, right):
    return jnp.dot(left, right, preferred_element_type=F32)


def dot_nt(left, right):
    return lax.dot_general(left, right, (((1,), (1,)), ((), ())), preferred_element_type=F32)


def normalised(values):
    centred = values - jnp.mean(values, axis=-1, keepdims=True)
    variance = jnp.mean(centred * centred, axis=-1, keepdims=True)
    scale = lax.rsqrt(variance + EPS)
    return centred * scale, scale


def gelu_parts(values):
    integral = 0.5 + 0.5 * lax.erf(values * math.sqrt(0.5))
    bell = jnp.exp(values * values * -0.5)
    return values * integral, integral + values * bell * (1.0 / math.sqrt(2.0 * math.pi))


def rotary_lanes(seq_len, lanes):
    rot_dims = HEAD // 4
    half = rot_dims // 2
    frequency = np.float32(10000.0) ** (-(np.arange(half, dtype=np.float32) * np.float32(2.0) / np.float32(rot_dims)))
    angles = np.arange(seq_len, dtype=np.float32)[:, None] * frequency.astype(np.float32)[None, :]
    cosine, sine = np.cos(angles).astype(np.float32), np.sin(angles).astype(np.float32)
    same = np.ones((seq_len, HEAD), np.float32)
    later = np.zeros((seq_len, HEAD), np.float32)
    earlier = np.zeros((seq_len, HEAD), np.float32)
    same[:, :half] = cosine
    same[:, half:rot_dims] = cosine
    later[:, :half] = -sine
    earlier[:, half:rot_dims] = sine
    return [np.tile(t, (1, lanes // HEAD)) for t in (same, later, earlier)]


def turned(values, same, later, earlier, sign):
    half = HEAD // 8
    width = values.shape[1]
    same, later, earlier = (jnp.concatenate([t] * (width // t.shape[1]), axis=1) for t in (same, later, earlier))
    ahead = pltpu.roll(values, width - half, 1)
    behind = pltpu.roll(values, half, 1)
    if sign > 0:
        return values * same + ahead * later + behind * earlier
    return values * same - ahead * later - behind * earlier


def blocked_bias(rows, length):
    out = []
    for start in range(0, rows, 128):
        keys = start + 128
        key_pos = lax.broadcasted_iota(jnp.int32, (keys, 2 * 128), 0)
        query_pos = start + (lax.broadcasted_iota(jnp.int32, (keys, 2 * 128), 1) & 127)
        out.append(jnp.where((key_pos <= query_pos) & (key_pos < length), 0.0, NEG_FILL))
    return out


def heads_apart(block, lane):
    zero = jnp.zeros_like(block)
    return jnp.concatenate([jnp.where(lane < HEAD, block, zero), jnp.where(lane < HEAD, zero, block)], axis=0)


def dot_tn(left, right):
    return lax.dot_general(left, right, (((0,), (0,)), ((), ())), preferred_element_type=F32)


def probs_rows(block):
    start = 128 * (block * (block + 1) // 2)
    return slice(start, start + 128 * (block + 1))


def some(offset, size):
    return slice(offset, offset + size) if isinstance(offset, int) else pl.ds(pl.multiple_of(offset, 128), size)


def spans(pair, width):
    return [slice(b * width + pair * 2 * HEAD, b * width + (pair + 1) * 2 * HEAD) for b in range(3)]


def forward_units(slot, length, ready, na, nb, wqkv, bqkv, wu, bu, tables, qkv, pt, mixed, hidden, slope, low_head, low_unit, lanes):
    rows = qkv.shape[1]
    whole_width, width = wqkv.shape[1], qkv.shape[2] // 3
    pairs = width // (2 * HEAD)
    chunk = hidden.shape[2] // pairs
    biases = blocked_bias(rows, length)
    lane = lax.broadcasted_iota(jnp.int32, (128, 2 * HEAD), 1)
    per = lanes // (2 * HEAD)
    for pair in range(pairs):
        if pair % per == 0:
            low = pair * 2 * HEAD
            ready("qkv", pair // per)

            def packed(block):
                at = some(block * whole_width + low_head + low, lanes)
                return dot(na[slot], wqkv[0, :, at]) + bqkv[:, at].astype(F32)

            qkv[slot, :, low : low + lanes] = (turned(packed(0), *tables, 1) * (HEAD**-0.5)).astype(BF16)
            qkv[slot, :, width + low : width + low + lanes] = turned(packed(1), *tables, 1).astype(BF16)
            qkv[slot, :, 2 * width + low : 2 * width + low + lanes] = packed(2).astype(BF16)
        span, span_k, span_v = spans(pair, width)
        all_scores = []
        for block, start in enumerate(range(0, rows, 128)):
            keys = start + 128
            q2 = heads_apart(qkv[slot, start:keys, span], lane)
            all_scores.append(dot_nt(qkv[slot, :keys, span_k], q2) + biases[block])
        ready("up", pair)
        there = some(low_unit + pair * chunk, chunk)
        up = dot(nb[slot], wu[0, :, there]) + bu[:, there].astype(F32)
        for block, start in enumerate(range(0, rows, 128)):
            keys = start + 128
            scores = all_scores[block]
            exponent = jnp.exp(scores - jnp.max(scores, axis=0, keepdims=True))
            probs = (exponent * (1.0 / jnp.sum(exponent, axis=0, keepdims=True))).astype(BF16)
            pt[slot, pair, probs_rows(block)] = probs
            both = dot_tn(probs, qkv[slot, :keys, span_v])
            mixed[slot, start:keys, span] = jnp.where(lane < HEAD, both[:128], both[128:]).astype(BF16)
        here = slice(pair * chunk, pair * chunk + chunk)
        hidden_f32, slope_f32 = gelu_parts(up)
        hidden[slot, :, here] = hidden_f32.astype(BF16)
        slope[slot, :, here] = slope_f32.astype(BF16)


def backward_units(slot, gy, wp, wd, tables, pt, qkv, slope, low_head, low_unit, lanes):
    rows = qkv.shape[1]
    width = qkv.shape[2] // 3
    pairs = width // (2 * HEAD)
    chunk = slope.shape[2] // pairs
    lane = lax.broadcasted_iota(jnp.int32, (128, 2 * HEAD), 1)
    per = lanes // (2 * HEAD)
    for pair in range(pairs):
        if pair % per == 0:
            gm_group = dot_nt(gy(), wp[0, some(low_head + pair * 2 * HEAD, lanes), :]).astype(BF16)
            group_q, group_k = [], []
        span, span_k, span_v = spans(pair, width)
        gm = gm_group[:, (pair % per) * 2 * HEAD : (pair % per + 1) * 2 * HEAD]
        gv_sum, gk_sum, gq_blocks = None, None, []
        for block, start in enumerate(range(0, rows, 128)):
            keys = start + 128
            gm2 = heads_apart(gm[start:keys], lane)
            q2 = heads_apart(qkv[slot, start:keys, span], lane)
            probs = pt[slot, pair, probs_rows(block)]
            weighted = probs.astype(F32) * dot_nt(qkv[slot, :keys, span_v], gm2)
            inner = jnp.sum(weighted, axis=0, keepdims=True)
            gs = (weighted - probs.astype(F32) * inner).astype(BF16)
            gv_part = dot(probs, gm2)
            gk_part = dot(gs, q2)
            gq_part = dot_tn(gs, qkv[slot, :keys, span_k])
            gq_blocks.append(jnp.where(lane < HEAD, gq_part[:128], gq_part[128:]))
            if gv_sum is None:
                gv_sum, gk_sum = gv_part, gk_part
            else:
                gv_sum = jnp.concatenate([gv_sum + gv_part[:start], gv_part[start:]], axis=0)
                gk_sum = jnp.concatenate([gk_sum + gk_part[:start], gk_part[start:]], axis=0)
        qkv[slot, :, span_v] = gv_sum.astype(BF16)
        group_q.append(jnp.concatenate(gq_blocks, axis=0))
        group_k.append(gk_sum)
        if pair % per == per - 1:
            low = pair // per * lanes
            gq = turned(jnp.concatenate(group_q, axis=1) * (HEAD**-0.5), *tables, -1)
            qkv[slot, :, low : low + lanes] = gq.astype(BF16)
            gk = turned(jnp.concatenate(group_k, axis=1), *tables, -1)
            qkv[slot, :, width + low : width + low + lanes] = gk.astype(BF16)
        here = slice(pair * chunk, pair * chunk + chunk)
        grad = dot_nt(gy(), wd[0, some(low_unit + pair * chunk, chunk), :])
        slope[slot, :, here] = (grad * slope[slot, :, here].astype(F32)).astype(BF16)


def forward_body(
    slot, length, inputs, ready, own, gain_a, shift_a, gain_b, shift_b, wqkv, bqkv, wp, bp, wu, bu, wd, bd, same, later, earlier,
    y_out, x_out, na_out, nb_out, qkv_out, pt_out, mixed_out, hidden_out, slope_out,
):
    ready("small", 0)
    x_low = inputs()
    x_out[slot] = x_low
    xhat, _ = normalised(x_low.astype(F32))
    na_out[slot] = (xhat * gain_a[...].astype(F32) + shift_a[...].astype(F32)).astype(BF16)
    nb_out[slot] = (xhat * gain_b[...].astype(F32) + shift_b[...].astype(F32)).astype(BF16)
    tables = (same[...], later[...], earlier[...])
    forward_units(
        slot, length, ready, na_out, nb_out, wqkv, bqkv, wu, bu, tables, qkv_out, pt_out, mixed_out, hidden_out, slope_out, 0, 0, LANES
    )
    ready("rest", 0)
    total = x_out[slot].astype(F32) + (bp[...].astype(F32) + bd[...].astype(F32))
    y_out[...] = (total + dot(mixed_out[slot], wp[0]) + dot(hidden_out[slot], wd[0])).astype(BF16)


def backward_body(
    slot, gy_source, x_in, gain_a, gain_b, wqkv, wp, wu, wd, same, later, earlier, pt_in, gx_out, qkv_io, slope_io, gy_out, vec_out
):
    width = gx_out.shape[1]
    gy_out[slot] = gy_source()
    tables = (same[...], later[...], earlier[...])
    backward_units(slot, lambda: gy_out[slot], wp, wd, tables, pt_in, qkv_io, slope_io, 0, 0, LANES)
    grad_b = dot_nt(slope_io[slot], wu[0])
    grad_a = dot_nt(qkv_io[slot], wqkv[0])
    xhat, scale = normalised(x_in[slot].astype(F32))
    norm_terms = (grad_a * xhat, grad_a, grad_b * xhat, grad_b, gy_out[slot].astype(F32))
    for row, terms in enumerate(norm_terms):
        vec_out[slot, row : row + 1, :width] = jnp.sum(terms, axis=0, keepdims=True)
    vec_out[slot, 5:6, :] = jnp.sum(slope_io[slot].astype(F32), axis=0, keepdims=True)
    vec_out[slot, 6:7, : 3 * width] = jnp.sum(qkv_io[slot].astype(F32), axis=0, keepdims=True)
    both = grad_a * gain_a[...].astype(F32) + grad_b * gain_b[...].astype(F32)
    inner = jnp.mean(both * xhat, axis=-1, keepdims=True)
    gx = gy_out[slot].astype(F32) + scale * (both - jnp.mean(both, axis=-1, keepdims=True) - xhat * inner)
    gx_out[...] = gx.astype(BF16)


def forward_first_kernel(tick, lengths, *refs):
    count = 17
    sources, held, outs, sems = refs[:count], refs[count : 2 * count], refs[2 * count : -1], refs[-1]
    copies = []
    waits = {}

    def fetch(name, part, index, at):
        source, target = (sources[index], held[index]) if at is None else (sources[index].at[at], held[index].at[at])
        copy = pltpu.make_async_copy(source, target, sems.at[len(copies)])
        copies.append(copy)
        waits.setdefault((name, part), []).append(copy)

    (own, gain_a, shift_a, gain_b, shift_b, wqkv, bqkv, wp, bp, wu, bu, wd, bd, same, later, earlier, _) = range(count)
    width = sources[wp].shape[1]
    units = sources[wu].shape[2]
    pairs = width // (2 * HEAD)
    groups = width // LANES
    for index in (own, gain_a, shift_a, gain_b, shift_b, bqkv, bp, bu, bd, same, later, earlier):
        fetch("small", 0, index, None)
    for pair in range(pairs):
        if pair * groups % pairs == 0:
            group = pair * groups // pairs
            for block in range(3):
                fetch("qkv", group, wqkv, (slice(None), slice(None), pl.ds(block * width + group * LANES, LANES)))
        fetch("up", pair, wu, (slice(None), slice(None), pl.ds(pair * (units // pairs), units // pairs)))
    fetch("rest", 0, wp, None)
    fetch("rest", 0, wd, None)
    for copy in copies:
        copy.start()

    def ready(name, part):
        for copy in waits[(name, part)]:
            copy.wait()

    section = lax.axis_index("section")
    slots = held[own].shape[0]
    slot = jnp.clip(tick - section, 0, slots - 1)
    forward_body(slot, lengths[slot], lambda: held[own][slot], ready, *held[:-1], *outs)


def backward_body(
    slot, gy_source, x_in, gain_a, gain_b, wqkv, wp, wu, wd, same, later, earlier,
    pt_in, gx_out, qkv_io, slope_io, gy_out, vec_out,
):
    rows, width = gx_out.shape
    units = wu.shape[2]
    pairs = width // (2 * HEAD)
    chunk = units // pairs
    gy_out[slot] = gy_source()
    lane = lax.broadcasted_iota(jnp.int32, (128, 2 * HEAD), 1)
    tables = (same[...], later[...], earlier[...])
    per = LANES // (2 * HEAD)
    for pair in range(pairs):
        if pair % per == 0:
            gm_group = dot_nt(gy_out[slot], wp[0, pair * 2 * HEAD : pair * 2 * HEAD + LANES, :]).astype(BF16)
            group_q, group_k = [], []
        span, span_k, span_v = (slice(b * width + pair * 2 * HEAD, b * width + (pair + 1) * 2 * HEAD) for b in range(3))
        gm = gm_group[:, (pair % per) * 2 * HEAD : (pair % per + 1) * 2 * HEAD]
        gv_sum, gk_sum, gq_blocks = None, None, []
        for block, start in enumerate(range(0, rows, 128)):
            keys = start + 128
            gm2 = heads_apart(gm[start:keys], lane)
            q2 = heads_apart(qkv_io[slot, start:keys, span], lane)
            pt = pt_in[slot, pair, probs_rows(block)]
            weighted = pt.astype(F32) * dot_nt(qkv_io[slot, :keys, span_v], gm2)
            inner = jnp.sum(weighted, axis=0, keepdims=True)
            gs = (weighted - pt.astype(F32) * inner).astype(BF16)
            gv_part = dot(pt, gm2)
            gk_part = dot(gs, q2)
            gq_part = dot_tn(gs, qkv_io[slot, :keys, span_k])
            gq_blocks.append(jnp.where(lane < HEAD, gq_part[:128], gq_part[128:]))
            if gv_sum is None:
                gv_sum, gk_sum = gv_part, gk_part
            else:
                gv_sum = jnp.concatenate([gv_sum + gv_part[:start], gv_part[start:]], axis=0)
                gk_sum = jnp.concatenate([gk_sum + gk_part[:start], gk_part[start:]], axis=0)
        qkv_io[slot, :, span_v] = gv_sum.astype(BF16)
        group_q.append(jnp.concatenate(gq_blocks, axis=0))
        group_k.append(gk_sum)
        if pair % per == per - 1:
            low = pair // per * LANES
            gq = turned(jnp.concatenate(group_q, axis=1) * (HEAD**-0.5), *tables, -1)
            qkv_io[slot, :, low : low + LANES] = gq.astype(BF16)
            gk = turned(jnp.concatenate(group_k, axis=1), *tables, -1)
            qkv_io[slot, :, width + low : width + low + LANES] = gk.astype(BF16)
        at = slice(pair * chunk, pair * chunk + chunk)
        slope_io[slot, :, at] = (dot_nt(gy_out[slot], wd[0, at, :]) * slope_io[slot, :, at].astype(F32)).astype(BF16)
    grad_b = dot_nt(slope_io[slot], wu[0])
    grad_a = dot_nt(qkv_io[slot], wqkv[0])
    xhat, scale = normalised(x_in[slot].astype(F32))
    norm_terms = (grad_a * xhat, grad_a, grad_b * xhat, grad_b, gy_out[slot].astype(F32))
    for row, terms in enumerate(norm_terms):
        vec_out[slot, row : row + 1, :width] = jnp.sum(terms, axis=0, keepdims=True)
    vec_out[slot, 5:6, :] = jnp.sum(slope_io[slot].astype(F32), axis=0, keepdims=True)
    vec_out[slot, 6:7, : 3 * width] = jnp.sum(qkv_io[slot].astype(F32), axis=0, keepdims=True)
    both = grad_a * gain_a[...].astype(F32) + grad_b * gain_b[...].astype(F32)
    inner = jnp.mean(both * xhat, axis=-1, keepdims=True)
    gx = gy_out[slot].astype(F32) + scale * (both - jnp.mean(both, axis=-1, keepdims=True) - xhat * inner)
    gx_out[...] = gx.astype(BF16)


VM = pl.BlockSpec(memory_space=pltpu.VMEM)
HBM = pl.BlockSpec(memory_space=pl.ANY)


def call(kernel, operands, out_shape, name, kept=(), scratch=(), flops=1 << 20, after=()):
    count = len(operands)
    after = list(after)

    def body(*refs):
        kernel(*refs[:count], *refs[count + len(kept) + len(after) :])

    return pl.pallas_call(
        body,
        in_specs=[pl.BlockSpec(memory_space=pltpu.SMEM) if o.dtype == jnp.int32 else VM for o in operands] + [VM] * len(kept) + [HBM] * len(after),
        out_specs=[VM] * (len(kept) + len(out_shape)),
        out_shape=[pltpu.VMEM(array.shape, array.dtype) for array in kept] + list(out_shape),
        input_output_aliases={count + i: i for i in range(len(kept))},
        scratch_shapes=list(scratch),
        compiler_params=pltpu.CompilerParams(vmem_limit_bytes=VMEM_BYTES),
        cost_estimate=pl.CostEstimate(flops=flops, bytes_accessed=1 << 16, transcendentals=0),
        name=name,
    )(*operands, *[pltpu.with_memory_space_constraint(array, pltpu.VMEM) for array in kept], *after)


def shape_of(array):
    return jax.ShapeDtypeStruct(array.shape, array.dtype)


def forward_shapes(local_rows, params):
    slots, rows, width = local_rows.shape
    units = params[8].shape[2]
    blocks = rows // 128
    probs = (slots, width // (2 * HEAD), 128 * (blocks * (blocks + 1) // 2), 2 * 128)
    columns = [width, width, width, 3 * width, None, width, units, units]
    return [jax.ShapeDtypeStruct((rows, width), BF16)] + [
        pltpu.VMEM(probs if n is None else (slots, rows, n), BF16) for n in columns
    ]


def forward_first(lengths, local_rows, params, tables):
    (gain_a, shift_a, w_qkv, b_qkv, w_proj, b_proj, gain_b, shift_b, w_up, b_up, w_down, b_down) = params
    held = [local_rows, gain_a, shift_a, gain_b, shift_b, w_qkv, b_qkv, w_proj, b_proj, w_up, b_up, w_down, b_down] + list(tables)
    shapes = [shape_of(array) for array in held] + forward_shapes(local_rows, params)

    def kernel(lengths_ref, *refs):
        count = len(held)
        forward_first_kernel(0, lengths_ref, *refs[:count], None, *refs[count : 2 * count], None, *refs[2 * count :])

    outs = pl.pallas_call(
        kernel,
        in_specs=[pl.BlockSpec(memory_space=pltpu.SMEM)] + [pl.BlockSpec(memory_space=pltpu.HBM)] * len(held),
        out_specs=[VM] * len(shapes),
        out_shape=shapes,
        scratch_shapes=[pltpu.SemaphoreType.DMA((40,))],
        compiler_params=pltpu.CompilerParams(vmem_limit_bytes=FIRST_VMEM_BYTES),
        cost_estimate=pl.CostEstimate(flops=1 << 20, bytes_accessed=1 << 16, transcendentals=0),
        name="layer_forward_first",
    )(lengths, *[pltpu.with_memory_space_constraint(array, pltpu.HBM) for array in held])
    count = len(held)
    return outs[count], outs[count + 1 :], outs[:count]


def swap(shard, bit, count):
    return lax.ppermute(shard, "dp", [(i, i ^ (1 << bit)) for i in range(count)])


def parted(values, position, mine):
    count = values.shape[0]
    shaped = values.reshape((count >> (position + 1), 2, 1 << position) + values.shape[1:])
    out = []
    for side in (mine, 1 - mine):
        piece = lax.dynamic_index_in_dim(shaped, side, axis=1, keepdims=False)
        out.append(piece.reshape((count // 2,) + values.shape[1:]))
    return out


def halving_sum(keep, send, order, count, bits, final):
    left = sorted(order)
    for number, bit in enumerate(order):
        left.remove(bit)
        arrived = swap(send, bit, count)
        if number + 1 == len(order):
            return (keep.astype(F32) + arrived.astype(F32)).astype(final)[0]
        position = left.index(order[number + 1])
        keep_a, send_a = parted(keep, position, bits[order[number + 1]])
        keep_b, send_b = parted(arrived, position, bits[order[number + 1]])
        send = (send_a.astype(F32) + send_b.astype(F32)).astype(send_a.dtype)
        keep = (keep_a.astype(F32) + keep_b.astype(F32)).astype(send_a.dtype)


def plain_grads(left, right, count):
    rows = left.shape[0] * left.shape[1]
    product = lax.dot_general(
        left.reshape(rows, -1), right.reshape(rows, -1), (((0,), (0,)), ((), ())), preferred_element_type=F32
    ).astype(BF16)
    return product.reshape(count, product.shape[0] // count, product.shape[1])


def partner_forward(half, lengths, rows_of, gain_a, shift_a, gain_b, shift_b, wqkv, bqkv, wu, bu, tables, nap, nbp, qkvp, ptp, mixedp, hidp, slopep):
    for s in range(nap.shape[0]):
        xhat, _ = normalised(rows_of(s).astype(F32))
        nap[s] = (xhat * gain_a[...].astype(F32) + shift_a[...].astype(F32)).astype(BF16)
        nbp[s] = (xhat * gain_b[...].astype(F32) + shift_b[...].astype(F32)).astype(BF16)
        lanes = mixedp.shape[2]
        forward_units(
            s, lengths[s], lambda name, part: None, nap, nbp, wqkv, bqkv, wu, bu, tables, qkvp, ptp, mixedp, hidp, slopep,
            half * lanes, half * hidp.shape[2], lanes,
        )


def partner_backward(s, half, gy, wp, wd, tables, ptp, qkvp, slopep):
    lanes = qkvp.shape[2] // 3
    backward_units(s, gy, wp, wd, tables, ptp, qkvp, slopep, half * lanes, half * slopep.shape[2], lanes)


SUM_FLOPS = 6 << 30
ORDERS = {"down": (0, 1, 2), "up": (1, 2, 0), "attn": (2, 0, 1)}


def dp_bit(bit):
    return (lax.axis_index("dp") >> bit) & 1


def eighth_row(chunk, order, rows):
    first, second, third = ((chunk >> bit) & 1 for bit in order)
    return ((first ^ dp_bit(order[0])) * 4 + second * 2 + third) * rows


def row_slice(start, rows):
    return pl.ds(pl.multiple_of(start, 16), rows)


def flat_rows(ref, at=slice(None)):
    values = ref[:, :, at]
    return values.reshape(values.shape[0] * values.shape[1], values.shape[2])


def ones_dot(values):
    return dot(jnp.ones((16, values.shape[0]), BF16), values)[:8]


def sixteenths(ref, left, order, tokens_from):
    turned_ref = flat_rows(ref).T
    low = turned_ref.shape[0] // 16
    for chunk in range(16):
        start = eighth_row(chunk & 7, order, 2 * low) + (chunk >> 3) * low
        left[row_slice(start, low), tokens_from : tokens_from + turned_ref.shape[1]] = turned_ref[chunk * low : chunk * low + low]


def eighths(turned_rows, left, order, tokens_from):
    low = turned_rows.shape[0] // 8
    for chunk in range(8):
        left[row_slice(eighth_row(chunk, order, low), low), tokens_from : tokens_from + turned_rows.shape[1]] = turned_rows[
            chunk * low : chunk * low + low
        ]


def up_group_kernel(nb, nbp, gu, gup, keep, send, left):
    half = dp_bit(3)
    tokens = nb.shape[0] * nb.shape[1]
    units = gup.shape[2]
    sixteenths(nb, left, ORDERS["up"], 0)
    sixteenths(nbp, left, ORDERS["up"], tokens)
    rows = left.shape[0] // 8
    for low in range(0, units, 512):
        at = slice(low, low + 512)
        product = dot(left[:, :tokens], flat_rows(gu, some(half * units + low, 512))) + dot(left[:, tokens:], flat_rows(gup, at))
        product = product.astype(BF16).reshape(8, rows, 512)
        keep[:, :, at] = product[:4]
        send[:, :, at] = product[4:]


def attn_group_kernel(na, nap, gp, gpp, mixed, mixedp, gy, gyp_of, vec, keep, send, left, left_mixed):
    half = dp_bit(3)
    tokens = na.shape[0] * na.shape[1]
    width = na.shape[2]
    lanes = mixedp.shape[2]
    order = ORDERS["attn"]
    sixteenths(na, left, order, 0)
    sixteenths(nap, left, order, tokens)
    rows = left.shape[0] // 8
    for block in range(3):
        at = slice(block * lanes, block * lanes + lanes)
        own = flat_rows(gp, some(block * width + half * lanes, lanes))
        product = dot(left[:, :tokens], own) + dot(left[:, tokens:], flat_rows(gpp, at))
        product = product.astype(BF16).reshape(8, rows, lanes)
        keep[:, :rows, at] = product[:4]
        send[:, :rows, at] = product[4:]
    eighths(flat_rows(mixed, some(half * lanes, lanes)).T, left_mixed, order, 0)
    eighths(flat_rows(mixedp).T, left_mixed, order, tokens)
    own_gy = flat_rows(gy)
    other_gy = jnp.concatenate([gyp_of(s) for s in range(gy.shape[0])], axis=0)
    product = dot(left_mixed[:, :tokens], own_gy) + dot(left_mixed[:, tokens:], other_gy)
    low = left_mixed.shape[0] // 8
    product = product.astype(BF16).reshape(8, low, width)
    keep[:, rows:, :width] = product[:4]
    send[:, rows:, :width] = product[4:]
    row_index = lax.broadcasted_iota(jnp.int32, (16, lanes), 0)
    totals = vec[0] + vec[1]
    sums = [totals[i : i + 1, :width] for i in range(5)] + [totals[5:6], totals[6:7, : 3 * width]]

    def bias_block(chunk):
        block = jnp.zeros((16, lanes), F32)
        for row, values in enumerate(sums):
            size = values.shape[1] // 16
            piece = jnp.concatenate([values[:, chunk * size : chunk * size + size], jnp.zeros((1, lanes - size), F32)], axis=1)
            block = jnp.where(row_index == row, jnp.broadcast_to(piece, (16, lanes)), block)
        return block.astype(BF16)

    first_bit = 1 << order[0]
    for chunk in range(16):
        if chunk & first_bit:
            continue
        blocks = bias_block(chunk), bias_block(chunk | first_bit)
        second, third = (chunk >> order[1]) & 1, (chunk >> order[2]) & 1
        place_at = slice(rows + (chunk >> 3) * 16, rows + (chunk >> 3) * 16 + 16)
        mine = dp_bit(order[0]) == 0
        keep[second * 2 + third, place_at, width:] = jnp.where(mine, blocks[0], blocks[1])
        send[second * 2 + third, place_at, width:] = jnp.where(mine, blocks[1], blocks[0])


def down_group_kernel(hidden, hidp, gy, gyp_of, keep, send, left):
    half = dp_bit(3)
    tokens = gy.shape[0] * gy.shape[1]
    units = hidp.shape[2]
    order = ORDERS["down"]
    eighths(flat_rows(hidden, some(half * units, units)).T, left, order, 0)
    eighths(flat_rows(hidp).T, left, order, tokens)
    own_gy = flat_rows(gy)
    other_gy = jnp.concatenate([gyp_of(s) for s in range(gy.shape[0])], axis=0)
    size = units // 2
    for side, out in enumerate((keep, send)):
        at = slice(side * size, side * size + size)
        product = dot(left[at, :tokens], own_gy) + dot(left[at, tokens:], other_gy)
        out[...] = product.astype(BF16).reshape(out.shape)


def plus(left, right):
    return left.astype(F32) + right.astype(F32)


def add_kernel(bit, keep, arrived, keep_out, send_out):
    size = keep_out.shape[0]
    mine = dp_bit(bit) * size
    keep_out[...] = plus(keep[pl.ds(mine, size)], arrived[pl.ds(mine, size)]).astype(BF16)
    send_out[...] = plus(keep[pl.ds(size - mine, size)], arrived[pl.ds(size - mine, size)]).astype(BF16)


def swap_over(shard, bit, sections=(0, 1)):
    count = lax.axis_size("dp")
    pairs = [(s * count + i, s * count + (i ^ (1 << bit))) for s in sections for i in range(count)]
    return lax.ppermute(shard, ("section", "dp"), pairs)


def cross_swap(shard, section, bit):
    count = lax.axis_size("dp")
    return lax.ppermute(shard, ("section", "dp"), [(section * count + i, (1 - section) * count + (i ^ (1 << bit))) for i in range(count)])


def struct(*shape, dtype=BF16):
    return jax.ShapeDtypeStruct(shape, dtype)


def halved(parts, order, stage, name, after=()):
    keep, send = parts
    arrived = swap_over(send, order[stage])
    shape = (keep.shape[0] // 2,) + keep.shape[1:]
    return call(functools.partial(add_kernel, order[stage + 1]), [keep, arrived], [struct(*shape)] * 2, name, after=after, flops=SUM_FLOPS)


def down_sum_kernel(keep, arrived, out):
    out[...] = plus(keep[0], arrived[0])


def halves_sum_kernel(up_keep, up_arrived, attn_keep, attn_arrived, up_mine, qkv_mine, small_mine, proj, other):
    half = dp_bit(3)
    low = up_mine.shape[0]
    units = up_mine.shape[1]
    width = proj.shape[1]
    mine, theirs = row_slice(half * low, low), row_slice((1 - half) * low, low)
    up_mine[...] = plus(up_keep[0, mine], up_arrived[0, mine])
    other[:, :units] = plus(up_keep[0, theirs], up_arrived[0, theirs]).astype(BF16)
    qkv_mine[...] = plus(attn_keep[0, mine], attn_arrived[0, mine])
    other[:, units : units + qkv_mine.shape[1]] = plus(attn_keep[0, theirs], attn_arrived[0, theirs]).astype(BF16)
    proj[...] = plus(attn_keep[0, 2 * low :, :width], attn_arrived[0, 2 * low :, :width])
    mine, theirs = row_slice(2 * low + half * 16, 16), row_slice(2 * low + (1 - half) * 16, 16)
    small_mine[...] = plus(attn_keep[0, mine, width:], attn_arrived[0, mine, width:])
    small = plus(attn_keep[0, theirs, width:], attn_arrived[0, theirs, width:]).astype(BF16)
    for part in range(small.shape[1] // 128):
        other[part * 16 : part * 16 + 16, other.shape[1] - 128 :] = small[:, part * 128 : part * 128 + 128]


def joined_kernel(up_mine, qkv_mine, small_mine, other, up, qkv, *vectors):
    half = dp_bit(3)
    low = up_mine.shape[0]
    units = up_mine.shape[1]
    lanes = qkv_mine.shape[1] // 3
    up[:, some(half * units, units)] = up_mine[...]
    up[:, some((1 - half) * units, units)] = other[:, :units].astype(F32)
    for block in range(3):
        at = slice(block * lanes, block * lanes + lanes)
        qkv[:, some((2 * block + half) * lanes, lanes)] = qkv_mine[:, at]
        qkv[:, some((2 * block + 1 - half) * lanes, lanes)] = other[:, units + block * lanes : units + (block + 1) * lanes].astype(F32)
    rest = other[:, other.shape[1] - 128 :].astype(F32)
    small = small_mine[...] + jnp.concatenate([rest[part : part + 16] for part in range(0, low, 16)], axis=1)
    for row, out in zip((0, 1, 2, 3, 4, 4, 5, 6), vectors):
        out[...] = small[row : row + 1, : out.shape[1]]


def paired_gradients(boundary, lengths, params, tables, swapped):
    slots = lengths.shape[0]
    width = boundary.shape[2]
    rows = boundary.shape[1] // slots
    units = params[8].shape[2]
    local_rows = boundary.reshape(slots, rows, width)
    low, tall = width // 16, units // 16
    tokens = slots * rows

    partner_lengths = swap_over(lengths, 3)
    cut = rows * slots * 3 // 4
    other_a = swap_over(boundary[0, :cut], 3, (0,))
    other_b = swap_over(boundary[0, cut:], 3, (0,))
    other_gy = swap_over(local_rows, 3, (1,))
    result_0, saved, held = forward_first(lengths, local_rows, params, tables)
    own, gain_a, shift_a, gain_b, shift_b, w_qkv, b_qkv, w_proj, b_proj, w_up, b_up, w_down, b_down, *tabs = held
    arrived_1 = lax.ppermute(result_0, "section", swapped)
    count = len(held)

    def forward_both(lengths_ref, arriving, *refs):
        section = lax.axis_index("section")
        slot = 1 - section
        inputs = lambda: jnp.where(section == 0, refs[0][slot], arriving[...])
        outs = refs[count:]
        forward_body(slot, lengths_ref[slot], inputs, lambda name, part: None, *refs[:count], outs[-1], *outs[:-1])

    *saved, result_1 = call(forward_both, [lengths, arrived_1, *held], [struct(rows, width)], "forward_1", kept=saved, after=[partner_lengths, other_a])
    arrived_2 = lax.ppermute(result_1, "section", swapped)

    def forward_last(lengths_ref, arriving, *refs):
        outs = refs[count:]
        slot = slots - 1

        @pl.when(lax.axis_index("section") == 1)
        def _():
            forward_body(
                slot, lengths_ref[slot], lambda: arriving[...], lambda name, part: None, *refs[:count], outs[len(saved)], *outs[: len(saved)]
            )

    *saved, result_2 = call(forward_last, [lengths, arrived_2, *held], [struct(rows, width)], "forward_2", kept=saved, after=[other_b])
    x_s, na_s, nb_s, qkv_s, pt_s, mixed_s, hidden_s, slope_s = saved
    partner_x = swap_over(x_s, 3, (1,))

    back_operands = [x_s, gain_a, gain_b, w_qkv, w_proj, w_up, w_down, *tabs, pt_s]
    back_count = len(back_operands)
    shared_operands = [gain_a, shift_a, gain_b, shift_b, w_qkv, b_qkv, w_up, b_up, *tabs]
    shared_count = len(shared_operands)
    shared_shapes = [
        pltpu.VMEM(shape, BF16)
        for shape in (
            (slots, rows, width), (slots, rows, width), (slots, rows, 3 * width // 2), (slots, pt_s.shape[1] // 2) + pt_s.shape[2:],
            (slots, rows, width // 2), (slots, rows, units // 2), (slots, rows, units // 2),
        )
    ]

    def share(lengths_ref, rows_of, refs, outs):
        weights, tabs_refs = refs[:-3], refs[-3:]
        partner_forward(dp_bit(3), lengths_ref, rows_of, *weights, tuple(t[...] for t in tabs_refs), *outs)

    def backward_first(lengths_ref, own_ref, ref_a, ref_b, *refs):
        operands, shared, (qkv_io, slope_io, gy, vec, gx, *outs) = (
            refs[:back_count], refs[back_count : back_count + shared_count], refs[back_count + shared_count :],
        )
        section = lax.axis_index("section")

        def rows_of(s):
            low, high = s * rows, s * rows + rows
            parts = [ref_a[low : min(high, cut)], ref_b[max(low, cut) - cut : high - cut]] if high > cut else [ref_a[low:high]]
            return jnp.concatenate(parts, axis=0)

        @pl.when(section == 1)
        def _():
            backward_body(0, lambda: own_ref[0], *operands, gx, qkv_io, slope_io, gy, vec)

        @pl.when(section == 0)
        def _():
            share(lengths_ref, rows_of, shared, outs)

    outs = call(
        backward_first, [partner_lengths, own, other_a, other_b, *back_operands, *shared_operands],
        [pltpu.VMEM((slots, rows, width), BF16), pltpu.VMEM((slots, 8, units), F32), struct(rows, width)] + shared_shapes,
        "backward_0", kept=[qkv_s, slope_s],
    )
    grads, back_0, shared = outs[:4], outs[4], outs[5:]
    arrived_4 = lax.ppermute(back_0, "section", swapped)
    partner_4 = swap_over(arrived_4, 3, (0,))

    def backward_both(own_ref, arriving, *refs):
        section = lax.axis_index("section")
        outs = refs[back_count:]
        source = lambda: jnp.where(section == 0, arriving[...], own_ref[section])
        backward_body(section, source, *refs[:back_count], outs[-1], *outs[:-1])

    *grads, back_1 = call(backward_both, [own, arrived_4, *back_operands], [struct(rows, width)], "backward_1", kept=grads, after=[other_gy])
    arrived_5 = lax.ppermute(back_1, "section", swapped)
    partner_5 = cross_swap(back_1, 1, 3)

    def backward_last(lengths_ref, arriving, other_ref, *refs):
        operands, shared_in, (qkv_io, slope_io, gy, vec, *outs) = (
            refs[:back_count], refs[back_count : back_count + shared_count], refs[back_count + shared_count :],
        )
        section = lax.axis_index("section")

        @pl.when(section == 0)
        def _():
            backward_body(slots - 1, lambda: arriving[...], *operands, outs[-1], qkv_io, slope_io, gy, vec)

        @pl.when(section == 1)
        def _():
            share(lengths_ref, lambda s: other_ref[s], shared_in, outs[:-1])

    outs = call(
        backward_last, [partner_lengths, arrived_5, partner_x, *back_operands, *shared_operands], [struct(rows, width)],
        "backward_2", kept=[*grads, *shared],
    )
    gp_s, gu_s, gy_s, vec_s, nap, nbp, qkvp, ptp, mixedp, hidp, slopep, back_2 = outs

    gpp, gup = qkvp, slopep
    gyp_s = []
    for s, partner_gy in enumerate((partner_4, partner_5)):

        def backward_shared(other_ref, partner_ref, wp, wd, same, later, earlier, ptp_ref, qkvp_ref, slopep_ref, gyp, s=s):
            gyp[...] = jnp.where(lax.axis_index("section") == 0, partner_ref[...], other_ref[s])
            tables_in = (same[...], later[...], earlier[...])
            partner_backward(s, dp_bit(3), lambda: gyp[...], wp, wd, tables_in, ptp_ref, qkvp_ref, slopep_ref)

        gpp, gup, gyp = call(
            backward_shared, [other_gy, partner_gy, w_proj, w_down, *tabs, ptp], [struct(rows, width)], f"backward_shared_{s}", kept=[gpp, gup]
        )
        gyp_s.append(gyp)

    def group(rows_of_eighth, columns):
        return [struct(4, rows_of_eighth, columns)] * 2

    up = call(
        up_group_kernel, [nb_s, nbp, gu_s, gup], group(2 * low, units // 2), "up_grads", scratch=[pltpu.VMEM((width, 2 * tokens), BF16)]
    )

    def attn_group(na, nap_ref, gp, gpp_ref, mixed, mixedp_ref, gy, gyp_a, gyp_b, *refs):
        attn_group_kernel(na, nap_ref, gp, gpp_ref, mixed, mixedp_ref, gy, lambda s: (gyp_a, gyp_b)[s][...], *refs)

    attn = call(
        attn_group, [na_s, nap, gp_s, gpp, mixed_s, mixedp, gy_s, *gyp_s, vec_s], group(3 * low, 3 * width // 2), "attn_grads",
        scratch=[pltpu.VMEM((width, 2 * tokens), BF16), pltpu.VMEM((width // 2, 2 * tokens), BF16)], after=up[:1],
    )

    def down_group(hidden, hidp_ref, gy, gyp_a, gyp_b, *refs):
        down_group_kernel(hidden, hidp_ref, gy, lambda s: (gyp_a, gyp_b)[s][...], *refs)

    down = call(
        down_group, [hidden_s, hidp, gy_s, *gyp_s], group(tall, width), "down_grads",
        scratch=[pltpu.VMEM((units // 2, 2 * tokens), BF16)], after=attn[:1],
    )

    up = halved(up, ORDERS["up"], 0, "up_sum_1", after=down[:1])
    attn = halved(attn, ORDERS["attn"], 0, "attn_sum_1", after=up[:1])
    down = halved(down, ORDERS["down"], 0, "down_sum_1", after=attn[:1])
    up = halved(up, ORDERS["up"], 1, "up_sum_2", after=down[:1])
    attn = halved(attn, ORDERS["attn"], 1, "attn_sum_2", after=up[:1])
    down = halved(down, ORDERS["down"], 1, "down_sum_2", after=attn[:1])
    up_last, attn_last = swap_over(up[1], ORDERS["up"][2]), swap_over(attn[1], ORDERS["attn"][2])
    up_mine, qkv_mine, small_mine, proj, others = call(
        halves_sum_kernel, [up[0], up_last, attn[0], attn_last],
        [struct(low, units // 2, dtype=F32), struct(low, 3 * width // 2, dtype=F32), struct(16, width // 2, dtype=F32),
         struct(low, width, dtype=F32), struct(low, units // 2 + 3 * width // 2 + 128)], "up_qkv_sum_3", after=down[:1],
    )
    (down_out,) = call(down_sum_kernel, [down[0], swap_over(down[1], ORDERS["down"][2])], [struct(tall, width, dtype=F32)], "down_sum_3")
    vectors = [low] * 6 + [tall, 3 * low]
    up_out, qkv_out, *vectors = call(
        joined_kernel, [up_mine, qkv_mine, small_mine, swap_over(others, 3)],
        [struct(low, units, dtype=F32), struct(low, 3 * width, dtype=F32)] + [struct(1, size, dtype=F32) for size in vectors], "up_qkv_joined",
    )
    joined = jnp.where(
        lax.axis_index("section") == 0, jnp.concatenate([back_1, back_2], axis=0), jnp.concatenate([result_1, result_2], axis=0)
    )
    gain_a, shift_a, gain_b, shift_b, bias_proj, bias_down, bias_up, bias_qkv = (vector[0] for vector in vectors)
    return joined, gain_a, shift_a, qkv_out, bias_qkv, proj, bias_proj, gain_b, shift_b, up_out, bias_up, down_out, bias_down


def plain_gradients(boundary, lengths, params, tables, swapped, bits):
    count = lax.axis_size("dp")
    slots = lengths.shape[0]
    width = boundary.shape[2]
    rows = boundary.shape[1] // slots
    units = params[8].shape[2]
    ticks = slots + 1
    result, saved, held = forward_first(lengths, boundary.reshape(slots, rows, width), params, tables)
    own, gain_a, shift_a, gain_b, shift_b, w_qkv, b_qkv, w_proj, b_proj, w_up, b_up, w_down, b_down, *tabs = held
    held_count = len(held)
    finals = [result]
    for t in range(1, ticks):
        arriving = lax.ppermute(result, "section", swapped)

        def forward_step(lengths_ref, arriving_ref, *refs, tick=t):
            section = lax.axis_index("section")
            slot = jnp.clip(tick - section, 0, slots - 1)
            inputs = lambda: jnp.where(section == 0, refs[0][slot], arriving_ref[...])
            outs = refs[held_count:]
            forward_body(slot, lengths_ref[slot], inputs, lambda name, part: None, *refs[:held_count], outs[-1], *outs[:-1])

        *saved, result = call(forward_step, [lengths, arriving, *held], [struct(rows, width)], "forward", kept=saved)
        finals.append(result)
    x_s, na_s, nb_s, qkv_s, pt_s, mixed_s, hidden_s, slope_s = saved
    operands = [x_s, gain_a, gain_b, w_qkv, w_proj, w_up, w_down, *tabs, pt_s]
    grads = [qkv_s, slope_s]
    input_grads = []
    arriving = own[0]
    for t in range(ticks):

        def backward_step(own_ref, arriving_ref, *refs, tick=t):
            section = lax.axis_index("section")
            slot = tick - 1 + section
            *io, gx_out = refs[len(operands) :]

            @pl.when((slot >= 0) & (slot < slots))
            def _():
                source = lambda: jnp.where(section == 0, arriving_ref[...], own_ref[slot])
                backward_body(slot, source, *refs[: len(operands)], gx_out, *io)

        shapes = [pltpu.VMEM((slots, rows, width), BF16), pltpu.VMEM((slots, 8, units), F32)] if t == 0 else []
        *grads, result = call(backward_step, [own, arriving, *operands], shapes + [struct(rows, width)], "backward", kept=grads)
        input_grads.append(result)
        if t + 1 < ticks:
            arriving = lax.ppermute(result, "section", swapped)
    gp_s, gu_s, gy_s, vec_s = grads
    order = list(range(len(bits)))

    def summed(full):
        keep, send = parted(full, 0, bits[0])
        return halving_sum(keep, send, order, count, bits, F32)

    both = jnp.concatenate([plain_grads(hidden_s, gy_s, count), plain_grads(mixed_s, gy_s, count)], axis=1)
    down, up, qkv = summed(both), summed(plain_grads(nb_s, gu_s, count)), summed(plain_grads(na_s, gp_s, count))
    tall = units // count
    totals = jnp.sum(vec_s, axis=0)
    sums = [totals[i, :width] for i in range(5)] + [totals[5], totals[6, : 3 * width]]
    return finals[1:], input_grads[1:], sums, down[:tall], down[tall:], up, qkv


def per_device(boundary, lengths, *params):
    section = lax.axis_index("section")
    count = lax.axis_size("dp")
    bits = [(lax.axis_index("dp") >> b) & 1 for b in range(count.bit_length() - 1)]
    slots = lengths.shape[0]
    width = boundary.shape[2]
    units = params[8].shape[2]
    tables = [jnp.asarray(table) for table in rotary_lanes(boundary.shape[1] // slots, 2 * HEAD)]
    swapped = [(0, 1), (1, 0)]
    if count == 16 and slots == 2 and width % 768 == 0:
        results = paired_gradients(boundary, lengths, params, tables, swapped)
        return tuple(result[None] for result in results)
    finals, input_grads, sums, down, proj, up, qkv = plain_gradients(
        boundary, lengths, params, tables, swapped, bits
    )
    small = jnp.concatenate([piece.reshape(count, -1) for piece in sums], axis=1)
    small = halving_sum(*parted(small, 0, bits[0]), list(range(len(bits))), count, bits, F32)
    low, tall = width // count, units // count
    gain_a, shift_a, gain_b, shift_b, bias_y, bias_up, bias_qkv = jnp.split(small, np.cumsum([low] * 5 + [tall]), axis=0)
    joined = jnp.where(section == 0, jnp.concatenate(input_grads, axis=0), jnp.concatenate(finals, axis=0))
    results = (joined, gain_a, shift_a, qkv, bias_qkv, proj, bias_y, gain_b, shift_b, up, bias_up, down, bias_y)
    return tuple(result[None] for result in results)


def solution(mesh):
    split = P("section", "dp")
    deep = P("section", "dp", None)
    flat, matrix = P("section", None), P("section", None, None)
    return jax.shard_map(
        per_device,
        mesh=mesh,
        in_specs=(deep, P("dp"), flat, flat, matrix, flat, matrix, flat, flat, flat, matrix, flat, matrix, flat),
        out_specs=(deep, split, split, deep, split, deep, split, split, split, deep, split, deep, split),
        check_vma=False,
    )
```

```python
import functools
import math

import jax
import jax.numpy as jnp
import numpy as np
from jax import lax
from jax.experimental import pallas as pl
from jax.experimental.pallas import tpu as pltpu
from jax.sharding import PartitionSpec as P

HEAD = 64
LANES = 256
CHUNK = 512
EPS = 1e-05
NEG_FILL = -1e30
VMEM_BYTES = 7 * 1024 * 1024
FIRST_VMEM_BYTES = 7 * 1024 * 1024
F32 = jnp.float32
BF16 = jnp.bfloat16


def dot(left, right):
    return jnp.dot(left, right, preferred_element_type=F32)


def dot_nt(left, right):
    return lax.dot_general(left, right, (((1,), (1,)), ((), ())), preferred_element_type=F32)


def normalised(values):
    centred = values - jnp.mean(values, axis=-1, keepdims=True)
    variance = jnp.mean(centred * centred, axis=-1, keepdims=True)
    scale = lax.rsqrt(variance + EPS)
    return centred * scale, scale


def gelu_parts(values):
    integral = 0.5 + 0.5 * lax.erf(values * math.sqrt(0.5))
    bell = jnp.exp(values * values * -0.5)
    return values * integral, integral + values * bell * (1.0 / math.sqrt(2.0 * math.pi))


def rotary_lanes(seq_len, lanes):
    rot_dims = HEAD // 4
    half = rot_dims // 2
    frequency = np.float32(10000.0) ** (-(np.arange(half, dtype=np.float32) * np.float32(2.0) / np.float32(rot_dims)))
    angles = np.arange(seq_len, dtype=np.float32)[:, None] * frequency.astype(np.float32)[None, :]
    cosine, sine = np.cos(angles).astype(np.float32), np.sin(angles).astype(np.float32)
    same = np.ones((seq_len, HEAD), np.float32)
    later = np.zeros((seq_len, HEAD), np.float32)
    earlier = np.zeros((seq_len, HEAD), np.float32)
    same[:, :half] = cosine
    same[:, half:rot_dims] = cosine
    later[:, :half] = -sine
    earlier[:, half:rot_dims] = sine
    return [np.tile(t, (1, lanes // HEAD)) for t in (same, later, earlier)]


def turned(values, same, later, earlier, sign):
    half = HEAD // 8
    width = values.shape[1]
    same, later, earlier = (jnp.concatenate([t] * (width // t.shape[1]), axis=1) for t in (same, later, earlier))
    ahead = pltpu.roll(values, width - half, 1)
    behind = pltpu.roll(values, half, 1)
    if sign > 0:
        return values * same + ahead * later + behind * earlier
    return values * same - ahead * later - behind * earlier


def blocked_bias(rows, length):
    out = []
    for start in range(0, rows, 128):
        keys = start + 128
        key_pos = lax.broadcasted_iota(jnp.int32, (keys, 2 * 128), 0)
        query_pos = start + (lax.broadcasted_iota(jnp.int32, (keys, 2 * 128), 1) & 127)
        out.append(jnp.where((key_pos <= query_pos) & (key_pos < length), 0.0, NEG_FILL))
    return out


def heads_apart(block, lane):
    zero = jnp.zeros_like(block)
    return jnp.concatenate([jnp.where(lane < HEAD, block, zero), jnp.where(lane < HEAD, zero, block)], axis=0)


def dot_tn(left, right):
    return lax.dot_general(left, right, (((0,), (0,)), ((), ())), preferred_element_type=F32)


def probs_rows(block):
    start = 128 * (block * (block + 1) // 2)
    return slice(start, start + 128 * (block + 1))


def some(offset, size):
    return slice(offset, offset + size) if isinstance(offset, int) else pl.ds(pl.multiple_of(offset, 128), size)


def spans(pair, width):
    return [slice(b * width + pair * 2 * HEAD, b * width + (pair + 1) * 2 * HEAD) for b in range(3)]


def forward_units(slot, length, ready, na, nb, wqkv, bqkv, wu, bu, tables, qkv, pt, mixed, hidden, slope, low_head, low_unit, lanes):
    rows = qkv.shape[1]
    whole_width, width = wqkv.shape[1], qkv.shape[2] // 3
    pairs = width // (2 * HEAD)
    chunk = hidden.shape[2] // pairs
    biases = blocked_bias(rows, length)
    lane = lax.broadcasted_iota(jnp.int32, (128, 2 * HEAD), 1)
    per = lanes // (2 * HEAD)
    for pair in range(pairs):
        if pair % per == 0:
            low = pair * 2 * HEAD
            ready("qkv", pair // per)

            def packed(block):
                at = some(block * whole_width + low_head + low, lanes)
                return dot(na[slot], wqkv[0, :, at]) + bqkv[:, at].astype(F32)

            qkv[slot, :, low : low + lanes] = (turned(packed(0), *tables, 1) * (HEAD**-0.5)).astype(BF16)
            qkv[slot, :, width + low : width + low + lanes] = turned(packed(1), *tables, 1).astype(BF16)
            qkv[slot, :, 2 * width + low : 2 * width + low + lanes] = packed(2).astype(BF16)
        span, span_k, span_v = spans(pair, width)
        all_scores = []
        for block, start in enumerate(range(0, rows, 128)):
            keys = start + 128
            q2 = heads_apart(qkv[slot, start:keys, span], lane)
            all_scores.append(dot_nt(qkv[slot, :keys, span_k], q2) + biases[block])
        ready("up", pair)
        there = some(low_unit + pair * chunk, chunk)
        up = dot(nb[slot], wu[0, :, there]) + bu[:, there].astype(F32)
        for block, start in enumerate(range(0, rows, 128)):
            keys = start + 128
            scores = all_scores[block]
            exponent = jnp.exp(scores - jnp.max(scores, axis=0, keepdims=True))
            probs = (exponent * (1.0 / jnp.sum(exponent, axis=0, keepdims=True))).astype(BF16)
            pt[slot, pair, probs_rows(block)] = probs
            both = dot_tn(probs, qkv[slot, :keys, span_v])
            mixed[slot, start:keys, span] = jnp.where(lane < HEAD, both[:128], both[128:]).astype(BF16)
        here = slice(pair * chunk, pair * chunk + chunk)
        hidden_f32, slope_f32 = gelu_parts(up)
        hidden[slot, :, here] = hidden_f32.astype(BF16)
        slope[slot, :, here] = slope_f32.astype(BF16)


def backward_units(slot, gy, wp, wd, tables, pt, qkv, slope, low_head, low_unit, lanes):
    rows = qkv.shape[1]
    width = qkv.shape[2] // 3
    pairs = width // (2 * HEAD)
    chunk = slope.shape[2] // pairs
    lane = lax.broadcasted_iota(jnp.int32, (128, 2 * HEAD), 1)
    per = lanes // (2 * HEAD)
    for pair in range(pairs):
        if pair % per == 0:
            gm_group = dot_nt(gy(), wp[0, some(low_head + pair * 2 * HEAD, lanes), :]).astype(BF16)
            group_q, group_k = [], []
        span, span_k, span_v = spans(pair, width)
        gm = gm_group[:, (pair % per) * 2 * HEAD : (pair % per + 1) * 2 * HEAD]
        gv_sum, gk_sum, gq_blocks = None, None, []
        for block, start in enumerate(range(0, rows, 128)):
            keys = start + 128
            gm2 = heads_apart(gm[start:keys], lane)
            q2 = heads_apart(qkv[slot, start:keys, span], lane)
            probs = pt[slot, pair, probs_rows(block)]
            weighted = probs.astype(F32) * dot_nt(qkv[slot, :keys, span_v], gm2)
            inner = jnp.sum(weighted, axis=0, keepdims=True)
            gs = (weighted - probs.astype(F32) * inner).astype(BF16)
            gv_part = dot(probs, gm2)
            gk_part = dot(gs, q2)
            gq_part = dot_tn(gs, qkv[slot, :keys, span_k])
            gq_blocks.append(jnp.where(lane < HEAD, gq_part[:128], gq_part[128:]))
            if gv_sum is None:
                gv_sum, gk_sum = gv_part, gk_part
            else:
                gv_sum = jnp.concatenate([gv_sum + gv_part[:start], gv_part[start:]], axis=0)
                gk_sum = jnp.concatenate([gk_sum + gk_part[:start], gk_part[start:]], axis=0)
        qkv[slot, :, span_v] = gv_sum.astype(BF16)
        group_q.append(jnp.concatenate(gq_blocks, axis=0))
        group_k.append(gk_sum)
        if pair % per == per - 1:
            low = pair // per * lanes
            gq = turned(jnp.concatenate(group_q, axis=1) * (HEAD**-0.5), *tables, -1)
            qkv[slot, :, low : low + lanes] = gq.astype(BF16)
            gk = turned(jnp.concatenate(group_k, axis=1), *tables, -1)
            qkv[slot, :, width + low : width + low + lanes] = gk.astype(BF16)
        here = slice(pair * chunk, pair * chunk + chunk)
        grad = dot_nt(gy(), wd[0, some(low_unit + pair * chunk, chunk), :])
        slope[slot, :, here] = (grad * slope[slot, :, here].astype(F32)).astype(BF16)


def forward_body(
    slot, length, inputs, ready, own, gain_a, shift_a, gain_b, shift_b, wqkv, bqkv, wp, bp, wu, bu, wd, bd, same, later, earlier,
    y_out, x_out, na_out, nb_out, qkv_out, pt_out, mixed_out, hidden_out, slope_out,
):
    ready("small", 0)
    x_low = inputs()
    x_out[slot] = x_low
    xhat, _ = normalised(x_low.astype(F32))
    na_out[slot] = (xhat * gain_a[...].astype(F32) + shift_a[...].astype(F32)).astype(BF16)
    nb_out[slot] = (xhat * gain_b[...].astype(F32) + shift_b[...].astype(F32)).astype(BF16)
    tables = (same[...], later[...], earlier[...])
    forward_units(
        slot, length, ready, na_out, nb_out, wqkv, bqkv, wu, bu, tables, qkv_out, pt_out, mixed_out, hidden_out, slope_out, 0, 0, LANES
    )
    ready("rest", 0)
    total = x_out[slot].astype(F32) + (bp[...].astype(F32) + bd[...].astype(F32))
    y_out[...] = (total + dot(mixed_out[slot], wp[0]) + dot(hidden_out[slot], wd[0])).astype(BF16)


def backward_body(
    slot, gy_source, x_in, gain_a, gain_b, wqkv, wp, wu, wd, same, later, earlier, pt_in, gx_out, qkv_io, slope_io, gy_out, vec_out
):
    width = gx_out.shape[1]
    gy_out[slot] = gy_source()
    tables = (same[...], later[...], earlier[...])
    backward_units(slot, lambda: gy_out[slot], wp, wd, tables, pt_in, qkv_io, slope_io, 0, 0, LANES)
    grad_b = dot_nt(slope_io[slot], wu[0])
    grad_a = dot_nt(qkv_io[slot], wqkv[0])
    xhat, scale = normalised(x_in[slot].astype(F32))
    norm_terms = (grad_a * xhat, grad_a, grad_b * xhat, grad_b, gy_out[slot].astype(F32))
    for row, terms in enumerate(norm_terms):
        vec_out[slot, row : row + 1, :width] = jnp.sum(terms, axis=0, keepdims=True)
    vec_out[slot, 5:6, :] = jnp.sum(slope_io[slot].astype(F32), axis=0, keepdims=True)
    vec_out[slot, 6:7, : 3 * width] = jnp.sum(qkv_io[slot].astype(F32), axis=0, keepdims=True)
    both = grad_a * gain_a[...].astype(F32) + grad_b * gain_b[...].astype(F32)
    inner = jnp.mean(both * xhat, axis=-1, keepdims=True)
    gx = gy_out[slot].astype(F32) + scale * (both - jnp.mean(both, axis=-1, keepdims=True) - xhat * inner)
    gx_out[...] = gx.astype(BF16)


def forward_first_kernel(tick, lengths, *refs):
    count = 17
    sources, held, outs, sems = refs[:count], refs[count : 2 * count], refs[2 * count : -1], refs[-1]
    copies = []
    waits = {}

    def fetch(name, part, index, at):
        source, target = (sources[index], held[index]) if at is None else (sources[index].at[at], held[index].at[at])
        copy = pltpu.make_async_copy(source, target, sems.at[len(copies)])
        copies.append(copy)
        waits.setdefault((name, part), []).append(copy)

    (own, gain_a, shift_a, gain_b, shift_b, wqkv, bqkv, wp, bp, wu, bu, wd, bd, same, later, earlier, _) = range(count)
    width = sources[wp].shape[1]
    units = sources[wu].shape[2]
    pairs = width // (2 * HEAD)
    groups = width // LANES
    for index in (own, gain_a, shift_a, gain_b, shift_b, bqkv, bp, bu, bd, same, later, earlier):
        fetch("small", 0, index, None)
    for pair in range(pairs):
        if pair * groups % pairs == 0:
            group = pair * groups // pairs
            for block in range(3):
                fetch("qkv", group, wqkv, (slice(None), slice(None), pl.ds(block * width + group * LANES, LANES)))
        fetch("up", pair, wu, (slice(None), slice(None), pl.ds(pair * (units // pairs), units // pairs)))
    fetch("rest", 0, wp, None)
    fetch("rest", 0, wd, None)
    for copy in copies:
        copy.start()

    def ready(name, part):
        for copy in waits[(name, part)]:
            copy.wait()

    section = lax.axis_index("section")
    slots = held[own].shape[0]
    slot = jnp.clip(tick - section, 0, slots - 1)
    forward_body(slot, lengths[slot], lambda: held[own][slot], ready, *held[:-1], *outs)


def backward_body(
    slot, gy_source, x_in, gain_a, gain_b, wqkv, wp, wu, wd, same, later, earlier,
    pt_in, gx_out, qkv_io, slope_io, gy_out, vec_out,
):
    rows, width = gx_out.shape
    units = wu.shape[2]
    pairs = width // (2 * HEAD)
    chunk = units // pairs
    gy_out[slot] = gy_source()
    lane = lax.broadcasted_iota(jnp.int32, (128, 2 * HEAD), 1)
    tables = (same[...], later[...], earlier[...])
    per = LANES // (2 * HEAD)
    for pair in range(pairs):
        if pair % per == 0:
            gm_group = dot_nt(gy_out[slot], wp[0, pair * 2 * HEAD : pair * 2 * HEAD + LANES, :]).astype(BF16)
            group_q, group_k = [], []
        span, span_k, span_v = (slice(b * width + pair * 2 * HEAD, b * width + (pair + 1) * 2 * HEAD) for b in range(3))
        gm = gm_group[:, (pair % per) * 2 * HEAD : (pair % per + 1) * 2 * HEAD]
        gv_sum, gk_sum, gq_blocks = None, None, []
        for block, start in enumerate(range(0, rows, 128)):
            keys = start + 128
            gm2 = heads_apart(gm[start:keys], lane)
            q2 = heads_apart(qkv_io[slot, start:keys, span], lane)
            pt = pt_in[slot, pair, probs_rows(block)]
            weighted = pt.astype(F32) * dot_nt(qkv_io[slot, :keys, span_v], gm2)
            inner = jnp.sum(weighted, axis=0, keepdims=True)
            gs = (weighted - pt.astype(F32) * inner).astype(BF16)
            gv_part = dot(pt, gm2)
            gk_part = dot(gs, q2)
            gq_part = dot_tn(gs, qkv_io[slot, :keys, span_k])
            gq_blocks.append(jnp.where(lane < HEAD, gq_part[:128], gq_part[128:]))
            if gv_sum is None:
                gv_sum, gk_sum = gv_part, gk_part
            else:
                gv_sum = jnp.concatenate([gv_sum + gv_part[:start], gv_part[start:]], axis=0)
                gk_sum = jnp.concatenate([gk_sum + gk_part[:start], gk_part[start:]], axis=0)
        qkv_io[slot, :, span_v] = gv_sum.astype(BF16)
        group_q.append(jnp.concatenate(gq_blocks, axis=0))
        group_k.append(gk_sum)
        if pair % per == per - 1:
            low = pair // per * LANES
            gq = turned(jnp.concatenate(group_q, axis=1) * (HEAD**-0.5), *tables, -1)
            qkv_io[slot, :, low : low + LANES] = gq.astype(BF16)
            gk = turned(jnp.concatenate(group_k, axis=1), *tables, -1)
            qkv_io[slot, :, width + low : width + low + LANES] = gk.astype(BF16)
        at = slice(pair * chunk, pair * chunk + chunk)
        slope_io[slot, :, at] = (dot_nt(gy_out[slot], wd[0, at, :]) * slope_io[slot, :, at].astype(F32)).astype(BF16)
    grad_b = dot_nt(slope_io[slot], wu[0])
    grad_a = dot_nt(qkv_io[slot], wqkv[0])
    xhat, scale = normalised(x_in[slot].astype(F32))
    norm_terms = (grad_a * xhat, grad_a, grad_b * xhat, grad_b, gy_out[slot].astype(F32))
    for row, terms in enumerate(norm_terms):
        vec_out[slot, row : row + 1, :width] = jnp.sum(terms, axis=0, keepdims=True)
    vec_out[slot, 5:6, :] = jnp.sum(slope_io[slot].astype(F32), axis=0, keepdims=True)
    vec_out[slot, 6:7, : 3 * width] = jnp.sum(qkv_io[slot].astype(F32), axis=0, keepdims=True)
    both = grad_a * gain_a[...].astype(F32) + grad_b * gain_b[...].astype(F32)
    inner = jnp.mean(both * xhat, axis=-1, keepdims=True)
    gx = gy_out[slot].astype(F32) + scale * (both - jnp.mean(both, axis=-1, keepdims=True) - xhat * inner)
    gx_out[...] = gx.astype(BF16)


VM = pl.BlockSpec(memory_space=pltpu.VMEM)
HBM = pl.BlockSpec(memory_space=pl.ANY)


def call(kernel, operands, out_shape, name, kept=(), scratch=(), flops=1 << 20, after=()):
    count = len(operands)
    after = list(after)

    def body(*refs):
        kernel(*refs[:count], *refs[count + len(kept) + len(after) :])

    return pl.pallas_call(
        body,
        in_specs=[pl.BlockSpec(memory_space=pltpu.SMEM) if o.dtype == jnp.int32 else VM for o in operands] + [VM] * len(kept) + [HBM] * len(after),
        out_specs=[VM] * (len(kept) + len(out_shape)),
        out_shape=[pltpu.VMEM(array.shape, array.dtype) for array in kept] + list(out_shape),
        input_output_aliases={count + i: i for i in range(len(kept))},
        scratch_shapes=list(scratch),
        compiler_params=pltpu.CompilerParams(vmem_limit_bytes=VMEM_BYTES),
        cost_estimate=pl.CostEstimate(flops=flops, bytes_accessed=1 << 16, transcendentals=0),
        name=name,
    )(*operands, *[pltpu.with_memory_space_constraint(array, pltpu.VMEM) for array in kept], *after)


def shape_of(array):
    return jax.ShapeDtypeStruct(array.shape, array.dtype)


def forward_shapes(local_rows, params):
    slots, rows, width = local_rows.shape
    units = params[8].shape[2]
    blocks = rows // 128
    probs = (slots, width // (2 * HEAD), 128 * (blocks * (blocks + 1) // 2), 2 * 128)
    columns = [width, width, width, 3 * width, None, width, units, units]
    return [jax.ShapeDtypeStruct((rows, width), BF16)] + [
        pltpu.VMEM(probs if n is None else (slots, rows, n), BF16) for n in columns
    ]


def forward_first(lengths, local_rows, params, tables):
    (gain_a, shift_a, w_qkv, b_qkv, w_proj, b_proj, gain_b, shift_b, w_up, b_up, w_down, b_down) = params
    held = [local_rows, gain_a, shift_a, gain_b, shift_b, w_qkv, b_qkv, w_proj, b_proj, w_up, b_up, w_down, b_down] + list(tables)
    shapes = [shape_of(array) for array in held] + forward_shapes(local_rows, params)

    def kernel(lengths_ref, *refs):
        count = len(held)
        forward_first_kernel(0, lengths_ref, *refs[:count], None, *refs[count : 2 * count], None, *refs[2 * count :])

    outs = pl.pallas_call(
        kernel,
        in_specs=[pl.BlockSpec(memory_space=pltpu.SMEM)] + [pl.BlockSpec(memory_space=pltpu.HBM)] * len(held),
        out_specs=[VM] * len(shapes),
        out_shape=shapes,
        scratch_shapes=[pltpu.SemaphoreType.DMA((40,))],
        compiler_params=pltpu.CompilerParams(vmem_limit_bytes=FIRST_VMEM_BYTES),
        cost_estimate=pl.CostEstimate(flops=1 << 20, bytes_accessed=1 << 16, transcendentals=0),
        name="layer_forward_first",
    )(lengths, *[pltpu.with_memory_space_constraint(array, pltpu.HBM) for array in held])
    count = len(held)
    return outs[count], outs[count + 1 :], outs[:count]


def swap(shard, bit, count):
    return lax.ppermute(shard, "dp", [(i, i ^ (1 << bit)) for i in range(count)])


def parted(values, position, mine):
    count = values.shape[0]
    shaped = values.reshape((count >> (position + 1), 2, 1 << position) + values.shape[1:])
    out = []
    for side in (mine, 1 - mine):
        piece = lax.dynamic_index_in_dim(shaped, side, axis=1, keepdims=False)
        out.append(piece.reshape((count // 2,) + values.shape[1:]))
    return out


def halving_sum(keep, send, order, count, bits, final):
    left = sorted(order)
    for number, bit in enumerate(order):
        left.remove(bit)
        arrived = swap(send, bit, count)
        if number + 1 == len(order):
            return (keep.astype(F32) + arrived.astype(F32)).astype(final)[0]
        position = left.index(order[number + 1])
        keep_a, send_a = parted(keep, position, bits[order[number + 1]])
        keep_b, send_b = parted(arrived, position, bits[order[number + 1]])
        send = (send_a.astype(F32) + send_b.astype(F32)).astype(send_a.dtype)
        keep = (keep_a.astype(F32) + keep_b.astype(F32)).astype(send_a.dtype)


def plain_grads(left, right, count):
    rows = left.shape[0] * left.shape[1]
    product = lax.dot_general(
        left.reshape(rows, -1), right.reshape(rows, -1), (((0,), (0,)), ((), ())), preferred_element_type=F32
    ).astype(BF16)
    return product.reshape(count, product.shape[0] // count, product.shape[1])


def partner_forward(half, lengths, rows_of, gain_a, shift_a, gain_b, shift_b, wqkv, bqkv, wu, bu, tables, nap, nbp, qkvp, ptp, mixedp, hidp, slopep):
    for s in range(nap.shape[0]):
        xhat, _ = normalised(rows_of(s).astype(F32))
        nap[s] = (xhat * gain_a[...].astype(F32) + shift_a[...].astype(F32)).astype(BF16)
        nbp[s] = (xhat * gain_b[...].astype(F32) + shift_b[...].astype(F32)).astype(BF16)
        lanes = mixedp.shape[2]
        forward_units(
            s, lengths[s], lambda name, part: None, nap, nbp, wqkv, bqkv, wu, bu, tables, qkvp, ptp, mixedp, hidp, slopep,
            half * lanes, half * hidp.shape[2], lanes,
        )


def partner_backward(s, half, gy, wp, wd, tables, ptp, qkvp, slopep):
    lanes = qkvp.shape[2] // 3
    backward_units(s, gy, wp, wd, tables, ptp, qkvp, slopep, half * lanes, half * slopep.shape[2], lanes)


SUM_FLOPS = 6 << 30
ORDERS = {"down": (0, 1, 2), "up": (1, 2, 0), "attn": (2, 0, 1)}


def dp_bit(bit):
    return (lax.axis_index("dp") >> bit) & 1


def eighth_row(chunk, order, rows):
    first, second, third = ((chunk >> bit) & 1 for bit in order)
    return ((first ^ dp_bit(order[0])) * 4 + second * 2 + third) * rows


def row_slice(start, rows):
    return pl.ds(pl.multiple_of(start, 16), rows)


def flat_rows(ref, at=slice(None)):
    values = ref[:, :, at]
    return values.reshape(values.shape[0] * values.shape[1], values.shape[2])


def ones_dot(values):
    return dot(jnp.ones((16, values.shape[0]), BF16), values)[:8]


def sixteenths(ref, left, order, tokens_from):
    turned_ref = flat_rows(ref).T
    low = turned_ref.shape[0] // 16
    for chunk in range(16):
        start = eighth_row(chunk & 7, order, 2 * low) + (chunk >> 3) * low
        left[row_slice(start, low), tokens_from : tokens_from + turned_ref.shape[1]] = turned_ref[chunk * low : chunk * low + low]


def eighths(turned_rows, left, order, tokens_from):
    low = turned_rows.shape[0] // 8
    for chunk in range(8):
        left[row_slice(eighth_row(chunk, order, low), low), tokens_from : tokens_from + turned_rows.shape[1]] = turned_rows[
            chunk * low : chunk * low + low
        ]


def own_group_kernel(nb, na, gu, gp, hidden, mixed, gy, vec, up_own, attn_own, down_own, left, left_mixed, left_down):
    half = dp_bit(3)
    units, rows = up_own.shape[2], up_own.shape[1]
    width, lanes = na.shape[2], attn_own.shape[2] // 3
    low = rows // 2
    sixteenths(nb, left, ORDERS["up"], 0)
    for start in range(0, units, 512):
        product = dot(left[...], flat_rows(gu, some(half * units + start, 512)))
        up_own[:, :, start : start + 512] = product.reshape(8, rows, 512)
    order = ORDERS["attn"]
    sixteenths(na, left, order, 0)
    for block in range(3):
        product = dot(left[...], flat_rows(gp, some(block * width + half * lanes, lanes)))
        attn_own[:, :rows, block * lanes : block * lanes + lanes] = product.reshape(8, rows, lanes)
    grad = flat_rows(gy)
    eighths(flat_rows(mixed, some(half * lanes, lanes)).T, left_mixed, order, 0)
    attn_own[:, rows:, :width] = dot(left_mixed[...], grad).reshape(8, low, width)
    row_index = lax.broadcasted_iota(jnp.int32, (16, lanes), 0)
    totals = vec[0] + vec[1]
    sums = [totals[i : i + 1, :width] for i in range(5)] + [totals[5:6], totals[6:7, : 3 * width]]
    for chunk in range(16):
        block = jnp.zeros((16, lanes), F32)
        for row, values in enumerate(sums):
            size = values.shape[1] // 16
            piece = jnp.concatenate([values[:, chunk * size : chunk * size + size], jnp.zeros((1, lanes - size), F32)], axis=1)
            block = jnp.where(row_index == row, jnp.broadcast_to(piece, (16, lanes)), block)
        place_at = slice(rows + (chunk >> 3) * 16, rows + (chunk >> 3) * 16 + 16)
        attn_own[eighth_row(chunk & 7, order, 1), place_at, width:] = block
    eighths(flat_rows(hidden, some(half * units, units)).T, left_down, ORDERS["down"], 0)
    size = units // 4
    for part in range(4):
        product = dot(left_down[part * size : part * size + size], grad)
        down_own[part * 2 : part * 2 + 2] = product.reshape(2, size // 2, width)


def up_group_kernel(nbp, gup, up_own, keep, send, left):
    units = gup.shape[2]
    sixteenths(nbp, left, ORDERS["up"], 0)
    rows = left.shape[0] // 8
    for low in range(0, units, 512):
        at = slice(low, low + 512)
        product = (up_own[:, :, at] + dot(left[...], flat_rows(gup, at)).reshape(8, rows, 512)).astype(BF16)
        keep[:, :, at] = product[:4]
        send[:, :, at] = product[4:]


def attn_group_kernel(nap, gpp, mixedp, gyp_of, attn_own, keep, send, left, left_mixed):
    lanes = mixedp.shape[2]
    width = nap.shape[2]
    order = ORDERS["attn"]
    sixteenths(nap, left, order, 0)
    rows = left.shape[0] // 8
    for block in range(3):
        at = slice(block * lanes, block * lanes + lanes)
        product = (attn_own[:, :rows, at] + dot(left[...], flat_rows(gpp, at)).reshape(8, rows, lanes)).astype(BF16)
        keep[:, :rows, at] = product[:4]
        send[:, :rows, at] = product[4:]
    eighths(flat_rows(mixedp).T, left_mixed, order, 0)
    other_gy = jnp.concatenate([gyp_of(s) for s in range(nap.shape[0])], axis=0)
    low = left_mixed.shape[0] // 8
    product = (attn_own[:, rows:, :width] + dot(left_mixed[...], other_gy).reshape(8, low, width)).astype(BF16)
    keep[:, rows:, :width] = product[:4]
    send[:, rows:, :width] = product[4:]
    keep[:, rows:, width:] = attn_own[:4, rows:, width:].astype(BF16)
    send[:, rows:, width:] = attn_own[4:, rows:, width:].astype(BF16)


def down_group_kernel(hidp, gyp_of, down_own, keep, send, left):
    units = hidp.shape[2]
    eighths(flat_rows(hidp).T, left, ORDERS["down"], 0)
    other_gy = jnp.concatenate([gyp_of(s) for s in range(hidp.shape[0])], axis=0)
    size = units // 2
    for side, out in enumerate((keep, send)):
        product = dot(left[side * size : side * size + size], other_gy).reshape(out.shape)
        out[...] = (down_own[side * 4 : side * 4 + 4] + product).astype(BF16)


def plus(left, right):
    return left.astype(F32) + right.astype(F32)


def add_kernel(bit, keep, arrived, keep_out, send_out):
    size = keep_out.shape[0]
    mine = dp_bit(bit) * size
    keep_out[...] = plus(keep[pl.ds(mine, size)], arrived[pl.ds(mine, size)]).astype(BF16)
    send_out[...] = plus(keep[pl.ds(size - mine, size)], arrived[pl.ds(size - mine, size)]).astype(BF16)


def swap_over(shard, bit, sections=(0, 1)):
    count = lax.axis_size("dp")
    pairs = [(s * count + i, s * count + (i ^ (1 << bit))) for s in sections for i in range(count)]
    return lax.ppermute(shard, ("section", "dp"), pairs)


def cross_swap(shard, section, bit):
    count = lax.axis_size("dp")
    return lax.ppermute(shard, ("section", "dp"), [(section * count + i, (1 - section) * count + (i ^ (1 << bit))) for i in range(count)])


def struct(*shape, dtype=BF16):
    return jax.ShapeDtypeStruct(shape, dtype)


def halved(parts, order, stage, name, after=()):
    keep, send = parts
    arrived = swap_over(send, order[stage])
    shape = (keep.shape[0] // 2,) + keep.shape[1:]
    return call(functools.partial(add_kernel, order[stage + 1]), [keep, arrived], [struct(*shape)] * 2, name, after=after, flops=SUM_FLOPS)


def down_sum_kernel(keep, arrived, out):
    out[...] = plus(keep[0], arrived[0])


def halves_sum_kernel(up_keep, up_arrived, attn_keep, attn_arrived, up_mine, qkv_mine, small_mine, proj, other):
    half = dp_bit(3)
    low = up_mine.shape[0]
    units = up_mine.shape[1]
    width = proj.shape[1]
    mine, theirs = row_slice(half * low, low), row_slice((1 - half) * low, low)
    up_mine[...] = plus(up_keep[0, mine], up_arrived[0, mine])
    other[:, :units] = plus(up_keep[0, theirs], up_arrived[0, theirs]).astype(BF16)
    qkv_mine[...] = plus(attn_keep[0, mine], attn_arrived[0, mine])
    other[:, units : units + qkv_mine.shape[1]] = plus(attn_keep[0, theirs], attn_arrived[0, theirs]).astype(BF16)
    proj[...] = plus(attn_keep[0, 2 * low :, :width], attn_arrived[0, 2 * low :, :width])
    mine, theirs = row_slice(2 * low + half * 16, 16), row_slice(2 * low + (1 - half) * 16, 16)
    small_mine[...] = plus(attn_keep[0, mine, width:], attn_arrived[0, mine, width:])
    small = plus(attn_keep[0, theirs, width:], attn_arrived[0, theirs, width:]).astype(BF16)
    for part in range(small.shape[1] // 128):
        other[part * 16 : part * 16 + 16, other.shape[1] - 128 :] = small[:, part * 128 : part * 128 + 128]


def joined_kernel(up_mine, qkv_mine, small_mine, other, up, qkv, *vectors):
    half = dp_bit(3)
    low = up_mine.shape[0]
    units = up_mine.shape[1]
    lanes = qkv_mine.shape[1] // 3
    up[:, some(half * units, units)] = up_mine[...]
    up[:, some((1 - half) * units, units)] = other[:, :units].astype(F32)
    for block in range(3):
        at = slice(block * lanes, block * lanes + lanes)
        qkv[:, some((2 * block + half) * lanes, lanes)] = qkv_mine[:, at]
        qkv[:, some((2 * block + 1 - half) * lanes, lanes)] = other[:, units + block * lanes : units + (block + 1) * lanes].astype(F32)
    rest = other[:, other.shape[1] - 128 :].astype(F32)
    small = small_mine[...] + jnp.concatenate([rest[part : part + 16] for part in range(0, low, 16)], axis=1)
    for row, out in zip((0, 1, 2, 3, 4, 4, 5, 6), vectors):
        out[...] = small[row : row + 1, : out.shape[1]]


def paired_gradients(boundary, lengths, params, tables, swapped):
    slots = lengths.shape[0]
    width = boundary.shape[2]
    rows = boundary.shape[1] // slots
    units = params[8].shape[2]
    local_rows = boundary.reshape(slots, rows, width)
    low, tall = width // 16, units // 16
    tokens = slots * rows

    partner_lengths = swap_over(lengths, 3)
    cut = rows * slots * 3 // 4
    other_a = swap_over(boundary[0, :cut], 3, (0,))
    other_b = swap_over(boundary[0, cut:], 3, (0,))
    other_gy = swap_over(local_rows, 3, (1,))
    result_0, saved, held = forward_first(lengths, local_rows, params, tables)
    own, gain_a, shift_a, gain_b, shift_b, w_qkv, b_qkv, w_proj, b_proj, w_up, b_up, w_down, b_down, *tabs = held
    arrived_1 = lax.ppermute(result_0, "section", swapped)
    count = len(held)

    def forward_both(lengths_ref, arriving, *refs):
        section = lax.axis_index("section")
        slot = 1 - section
        inputs = lambda: jnp.where(section == 0, refs[0][slot], arriving[...])
        outs = refs[count:]
        forward_body(slot, lengths_ref[slot], inputs, lambda name, part: None, *refs[:count], outs[-1], *outs[:-1])

    *saved, result_1 = call(forward_both, [lengths, arrived_1, *held], [struct(rows, width)], "forward_1", kept=saved, after=[partner_lengths, other_a])
    arrived_2 = lax.ppermute(result_1, "section", swapped)

    def forward_last(lengths_ref, arriving, *refs):
        outs = refs[count:]
        slot = slots - 1

        @pl.when(lax.axis_index("section") == 1)
        def _():
            forward_body(
                slot, lengths_ref[slot], lambda: arriving[...], lambda name, part: None, *refs[:count], outs[len(saved)], *outs[: len(saved)]
            )

    *saved, result_2 = call(forward_last, [lengths, arrived_2, *held], [struct(rows, width)], "forward_2", kept=saved, after=[other_b])
    x_s, na_s, nb_s, qkv_s, pt_s, mixed_s, hidden_s, slope_s = saved
    partner_x = swap_over(x_s, 3, (1,))

    back_operands = [x_s, gain_a, gain_b, w_qkv, w_proj, w_up, w_down, *tabs, pt_s]
    back_count = len(back_operands)
    shared_operands = [gain_a, shift_a, gain_b, shift_b, w_qkv, b_qkv, w_up, b_up, *tabs]
    shared_count = len(shared_operands)
    shared_shapes = [
        pltpu.VMEM(shape, BF16)
        for shape in (
            (slots, rows, width), (slots, rows, width), (slots, rows, 3 * width // 2), (slots, pt_s.shape[1] // 2) + pt_s.shape[2:],
            (slots, rows, width // 2), (slots, rows, units // 2), (slots, rows, units // 2),
        )
    ]

    def share(lengths_ref, rows_of, refs, outs):
        weights, tabs_refs = refs[:-3], refs[-3:]
        partner_forward(dp_bit(3), lengths_ref, rows_of, *weights, tuple(t[...] for t in tabs_refs), *outs)

    def backward_first(lengths_ref, own_ref, ref_a, ref_b, *refs):
        operands, shared, (qkv_io, slope_io, gy, vec, gx, *outs) = (
            refs[:back_count], refs[back_count : back_count + shared_count], refs[back_count + shared_count :],
        )
        section = lax.axis_index("section")

        def rows_of(s):
            low, high = s * rows, s * rows + rows
            parts = [ref_a[low : min(high, cut)], ref_b[max(low, cut) - cut : high - cut]] if high > cut else [ref_a[low:high]]
            return jnp.concatenate(parts, axis=0)

        @pl.when(section == 1)
        def _():
            backward_body(0, lambda: own_ref[0], *operands, gx, qkv_io, slope_io, gy, vec)

        @pl.when(section == 0)
        def _():
            share(lengths_ref, rows_of, shared, outs)

    outs = call(
        backward_first, [partner_lengths, own, other_a, other_b, *back_operands, *shared_operands],
        [pltpu.VMEM((slots, rows, width), BF16), pltpu.VMEM((slots, 8, units), F32), struct(rows, width)] + shared_shapes,
        "backward_0", kept=[qkv_s, slope_s],
    )
    grads, back_0, shared = outs[:4], outs[4], outs[5:]
    arrived_4 = lax.ppermute(back_0, "section", swapped)

    def backward_both(own_ref, arriving, *refs):
        section = lax.axis_index("section")
        outs = refs[back_count:]
        source = lambda: jnp.where(section == 0, arriving[...], own_ref[section])
        backward_body(section, source, *refs[:back_count], outs[-1], *outs[:-1])

    *grads, back_1 = call(backward_both, [own, arrived_4, *back_operands], [struct(rows, width)], "backward_1", kept=grads, after=[other_gy])
    arrived_5 = lax.ppermute(back_1, "section", swapped)

    def backward_last(lengths_ref, arriving, other_ref, *refs):
        operands, shared_in, (qkv_io, slope_io, gy, vec, *outs) = (
            refs[:back_count], refs[back_count : back_count + shared_count], refs[back_count + shared_count :],
        )
        section = lax.axis_index("section")

        @pl.when(section == 0)
        def _():
            backward_body(slots - 1, lambda: arriving[...], *operands, outs[-1], qkv_io, slope_io, gy, vec)

        @pl.when(section == 1)
        def _():
            share(lengths_ref, lambda s: other_ref[s], shared_in, outs[:-1])

    outs = call(
        backward_last, [partner_lengths, arrived_5, partner_x, *back_operands, *shared_operands], [struct(rows, width)],
        "backward_2", kept=[*grads, *shared],
    )
    gp_s, gu_s, gy_s, vec_s, nap, nbp, qkvp, ptp, mixedp, hidp, slopep, back_2 = outs

    partner_gy = swap_over(gy_s, 3, (0,))
    up_own, attn_own, down_own = call(
        own_group_kernel, [nb_s, na_s, gu_s, gp_s, hidden_s, mixed_s, gy_s, vec_s],
        [struct(8, 2 * low, units // 2, dtype=F32), struct(8, 3 * low, 3 * width // 2, dtype=F32), struct(8, tall, width, dtype=F32)], "own_grads",
        scratch=[pltpu.VMEM((width, tokens), BF16), pltpu.VMEM((width // 2, tokens), BF16), pltpu.VMEM((units // 2, tokens), BF16)],
    )

    def backward_shared(other_ref, partner_ref, wp, wd, same, later, earlier, ptp_ref, qkvp_ref, slopep_ref, gyp):
        gyp[...] = jnp.where(lax.axis_index("section") == 0, partner_ref[...], other_ref[...])
        tables_in = (same[...], later[...], earlier[...])
        for s in range(slots):
            partner_backward(s, dp_bit(3), lambda: gyp[s], wp, wd, tables_in, ptp_ref, qkvp_ref, slopep_ref)

    gpp, gup, gyp_s = call(
        backward_shared, [other_gy, partner_gy, w_proj, w_down, *tabs, ptp], [struct(slots, rows, width)], "backward_shared",
        kept=[qkvp, slopep], after=[up_own],
    )

    def group(rows_of_eighth, columns):
        return [struct(4, rows_of_eighth, columns)] * 2

    up = call(
        up_group_kernel, [nbp, gup, up_own], group(2 * low, units // 2), "up_grads", scratch=[pltpu.VMEM((width, tokens), BF16)]
    )

    def attn_group(nap_ref, gpp_ref, mixedp_ref, gyp, *refs):
        attn_group_kernel(nap_ref, gpp_ref, mixedp_ref, lambda s: gyp[s], *refs)

    attn = call(
        attn_group, [nap, gpp, mixedp, gyp_s, attn_own], group(3 * low, 3 * width // 2), "attn_grads",
        scratch=[pltpu.VMEM((width, tokens), BF16), pltpu.VMEM((width // 2, tokens), BF16)], after=up[:1],
    )

    def down_group(hidp_ref, gyp, *refs):
        down_group_kernel(hidp_ref, lambda s: gyp[s], *refs)

    down = call(
        down_group, [hidp, gyp_s, down_own], group(tall, width), "down_grads",
        scratch=[pltpu.VMEM((units // 2, tokens), BF16)], after=attn[:1],
    )

    up = halved(up, ORDERS["up"], 0, "up_sum_1", after=down[:1])
    attn = halved(attn, ORDERS["attn"], 0, "attn_sum_1", after=up[:1])
    down = halved(down, ORDERS["down"], 0, "down_sum_1", after=attn[:1])
    up = halved(up, ORDERS["up"], 1, "up_sum_2", after=down[:1])
    attn = halved(attn, ORDERS["attn"], 1, "attn_sum_2", after=up[:1])
    down = halved(down, ORDERS["down"], 1, "down_sum_2", after=attn[:1])
    up_last, attn_last = swap_over(up[1], ORDERS["up"][2]), swap_over(attn[1], ORDERS["attn"][2])
    up_mine, qkv_mine, small_mine, proj, others = call(
        halves_sum_kernel, [up[0], up_last, attn[0], attn_last],
        [struct(low, units // 2, dtype=F32), struct(low, 3 * width // 2, dtype=F32), struct(16, width // 2, dtype=F32),
         struct(low, width, dtype=F32), struct(low, units // 2 + 3 * width // 2 + 128)], "up_qkv_sum_3", after=down[:1],
    )
    (down_out,) = call(down_sum_kernel, [down[0], swap_over(down[1], ORDERS["down"][2])], [struct(tall, width, dtype=F32)], "down_sum_3")
    vectors = [low] * 6 + [tall, 3 * low]
    up_out, qkv_out, *vectors = call(
        joined_kernel, [up_mine, qkv_mine, small_mine, swap_over(others, 3)],
        [struct(low, units, dtype=F32), struct(low, 3 * width, dtype=F32)] + [struct(1, size, dtype=F32) for size in vectors], "up_qkv_joined",
    )
    joined = jnp.where(
        lax.axis_index("section") == 0, jnp.concatenate([back_1, back_2], axis=0), jnp.concatenate([result_1, result_2], axis=0)
    )
    gain_a, shift_a, gain_b, shift_b, bias_proj, bias_down, bias_up, bias_qkv = (vector[0] for vector in vectors)
    return joined, gain_a, shift_a, qkv_out, bias_qkv, proj, bias_proj, gain_b, shift_b, up_out, bias_up, down_out, bias_down


def plain_gradients(boundary, lengths, params, tables, swapped, bits):
    count = lax.axis_size("dp")
    slots = lengths.shape[0]
    width = boundary.shape[2]
    rows = boundary.shape[1] // slots
    units = params[8].shape[2]
    ticks = slots + 1
    result, saved, held = forward_first(lengths, boundary.reshape(slots, rows, width), params, tables)
    own, gain_a, shift_a, gain_b, shift_b, w_qkv, b_qkv, w_proj, b_proj, w_up, b_up, w_down, b_down, *tabs = held
    held_count = len(held)
    finals = [result]
    for t in range(1, ticks):
        arriving = lax.ppermute(result, "section", swapped)

        def forward_step(lengths_ref, arriving_ref, *refs, tick=t):
            section = lax.axis_index("section")
            slot = jnp.clip(tick - section, 0, slots - 1)
            inputs = lambda: jnp.where(section == 0, refs[0][slot], arriving_ref[...])
            outs = refs[held_count:]
            forward_body(slot, lengths_ref[slot], inputs, lambda name, part: None, *refs[:held_count], outs[-1], *outs[:-1])

        *saved, result = call(forward_step, [lengths, arriving, *held], [struct(rows, width)], "forward", kept=saved)
        finals.append(result)
    x_s, na_s, nb_s, qkv_s, pt_s, mixed_s, hidden_s, slope_s = saved
    operands = [x_s, gain_a, gain_b, w_qkv, w_proj, w_up, w_down, *tabs, pt_s]
    grads = [qkv_s, slope_s]
    input_grads = []
    arriving = own[0]
    for t in range(ticks):

        def backward_step(own_ref, arriving_ref, *refs, tick=t):
            section = lax.axis_index("section")
            slot = tick - 1 + section
            *io, gx_out = refs[len(operands) :]

            @pl.when((slot >= 0) & (slot < slots))
            def _():
                source = lambda: jnp.where(section == 0, arriving_ref[...], own_ref[slot])
                backward_body(slot, source, *refs[: len(operands)], gx_out, *io)

        shapes = [pltpu.VMEM((slots, rows, width), BF16), pltpu.VMEM((slots, 8, units), F32)] if t == 0 else []
        *grads, result = call(backward_step, [own, arriving, *operands], shapes + [struct(rows, width)], "backward", kept=grads)
        input_grads.append(result)
        if t + 1 < ticks:
            arriving = lax.ppermute(result, "section", swapped)
    gp_s, gu_s, gy_s, vec_s = grads
    order = list(range(len(bits)))

    def summed(full):
        keep, send = parted(full, 0, bits[0])
        return halving_sum(keep, send, order, count, bits, F32)

    both = jnp.concatenate([plain_grads(hidden_s, gy_s, count), plain_grads(mixed_s, gy_s, count)], axis=1)
    down, up, qkv = summed(both), summed(plain_grads(nb_s, gu_s, count)), summed(plain_grads(na_s, gp_s, count))
    tall = units // count
    totals = jnp.sum(vec_s, axis=0)
    sums = [totals[i, :width] for i in range(5)] + [totals[5], totals[6, : 3 * width]]
    return finals[1:], input_grads[1:], sums, down[:tall], down[tall:], up, qkv


def per_device(boundary, lengths, *params):
    section = lax.axis_index("section")
    count = lax.axis_size("dp")
    bits = [(lax.axis_index("dp") >> b) & 1 for b in range(count.bit_length() - 1)]
    slots = lengths.shape[0]
    width = boundary.shape[2]
    units = params[8].shape[2]
    tables = [jnp.asarray(table) for table in rotary_lanes(boundary.shape[1] // slots, 2 * HEAD)]
    swapped = [(0, 1), (1, 0)]
    if count == 16 and slots == 2 and width % 768 == 0:
        results = paired_gradients(boundary, lengths, params, tables, swapped)
        return tuple(result[None] for result in results)
    finals, input_grads, sums, down, proj, up, qkv = plain_gradients(
        boundary, lengths, params, tables, swapped, bits
    )
    small = jnp.concatenate([piece.reshape(count, -1) for piece in sums], axis=1)
    small = halving_sum(*parted(small, 0, bits[0]), list(range(len(bits))), count, bits, F32)
    low, tall = width // count, units // count
    gain_a, shift_a, gain_b, shift_b, bias_y, bias_up, bias_qkv = jnp.split(small, np.cumsum([low] * 5 + [tall]), axis=0)
    joined = jnp.where(section == 0, jnp.concatenate(input_grads, axis=0), jnp.concatenate(finals, axis=0))
    results = (joined, gain_a, shift_a, qkv, bias_qkv, proj, bias_y, gain_b, shift_b, up, bias_up, down, bias_y)
    return tuple(result[None] for result in results)


def solution(mesh):
    split = P("section", "dp")
    deep = P("section", "dp", None)
    flat, matrix = P("section", None), P("section", None, None)
    return jax.shard_map(
        per_device,
        mesh=mesh,
        in_specs=(deep, P("dp"), flat, flat, matrix, flat, matrix, flat, flat, flat, matrix, flat, matrix, flat),
        out_specs=(deep, split, split, deep, split, deep, split, split, split, deep, split, deep, split),
        check_vma=False,
    )
```

```python
import functools
import math

import jax
import jax.numpy as jnp
import numpy as np
from jax import lax
from jax.experimental import pallas as pl
from jax.experimental.pallas import tpu as pltpu
from jax.sharding import PartitionSpec as P

HEAD = 64
LANES = 256
CHUNK = 512
EPS = 1e-05
NEG_FILL = -1e30
VMEM_BYTES = 7 * 1024 * 1024
FIRST_VMEM_BYTES = 7 * 1024 * 1024
F32 = jnp.float32
BF16 = jnp.bfloat16


def dot(left, right):
    return jnp.dot(left, right, preferred_element_type=F32)


def dot_nt(left, right):
    return lax.dot_general(left, right, (((1,), (1,)), ((), ())), preferred_element_type=F32)


def normalised(values):
    centred = values - jnp.mean(values, axis=-1, keepdims=True)
    variance = jnp.mean(centred * centred, axis=-1, keepdims=True)
    scale = lax.rsqrt(variance + EPS)
    return centred * scale, scale


def gelu_parts(values):
    integral = 0.5 + 0.5 * lax.erf(values * math.sqrt(0.5))
    bell = jnp.exp(values * values * -0.5)
    return values * integral, integral + values * bell * (1.0 / math.sqrt(2.0 * math.pi))


def rotary_lanes(seq_len, lanes):
    rot_dims = HEAD // 4
    half = rot_dims // 2
    frequency = np.float32(10000.0) ** (-(np.arange(half, dtype=np.float32) * np.float32(2.0) / np.float32(rot_dims)))
    angles = np.arange(seq_len, dtype=np.float32)[:, None] * frequency.astype(np.float32)[None, :]
    cosine, sine = np.cos(angles).astype(np.float32), np.sin(angles).astype(np.float32)
    same = np.ones((seq_len, HEAD), np.float32)
    later = np.zeros((seq_len, HEAD), np.float32)
    earlier = np.zeros((seq_len, HEAD), np.float32)
    same[:, :half] = cosine
    same[:, half:rot_dims] = cosine
    later[:, :half] = -sine
    earlier[:, half:rot_dims] = sine
    return [np.tile(t, (1, lanes // HEAD)) for t in (same, later, earlier)]


def turned(values, same, later, earlier, sign):
    half = HEAD // 8
    width = values.shape[1]
    same, later, earlier = (jnp.concatenate([t] * (width // t.shape[1]), axis=1) for t in (same, later, earlier))
    ahead = pltpu.roll(values, width - half, 1)
    behind = pltpu.roll(values, half, 1)
    if sign > 0:
        return values * same + ahead * later + behind * earlier
    return values * same - ahead * later - behind * earlier


def blocked_bias(rows, length):
    out = []
    for start in range(0, rows, 128):
        keys = start + 128
        key_pos = lax.broadcasted_iota(jnp.int32, (keys, 2 * 128), 0)
        query_pos = start + (lax.broadcasted_iota(jnp.int32, (keys, 2 * 128), 1) & 127)
        out.append(jnp.where((key_pos <= query_pos) & (key_pos.astype(F32) < length), 0.0, NEG_FILL))
    return out


def heads_apart(block, lane):
    zero = jnp.zeros_like(block)
    return jnp.concatenate([jnp.where(lane < HEAD, block, zero), jnp.where(lane < HEAD, zero, block)], axis=0)


def dot_tn(left, right):
    return lax.dot_general(left, right, (((0,), (0,)), ((), ())), preferred_element_type=F32)


def probs_rows(block):
    start = 128 * (block * (block + 1) // 2)
    return slice(start, start + 128 * (block + 1))


def some(offset, size):
    return slice(offset, offset + size) if isinstance(offset, int) else pl.ds(pl.multiple_of(offset, 128), size)


def spans(pair, width):
    return [slice(b * width + pair * 2 * HEAD, b * width + (pair + 1) * 2 * HEAD) for b in range(3)]


def forward_units(slot, length, ready, na, nb, wqkv, bqkv, wu, bu, tables, qkv, pt, mixed, hidden, slope, low_head, low_unit, lanes):
    rows = qkv.shape[1]
    whole_width, width = wqkv.shape[1], qkv.shape[2] // 3
    pairs = width // (2 * HEAD)
    chunk = hidden.shape[2] // pairs
    biases = blocked_bias(rows, length)
    lane = lax.broadcasted_iota(jnp.int32, (128, 2 * HEAD), 1)
    per = lanes // (2 * HEAD)
    for pair in range(pairs):
        if pair % per == 0:
            low = pair * 2 * HEAD
            ready("qkv", pair // per)

            def packed(block):
                at = some(block * whole_width + low_head + low, lanes)
                return dot(na[slot], wqkv[0, :, at]) + bqkv[:, at].astype(F32)

            qkv[slot, :, low : low + lanes] = (turned(packed(0), *tables, 1) * (HEAD**-0.5)).astype(BF16)
            qkv[slot, :, width + low : width + low + lanes] = turned(packed(1), *tables, 1).astype(BF16)
            qkv[slot, :, 2 * width + low : 2 * width + low + lanes] = packed(2).astype(BF16)
        span, span_k, span_v = spans(pair, width)
        all_scores = []
        for block, start in enumerate(range(0, rows, 128)):
            keys = start + 128
            q2 = heads_apart(qkv[slot, start:keys, span], lane)
            all_scores.append(dot_nt(qkv[slot, :keys, span_k], q2) + biases[block])
        ready("up", pair)
        there = some(low_unit + pair * chunk, chunk)
        up = dot(nb[slot], wu[0, :, there]) + bu[:, there].astype(F32)
        for block, start in enumerate(range(0, rows, 128)):
            keys = start + 128
            scores = all_scores[block]
            exponent = jnp.exp(scores - jnp.max(scores, axis=0, keepdims=True))
            probs = (exponent * (1.0 / jnp.sum(exponent, axis=0, keepdims=True))).astype(BF16)
            pt[slot, pair, probs_rows(block)] = probs
            both = dot_tn(probs, qkv[slot, :keys, span_v])
            mixed[slot, start:keys, span] = jnp.where(lane < HEAD, both[:128], both[128:]).astype(BF16)
        here = slice(pair * chunk, pair * chunk + chunk)
        hidden_f32, slope_f32 = gelu_parts(up)
        hidden[slot, :, here] = hidden_f32.astype(BF16)
        slope[slot, :, here] = slope_f32.astype(BF16)


def backward_units(slot, gy, wp, wd, tables, pt, qkv, slope, low_head, low_unit, lanes):
    rows = qkv.shape[1]
    width = qkv.shape[2] // 3
    pairs = width // (2 * HEAD)
    chunk = slope.shape[2] // pairs
    lane = lax.broadcasted_iota(jnp.int32, (128, 2 * HEAD), 1)
    per = lanes // (2 * HEAD)
    for pair in range(pairs):
        if pair % per == 0:
            gm_group = dot_nt(gy(), wp[0, some(low_head + pair * 2 * HEAD, lanes), :]).astype(BF16)
            group_q, group_k = [], []
        span, span_k, span_v = spans(pair, width)
        gm = gm_group[:, (pair % per) * 2 * HEAD : (pair % per + 1) * 2 * HEAD]
        gv_sum, gk_sum, gq_blocks = None, None, []
        for block, start in enumerate(range(0, rows, 128)):
            keys = start + 128
            gm2 = heads_apart(gm[start:keys], lane)
            q2 = heads_apart(qkv[slot, start:keys, span], lane)
            probs = pt[slot, pair, probs_rows(block)]
            weighted = probs.astype(F32) * dot_nt(qkv[slot, :keys, span_v], gm2)
            inner = jnp.sum(weighted, axis=0, keepdims=True)
            gs = (weighted - probs.astype(F32) * inner).astype(BF16)
            gv_part = dot(probs, gm2)
            gk_part = dot(gs, q2)
            gq_part = dot_tn(gs, qkv[slot, :keys, span_k])
            gq_blocks.append(jnp.where(lane < HEAD, gq_part[:128], gq_part[128:]))
            if gv_sum is None:
                gv_sum, gk_sum = gv_part, gk_part
            else:
                gv_sum = jnp.concatenate([gv_sum + gv_part[:start], gv_part[start:]], axis=0)
                gk_sum = jnp.concatenate([gk_sum + gk_part[:start], gk_part[start:]], axis=0)
        qkv[slot, :, span_v] = gv_sum.astype(BF16)
        group_q.append(jnp.concatenate(gq_blocks, axis=0))
        group_k.append(gk_sum)
        if pair % per == per - 1:
            low = pair // per * lanes
            gq = turned(jnp.concatenate(group_q, axis=1) * (HEAD**-0.5), *tables, -1)
            qkv[slot, :, low : low + lanes] = gq.astype(BF16)
            gk = turned(jnp.concatenate(group_k, axis=1), *tables, -1)
            qkv[slot, :, width + low : width + low + lanes] = gk.astype(BF16)
        here = slice(pair * chunk, pair * chunk + chunk)
        grad = dot_nt(gy(), wd[0, some(low_unit + pair * chunk, chunk), :])
        slope[slot, :, here] = (grad * slope[slot, :, here].astype(F32)).astype(BF16)


def forward_body(
    slot, length, inputs, ready, own, gain_a, shift_a, gain_b, shift_b, wqkv, bqkv, wp, bp, wu, bu, wd, bd, same, later, earlier,
    y_out, x_out, na_out, nb_out, qkv_out, pt_out, mixed_out, hidden_out, slope_out,
):
    ready("small", 0)
    x_low = inputs()
    x_out[slot] = x_low
    xhat, _ = normalised(x_low.astype(F32))
    na_out[slot] = (xhat * gain_a[...].astype(F32) + shift_a[...].astype(F32)).astype(BF16)
    nb_out[slot] = (xhat * gain_b[...].astype(F32) + shift_b[...].astype(F32)).astype(BF16)
    tables = (same[...], later[...], earlier[...])
    forward_units(
        slot, length, ready, na_out, nb_out, wqkv, bqkv, wu, bu, tables, qkv_out, pt_out, mixed_out, hidden_out, slope_out, 0, 0, LANES
    )
    ready("rest", 0)
    total = x_out[slot].astype(F32) + (bp[...].astype(F32) + bd[...].astype(F32))
    y_out[...] = (total + dot(mixed_out[slot], wp[0]) + dot(hidden_out[slot], wd[0])).astype(BF16)


def backward_body(
    slot, gy_source, x_in, gain_a, gain_b, wqkv, wp, wu, wd, same, later, earlier, pt_in, gx_out, qkv_io, slope_io, gy_out, vec_out
):
    width = gx_out.shape[1]
    gy_out[slot] = gy_source()
    tables = (same[...], later[...], earlier[...])
    backward_units(slot, lambda: gy_out[slot], wp, wd, tables, pt_in, qkv_io, slope_io, 0, 0, LANES)
    grad_b = dot_nt(slope_io[slot], wu[0])
    grad_a = dot_nt(qkv_io[slot], wqkv[0])
    xhat, scale = normalised(x_in[slot].astype(F32))
    norm_terms = (grad_a * xhat, grad_a, grad_b * xhat, grad_b, gy_out[slot].astype(F32))
    for row, terms in enumerate(norm_terms):
        vec_out[slot, row : row + 1, :width] = jnp.sum(terms, axis=0, keepdims=True)
    vec_out[slot, 5:6, :] = jnp.sum(slope_io[slot].astype(F32), axis=0, keepdims=True)
    vec_out[slot, 6:7, : 3 * width] = jnp.sum(qkv_io[slot].astype(F32), axis=0, keepdims=True)
    both = grad_a * gain_a[...].astype(F32) + grad_b * gain_b[...].astype(F32)
    inner = jnp.mean(both * xhat, axis=-1, keepdims=True)
    gx = gy_out[slot].astype(F32) + scale * (both - jnp.mean(both, axis=-1, keepdims=True) - xhat * inner)
    gx_out[...] = gx.astype(BF16)


def forward_first_kernel(tick, lengths, *refs):
    count = 17
    sources, held, outs, sems = refs[:count], refs[count : 2 * count], refs[2 * count : -1], refs[-1]
    copies = []
    waits = {}

    def fetch(name, part, index, at):
        source, target = (sources[index], held[index]) if at is None else (sources[index].at[at], held[index].at[at])
        copy = pltpu.make_async_copy(source, target, sems.at[len(copies)])
        copies.append(copy)
        waits.setdefault((name, part), []).append(copy)

    (own, gain_a, shift_a, gain_b, shift_b, wqkv, bqkv, wp, bp, wu, bu, wd, bd, same, later, earlier, _) = range(count)
    width = sources[wp].shape[1]
    units = sources[wu].shape[2]
    pairs = width // (2 * HEAD)
    groups = width // LANES
    for index in (own, gain_a, shift_a, gain_b, shift_b, bqkv, bp, bu, bd, same, later, earlier):
        fetch("small", 0, index, None)
    for pair in range(pairs):
        if pair * groups % pairs == 0:
            group = pair * groups // pairs
            for block in range(3):
                fetch("qkv", group, wqkv, (slice(None), slice(None), pl.ds(block * width + group * LANES, LANES)))
        fetch("up", pair, wu, (slice(None), slice(None), pl.ds(pair * (units // pairs), units // pairs)))
    fetch("rest", 0, wp, None)
    fetch("rest", 0, wd, None)
    for copy in copies:
        copy.start()

    def ready(name, part):
        for copy in waits[(name, part)]:
            copy.wait()

    section = lax.axis_index("section")
    slots = held[own].shape[0]
    slot = jnp.clip(tick - section, 0, slots - 1)
    forward_body(slot, lengths[slot].astype(F32), lambda: held[own][slot], ready, *held[:-1], *outs)


def backward_body(
    slot, gy_source, x_in, gain_a, gain_b, wqkv, wp, wu, wd, same, later, earlier,
    pt_in, gx_out, qkv_io, slope_io, gy_out, vec_out,
):
    rows, width = gx_out.shape
    units = wu.shape[2]
    pairs = width // (2 * HEAD)
    chunk = units // pairs
    gy_out[slot] = gy_source()
    lane = lax.broadcasted_iota(jnp.int32, (128, 2 * HEAD), 1)
    tables = (same[...], later[...], earlier[...])
    per = LANES // (2 * HEAD)
    for pair in range(pairs):
        if pair % per == 0:
            gm_group = dot_nt(gy_out[slot], wp[0, pair * 2 * HEAD : pair * 2 * HEAD + LANES, :]).astype(BF16)
            group_q, group_k = [], []
        span, span_k, span_v = (slice(b * width + pair * 2 * HEAD, b * width + (pair + 1) * 2 * HEAD) for b in range(3))
        gm = gm_group[:, (pair % per) * 2 * HEAD : (pair % per + 1) * 2 * HEAD]
        gv_sum, gk_sum, gq_blocks = None, None, []
        for block, start in enumerate(range(0, rows, 128)):
            keys = start + 128
            gm2 = heads_apart(gm[start:keys], lane)
            q2 = heads_apart(qkv_io[slot, start:keys, span], lane)
            pt = pt_in[slot, pair, probs_rows(block)]
            weighted = pt.astype(F32) * dot_nt(qkv_io[slot, :keys, span_v], gm2)
            inner = jnp.sum(weighted, axis=0, keepdims=True)
            gs = (weighted - pt.astype(F32) * inner).astype(BF16)
            gv_part = dot(pt, gm2)
            gk_part = dot(gs, q2)
            gq_part = dot_tn(gs, qkv_io[slot, :keys, span_k])
            gq_blocks.append(jnp.where(lane < HEAD, gq_part[:128], gq_part[128:]))
            if gv_sum is None:
                gv_sum, gk_sum = gv_part, gk_part
            else:
                gv_sum = jnp.concatenate([gv_sum + gv_part[:start], gv_part[start:]], axis=0)
                gk_sum = jnp.concatenate([gk_sum + gk_part[:start], gk_part[start:]], axis=0)
        qkv_io[slot, :, span_v] = gv_sum.astype(BF16)
        group_q.append(jnp.concatenate(gq_blocks, axis=0))
        group_k.append(gk_sum)
        if pair % per == per - 1:
            low = pair // per * LANES
            gq = turned(jnp.concatenate(group_q, axis=1) * (HEAD**-0.5), *tables, -1)
            qkv_io[slot, :, low : low + LANES] = gq.astype(BF16)
            gk = turned(jnp.concatenate(group_k, axis=1), *tables, -1)
            qkv_io[slot, :, width + low : width + low + LANES] = gk.astype(BF16)
        at = slice(pair * chunk, pair * chunk + chunk)
        slope_io[slot, :, at] = (dot_nt(gy_out[slot], wd[0, at, :]) * slope_io[slot, :, at].astype(F32)).astype(BF16)
    grad_b = dot_nt(slope_io[slot], wu[0])
    grad_a = dot_nt(qkv_io[slot], wqkv[0])
    xhat, scale = normalised(x_in[slot].astype(F32))
    norm_terms = (grad_a * xhat, grad_a, grad_b * xhat, grad_b, gy_out[slot].astype(F32))
    for row, terms in enumerate(norm_terms):
        vec_out[slot, row : row + 1, :width] = jnp.sum(terms, axis=0, keepdims=True)
    vec_out[slot, 5:6, :] = jnp.sum(slope_io[slot].astype(F32), axis=0, keepdims=True)
    vec_out[slot, 6:7, : 3 * width] = jnp.sum(qkv_io[slot].astype(F32), axis=0, keepdims=True)
    both = grad_a * gain_a[...].astype(F32) + grad_b * gain_b[...].astype(F32)
    inner = jnp.mean(both * xhat, axis=-1, keepdims=True)
    gx = gy_out[slot].astype(F32) + scale * (both - jnp.mean(both, axis=-1, keepdims=True) - xhat * inner)
    gx_out[...] = gx.astype(BF16)


VM = pl.BlockSpec(memory_space=pltpu.VMEM)
HBM = pl.BlockSpec(memory_space=pl.ANY)


def call(kernel, operands, out_shape, name, kept=(), scratch=(), flops=1 << 20, after=()):
    count = len(operands)
    after = list(after)

    def body(*refs):
        kernel(*refs[:count], *refs[count + len(kept) + len(after) :])

    return pl.pallas_call(
        body,
        in_specs=[pl.BlockSpec(memory_space=pltpu.SMEM) if o.dtype == jnp.int32 else VM for o in operands] + [VM] * len(kept) + [HBM] * len(after),
        out_specs=[VM] * (len(kept) + len(out_shape)),
        out_shape=[pltpu.VMEM(array.shape, array.dtype) for array in kept] + list(out_shape),
        input_output_aliases={count + i: i for i in range(len(kept))},
        scratch_shapes=list(scratch),
        compiler_params=pltpu.CompilerParams(vmem_limit_bytes=VMEM_BYTES),
        cost_estimate=pl.CostEstimate(flops=flops, bytes_accessed=1 << 16, transcendentals=0),
        name=name,
    )(*operands, *[pltpu.with_memory_space_constraint(array, pltpu.VMEM) for array in kept], *after)


def shape_of(array):
    return jax.ShapeDtypeStruct(array.shape, array.dtype)


def forward_shapes(local_rows, params):
    slots, rows, width = local_rows.shape
    units = params[8].shape[2]
    blocks = rows // 128
    probs = (slots, width // (2 * HEAD), 128 * (blocks * (blocks + 1) // 2), 2 * 128)
    columns = [width, width, width, 3 * width, None, width, units, units]
    return [jax.ShapeDtypeStruct((rows, width), BF16)] + [
        pltpu.VMEM(probs if n is None else (slots, rows, n), BF16) for n in columns
    ]


def forward_first(lengths, local_rows, params, tables):
    (gain_a, shift_a, w_qkv, b_qkv, w_proj, b_proj, gain_b, shift_b, w_up, b_up, w_down, b_down) = params
    held = [local_rows, gain_a, shift_a, gain_b, shift_b, w_qkv, b_qkv, w_proj, b_proj, w_up, b_up, w_down, b_down] + list(tables)
    shapes = [shape_of(array) for array in held] + forward_shapes(local_rows, params)

    def kernel(lengths_ref, *refs):
        count = len(held)
        forward_first_kernel(0, lengths_ref, *refs[:count], None, *refs[count : 2 * count], None, *refs[2 * count :])

    outs = pl.pallas_call(
        kernel,
        in_specs=[pl.BlockSpec(memory_space=pltpu.SMEM)] + [pl.BlockSpec(memory_space=pltpu.HBM)] * len(held),
        out_specs=[VM] * len(shapes),
        out_shape=shapes,
        scratch_shapes=[pltpu.SemaphoreType.DMA((40,))],
        compiler_params=pltpu.CompilerParams(vmem_limit_bytes=FIRST_VMEM_BYTES),
        cost_estimate=pl.CostEstimate(flops=1 << 20, bytes_accessed=1 << 16, transcendentals=0),
        name="layer_forward_first",
    )(lengths, *[pltpu.with_memory_space_constraint(array, pltpu.HBM) for array in held])
    count = len(held)
    return outs[count], outs[count + 1 :], outs[:count]


def swap(shard, bit, count):
    return lax.ppermute(shard, "dp", [(i, i ^ (1 << bit)) for i in range(count)])


def parted(values, position, mine):
    count = values.shape[0]
    shaped = values.reshape((count >> (position + 1), 2, 1 << position) + values.shape[1:])
    out = []
    for side in (mine, 1 - mine):
        piece = lax.dynamic_index_in_dim(shaped, side, axis=1, keepdims=False)
        out.append(piece.reshape((count // 2,) + values.shape[1:]))
    return out


def halving_sum(keep, send, order, count, bits, final):
    left = sorted(order)
    for number, bit in enumerate(order):
        left.remove(bit)
        arrived = swap(send, bit, count)
        if number + 1 == len(order):
            return (keep.astype(F32) + arrived.astype(F32)).astype(final)[0]
        position = left.index(order[number + 1])
        keep_a, send_a = parted(keep, position, bits[order[number + 1]])
        keep_b, send_b = parted(arrived, position, bits[order[number + 1]])
        send = (send_a.astype(F32) + send_b.astype(F32)).astype(send_a.dtype)
        keep = (keep_a.astype(F32) + keep_b.astype(F32)).astype(send_a.dtype)


def plain_grads(left, right, count):
    rows = left.shape[0] * left.shape[1]
    product = lax.dot_general(
        left.reshape(rows, -1), right.reshape(rows, -1), (((0,), (0,)), ((), ())), preferred_element_type=F32
    ).astype(BF16)
    return product.reshape(count, product.shape[0] // count, product.shape[1])


def partner_forward(s, half, length, rows_of, gain_a, shift_a, gain_b, shift_b, wqkv, bqkv, wu, bu, tables, nap, nbp, qkvp, ptp, mixedp, hidp, slopep):
    lanes = mixedp.shape[2]
    xhat, _ = normalised(rows_of(s).astype(F32))
    nap[s] = (xhat * gain_a[...].astype(F32) + shift_a[...].astype(F32)).astype(BF16)
    nbp[s] = (xhat * gain_b[...].astype(F32) + shift_b[...].astype(F32)).astype(BF16)
    forward_units(
        s, length, lambda name, part: None, nap, nbp, wqkv, bqkv, wu, bu, tables, qkvp, ptp, mixedp, hidp, slopep,
        half * lanes, half * hidp.shape[2], lanes,
    )


def partner_backward(s, half, gy, wp, wd, tables, ptp, qkvp, slopep):
    lanes = qkvp.shape[2] // 3
    backward_units(s, gy, wp, wd, tables, ptp, qkvp, slopep, half * lanes, half * slopep.shape[2], lanes)


SUM_FLOPS = 6 << 30
ORDERS = {"down": (0, 1, 2), "up": (1, 2, 0), "attn": (2, 0, 1)}


def dp_bit(bit):
    return (lax.axis_index("dp") >> bit) & 1


def eighth_row(chunk, order, rows):
    first, second, third = ((chunk >> bit) & 1 for bit in order)
    return ((first ^ dp_bit(order[0])) * 4 + second * 2 + third) * rows


def row_slice(start, rows):
    return pl.ds(pl.multiple_of(start, 16), rows)


def flat_rows(ref, at=slice(None)):
    values = ref[:, :, at]
    return values.reshape(values.shape[0] * values.shape[1], values.shape[2])


def ones_dot(values):
    return dot(jnp.ones((16, values.shape[0]), BF16), values)[:8]


def sixteenths(ref, left, order, tokens_from):
    turned_ref = flat_rows(ref).T
    low = turned_ref.shape[0] // 16
    for chunk in range(16):
        start = eighth_row(chunk & 7, order, 2 * low) + (chunk >> 3) * low
        left[row_slice(start, low), tokens_from : tokens_from + turned_ref.shape[1]] = turned_ref[chunk * low : chunk * low + low]


def eighths(turned_rows, left, order, tokens_from):
    low = turned_rows.shape[0] // 8
    for chunk in range(8):
        left[row_slice(eighth_row(chunk, order, low), low), tokens_from : tokens_from + turned_rows.shape[1]] = turned_rows[
            chunk * low : chunk * low + low
        ]


def own_group_kernel(nb, na, gu, gp, hidden, mixed, gy, vec, up_own, attn_own, down_own, left, left_mixed, left_down):
    half = dp_bit(3)
    units, rows = up_own.shape[2], up_own.shape[1]
    width, lanes = na.shape[2], attn_own.shape[2] // 3
    low = rows // 2
    sixteenths(nb, left, ORDERS["up"], 0)
    for start in range(0, units, 512):
        product = dot(left[...], flat_rows(gu, some(half * units + start, 512)))
        up_own[:, :, start : start + 512] = product.reshape(8, rows, 512)
    order = ORDERS["attn"]
    sixteenths(na, left, order, 0)
    for block in range(3):
        product = dot(left[...], flat_rows(gp, some(block * width + half * lanes, lanes)))
        attn_own[:, :rows, block * lanes : block * lanes + lanes] = product.reshape(8, rows, lanes)
    grad = flat_rows(gy)
    eighths(flat_rows(mixed, some(half * lanes, lanes)).T, left_mixed, order, 0)
    attn_own[:, rows:, :width] = dot(left_mixed[...], grad).reshape(8, low, width)
    row_index = lax.broadcasted_iota(jnp.int32, (16, lanes), 0)
    totals = vec[0] + vec[1]
    sums = [totals[i : i + 1, :width] for i in range(5)] + [totals[5:6], totals[6:7, : 3 * width]]
    for chunk in range(16):
        block = jnp.zeros((16, lanes), F32)
        for row, values in enumerate(sums):
            size = values.shape[1] // 16
            piece = jnp.concatenate([values[:, chunk * size : chunk * size + size], jnp.zeros((1, lanes - size), F32)], axis=1)
            block = jnp.where(row_index == row, jnp.broadcast_to(piece, (16, lanes)), block)
        place_at = slice(rows + (chunk >> 3) * 16, rows + (chunk >> 3) * 16 + 16)
        attn_own[eighth_row(chunk & 7, order, 1), place_at, width:] = block
    eighths(flat_rows(hidden, some(half * units, units)).T, left_down, ORDERS["down"], 0)
    size = units // 4
    for part in range(4):
        product = dot(left_down[part * size : part * size + size], grad)
        down_own[part * 2 : part * 2 + 2] = product.reshape(2, size // 2, width)


def up_group_kernel(nbp, gup, up_own, keep, send, left):
    units = gup.shape[2]
    sixteenths(nbp, left, ORDERS["up"], 0)
    rows = left.shape[0] // 8
    for low in range(0, units, 512):
        at = slice(low, low + 512)
        product = (up_own[:, :, at] + dot(left[...], flat_rows(gup, at)).reshape(8, rows, 512)).astype(BF16)
        keep[:, :, at] = product[:4]
        send[:, :, at] = product[4:]


def attn_group_kernel(nap, gpp, mixedp, gyp_of, attn_own, keep, send, left, left_mixed):
    lanes = mixedp.shape[2]
    width = nap.shape[2]
    order = ORDERS["attn"]
    sixteenths(nap, left, order, 0)
    rows = left.shape[0] // 8
    for block in range(3):
        at = slice(block * lanes, block * lanes + lanes)
        product = (attn_own[:, :rows, at] + dot(left[...], flat_rows(gpp, at)).reshape(8, rows, lanes)).astype(BF16)
        keep[:, :rows, at] = product[:4]
        send[:, :rows, at] = product[4:]
    eighths(flat_rows(mixedp).T, left_mixed, order, 0)
    other_gy = jnp.concatenate([gyp_of(s) for s in range(nap.shape[0])], axis=0)
    low = left_mixed.shape[0] // 8
    product = (attn_own[:, rows:, :width] + dot(left_mixed[...], other_gy).reshape(8, low, width)).astype(BF16)
    keep[:, rows:, :width] = product[:4]
    send[:, rows:, :width] = product[4:]
    keep[:, rows:, width:] = attn_own[:4, rows:, width:].astype(BF16)
    send[:, rows:, width:] = attn_own[4:, rows:, width:].astype(BF16)


def down_group_kernel(hidp, gyp_of, down_own, keep, send, left):
    units = hidp.shape[2]
    eighths(flat_rows(hidp).T, left, ORDERS["down"], 0)
    other_gy = jnp.concatenate([gyp_of(s) for s in range(hidp.shape[0])], axis=0)
    size = units // 2
    for side, out in enumerate((keep, send)):
        product = dot(left[side * size : side * size + size], other_gy).reshape(out.shape)
        out[...] = (down_own[side * 4 : side * 4 + 4] + product).astype(BF16)


def plus(left, right):
    return left.astype(F32) + right.astype(F32)


def add_kernel(bit, keep, arrived, keep_out, send_out):
    size = keep_out.shape[0]
    mine = dp_bit(bit) * size
    keep_out[...] = plus(keep[pl.ds(mine, size)], arrived[pl.ds(mine, size)]).astype(BF16)
    send_out[...] = plus(keep[pl.ds(size - mine, size)], arrived[pl.ds(size - mine, size)]).astype(BF16)


def swap_over(shard, bit, sections=(0, 1)):
    count = lax.axis_size("dp")
    pairs = [(s * count + i, s * count + (i ^ (1 << bit))) for s in sections for i in range(count)]
    return lax.ppermute(shard, ("section", "dp"), pairs)


def cross_swap(shard, section, bit):
    count = lax.axis_size("dp")
    return lax.ppermute(shard, ("section", "dp"), [(section * count + i, (1 - section) * count + (i ^ (1 << bit))) for i in range(count)])


def struct(*shape, dtype=BF16):
    return jax.ShapeDtypeStruct(shape, dtype)


def halved(parts, order, stage, name, after=()):
    keep, send = parts
    arrived = swap_over(send, order[stage])
    shape = (keep.shape[0] // 2,) + keep.shape[1:]
    return call(functools.partial(add_kernel, order[stage + 1]), [keep, arrived], [struct(*shape)] * 2, name, after=after, flops=SUM_FLOPS)


def down_sum_kernel(keep, arrived, out):
    out[...] = plus(keep[0], arrived[0])


def halves_sum_kernel(up_keep, up_arrived, attn_keep, attn_arrived, up_mine, qkv_mine, small_mine, proj, other):
    half = dp_bit(3)
    low = up_mine.shape[0]
    units = up_mine.shape[1]
    width = proj.shape[1]
    mine, theirs = row_slice(half * low, low), row_slice((1 - half) * low, low)
    up_mine[...] = plus(up_keep[0, mine], up_arrived[0, mine])
    other[:, :units] = plus(up_keep[0, theirs], up_arrived[0, theirs]).astype(BF16)
    qkv_mine[...] = plus(attn_keep[0, mine], attn_arrived[0, mine])
    other[:, units : units + qkv_mine.shape[1]] = plus(attn_keep[0, theirs], attn_arrived[0, theirs]).astype(BF16)
    proj[...] = plus(attn_keep[0, 2 * low :, :width], attn_arrived[0, 2 * low :, :width])
    mine, theirs = row_slice(2 * low + half * 16, 16), row_slice(2 * low + (1 - half) * 16, 16)
    small_mine[...] = plus(attn_keep[0, mine, width:], attn_arrived[0, mine, width:])
    small = plus(attn_keep[0, theirs, width:], attn_arrived[0, theirs, width:]).astype(BF16)
    for part in range(small.shape[1] // 128):
        other[part * 16 : part * 16 + 16, other.shape[1] - 128 :] = small[:, part * 128 : part * 128 + 128]


def joined_kernel(up_mine, qkv_mine, small_mine, other, up, qkv, *vectors):
    half = dp_bit(3)
    low = up_mine.shape[0]
    units = up_mine.shape[1]
    lanes = qkv_mine.shape[1] // 3
    up[:, some(half * units, units)] = up_mine[...]
    up[:, some((1 - half) * units, units)] = other[:, :units].astype(F32)
    for block in range(3):
        at = slice(block * lanes, block * lanes + lanes)
        qkv[:, some((2 * block + half) * lanes, lanes)] = qkv_mine[:, at]
        qkv[:, some((2 * block + 1 - half) * lanes, lanes)] = other[:, units + block * lanes : units + (block + 1) * lanes].astype(F32)
    rest = other[:, other.shape[1] - 128 :].astype(F32)
    small = small_mine[...] + jnp.concatenate([rest[part : part + 16] for part in range(0, low, 16)], axis=1)
    for row, out in zip((0, 1, 2, 3, 4, 4, 5, 6), vectors):
        out[...] = small[row : row + 1, : out.shape[1]]


def paired_gradients(boundary, lengths, params, tables, swapped):
    slots = lengths.shape[0]
    width = boundary.shape[2]
    rows = boundary.shape[1] // slots
    units = params[8].shape[2]
    local_rows = boundary.reshape(slots, rows, width)
    low, tall = width // 16, units // 16
    tokens = slots * rows

    cut = rows + rows // 2 - 16
    length_rows = jnp.broadcast_to(jnp.repeat(lengths.astype(BF16), 8)[:, None], (8 * slots, width))
    other_a = swap_over(jnp.concatenate([boundary[0, :cut], length_rows], axis=0), 3, (0,))
    other_b = swap_over(boundary[0, cut:], 3, (0,))
    other_gy = swap_over(local_rows, 3, (1,))
    result_0, saved, held = forward_first(lengths, local_rows, params, tables)
    own, gain_a, shift_a, gain_b, shift_b, w_qkv, b_qkv, w_proj, b_proj, w_up, b_up, w_down, b_down, *tabs = held
    arrived_1 = lax.ppermute(result_0, "section", swapped)
    count = len(held)

    def forward_both(lengths_ref, arriving, *refs):
        section = lax.axis_index("section")
        slot = 1 - section
        inputs = lambda: jnp.where(section == 0, refs[0][slot], arriving[...])
        outs = refs[count:]
        forward_body(slot, lengths_ref[slot].astype(F32), inputs, lambda name, part: None, *refs[:count], outs[-1], *outs[:-1])

    *saved, result_1 = call(forward_both, [lengths, arrived_1, *held], [struct(rows, width)], "forward_1", kept=saved, after=[other_a])
    arrived_2 = lax.ppermute(result_1, "section", swapped)

    def forward_last(lengths_ref, arriving, *refs):
        slot = slots - 1
        *kept, y, x_long = refs[count:]

        @pl.when(lax.axis_index("section") == 1)
        def _():
            x_long[:rows] = kept[0][0]
            x_long[rows : 2 * rows] = arriving[...]
            for s in range(slots):
                at = slots * rows + 8 * s
                x_long[at : at + 8] = jnp.full((8, width), lengths_ref[s].astype(F32), F32).astype(BF16)
            forward_body(
                slot, lengths_ref[slot].astype(F32), lambda: arriving[...], lambda name, part: None, *refs[:count], y, *kept
            )

    *saved, result_2, x_long = call(
        forward_last, [lengths, arrived_2, *held], [struct(rows, width), struct(slots * rows + 8 * slots, width)], "forward_2",
        kept=saved, after=[other_b],
    )
    x_s, na_s, nb_s, qkv_s, pt_s, mixed_s, hidden_s, slope_s = saved
    partner_x = swap_over(x_long, 3, (1,))

    back_operands = [x_s, gain_a, gain_b, w_qkv, w_proj, w_up, w_down, *tabs, pt_s]
    back_count = len(back_operands)
    shared_operands = [gain_a, shift_a, gain_b, shift_b, w_qkv, b_qkv, w_up, b_up, *tabs]
    shared_count = len(shared_operands)
    shared_shapes = [
        pltpu.VMEM(shape, BF16)
        for shape in (
            (slots, rows, width), (slots, rows, width), (slots, rows, 3 * width // 2), (slots, pt_s.shape[1] // 2) + pt_s.shape[2:],
            (slots, rows, width // 2), (slots, rows, units // 2), (slots, rows, units // 2),
        )
    ]

    def share(s, length, x_rows, refs, outs):
        weights, tabs_refs = refs[:-3], refs[-3:]
        partner_forward(s, dp_bit(3), length.astype(F32), lambda s: x_rows, *weights, tuple(t[...] for t in tabs_refs), *outs)

    def backward_first(own_ref, ref_a, ref_b, *refs):
        operands, shared, (qkv_io, slope_io, gy, vec, gx, *outs) = (
            refs[:back_count], refs[back_count : back_count + shared_count], refs[back_count + shared_count :],
        )
        section = lax.axis_index("section")

        @pl.when(section == 1)
        def _():
            backward_body(0, lambda: own_ref[0], *operands, gx, qkv_io, slope_io, gy, vec)

        @pl.when(section == 0)
        def _():
            x_rows = (ref_a[:rows], jnp.concatenate([ref_a[rows:cut], ref_b[...]], axis=0))
            for s in range(slots):
                share(s, ref_a[cut + 8 * s : cut + 8 * s + 1, : 2 * 128], x_rows[s], shared, outs)

    outs = call(
        backward_first, [own, other_a, other_b, *back_operands, *shared_operands],
        [pltpu.VMEM((slots, rows, width), BF16), pltpu.VMEM((slots, 8, units), F32), struct(rows, width)] + shared_shapes,
        "backward_0", kept=[qkv_s, slope_s],
    )
    grads, back_0, shared = outs[:4], outs[4], outs[5:]
    arrived_4 = lax.ppermute(back_0, "section", swapped)

    def backward_both(own_ref, arriving, *refs):
        section = lax.axis_index("section")
        outs = refs[back_count:]
        source = lambda: jnp.where(section == 0, arriving[...], own_ref[section])
        backward_body(section, source, *refs[:back_count], outs[-1], *outs[:-1])

    *grads, back_1 = call(backward_both, [own, arrived_4, *back_operands], [struct(rows, width)], "backward_1", kept=grads, after=[other_gy])
    arrived_5 = lax.ppermute(back_1, "section", swapped)

    def backward_last(arriving, other_ref, *refs):
        operands, shared_in, (qkv_io, slope_io, gy, vec, *outs) = (
            refs[:back_count], refs[back_count : back_count + shared_count], refs[back_count + shared_count :],
        )
        section = lax.axis_index("section")

        @pl.when(section == 0)
        def _():
            backward_body(slots - 1, lambda: arriving[...], *operands, outs[-1], qkv_io, slope_io, gy, vec)

        @pl.when(section == 1)
        def _():
            for s in range(slots):
                at = slots * rows + 8 * s
                share(s, other_ref[at : at + 1, : 2 * 128], other_ref[s * rows : s * rows + rows], shared_in, outs[:-1])

    outs = call(
        backward_last, [arrived_5, partner_x, *back_operands, *shared_operands], [struct(rows, width)],
        "backward_2", kept=[*grads, *shared],
    )
    gp_s, gu_s, gy_s, vec_s, nap, nbp, qkvp, ptp, mixedp, hidp, slopep, back_2 = outs

    partner_gy = swap_over(gy_s, 3, (0,))
    up_own, attn_own, down_own = call(
        own_group_kernel, [nb_s, na_s, gu_s, gp_s, hidden_s, mixed_s, gy_s, vec_s],
        [struct(8, 2 * low, units // 2, dtype=F32), struct(8, 3 * low, 3 * width // 2, dtype=F32), struct(8, tall, width, dtype=F32)], "own_grads",
        scratch=[pltpu.VMEM((width, tokens), BF16), pltpu.VMEM((width // 2, tokens), BF16), pltpu.VMEM((units // 2, tokens), BF16)],
    )

    def backward_shared(other_ref, partner_ref, wp, wd, same, later, earlier, ptp_ref, qkvp_ref, slopep_ref, gyp):
        gyp[...] = jnp.where(lax.axis_index("section") == 0, partner_ref[...], other_ref[...])
        tables_in = (same[...], later[...], earlier[...])
        for s in range(slots):
            partner_backward(s, dp_bit(3), lambda: gyp[s], wp, wd, tables_in, ptp_ref, qkvp_ref, slopep_ref)

    gpp, gup, gyp_s = call(
        backward_shared, [other_gy, partner_gy, w_proj, w_down, *tabs, ptp], [struct(slots, rows, width)], "backward_shared",
        kept=[qkvp, slopep], after=[up_own],
    )

    def group(rows_of_eighth, columns):
        return [struct(4, rows_of_eighth, columns)] * 2

    up = call(
        up_group_kernel, [nbp, gup, up_own], group(2 * low, units // 2), "up_grads", scratch=[pltpu.VMEM((width, tokens), BF16)]
    )

    def attn_group(nap_ref, gpp_ref, mixedp_ref, gyp, *refs):
        attn_group_kernel(nap_ref, gpp_ref, mixedp_ref, lambda s: gyp[s], *refs)

    attn = call(
        attn_group, [nap, gpp, mixedp, gyp_s, attn_own], group(3 * low, 3 * width // 2), "attn_grads",
        scratch=[pltpu.VMEM((width, tokens), BF16), pltpu.VMEM((width // 2, tokens), BF16)], after=up[:1],
    )

    def down_group(hidp_ref, gyp, *refs):
        down_group_kernel(hidp_ref, lambda s: gyp[s], *refs)

    down = call(
        down_group, [hidp, gyp_s, down_own], group(tall, width), "down_grads",
        scratch=[pltpu.VMEM((units // 2, tokens), BF16)], after=attn[:1],
    )

    up = halved(up, ORDERS["up"], 0, "up_sum_1", after=down[:1])
    attn = halved(attn, ORDERS["attn"], 0, "attn_sum_1", after=up[:1])
    down = halved(down, ORDERS["down"], 0, "down_sum_1", after=attn[:1])
    up = halved(up, ORDERS["up"], 1, "up_sum_2", after=down[:1])
    attn = halved(attn, ORDERS["attn"], 1, "attn_sum_2", after=up[:1])
    down = halved(down, ORDERS["down"], 1, "down_sum_2", after=attn[:1])
    up_last, attn_last = swap_over(up[1], ORDERS["up"][2]), swap_over(attn[1], ORDERS["attn"][2])
    up_mine, qkv_mine, small_mine, proj, others = call(
        halves_sum_kernel, [up[0], up_last, attn[0], attn_last],
        [struct(low, units // 2, dtype=F32), struct(low, 3 * width // 2, dtype=F32), struct(16, width // 2, dtype=F32),
         struct(low, width, dtype=F32), struct(low, units // 2 + 3 * width // 2 + 128)], "up_qkv_sum_3", after=down[:1],
    )
    (down_out,) = call(down_sum_kernel, [down[0], swap_over(down[1], ORDERS["down"][2])], [struct(tall, width, dtype=F32)], "down_sum_3")
    vectors = [low] * 6 + [tall, 3 * low]
    up_out, qkv_out, *vectors = call(
        joined_kernel, [up_mine, qkv_mine, small_mine, swap_over(others, 3)],
        [struct(low, units, dtype=F32), struct(low, 3 * width, dtype=F32)] + [struct(1, size, dtype=F32) for size in vectors], "up_qkv_joined",
    )
    joined = jnp.where(
        lax.axis_index("section") == 0, jnp.concatenate([back_1, back_2], axis=0), jnp.concatenate([result_1, result_2], axis=0)
    )
    gain_a, shift_a, gain_b, shift_b, bias_proj, bias_down, bias_up, bias_qkv = (vector[0] for vector in vectors)
    return joined, gain_a, shift_a, qkv_out, bias_qkv, proj, bias_proj, gain_b, shift_b, up_out, bias_up, down_out, bias_down


def plain_gradients(boundary, lengths, params, tables, swapped, bits):
    count = lax.axis_size("dp")
    slots = lengths.shape[0]
    width = boundary.shape[2]
    rows = boundary.shape[1] // slots
    units = params[8].shape[2]
    ticks = slots + 1
    result, saved, held = forward_first(lengths, boundary.reshape(slots, rows, width), params, tables)
    own, gain_a, shift_a, gain_b, shift_b, w_qkv, b_qkv, w_proj, b_proj, w_up, b_up, w_down, b_down, *tabs = held
    held_count = len(held)
    finals = [result]
    for t in range(1, ticks):
        arriving = lax.ppermute(result, "section", swapped)

        def forward_step(lengths_ref, arriving_ref, *refs, tick=t):
            section = lax.axis_index("section")
            slot = jnp.clip(tick - section, 0, slots - 1)
            inputs = lambda: jnp.where(section == 0, refs[0][slot], arriving_ref[...])
            outs = refs[held_count:]
            forward_body(slot, lengths_ref[slot].astype(F32), inputs, lambda name, part: None, *refs[:held_count], outs[-1], *outs[:-1])

        *saved, result = call(forward_step, [lengths, arriving, *held], [struct(rows, width)], "forward", kept=saved)
        finals.append(result)
    x_s, na_s, nb_s, qkv_s, pt_s, mixed_s, hidden_s, slope_s = saved
    operands = [x_s, gain_a, gain_b, w_qkv, w_proj, w_up, w_down, *tabs, pt_s]
    grads = [qkv_s, slope_s]
    input_grads = []
    arriving = own[0]
    for t in range(ticks):

        def backward_step(own_ref, arriving_ref, *refs, tick=t):
            section = lax.axis_index("section")
            slot = tick - 1 + section
            *io, gx_out = refs[len(operands) :]

            @pl.when((slot >= 0) & (slot < slots))
            def _():
                source = lambda: jnp.where(section == 0, arriving_ref[...], own_ref[slot])
                backward_body(slot, source, *refs[: len(operands)], gx_out, *io)

        shapes = [pltpu.VMEM((slots, rows, width), BF16), pltpu.VMEM((slots, 8, units), F32)] if t == 0 else []
        *grads, result = call(backward_step, [own, arriving, *operands], shapes + [struct(rows, width)], "backward", kept=grads)
        input_grads.append(result)
        if t + 1 < ticks:
            arriving = lax.ppermute(result, "section", swapped)
    gp_s, gu_s, gy_s, vec_s = grads
    order = list(range(len(bits)))

    def summed(full):
        keep, send = parted(full, 0, bits[0])
        return halving_sum(keep, send, order, count, bits, F32)

    both = jnp.concatenate([plain_grads(hidden_s, gy_s, count), plain_grads(mixed_s, gy_s, count)], axis=1)
    down, up, qkv = summed(both), summed(plain_grads(nb_s, gu_s, count)), summed(plain_grads(na_s, gp_s, count))
    tall = units // count
    totals = jnp.sum(vec_s, axis=0)
    sums = [totals[i, :width] for i in range(5)] + [totals[5], totals[6, : 3 * width]]
    return finals[1:], input_grads[1:], sums, down[:tall], down[tall:], up, qkv


def per_device(boundary, lengths, *params):
    section = lax.axis_index("section")
    count = lax.axis_size("dp")
    bits = [(lax.axis_index("dp") >> b) & 1 for b in range(count.bit_length() - 1)]
    slots = lengths.shape[0]
    width = boundary.shape[2]
    units = params[8].shape[2]
    tables = [jnp.asarray(table) for table in rotary_lanes(boundary.shape[1] // slots, 2 * HEAD)]
    swapped = [(0, 1), (1, 0)]
    if count == 16 and slots == 2 and width % 768 == 0:
        results = paired_gradients(boundary, lengths, params, tables, swapped)
        return tuple(result[None] for result in results)
    finals, input_grads, sums, down, proj, up, qkv = plain_gradients(
        boundary, lengths, params, tables, swapped, bits
    )
    small = jnp.concatenate([piece.reshape(count, -1) for piece in sums], axis=1)
    small = halving_sum(*parted(small, 0, bits[0]), list(range(len(bits))), count, bits, F32)
    low, tall = width // count, units // count
    gain_a, shift_a, gain_b, shift_b, bias_y, bias_up, bias_qkv = jnp.split(small, np.cumsum([low] * 5 + [tall]), axis=0)
    joined = jnp.where(section == 0, jnp.concatenate(input_grads, axis=0), jnp.concatenate(finals, axis=0))
    results = (joined, gain_a, shift_a, qkv, bias_qkv, proj, bias_y, gain_b, shift_b, up, bias_up, down, bias_y)
    return tuple(result[None] for result in results)


def solution(mesh):
    split = P("section", "dp")
    deep = P("section", "dp", None)
    flat, matrix = P("section", None), P("section", None, None)
    return jax.shard_map(
        per_device,
        mesh=mesh,
        in_specs=(deep, P("dp"), flat, flat, matrix, flat, matrix, flat, flat, flat, matrix, flat, matrix, flat),
        out_specs=(deep, split, split, deep, split, deep, split, split, split, deep, split, deep, split),
        check_vma=False,
    )
```

```python
import functools
import math

import jax
import jax.numpy as jnp
import numpy as np
from jax import lax
from jax.experimental import pallas as pl
from jax.experimental.pallas import tpu as pltpu
from jax.sharding import PartitionSpec as P

HEAD = 64
LANES = 256
CHUNK = 512
EPS = 1e-05
NEG_FILL = -1e30
VMEM_BYTES = 7 * 1024 * 1024
FIRST_VMEM_BYTES = 7 * 1024 * 1024
F32 = jnp.float32
BF16 = jnp.bfloat16


def dot(left, right):
    return jnp.dot(left, right, preferred_element_type=F32)


def dot_nt(left, right):
    return lax.dot_general(left, right, (((1,), (1,)), ((), ())), preferred_element_type=F32)


def normalised(values):
    centred = values - jnp.mean(values, axis=-1, keepdims=True)
    variance = jnp.mean(centred * centred, axis=-1, keepdims=True)
    scale = lax.rsqrt(variance + EPS)
    return centred * scale, scale


def gelu_parts(values):
    integral = 0.5 + 0.5 * lax.erf(values * math.sqrt(0.5))
    bell = jnp.exp(values * values * -0.5)
    return values * integral, integral + values * bell * (1.0 / math.sqrt(2.0 * math.pi))


def rotary_lanes(seq_len, lanes):
    rot_dims = HEAD // 4
    half = rot_dims // 2
    frequency = np.float32(10000.0) ** (-(np.arange(half, dtype=np.float32) * np.float32(2.0) / np.float32(rot_dims)))
    angles = np.arange(seq_len, dtype=np.float32)[:, None] * frequency.astype(np.float32)[None, :]
    cosine, sine = np.cos(angles).astype(np.float32), np.sin(angles).astype(np.float32)
    same = np.ones((seq_len, HEAD), np.float32)
    later = np.zeros((seq_len, HEAD), np.float32)
    earlier = np.zeros((seq_len, HEAD), np.float32)
    same[:, :half] = cosine
    same[:, half:rot_dims] = cosine
    later[:, :half] = -sine
    earlier[:, half:rot_dims] = sine
    return [np.tile(t, (1, lanes // HEAD)) for t in (same, later, earlier)]


def turned(values, same, later, earlier, sign):
    half = HEAD // 8
    width = values.shape[1]
    same, later, earlier = (jnp.concatenate([t] * (width // t.shape[1]), axis=1) for t in (same, later, earlier))
    ahead = pltpu.roll(values, width - half, 1)
    behind = pltpu.roll(values, half, 1)
    if sign > 0:
        return values * same + ahead * later + behind * earlier
    return values * same - ahead * later - behind * earlier


def blocked_bias(rows, length):
    out = []
    for start in range(0, rows, 128):
        keys = start + 128
        key_pos = lax.broadcasted_iota(jnp.int32, (keys, 2 * 128), 0)
        query_pos = start + (lax.broadcasted_iota(jnp.int32, (keys, 2 * 128), 1) & 127)
        out.append(jnp.where((key_pos <= query_pos) & (key_pos.astype(F32) < length), 0.0, NEG_FILL))
    return out


def heads_apart(block, lane):
    zero = jnp.zeros_like(block)
    return jnp.concatenate([jnp.where(lane < HEAD, block, zero), jnp.where(lane < HEAD, zero, block)], axis=0)


def dot_tn(left, right):
    return lax.dot_general(left, right, (((0,), (0,)), ((), ())), preferred_element_type=F32)


def probs_rows(block):
    start = 128 * (block * (block + 1) // 2)
    return slice(start, start + 128 * (block + 1))


def some(offset, size):
    return slice(offset, offset + size) if isinstance(offset, int) else pl.ds(pl.multiple_of(offset, 128), size)


def spans(pair, width):
    return [slice(b * width + pair * 2 * HEAD, b * width + (pair + 1) * 2 * HEAD) for b in range(3)]


def forward_units(slot, length, ready, na, nb, wqkv, bqkv, wu, bu, tables, qkv, pt, mixed, hidden, slope, low_head, low_unit, lanes):
    rows = qkv.shape[1]
    whole_width, width = wqkv.shape[1], qkv.shape[2] // 3
    pairs = width // (2 * HEAD)
    chunk = hidden.shape[2] // pairs
    biases = blocked_bias(rows, length)
    lane = lax.broadcasted_iota(jnp.int32, (128, 2 * HEAD), 1)
    per = lanes // (2 * HEAD)
    for pair in range(pairs):
        if pair % per == 0:
            low = pair * 2 * HEAD
            ready("qkv", pair // per)

            def packed(block):
                at = some(block * whole_width + low_head + low, lanes)
                return dot(na[slot], wqkv[0, :, at]) + bqkv[:, at].astype(F32)

            qkv[slot, :, low : low + lanes] = (turned(packed(0), *tables, 1) * (HEAD**-0.5)).astype(BF16)
            qkv[slot, :, width + low : width + low + lanes] = turned(packed(1), *tables, 1).astype(BF16)
            qkv[slot, :, 2 * width + low : 2 * width + low + lanes] = packed(2).astype(BF16)
        span, span_k, span_v = spans(pair, width)
        all_scores = []
        for block, start in enumerate(range(0, rows, 128)):
            keys = start + 128
            q2 = heads_apart(qkv[slot, start:keys, span], lane)
            all_scores.append(dot_nt(qkv[slot, :keys, span_k], q2) + biases[block])
        ready("up", pair)
        there = some(low_unit + pair * chunk, chunk)
        up = dot(nb[slot], wu[0, :, there]) + bu[:, there].astype(F32)
        for block, start in enumerate(range(0, rows, 128)):
            keys = start + 128
            scores = all_scores[block]
            exponent = jnp.exp(scores - jnp.max(scores, axis=0, keepdims=True))
            probs = (exponent * (1.0 / jnp.sum(exponent, axis=0, keepdims=True))).astype(BF16)
            pt[slot, pair, probs_rows(block)] = probs
            both = dot_tn(probs, qkv[slot, :keys, span_v])
            mixed[slot, start:keys, span] = jnp.where(lane < HEAD, both[:128], both[128:]).astype(BF16)
        here = slice(pair * chunk, pair * chunk + chunk)
        hidden_f32, slope_f32 = gelu_parts(up)
        hidden[slot, :, here] = hidden_f32.astype(BF16)
        slope[slot, :, here] = slope_f32.astype(BF16)


def backward_units(slot, gy, wp, wd, tables, pt, qkv, slope, low_head, low_unit, lanes):
    rows = qkv.shape[1]
    width = qkv.shape[2] // 3
    pairs = width // (2 * HEAD)
    chunk = slope.shape[2] // pairs
    lane = lax.broadcasted_iota(jnp.int32, (128, 2 * HEAD), 1)
    per = lanes // (2 * HEAD)
    for pair in range(pairs):
        if pair % per == 0:
            gm_group = dot_nt(gy(), wp[0, some(low_head + pair * 2 * HEAD, lanes), :]).astype(BF16)
            group_q, group_k = [], []
        span, span_k, span_v = spans(pair, width)
        gm = gm_group[:, (pair % per) * 2 * HEAD : (pair % per + 1) * 2 * HEAD]
        gv_sum, gk_sum, gq_blocks = None, None, []
        for block, start in enumerate(range(0, rows, 128)):
            keys = start + 128
            gm2 = heads_apart(gm[start:keys], lane)
            q2 = heads_apart(qkv[slot, start:keys, span], lane)
            probs = pt[slot, pair, probs_rows(block)]
            weighted = probs.astype(F32) * dot_nt(qkv[slot, :keys, span_v], gm2)
            inner = jnp.sum(weighted, axis=0, keepdims=True)
            gs = (weighted - probs.astype(F32) * inner).astype(BF16)
            gv_part = dot(probs, gm2)
            gk_part = dot(gs, q2)
            gq_part = dot_tn(gs, qkv[slot, :keys, span_k])
            gq_blocks.append(jnp.where(lane < HEAD, gq_part[:128], gq_part[128:]))
            if gv_sum is None:
                gv_sum, gk_sum = gv_part, gk_part
            else:
                gv_sum = jnp.concatenate([gv_sum + gv_part[:start], gv_part[start:]], axis=0)
                gk_sum = jnp.concatenate([gk_sum + gk_part[:start], gk_part[start:]], axis=0)
        qkv[slot, :, span_v] = gv_sum.astype(BF16)
        group_q.append(jnp.concatenate(gq_blocks, axis=0))
        group_k.append(gk_sum)
        if pair % per == per - 1:
            low = pair // per * lanes
            gq = turned(jnp.concatenate(group_q, axis=1) * (HEAD**-0.5), *tables, -1)
            qkv[slot, :, low : low + lanes] = gq.astype(BF16)
            gk = turned(jnp.concatenate(group_k, axis=1), *tables, -1)
            qkv[slot, :, width + low : width + low + lanes] = gk.astype(BF16)
        here = slice(pair * chunk, pair * chunk + chunk)
        grad = dot_nt(gy(), wd[0, some(low_unit + pair * chunk, chunk), :])
        slope[slot, :, here] = (grad * slope[slot, :, here].astype(F32)).astype(BF16)


def forward_body(
    slot, length, inputs, ready, own, gain_a, shift_a, gain_b, shift_b, wqkv, bqkv, wp, bp, wu, bu, wd, bd, same, later, earlier,
    y_out, x_out, na_out, nb_out, qkv_out, pt_out, mixed_out, hidden_out, slope_out,
):
    ready("small", 0)
    x_low = inputs()
    x_out[slot] = x_low
    xhat, _ = normalised(x_low.astype(F32))
    na_out[slot] = (xhat * gain_a[...].astype(F32) + shift_a[...].astype(F32)).astype(BF16)
    nb_out[slot] = (xhat * gain_b[...].astype(F32) + shift_b[...].astype(F32)).astype(BF16)
    tables = (same[...], later[...], earlier[...])
    forward_units(
        slot, length, ready, na_out, nb_out, wqkv, bqkv, wu, bu, tables, qkv_out, pt_out, mixed_out, hidden_out, slope_out, 0, 0, LANES
    )
    ready("rest", 0)
    total = x_out[slot].astype(F32) + (bp[...].astype(F32) + bd[...].astype(F32))
    y_out[...] = (total + dot(mixed_out[slot], wp[0]) + dot(hidden_out[slot], wd[0])).astype(BF16)


def backward_body(
    slot, gy_source, x_in, gain_a, gain_b, wqkv, wp, wu, wd, same, later, earlier, pt_in, gx_out, qkv_io, slope_io, gy_out, vec_out
):
    width = gx_out.shape[1]
    gy_out[slot] = gy_source()
    tables = (same[...], later[...], earlier[...])
    backward_units(slot, lambda: gy_out[slot], wp, wd, tables, pt_in, qkv_io, slope_io, 0, 0, LANES)
    grad_b = dot_nt(slope_io[slot], wu[0])
    grad_a = dot_nt(qkv_io[slot], wqkv[0])
    xhat, scale = normalised(x_in[slot].astype(F32))
    norm_terms = (grad_a * xhat, grad_a, grad_b * xhat, grad_b, gy_out[slot].astype(F32))
    for row, terms in enumerate(norm_terms):
        vec_out[slot, row : row + 1, :width] = jnp.sum(terms, axis=0, keepdims=True)
    vec_out[slot, 5:6, :] = jnp.sum(slope_io[slot].astype(F32), axis=0, keepdims=True)
    vec_out[slot, 6:7, : 3 * width] = jnp.sum(qkv_io[slot].astype(F32), axis=0, keepdims=True)
    both = grad_a * gain_a[...].astype(F32) + grad_b * gain_b[...].astype(F32)
    inner = jnp.mean(both * xhat, axis=-1, keepdims=True)
    gx = gy_out[slot].astype(F32) + scale * (both - jnp.mean(both, axis=-1, keepdims=True) - xhat * inner)
    gx_out[...] = gx.astype(BF16)


def forward_first_kernel(tick, lengths, *refs):
    count = 17
    sources, held, outs, sems = refs[:count], refs[count : 2 * count], refs[2 * count : -1], refs[-1]
    copies = []
    waits = {}

    def fetch(name, part, index, at):
        source, target = (sources[index], held[index]) if at is None else (sources[index].at[at], held[index].at[at])
        copy = pltpu.make_async_copy(source, target, sems.at[len(copies)])
        copies.append(copy)
        waits.setdefault((name, part), []).append(copy)

    (own, gain_a, shift_a, gain_b, shift_b, wqkv, bqkv, wp, bp, wu, bu, wd, bd, same, later, earlier, _) = range(count)
    width = sources[wp].shape[1]
    units = sources[wu].shape[2]
    pairs = width // (2 * HEAD)
    groups = width // LANES
    for index in (own, gain_a, shift_a, gain_b, shift_b, bqkv, bp, bu, bd, same, later, earlier):
        fetch("small", 0, index, None)
    for pair in range(pairs):
        if pair * groups % pairs == 0:
            group = pair * groups // pairs
            for block in range(3):
                fetch("qkv", group, wqkv, (slice(None), slice(None), pl.ds(block * width + group * LANES, LANES)))
        fetch("up", pair, wu, (slice(None), slice(None), pl.ds(pair * (units // pairs), units // pairs)))
    fetch("rest", 0, wp, None)
    fetch("rest", 0, wd, None)
    for copy in copies:
        copy.start()

    def ready(name, part):
        for copy in waits[(name, part)]:
            copy.wait()

    section = lax.axis_index("section")
    slots = held[own].shape[0]
    slot = jnp.clip(tick - section, 0, slots - 1)
    forward_body(slot, lengths[slot].astype(F32), lambda: held[own][slot], ready, *held[:-1], *outs)


def backward_body(
    slot, gy_source, x_in, gain_a, gain_b, wqkv, wp, wu, wd, same, later, earlier,
    pt_in, gx_out, qkv_io, slope_io, gy_out, vec_out,
):
    rows, width = gx_out.shape
    units = wu.shape[2]
    pairs = width // (2 * HEAD)
    chunk = units // pairs
    gy_out[slot] = gy_source()
    lane = lax.broadcasted_iota(jnp.int32, (128, 2 * HEAD), 1)
    tables = (same[...], later[...], earlier[...])
    per = LANES // (2 * HEAD)
    for pair in range(pairs):
        if pair % per == 0:
            gm_group = dot_nt(gy_out[slot], wp[0, pair * 2 * HEAD : pair * 2 * HEAD + LANES, :]).astype(BF16)
            group_q, group_k = [], []
        span, span_k, span_v = (slice(b * width + pair * 2 * HEAD, b * width + (pair + 1) * 2 * HEAD) for b in range(3))
        gm = gm_group[:, (pair % per) * 2 * HEAD : (pair % per + 1) * 2 * HEAD]
        gv_sum, gk_sum, gq_blocks = None, None, []
        for block, start in enumerate(range(0, rows, 128)):
            keys = start + 128
            gm2 = heads_apart(gm[start:keys], lane)
            q2 = heads_apart(qkv_io[slot, start:keys, span], lane)
            pt = pt_in[slot, pair, probs_rows(block)]
            weighted = pt.astype(F32) * dot_nt(qkv_io[slot, :keys, span_v], gm2)
            inner = jnp.sum(weighted, axis=0, keepdims=True)
            gs = (weighted - pt.astype(F32) * inner).astype(BF16)
            gv_part = dot(pt, gm2)
            gk_part = dot(gs, q2)
            gq_part = dot_tn(gs, qkv_io[slot, :keys, span_k])
            gq_blocks.append(jnp.where(lane < HEAD, gq_part[:128], gq_part[128:]))
            if gv_sum is None:
                gv_sum, gk_sum = gv_part, gk_part
            else:
                gv_sum = jnp.concatenate([gv_sum + gv_part[:start], gv_part[start:]], axis=0)
                gk_sum = jnp.concatenate([gk_sum + gk_part[:start], gk_part[start:]], axis=0)
        qkv_io[slot, :, span_v] = gv_sum.astype(BF16)
        group_q.append(jnp.concatenate(gq_blocks, axis=0))
        group_k.append(gk_sum)
        if pair % per == per - 1:
            low = pair // per * LANES
            gq = turned(jnp.concatenate(group_q, axis=1) * (HEAD**-0.5), *tables, -1)
            qkv_io[slot, :, low : low + LANES] = gq.astype(BF16)
            gk = turned(jnp.concatenate(group_k, axis=1), *tables, -1)
            qkv_io[slot, :, width + low : width + low + LANES] = gk.astype(BF16)
        at = slice(pair * chunk, pair * chunk + chunk)
        slope_io[slot, :, at] = (dot_nt(gy_out[slot], wd[0, at, :]) * slope_io[slot, :, at].astype(F32)).astype(BF16)
    grad_b = dot_nt(slope_io[slot], wu[0])
    grad_a = dot_nt(qkv_io[slot], wqkv[0])
    xhat, scale = normalised(x_in[slot].astype(F32))
    norm_terms = (grad_a * xhat, grad_a, grad_b * xhat, grad_b, gy_out[slot].astype(F32))
    for row, terms in enumerate(norm_terms):
        vec_out[slot, row : row + 1, :width] = jnp.sum(terms, axis=0, keepdims=True)
    vec_out[slot, 5:6, :] = jnp.sum(slope_io[slot].astype(F32), axis=0, keepdims=True)
    vec_out[slot, 6:7, : 3 * width] = jnp.sum(qkv_io[slot].astype(F32), axis=0, keepdims=True)
    both = grad_a * gain_a[...].astype(F32) + grad_b * gain_b[...].astype(F32)
    inner = jnp.mean(both * xhat, axis=-1, keepdims=True)
    gx = gy_out[slot].astype(F32) + scale * (both - jnp.mean(both, axis=-1, keepdims=True) - xhat * inner)
    gx_out[...] = gx.astype(BF16)


VM = pl.BlockSpec(memory_space=pltpu.VMEM)
HBM = pl.BlockSpec(memory_space=pl.ANY)


def call(kernel, operands, out_shape, name, kept=(), scratch=(), flops=1 << 20, after=()):
    count = len(operands)
    after = list(after)

    def body(*refs):
        kernel(*refs[:count], *refs[count + len(kept) + len(after) :])

    return pl.pallas_call(
        body,
        in_specs=[pl.BlockSpec(memory_space=pltpu.SMEM) if o.dtype == jnp.int32 else VM for o in operands] + [VM] * len(kept) + [HBM] * len(after),
        out_specs=[VM] * (len(kept) + len(out_shape)),
        out_shape=[pltpu.VMEM(array.shape, array.dtype) for array in kept] + list(out_shape),
        input_output_aliases={count + i: i for i in range(len(kept))},
        scratch_shapes=list(scratch),
        compiler_params=pltpu.CompilerParams(vmem_limit_bytes=VMEM_BYTES),
        cost_estimate=pl.CostEstimate(flops=flops, bytes_accessed=1 << 16, transcendentals=0),
        name=name,
    )(*operands, *[pltpu.with_memory_space_constraint(array, pltpu.VMEM) for array in kept], *after)


def shape_of(array):
    return jax.ShapeDtypeStruct(array.shape, array.dtype)


def forward_shapes(local_rows, params):
    slots, rows, width = local_rows.shape
    units = params[8].shape[2]
    blocks = rows // 128
    probs = (slots, width // (2 * HEAD), 128 * (blocks * (blocks + 1) // 2), 2 * 128)
    columns = [width, width, width, 3 * width, None, width, units, units]
    return [jax.ShapeDtypeStruct((rows, width), BF16)] + [
        pltpu.VMEM(probs if n is None else (slots, rows, n), BF16) for n in columns
    ]


def forward_first(lengths, local_rows, params, tables):
    (gain_a, shift_a, w_qkv, b_qkv, w_proj, b_proj, gain_b, shift_b, w_up, b_up, w_down, b_down) = params
    held = [local_rows, gain_a, shift_a, gain_b, shift_b, w_qkv, b_qkv, w_proj, b_proj, w_up, b_up, w_down, b_down] + list(tables)
    shapes = [shape_of(array) for array in held] + forward_shapes(local_rows, params)

    def kernel(lengths_ref, *refs):
        count = len(held)
        forward_first_kernel(0, lengths_ref, *refs[:count], None, *refs[count : 2 * count], None, *refs[2 * count :])

    outs = pl.pallas_call(
        kernel,
        in_specs=[pl.BlockSpec(memory_space=pltpu.SMEM)] + [pl.BlockSpec(memory_space=pltpu.HBM)] * len(held),
        out_specs=[VM] * len(shapes),
        out_shape=shapes,
        scratch_shapes=[pltpu.SemaphoreType.DMA((40,))],
        compiler_params=pltpu.CompilerParams(vmem_limit_bytes=FIRST_VMEM_BYTES),
        cost_estimate=pl.CostEstimate(flops=1 << 20, bytes_accessed=1 << 16, transcendentals=0),
        name="layer_forward_first",
    )(lengths, *[pltpu.with_memory_space_constraint(array, pltpu.HBM) for array in held])
    count = len(held)
    return outs[count], outs[count + 1 :], outs[:count]


def swap(shard, bit, count):
    return lax.ppermute(shard, "dp", [(i, i ^ (1 << bit)) for i in range(count)])


def parted(values, position, mine):
    count = values.shape[0]
    shaped = values.reshape((count >> (position + 1), 2, 1 << position) + values.shape[1:])
    out = []
    for side in (mine, 1 - mine):
        piece = lax.dynamic_index_in_dim(shaped, side, axis=1, keepdims=False)
        out.append(piece.reshape((count // 2,) + values.shape[1:]))
    return out


def halving_sum(keep, send, order, count, bits, final):
    left = sorted(order)
    for number, bit in enumerate(order):
        left.remove(bit)
        arrived = swap(send, bit, count)
        if number + 1 == len(order):
            return (keep.astype(F32) + arrived.astype(F32)).astype(final)[0]
        position = left.index(order[number + 1])
        keep_a, send_a = parted(keep, position, bits[order[number + 1]])
        keep_b, send_b = parted(arrived, position, bits[order[number + 1]])
        send = (send_a.astype(F32) + send_b.astype(F32)).astype(send_a.dtype)
        keep = (keep_a.astype(F32) + keep_b.astype(F32)).astype(send_a.dtype)


def plain_grads(left, right, count):
    rows = left.shape[0] * left.shape[1]
    product = lax.dot_general(
        left.reshape(rows, -1), right.reshape(rows, -1), (((0,), (0,)), ((), ())), preferred_element_type=F32
    ).astype(BF16)
    return product.reshape(count, product.shape[0] // count, product.shape[1])


def partner_forward(s, half, length, rows_of, gain_a, shift_a, gain_b, shift_b, wqkv, bqkv, wu, bu, tables, nap, nbp, qkvp, ptp, mixedp, hidp, slopep):
    lanes = mixedp.shape[2]
    xhat, _ = normalised(rows_of(s).astype(F32))
    nap[s] = (xhat * gain_a[...].astype(F32) + shift_a[...].astype(F32)).astype(BF16)
    nbp[s] = (xhat * gain_b[...].astype(F32) + shift_b[...].astype(F32)).astype(BF16)
    forward_units(
        s, length, lambda name, part: None, nap, nbp, wqkv, bqkv, wu, bu, tables, qkvp, ptp, mixedp, hidp, slopep,
        half * lanes, half * hidp.shape[2], lanes,
    )


def partner_backward(s, half, gy, wp, wd, tables, ptp, qkvp, slopep):
    lanes = qkvp.shape[2] // 3
    backward_units(s, gy, wp, wd, tables, ptp, qkvp, slopep, half * lanes, half * slopep.shape[2], lanes)


SUM_FLOPS = 6 << 30
ORDERS = {"down": (0, 1, 2), "up": (1, 2, 0), "attn": (2, 0, 1)}


def dp_bit(bit):
    return (lax.axis_index("dp") >> bit) & 1


def eighth_row(chunk, order, rows):
    first, second, third = ((chunk >> bit) & 1 for bit in order)
    return ((first ^ dp_bit(order[0])) * 4 + second * 2 + third) * rows


def row_slice(start, rows):
    return pl.ds(pl.multiple_of(start, 16), rows)


def flat_rows(ref, at=slice(None)):
    values = ref[:, :, at]
    return values.reshape(values.shape[0] * values.shape[1], values.shape[2])


def ones_dot(values):
    return dot(jnp.ones((16, values.shape[0]), BF16), values)[:8]


def sixteenths(ref, left, order, tokens_from):
    turned_ref = flat_rows(ref).T
    low = turned_ref.shape[0] // 16
    for chunk in range(16):
        start = eighth_row(chunk & 7, order, 2 * low) + (chunk >> 3) * low
        left[row_slice(start, low), tokens_from : tokens_from + turned_ref.shape[1]] = turned_ref[chunk * low : chunk * low + low]


def eighths(turned_rows, left, order, tokens_from):
    low = turned_rows.shape[0] // 8
    for chunk in range(8):
        left[row_slice(eighth_row(chunk, order, low), low), tokens_from : tokens_from + turned_rows.shape[1]] = turned_rows[
            chunk * low : chunk * low + low
        ]


def own_group_kernel(nb, na, gu, gp, hidden, mixed, gy, vec, up_own, attn_own, down_own, left, left_mixed, left_down):
    half = dp_bit(3)
    units, rows = up_own.shape[2], up_own.shape[1]
    width, lanes = na.shape[2], attn_own.shape[2] // 3
    low = rows // 2
    sixteenths(nb, left, ORDERS["up"], 0)
    for start in range(0, units, 512):
        product = dot(left[...], flat_rows(gu, some(half * units + start, 512)))
        up_own[:, :, start : start + 512] = product.reshape(8, rows, 512)
    order = ORDERS["attn"]
    sixteenths(na, left, order, 0)
    for block in range(3):
        product = dot(left[...], flat_rows(gp, some(block * width + half * lanes, lanes)))
        attn_own[:, :rows, block * lanes : block * lanes + lanes] = product.reshape(8, rows, lanes)
    grad = flat_rows(gy)
    eighths(flat_rows(mixed, some(half * lanes, lanes)).T, left_mixed, order, 0)
    attn_own[:, rows:, :width] = dot(left_mixed[...], grad).reshape(8, low, width)
    row_index = lax.broadcasted_iota(jnp.int32, (16, lanes), 0)
    totals = vec[0] + vec[1]
    sums = [totals[i : i + 1, :width] for i in range(5)] + [totals[5:6], totals[6:7, : 3 * width]]
    for chunk in range(16):
        block = jnp.zeros((16, lanes), F32)
        for row, values in enumerate(sums):
            size = values.shape[1] // 16
            piece = jnp.concatenate([values[:, chunk * size : chunk * size + size], jnp.zeros((1, lanes - size), F32)], axis=1)
            block = jnp.where(row_index == row, jnp.broadcast_to(piece, (16, lanes)), block)
        place_at = slice(rows + (chunk >> 3) * 16, rows + (chunk >> 3) * 16 + 16)
        attn_own[eighth_row(chunk & 7, order, 1), place_at, width:] = block
    eighths(flat_rows(hidden, some(half * units, units)).T, left_down, ORDERS["down"], 0)
    size = units // 4
    for part in range(4):
        product = dot(left_down[part * size : part * size + size], grad)
        down_own[part * 2 : part * 2 + 2] = product.reshape(2, size // 2, width)


def up_group_kernel(nbp, gup, up_own, keep, send, left):
    units = gup.shape[2]
    sixteenths(nbp, left, ORDERS["up"], 0)
    rows = left.shape[0] // 8
    for low in range(0, units, 512):
        at = slice(low, low + 512)
        product = (up_own[:, :, at] + dot(left[...], flat_rows(gup, at)).reshape(8, rows, 512)).astype(BF16)
        keep[:, :, at] = product[:4]
        send[:, :, at] = product[4:]


def attn_group_kernel(nap, gpp, mixedp, gyp_of, attn_own, keep, send, left, left_mixed):
    lanes = mixedp.shape[2]
    width = nap.shape[2]
    order = ORDERS["attn"]
    sixteenths(nap, left, order, 0)
    rows = left.shape[0] // 8
    for block in range(3):
        at = slice(block * lanes, block * lanes + lanes)
        product = (attn_own[:, :rows, at] + dot(left[...], flat_rows(gpp, at)).reshape(8, rows, lanes)).astype(BF16)
        keep[:, :rows, at] = product[:4]
        send[:, :rows, at] = product[4:]
    eighths(flat_rows(mixedp).T, left_mixed, order, 0)
    other_gy = jnp.concatenate([gyp_of(s) for s in range(nap.shape[0])], axis=0)
    low = left_mixed.shape[0] // 8
    product = (attn_own[:, rows:, :width] + dot(left_mixed[...], other_gy).reshape(8, low, width)).astype(BF16)
    keep[:, rows:, :width] = product[:4]
    send[:, rows:, :width] = product[4:]
    keep[:, rows:, width:] = attn_own[:4, rows:, width:].astype(BF16)
    send[:, rows:, width:] = attn_own[4:, rows:, width:].astype(BF16)


def down_group_kernel(hidp, gyp_of, down_own, keep, send, left):
    units = hidp.shape[2]
    eighths(flat_rows(hidp).T, left, ORDERS["down"], 0)
    other_gy = jnp.concatenate([gyp_of(s) for s in range(hidp.shape[0])], axis=0)
    size = units // 2
    for side, out in enumerate((keep, send)):
        product = dot(left[side * size : side * size + size], other_gy).reshape(out.shape)
        out[...] = (down_own[side * 4 : side * 4 + 4] + product).astype(BF16)


def plus(left, right):
    return left.astype(F32) + right.astype(F32)


def add_kernel(bit, keep, arrived, keep_out, send_out):
    size = keep_out.shape[0]
    mine = dp_bit(bit) * size
    keep_out[...] = plus(keep[pl.ds(mine, size)], arrived[pl.ds(mine, size)]).astype(BF16)
    send_out[...] = plus(keep[pl.ds(size - mine, size)], arrived[pl.ds(size - mine, size)]).astype(BF16)


def swap_over(shard, bit, sections=(0, 1)):
    count = lax.axis_size("dp")
    pairs = [(s * count + i, s * count + (i ^ (1 << bit))) for s in sections for i in range(count)]
    return lax.ppermute(shard, ("section", "dp"), pairs)


def cross_swap(shard, section, bit):
    count = lax.axis_size("dp")
    return lax.ppermute(shard, ("section", "dp"), [(section * count + i, (1 - section) * count + (i ^ (1 << bit))) for i in range(count)])


def struct(*shape, dtype=BF16):
    return jax.ShapeDtypeStruct(shape, dtype)


def halved(parts, order, stage, name, after=()):
    keep, send = parts
    arrived = swap_over(send, order[stage])
    shape = (keep.shape[0] // 2,) + keep.shape[1:]
    return call(functools.partial(add_kernel, order[stage + 1]), [keep, arrived], [struct(*shape)] * 2, name, after=after, flops=SUM_FLOPS)


def down_sum_kernel(keep, arrived, out):
    out[...] = plus(keep[0], arrived[0])


def halves_sum_kernel(up_keep, up_arrived, attn_keep, attn_arrived, up_mine, qkv_mine, small_mine, proj, other):
    half = dp_bit(3)
    low = up_mine.shape[0]
    units = up_mine.shape[1]
    width = proj.shape[1]
    mine, theirs = row_slice(half * low, low), row_slice((1 - half) * low, low)
    up_mine[...] = plus(up_keep[0, mine], up_arrived[0, mine])
    other[:, :units] = plus(up_keep[0, theirs], up_arrived[0, theirs]).astype(BF16)
    qkv_mine[...] = plus(attn_keep[0, mine], attn_arrived[0, mine])
    other[:, units : units + qkv_mine.shape[1]] = plus(attn_keep[0, theirs], attn_arrived[0, theirs]).astype(BF16)
    proj[...] = plus(attn_keep[0, 2 * low :, :width], attn_arrived[0, 2 * low :, :width])
    mine, theirs = row_slice(2 * low + half * 16, 16), row_slice(2 * low + (1 - half) * 16, 16)
    small_mine[...] = plus(attn_keep[0, mine, width:], attn_arrived[0, mine, width:])
    small = plus(attn_keep[0, theirs, width:], attn_arrived[0, theirs, width:]).astype(BF16)
    for part in range(small.shape[1] // 128):
        other[part * 16 : part * 16 + 16, other.shape[1] - 128 :] = small[:, part * 128 : part * 128 + 128]


def joined_kernel(up_mine, qkv_mine, small_mine, other, up, qkv, *vectors):
    half = dp_bit(3)
    low = up_mine.shape[0]
    units = up_mine.shape[1]
    lanes = qkv_mine.shape[1] // 3
    up[:, some(half * units, units)] = up_mine[...]
    up[:, some((1 - half) * units, units)] = other[:, :units].astype(F32)
    for block in range(3):
        at = slice(block * lanes, block * lanes + lanes)
        qkv[:, some((2 * block + half) * lanes, lanes)] = qkv_mine[:, at]
        qkv[:, some((2 * block + 1 - half) * lanes, lanes)] = other[:, units + block * lanes : units + (block + 1) * lanes].astype(F32)
    rest = other[:, other.shape[1] - 128 :].astype(F32)
    small = small_mine[...] + jnp.concatenate([rest[part : part + 16] for part in range(0, low, 16)], axis=1)
    for row, out in zip((0, 1, 2, 3, 4, 4, 5, 6), vectors):
        out[...] = small[row : row + 1, : out.shape[1]]


def paired_gradients(boundary, lengths, params, tables, swapped):
    slots = lengths.shape[0]
    width = boundary.shape[2]
    rows = boundary.shape[1] // slots
    units = params[8].shape[2]
    local_rows = boundary.reshape(slots, rows, width)
    low, tall = width // 16, units // 16
    tokens = slots * rows

    cut = rows + rows // 2 - 16
    length_rows = jnp.broadcast_to(jnp.repeat(lengths.astype(BF16), 8)[:, None], (8 * slots, width))
    other_a = swap_over(jnp.concatenate([boundary[0, :cut], length_rows], axis=0), 3, (0,))
    other_b = swap_over(boundary[0, cut:], 3, (0,))
    other_gy = swap_over(local_rows, 3, (1,))
    result_0, saved, held = forward_first(lengths, local_rows, params, tables)
    own, gain_a, shift_a, gain_b, shift_b, w_qkv, b_qkv, w_proj, b_proj, w_up, b_up, w_down, b_down, *tabs = held
    arrived_1 = lax.ppermute(result_0, "section", swapped)
    count = len(held)

    def forward_both(lengths_ref, arriving, *refs):
        section = lax.axis_index("section")
        slot = 1 - section
        inputs = lambda: jnp.where(section == 0, refs[0][slot], arriving[...])
        outs = refs[count:]
        forward_body(slot, lengths_ref[slot].astype(F32), inputs, lambda name, part: None, *refs[:count], outs[-1], *outs[:-1])

    *saved, result_1 = call(forward_both, [lengths, arrived_1, *held], [struct(rows, width)], "forward_1", kept=saved, after=[other_a])
    arrived_2 = lax.ppermute(result_1, "section", swapped)

    def forward_last(lengths_ref, arriving, *refs):
        slot = slots - 1
        *kept, y, x_long = refs[count:]

        @pl.when(lax.axis_index("section") == 1)
        def _():
            x_long[:rows] = kept[0][0]
            x_long[rows : 2 * rows] = arriving[...]
            for s in range(slots):
                at = slots * rows + 8 * s
                x_long[at : at + 8] = jnp.full((8, width), lengths_ref[s].astype(F32), F32).astype(BF16)
            forward_body(
                slot, lengths_ref[slot].astype(F32), lambda: arriving[...], lambda name, part: None, *refs[:count], y, *kept
            )

    *saved, result_2, x_long = call(
        forward_last, [lengths, arrived_2, *held], [struct(rows, width), struct(slots * rows + 8 * slots, width)], "forward_2",
        kept=saved, after=[other_b],
    )
    x_s, na_s, nb_s, qkv_s, pt_s, mixed_s, hidden_s, slope_s = saved
    partner_x = swap_over(x_long, 3, (1,))

    back_operands = [x_s, gain_a, gain_b, w_qkv, w_proj, w_up, w_down, *tabs, pt_s]
    back_count = len(back_operands)
    shared_operands = [gain_a, shift_a, gain_b, shift_b, w_qkv, b_qkv, w_up, b_up, *tabs]
    shared_count = len(shared_operands)
    shared_shapes = [
        pltpu.VMEM(shape, BF16)
        for shape in (
            (slots, rows, width), (slots, rows, width), (slots, rows, 3 * width // 2), (slots, pt_s.shape[1] // 2) + pt_s.shape[2:],
            (slots, rows, width // 2), (slots, rows, units // 2), (slots, rows, units // 2),
        )
    ]

    def share(s, length, x_rows, refs, outs):
        weights, tabs_refs = refs[:-3], refs[-3:]
        partner_forward(s, dp_bit(3), length.astype(F32), lambda s: x_rows, *weights, tuple(t[...] for t in tabs_refs), *outs)

    def backward_first(own_ref, ref_a, ref_b, *refs):
        operands, shared, (qkv_io, slope_io, gy, vec, gx, *outs) = (
            refs[:back_count], refs[back_count : back_count + shared_count], refs[back_count + shared_count :],
        )
        section = lax.axis_index("section")

        @pl.when(section == 1)
        def _():
            backward_body(0, lambda: own_ref[0], *operands, gx, qkv_io, slope_io, gy, vec)

        @pl.when(section == 0)
        def _():
            x_rows = (ref_a[:rows], jnp.concatenate([ref_a[rows:cut], ref_b[...]], axis=0))
            for s in range(slots):
                share(s, ref_a[cut + 8 * s : cut + 8 * s + 1, : 2 * 128], x_rows[s], shared, outs)

    outs = call(
        backward_first, [own, other_a, other_b, *back_operands, *shared_operands],
        [pltpu.VMEM((slots, rows, width), BF16), pltpu.VMEM((slots, 8, units), F32), struct(rows, width)] + shared_shapes,
        "backward_0", kept=[qkv_s, slope_s],
    )
    grads, back_0, shared = outs[:4], outs[4], outs[5:]
    arrived_4 = lax.ppermute(back_0, "section", swapped)
    partner_4 = swap_over(arrived_4, 3, (0,))

    def backward_both(own_ref, arriving, *refs):
        section = lax.axis_index("section")
        outs = refs[back_count:]
        source = lambda: jnp.where(section == 0, arriving[...], own_ref[section])
        backward_body(section, source, *refs[:back_count], outs[-1], *outs[:-1])

    *grads, back_1 = call(backward_both, [own, arrived_4, *back_operands], [struct(rows, width)], "backward_1", kept=grads, after=[other_gy])
    arrived_5 = lax.ppermute(back_1, "section", swapped)

    def backward_last(arriving, other_ref, *refs):
        operands, shared_in, (qkv_io, slope_io, gy, vec, *outs) = (
            refs[:back_count], refs[back_count : back_count + shared_count], refs[back_count + shared_count :],
        )
        section = lax.axis_index("section")

        @pl.when(section == 0)
        def _():
            backward_body(slots - 1, lambda: arriving[...], *operands, outs[-2], qkv_io, slope_io, gy, vec)
            outs[-1][...] = arriving[...]

        @pl.when(section == 1)
        def _():
            for s in range(slots):
                at = slots * rows + 8 * s
                share(s, other_ref[at : at + 1, : 2 * 128], other_ref[s * rows : s * rows + rows], shared_in, outs[:-2])

    outs = call(
        backward_last, [arrived_5, partner_x, *back_operands, *shared_operands], [struct(rows, width)] * 2,
        "backward_2", kept=[*grads, *shared],
    )
    gp_s, gu_s, gy_s, vec_s, nap, nbp, qkvp, ptp, mixedp, hidp, slopep, back_2, last_gy = outs

    partner_5 = swap_over(last_gy, 3, (0,))
    up_own, attn_own, down_own = call(
        own_group_kernel, [nb_s, na_s, gu_s, gp_s, hidden_s, mixed_s, gy_s, vec_s],
        [struct(8, 2 * low, units // 2, dtype=F32), struct(8, 3 * low, 3 * width // 2, dtype=F32), struct(8, tall, width, dtype=F32)], "own_grads",
        scratch=[pltpu.VMEM((width, tokens), BF16), pltpu.VMEM((width // 2, tokens), BF16), pltpu.VMEM((units // 2, tokens), BF16)],
    )

    gpp, gup = qkvp, slopep
    gyp_s = []
    for s, partner_gy in enumerate((partner_4, partner_5)):

        def backward_shared(other_ref, partner_ref, wp, wd, same, later, earlier, ptp_ref, qkvp_ref, slopep_ref, gyp, s=s):
            gyp[...] = jnp.where(lax.axis_index("section") == 0, partner_ref[...], other_ref[s])
            tables_in = (same[...], later[...], earlier[...])
            partner_backward(s, dp_bit(3), lambda: gyp[...], wp, wd, tables_in, ptp_ref, qkvp_ref, slopep_ref)

        gpp, gup, gyp = call(
            backward_shared, [other_gy, partner_gy, w_proj, w_down, *tabs, ptp], [struct(rows, width)], f"backward_shared_{s}",
            kept=[gpp, gup], after=[up_own],
        )
        gyp_s.append(gyp)

    def group(rows_of_eighth, columns):
        return [struct(4, rows_of_eighth, columns)] * 2

    up = call(
        up_group_kernel, [nbp, gup, up_own], group(2 * low, units // 2), "up_grads", scratch=[pltpu.VMEM((width, tokens), BF16)]
    )

    def attn_group(nap_ref, gpp_ref, mixedp_ref, gyp_a, gyp_b, *refs):
        attn_group_kernel(nap_ref, gpp_ref, mixedp_ref, lambda s: (gyp_a, gyp_b)[s][...], *refs)

    attn = call(
        attn_group, [nap, gpp, mixedp, *gyp_s, attn_own], group(3 * low, 3 * width // 2), "attn_grads",
        scratch=[pltpu.VMEM((width, tokens), BF16), pltpu.VMEM((width // 2, tokens), BF16)], after=up[:1],
    )

    def down_group(hidp_ref, gyp_a, gyp_b, *refs):
        down_group_kernel(hidp_ref, lambda s: (gyp_a, gyp_b)[s][...], *refs)

    down = call(
        down_group, [hidp, *gyp_s, down_own], group(tall, width), "down_grads",
        scratch=[pltpu.VMEM((units // 2, tokens), BF16)], after=attn[:1],
    )

    up = halved(up, ORDERS["up"], 0, "up_sum_1", after=down[:1])
    attn = halved(attn, ORDERS["attn"], 0, "attn_sum_1", after=up[:1])
    down = halved(down, ORDERS["down"], 0, "down_sum_1", after=attn[:1])
    up = halved(up, ORDERS["up"], 1, "up_sum_2", after=down[:1])
    attn = halved(attn, ORDERS["attn"], 1, "attn_sum_2", after=up[:1])
    down = halved(down, ORDERS["down"], 1, "down_sum_2", after=attn[:1])
    up_last, attn_last = swap_over(up[1], ORDERS["up"][2]), swap_over(attn[1], ORDERS["attn"][2])
    up_mine, qkv_mine, small_mine, proj, others = call(
        halves_sum_kernel, [up[0], up_last, attn[0], attn_last],
        [struct(low, units // 2, dtype=F32), struct(low, 3 * width // 2, dtype=F32), struct(16, width // 2, dtype=F32),
         struct(low, width, dtype=F32), struct(low, units // 2 + 3 * width // 2 + 128)], "up_qkv_sum_3", after=down[:1],
    )
    (down_out,) = call(down_sum_kernel, [down[0], swap_over(down[1], ORDERS["down"][2])], [struct(tall, width, dtype=F32)], "down_sum_3")
    vectors = [low] * 6 + [tall, 3 * low]
    up_out, qkv_out, *vectors = call(
        joined_kernel, [up_mine, qkv_mine, small_mine, swap_over(others, 3)],
        [struct(low, units, dtype=F32), struct(low, 3 * width, dtype=F32)] + [struct(1, size, dtype=F32) for size in vectors], "up_qkv_joined",
    )
    joined = jnp.where(
        lax.axis_index("section") == 0, jnp.concatenate([back_1, back_2], axis=0), jnp.concatenate([result_1, result_2], axis=0)
    )
    gain_a, shift_a, gain_b, shift_b, bias_proj, bias_down, bias_up, bias_qkv = (vector[0] for vector in vectors)
    return joined, gain_a, shift_a, qkv_out, bias_qkv, proj, bias_proj, gain_b, shift_b, up_out, bias_up, down_out, bias_down


def plain_gradients(boundary, lengths, params, tables, swapped, bits):
    count = lax.axis_size("dp")
    slots = lengths.shape[0]
    width = boundary.shape[2]
    rows = boundary.shape[1] // slots
    units = params[8].shape[2]
    ticks = slots + 1
    result, saved, held = forward_first(lengths, boundary.reshape(slots, rows, width), params, tables)
    own, gain_a, shift_a, gain_b, shift_b, w_qkv, b_qkv, w_proj, b_proj, w_up, b_up, w_down, b_down, *tabs = held
    held_count = len(held)
    finals = [result]
    for t in range(1, ticks):
        arriving = lax.ppermute(result, "section", swapped)

        def forward_step(lengths_ref, arriving_ref, *refs, tick=t):
            section = lax.axis_index("section")
            slot = jnp.clip(tick - section, 0, slots - 1)
            inputs = lambda: jnp.where(section == 0, refs[0][slot], arriving_ref[...])
            outs = refs[held_count:]
            forward_body(slot, lengths_ref[slot].astype(F32), inputs, lambda name, part: None, *refs[:held_count], outs[-1], *outs[:-1])

        *saved, result = call(forward_step, [lengths, arriving, *held], [struct(rows, width)], "forward", kept=saved)
        finals.append(result)
    x_s, na_s, nb_s, qkv_s, pt_s, mixed_s, hidden_s, slope_s = saved
    operands = [x_s, gain_a, gain_b, w_qkv, w_proj, w_up, w_down, *tabs, pt_s]
    grads = [qkv_s, slope_s]
    input_grads = []
    arriving = own[0]
    for t in range(ticks):

        def backward_step(own_ref, arriving_ref, *refs, tick=t):
            section = lax.axis_index("section")
            slot = tick - 1 + section
            *io, gx_out = refs[len(operands) :]

            @pl.when((slot >= 0) & (slot < slots))
            def _():
                source = lambda: jnp.where(section == 0, arriving_ref[...], own_ref[slot])
                backward_body(slot, source, *refs[: len(operands)], gx_out, *io)

        shapes = [pltpu.VMEM((slots, rows, width), BF16), pltpu.VMEM((slots, 8, units), F32)] if t == 0 else []
        *grads, result = call(backward_step, [own, arriving, *operands], shapes + [struct(rows, width)], "backward", kept=grads)
        input_grads.append(result)
        if t + 1 < ticks:
            arriving = lax.ppermute(result, "section", swapped)
    gp_s, gu_s, gy_s, vec_s = grads
    order = list(range(len(bits)))

    def summed(full):
        keep, send = parted(full, 0, bits[0])
        return halving_sum(keep, send, order, count, bits, F32)

    both = jnp.concatenate([plain_grads(hidden_s, gy_s, count), plain_grads(mixed_s, gy_s, count)], axis=1)
    down, up, qkv = summed(both), summed(plain_grads(nb_s, gu_s, count)), summed(plain_grads(na_s, gp_s, count))
    tall = units // count
    totals = jnp.sum(vec_s, axis=0)
    sums = [totals[i, :width] for i in range(5)] + [totals[5], totals[6, : 3 * width]]
    return finals[1:], input_grads[1:], sums, down[:tall], down[tall:], up, qkv


def per_device(boundary, lengths, *params):
    section = lax.axis_index("section")
    count = lax.axis_size("dp")
    bits = [(lax.axis_index("dp") >> b) & 1 for b in range(count.bit_length() - 1)]
    slots = lengths.shape[0]
    width = boundary.shape[2]
    units = params[8].shape[2]
    tables = [jnp.asarray(table) for table in rotary_lanes(boundary.shape[1] // slots, 2 * HEAD)]
    swapped = [(0, 1), (1, 0)]
    if count == 16 and slots == 2 and width % 768 == 0:
        results = paired_gradients(boundary, lengths, params, tables, swapped)
        return tuple(result[None] for result in results)
    finals, input_grads, sums, down, proj, up, qkv = plain_gradients(
        boundary, lengths, params, tables, swapped, bits
    )
    small = jnp.concatenate([piece.reshape(count, -1) for piece in sums], axis=1)
    small = halving_sum(*parted(small, 0, bits[0]), list(range(len(bits))), count, bits, F32)
    low, tall = width // count, units // count
    gain_a, shift_a, gain_b, shift_b, bias_y, bias_up, bias_qkv = jnp.split(small, np.cumsum([low] * 5 + [tall]), axis=0)
    joined = jnp.where(section == 0, jnp.concatenate(input_grads, axis=0), jnp.concatenate(finals, axis=0))
    results = (joined, gain_a, shift_a, qkv, bias_qkv, proj, bias_y, gain_b, shift_b, up, bias_up, down, bias_y)
    return tuple(result[None] for result in results)


def solution(mesh):
    split = P("section", "dp")
    deep = P("section", "dp", None)
    flat, matrix = P("section", None), P("section", None, None)
    return jax.shard_map(
        per_device,
        mesh=mesh,
        in_specs=(deep, P("dp"), flat, flat, matrix, flat, matrix, flat, flat, flat, matrix, flat, matrix, flat),
        out_specs=(deep, split, split, deep, split, deep, split, split, split, deep, split, deep, split),
        check_vma=False,
    )
```
